32 devices in a mesh: seq: 8 (over z, x), batch: 4 (over y, core).
Axes of the slice: x: 2, y: 2, z: 4, core: 2. Of those that a mesh axis runs over, the one named last changes fastest.
Arguments:
- inputs: bfloat16 [8, 4096, 768], P('batch', 'seq'), may hold values from -6 to 6
- global_inputs: bfloat16 [8, 128, 768], P('batch'), may hold values from -6 to 6
- lengths: int32 [8], P('batch'), may hold values from 2048 to 4096, as said below
- first_gain: float32 [768], replicated, may hold values from 0.5 to 1.5
- first_shift: float32 [768], replicated, may hold values from -3 to 3
- qkv_weight: bfloat16 [768, 2304], replicated, may hold values from -0.3125 to 0.3125
- out_weight: bfloat16 [768, 768], replicated, may hold values from -0.875 to 0.875
- second_gain: float32 [768], replicated, may hold values from 0.5 to 1.5
- second_shift: float32 [768], replicated, may hold values from -3 to 3
- inner_weight: bfloat16 [768, 3072], replicated, may hold values from -0.21875 to 0.21875
- inner_bias: float32 [3072], replicated, may hold values from -3 to 3
- outer_weight: bfloat16 [3072, 768], replicated, may hold values from -0.109375 to 0.109375
- output_cotangent: bfloat16 [8, 4096, 768], P('batch', 'seq'), may hold values from -6 to 6
- global_cotangent: bfloat16 [8, 128, 768], P('batch'), may hold values from -6 to 6
Outputs:
- layer_output: bfloat16 [8, 4096, 768], P('batch', 'seq')
- global_output: bfloat16 [8, 128, 768], P('batch')
- input_grad: bfloat16 [8, 4096, 768], P('batch', 'seq')
- global_input_grad: bfloat16 [8, 128, 768], P('batch')
- first_gain_grad: float32 [768], P('seq')
- first_shift_grad: float32 [768], P('seq')
- qkv_weight_grad: float32 [768, 2304], P('seq')
- out_weight_grad: float32 [768, 768], P('seq')
- second_gain_grad: float32 [768], P('seq')
- second_shift_grad: float32 [768], P('seq')
- inner_weight_grad: float32 [768, 3072], P('seq')
- inner_bias_grad: float32 [3072], P('seq')
- outer_weight_grad: float32 [3072, 768], P('seq')
The draws below stay inside these ranges and needn't reach their ends.
Inputs may be any that keep to these rules, and one draw needn't show every extreme that they name: `lengths`: rows come 2 to a batch index; in each such group one row, drawn from the seed, has length exactly 4096, the others any length in the range.
All inputs are finite; a program needn't handle non-finite values.
Results may differ from the reference program's by a relative error of at most 0.015.
Values may be sent and summed in bfloat16 or wider, within the bound.
A program may use at most 320 MiB of HBM per device.

```python
import jax
import jax.numpy as jnp
from jax import lax

D = 768
HEADS = 12
HEAD_DIM = 64
FF = 3072
GLOBALS = 128
BLOCK = 512
SHIFT = 256
ROWS_DEV = 2
ROWS = 8
SEQ = 4096
MIN_LEN = 2048


def draw_lengths(key, part):
    key = jax.random.fold_in(key, 11)
    pick_key, length_key = jax.random.split(key)
    group_count = ROWS // ROWS_DEV
    drawn = jax.random.randint(length_key, (group_count, ROWS_DEV), MIN_LEN, SEQ + 1)
    chosen = jax.random.randint(pick_key, (group_count, 1), 0, ROWS_DEV)
    slots = jnp.arange(ROWS_DEV)[None, :]
    drawn = jnp.where(slots == chosen, SEQ, drawn)
    return drawn.reshape(ROWS).astype(jnp.int32)


def with_spikes(array, stream_key, source, target, parts, factor):
    def block_of(dim):
        return (jnp.arange(array.shape[dim]) // (array.shape[dim] // parts)).reshape((-1,) + (1,) * (array.ndim - 1 - dim))

    near = jax.random.permutation(stream_key, parts)[block_of(target)]
    far = (block_of(target) + parts // 2) % parts
    return jnp.where((block_of(source) == near) | (block_of(source) == far), factor * array, array)


def steps_of(rng, shape, cuts, low, top_value):
    loudness = 1.0
    for position, shards_of in cuts:
        draws = jax.random.uniform(jax.random.fold_in(jax.random.fold_in(rng, 6), position), (shards_of,), jnp.float32, low / len(cuts), top_value / len(cuts))
        loudness = loudness * jnp.repeat(jnp.exp(draws), shape[position] // shards_of).reshape((-1,) + (1,) * (len(shape) - 1 - position))
    return loudness


def bell_draw(key, dims, width, most, cuts=(), kind=jnp.bfloat16):
    result = jax.random.normal(key, dims, jnp.float32) * width
    if len(cuts) > 0:
        result = steps_of(key, dims, cuts, -0.22, 0.18) * result
    return jnp.clip(result, min=-most, max=most).astype(kind)


def gaussian_with(key, extent, width, limit, cuts, heavy, held_as=jnp.bfloat16):
    entries = width * jax.random.normal(key, extent, jnp.float32)
    if cuts:
        entries = entries * steps_of(key, extent, cuts, -0.22, 0.18)
    return jnp.clip(with_spikes(entries, jax.random.fold_in(key, 3), *heavy), -limit, limit).astype(held_as)


def setup_inputs(seed: int = 0) -> dict:
    key_of = jax.random.split(jax.random.key(seed), 15)
    return {
        "inputs": gaussian_with(key_of[0], (ROWS, SEQ, D), 1.0, 6.0, ((0, 4), (1, 8)), (1, 2, 8, 2.0)),
        "global_inputs": bell_draw(key_of[1], (ROWS, GLOBALS, D), 1.0, 6.0, ((0, 4),)),
        "lengths": draw_lengths(jax.random.fold_in(key_of[14], 71), 0),
        "first_gain": jnp.clip(1.0 + 0.1 * jax.random.normal(key_of[3], (D,), jnp.float32), 0.5, 1.5),
        "first_shift": bell_draw(key_of[4], (D,), 0.3, 3.0, (), jnp.float32),
        "qkv_weight": bell_draw(key_of[5], (D, 3 * D), (D // 2) ** -0.5, 0.3125),
        "out_weight": bell_draw(key_of[6], (D, D), (D // 16) ** -0.5, 0.875),
        "second_gain": jnp.clip(1.0 + 0.1 * jax.random.normal(key_of[7], (D,), jnp.float32), 0.5, 1.5),
        "second_shift": bell_draw(key_of[8], (D,), 0.3, 3.0, (), jnp.float32),
        "inner_weight": bell_draw(key_of[9], (D, FF), D ** -0.5, 0.21875),
        "inner_bias": bell_draw(key_of[10], (FF,), 0.3, 3.0, (), jnp.float32),
        "outer_weight": bell_draw(key_of[11], (FF, D), FF ** -0.5, 0.109375),
        "output_cotangent": gaussian_with(key_of[12], (ROWS, SEQ, D), 1.0, 6.0, ((0, 4), (1, 8)), (1, 2, 8, 2.0)),
        "global_cotangent": bell_draw(key_of[13], (ROWS, GLOBALS, D), 1.0, 6.0, ((0, 4),)),
    }


EPS = 1e-05
NEG = -1e+30

@jax.custom_vjp
def low(v):
    return lax.optimization_barrier(v.astype(jnp.bfloat16)).astype(jnp.float32)

@jax.custom_vjp
def low_back(v):
    return v

def low_keep(v):
    return (low(v), None)

def low_pass(kept, grad):
    return (grad,)

def back_keep(v):
    return (v, None)

def back_low(kept, grad):
    return (low(grad),)
low.defvjp(low_keep, low_pass)
low_back.defvjp(back_keep, back_low)

def product(pattern, left_op, right_op):
    return jnp.einsum(pattern, left_op, right_op, precision=lax.Precision.HIGHEST)

def norm_apply(values, gain_vec, shift_vec):
    average = lax.optimization_barrier(jnp.mean(values, axis=-1, keepdims=True))
    centred = values - average
    variance = lax.optimization_barrier(jnp.mean(centred * centred, axis=-1, keepdims=True))
    return centred * lax.rsqrt(variance + EPS) * gain_vec + shift_vec

def masked_softmax(scores, allowed):
    masked = jnp.where(allowed, scores, NEG)
    highest = lax.optimization_barrier(jnp.max(masked, axis=-1, keepdims=True))
    expd = jnp.exp(masked - highest)
    return expd / lax.optimization_barrier(jnp.sum(expd, axis=-1, keepdims=True))

def branch_tail(residual_in, attended, weights_all):
    first_gain, first_shift, qkv_weight, out_weight, second_gain, second_shift, inner_weight, inner_bias, outer_weight = weights_all
    residual = residual_in + low_back(product('td,de->te', attended, out_weight))
    normed_second = low(norm_apply(residual, second_gain, second_shift))
    inner = low_back(product('td,df->tf', normed_second, inner_weight) + inner_bias)
    hidden = low(jax.nn.gelu(inner, approximate=False))
    return residual + low_back(product('tf,fd->td', hidden, outer_weight))

def row_forward(weights_all, row_tokens, row_globals, row_length):
    first_gain, first_shift, qkv_weight = (weights_all[0], weights_all[1], weights_all[2])
    positions = jnp.arange(SEQ, dtype=jnp.int32)
    valid_rows = positions < row_length
    score_scale = HEAD_DIM ** (-0.5)
    normed = low(norm_apply(row_tokens, first_gain, first_shift))
    global_normed = low(norm_apply(row_globals, first_gain, first_shift))
    projected = low_back(low(product('td,de->te', normed, qkv_weight)))
    global_projected = low_back(low(product('gd,de->ge', global_normed, qkv_weight)))
    queries = projected[:, :D].reshape(SEQ, HEADS, HEAD_DIM)
    keys_all = projected[:, D:2 * D].reshape(SEQ, HEADS, HEAD_DIM)
    values_all = projected[:, 2 * D:].reshape(SEQ, HEADS, HEAD_DIM)
    global_queries = global_projected[:, :D].reshape(GLOBALS, HEADS, HEAD_DIM)
    global_keys = global_projected[:, D:2 * D].reshape(GLOBALS, HEADS, HEAD_DIM)
    global_values = global_projected[:, 2 * D:].reshape(GLOBALS, HEADS, HEAD_DIM)
    block_count = SEQ // BLOCK + 1
    padding = ((SHIFT, SHIFT), (0, 0), (0, 0))
    query_blocks = jnp.pad(queries, padding).reshape(block_count, BLOCK, HEADS, HEAD_DIM)
    key_blocks = jnp.pad(keys_all, padding).reshape(block_count, BLOCK, HEADS, HEAD_DIM)
    value_blocks = jnp.pad(values_all, padding).reshape(block_count, BLOCK, HEADS, HEAD_DIM)
    ok_blocks = jnp.pad(valid_rows, (SHIFT, SHIFT)).reshape(block_count, BLOCK)
    global_ok = jnp.ones((GLOBALS,), dtype=bool)

    def block_attend(pieces):
        query_block, key_block, value_block, ok_block = pieces
        scores = jnp.concatenate([score_scale * product('qhd,khd->hqk', query_block, key_block), score_scale * product('qhd,ghd->hqg', query_block, global_keys)], axis=-1)
        scores = low_back(scores)
        allowed = jnp.concatenate([ok_block, global_ok])
        weights = low(masked_softmax(scores, allowed[None, None, :]))
        return product('hqk,khd->qhd', weights, jnp.concatenate([value_block, global_values], axis=0))
    mixed = lax.map(jax.checkpoint(block_attend), (query_blocks, key_blocks, value_blocks, ok_blocks))
    local_mix = mixed.reshape(block_count * BLOCK, HEADS, HEAD_DIM)[SHIFT:SHIFT + SEQ].reshape(SEQ, D)
    global_scores = jnp.concatenate([score_scale * product('ghd,thd->hgt', global_queries, keys_all), score_scale * product('ghd,khd->hgk', global_queries, global_keys)], axis=-1)
    global_scores = low_back(global_scores)
    global_allowed = jnp.concatenate([valid_rows, global_ok])
    global_weights = low(masked_softmax(global_scores, global_allowed[None, None, :]))
    global_mix = product('hgk,khd->ghd', global_weights, jnp.concatenate([values_all, global_values], axis=0)).reshape(GLOBALS, D)
    attended = low_back(low(local_mix))
    global_attended = low_back(low(global_mix))
    final = branch_tail(row_tokens, attended, weights_all) * valid_rows[:, None].astype(jnp.float32)
    global_final = branch_tail(row_globals, global_attended, weights_all)
    return (final, global_final)

def reference(inputs, global_inputs, lengths, first_gain, first_shift, qkv_weight, out_weight, second_gain, second_shift, inner_weight, inner_bias, outer_weight, output_cotangent, global_cotangent):
    weights_all = tuple((weight_item.astype(jnp.float32) for weight_item in (first_gain, first_shift, qkv_weight, out_weight, second_gain, second_shift, inner_weight, inner_bias, outer_weight)))

    def forward(weight_set, all_tokens, all_globals):

        def one_row(pieces):
            return jax.checkpoint(row_forward)(weight_set, pieces[0], pieces[1], pieces[2])
        return lax.map(one_row, (all_tokens, all_globals, lengths))
    outputs_pair, backward = jax.vjp(forward, weights_all, inputs.astype(jnp.float32), global_inputs.astype(jnp.float32))
    weight_grads, token_grad, global_grad = backward((output_cotangent.astype(jnp.float32), global_cotangent.astype(jnp.float32)))
    return (outputs_pair[0].astype(jnp.bfloat16), outputs_pair[1].astype(jnp.bfloat16), token_grad.astype(jnp.bfloat16), global_grad.astype(jnp.bfloat16), weight_grads[0], weight_grads[1], weight_grads[2], weight_grads[3], weight_grads[4], weight_grads[5], weight_grads[6], weight_grads[7], weight_grads[8])
```

```python
import functools
import jax
import jax.numpy as jnp
from jax import lax
from jax.experimental import pallas as pl
from jax.experimental.pallas import tpu as pltpu
from jax.sharding import PartitionSpec as P

HEADS = 12
NEG = -1e30
LANES = 128
TYPE0 = 3 * HEADS

def nt(a, b):
    return lax.dot_general(a, b, (((1,), (1,)), ((), ())), preferred_element_type=jnp.float32)

def tn(a, b):
    return lax.dot_general(a, b, (((0,), (0,)), ((), ())), preferred_element_type=jnp.float32)

def nn(a, b):
    return jnp.dot(a, b, preferred_element_type=jnp.float32)


def type_marks(rows, half, lane, row):
    kind = jnp.where(row < half, TYPE0, jnp.where(row < 2 * half, TYPE0 + 1, TYPE0 + 2))
    return (lane == kind)


def attend_kernel(half, scale, tq, q_ref, k_ref, v_ref, kaug_ref, o_ref, lse_ref):
    pair = pl.program_id(1)
    rows = q_ref.shape[1]
    zero = jnp.zeros((), jnp.bfloat16)
    k, v = k_ref[0], v_ref[0]
    kaug = kaug_ref[0]
    lane_all = lax.broadcasted_iota(jnp.int32, (rows, LANES), 1)
    low_all = lane_all < LANES // 2
    one = jnp.ones((), jnp.bfloat16)
    kx, vx = [], []
    for sel in (low_all, jnp.logical_not(low_all)):
        kx.append(jnp.concatenate([jnp.where(sel, k, zero), kaug], axis=1))
        vx.append(jnp.concatenate([jnp.where(sel, v, zero), jnp.where(sel, one, zero)], axis=1))
    for start in range(0, rows, tq):
        lane = lax.broadcasted_iota(jnp.int32, (tq, LANES), 1)
        row = lax.broadcasted_iota(jnp.int32, (tq, LANES), 0) + start
        low = lane < LANES // 2
        qaug = jnp.where(type_marks(rows, half, lane, row), one, zero)
        q = (q_ref[0, start:start + tq].astype(jnp.float32) * scale).astype(jnp.bfloat16)
        qx = jnp.concatenate([q, qaug], axis=1)
        acc = None
        peaks = []
        for a in (0, 1):
            s = nt(qx, kx[a])
            peak = jnp.max(s, axis=1, keepdims=True)
            p = jnp.exp(s - peak).astype(jnp.bfloat16)
            part = nn(p, vx[a])
            acc = part if acc is None else acc + part
            peaks.append(peak)
        total = acc[:, LANES:]
        o_ref[0, start:start + tq] = (acc[:, :LANES] / total).astype(jnp.bfloat16)
        lse = jnp.where(low, peaks[0], peaks[1]) + jnp.log(total)
        first, second = lse[:, 0:1], lse[:, LANES // 2:LANES // 2 + 1]
        prev = jnp.where(pair == 0, 0.0, lse_ref[0, start:start + tq])
        head = lax.rem(lane, HEADS)
        inside = lane < 3 * HEADS
        kept = jnp.where(inside & (head == 2 * pair), first, prev)
        lse_ref[0, start:start + tq] = jnp.where(inside & (head == 2 * pair + 1), second, kept)


def attend(qkv, kaug, half, tq=320):
    row_count, rows, cols = qkv.shape
    width = cols // 3
    pairs = width // LANES
    scale = (width // HEADS) ** (-0.5)
    spec = lambda off: pl.BlockSpec((1, rows, LANES), lambda r, p: (r, 0, off + p))
    return pl.pallas_call(
        functools.partial(attend_kernel, half, scale, tq),
        grid=(row_count, pairs),
        in_specs=[spec(0), spec(pairs), spec(2 * pairs), pl.BlockSpec((1, rows, LANES), lambda r, p: (r, 0, 0))],
        out_specs=[spec(0), pl.BlockSpec((1, rows, LANES), lambda r, p: (r, 0, 0))],
        out_shape=[
            jax.ShapeDtypeStruct((row_count, rows, width), jnp.bfloat16),
            jax.ShapeDtypeStruct((row_count, rows, LANES), jnp.float32),
        ],
        compiler_params=pltpu.CompilerParams(vmem_limit_bytes=48 * 1024 * 1024),
        name="attend",
    )(qkv, qkv, qkv, kaug)


def three_parts(values, lane):
    top = values.astype(jnp.bfloat16)
    rest = values - top.astype(jnp.float32)
    mid = rest.astype(jnp.bfloat16)
    low = (rest - mid.astype(jnp.float32)).astype(jnp.bfloat16)
    zero = jnp.zeros((), jnp.bfloat16)
    return jnp.where(lane < HEADS, top, jnp.where(lane < 2 * HEADS, mid, jnp.where(lane < 3 * HEADS, low, zero)))


def attend_back_kernel(half, scale, tk, q_ref, k_ref, v_ref, g_ref, lse_ref, delta_ref, kaug_ref, dq_ref, dk_ref, dv_ref):
    pair = pl.program_id(1)
    rows = q_ref.shape[1]
    zero = jnp.zeros((), jnp.bfloat16)
    one = jnp.ones((), jnp.bfloat16)
    lane = lax.broadcasted_iota(jnp.int32, (rows, LANES), 1)
    row = lax.broadcasted_iota(jnp.int32, (rows, LANES), 0)
    low = lane < LANES // 2
    q = (q_ref[0].astype(jnp.float32) * scale).astype(jnp.bfloat16)
    g = g_ref[0]
    qaug = jnp.where(type_marks(rows, half, lane, row), one, three_parts(lse_ref[0], lane))
    gaug = three_parts(delta_ref[0], lane)
    qx = jnp.concatenate([q, qaug], axis=1)
    gx = jnp.concatenate([g, gaug], axis=1)
    sels = (low, jnp.logical_not(low))
    qh = [jnp.where(sel, q, zero) for sel in sels]
    gh = [jnp.where(sel, g, zero) for sel in sels]
    dq = None
    for start in range(0, rows, tk):
        lane_k = lax.broadcasted_iota(jnp.int32, (tk, LANES), 1)
        low_k = lane_k < LANES // 2
        head = lax.rem(lane_k, HEADS)
        inside = lane_k < 3 * HEADS
        k = k_ref[0, start:start + tk]
        v = v_ref[0, start:start + tk]
        kaug = kaug_ref[0, start:start + tk]
        dk = dv = None
        for a, sel in ((0, low_k), (1, jnp.logical_not(low_k))):
            marks = inside & (head == 2 * pair + a)
            kh = jnp.where(sel, k, zero)
            kx = jnp.concatenate([kh, jnp.where(marks, -one, kaug)], axis=1)
            vx = jnp.concatenate([jnp.where(sel, v, zero), jnp.where(marks, -one, zero)], axis=1)
            p = jnp.exp(nt(kx, qx))
            ds = (p * nt(vx, gx)).astype(jnp.bfloat16)
            part_v = nn(p.astype(jnp.bfloat16), gh[a])
            part_k = nn(ds, qh[a])
            part_q = tn(ds, kh)
            dv = part_v if dv is None else dv + part_v
            dk = part_k if dk is None else dk + part_k
            dq = part_q if dq is None else dq + part_q
        dk_ref[0, start:start + tk] = dk.astype(jnp.bfloat16)
        dv_ref[0, start:start + tk] = dv.astype(jnp.bfloat16)
    dq_ref[0] = (dq * scale).astype(jnp.bfloat16)


def attend_back(qkv, grad, lse, delta, kaug, half, tk=320):
    row_count, rows, cols = qkv.shape
    width = cols // 3
    pairs = width // LANES
    scale = (width // HEADS) ** (-0.5)
    spec = lambda off: pl.BlockSpec((1, rows, LANES), lambda r, p: (r, 0, off + p))
    whole = pl.BlockSpec((1, rows, LANES), lambda r, p: (r, 0, 0))
    out = jax.ShapeDtypeStruct((row_count, rows, width), jnp.bfloat16)
    return pl.pallas_call(
        functools.partial(attend_back_kernel, half, scale, tk),
        grid=(row_count, pairs),
        in_specs=[spec(0), spec(pairs), spec(2 * pairs), spec(0), whole, whole, whole],
        out_specs=[spec(0)] * 3,
        out_shape=[out] * 3,
        compiler_params=pltpu.CompilerParams(vmem_limit_bytes=48 * 1024 * 1024),
        name="attend_back",
    )(qkv, qkv, qkv, grad, lse, delta, kaug)


EPS = 1e-05
MESH_ID = pl.DeviceIdType.MESH


def spread_kernel(count, sizes, same, *refs):
    ins, outs = refs[:sizes], refs[sizes:2 * sizes]
    send, recv, local = refs[2 * sizes:]
    me = lax.axis_index("seq")
    barrier = pltpu.get_barrier_semaphore()
    for step in range(1, count):
        pl.semaphore_signal(
            barrier, inc=1, device_id={"seq": lax.rem(me + step, count)}, device_id_type=MESH_ID
        )
    pl.semaphore_wait(barrier, count - 1)
    own = []
    for n in range(sizes):
        copy = pltpu.make_async_copy(ins[n] if same else ins[n].at[me], outs[n].at[me], local.at[n])
        copy.start()
        own.append(copy)
    copies = []
    for step in range(1, count):
        peer = lax.rem(me + step, count)
        for n in range(sizes):
            copy = pltpu.make_async_remote_copy(
                src_ref=ins[n] if same else ins[n].at[peer],
                dst_ref=outs[n].at[me],
                send_sem=send.at[n, step],
                recv_sem=recv.at[n, step],
                device_id={"seq": peer},
                device_id_type=MESH_ID,
            )
            copy.start()
            copies.append(copy)
    for copy in own:
        copy.wait()
    for copy in copies:
        copy.wait()


def spread(arrays, count, same, collective_id):
    sizes = len(arrays)
    shapes = [(count,) + a.shape if same else a.shape for a in arrays]
    vmem = pl.BlockSpec(memory_space=pltpu.VMEM)
    return pl.pallas_call(
        functools.partial(spread_kernel, count, sizes, same),
        in_specs=[vmem] * sizes,
        out_specs=[vmem] * sizes,
        out_shape=[jax.ShapeDtypeStruct(s, a.dtype) for s, a in zip(shapes, arrays)],
        scratch_shapes=[
            pltpu.SemaphoreType.DMA((sizes, count)),
            pltpu.SemaphoreType.DMA((sizes, count)),
            pltpu.SemaphoreType.DMA((sizes,)),
        ],
        compiler_params=pltpu.CompilerParams(
            collective_id=collective_id, has_side_effects=True, vmem_limit_bytes=32 * 1024 * 1024
        ),
        name="spread",
    )(*arrays)


def norm_parts(values):
    average = jnp.mean(values, axis=-1, keepdims=True)
    centred = values - average
    variance = jnp.mean(centred * centred, axis=-1, keepdims=True)
    inv = lax.rsqrt(variance + EPS)
    return centred * inv, inv


def norm_back(grad, n, inv, gain):
    eg = grad * gain
    through = (
        eg - jnp.mean(eg, axis=-1, keepdims=True) - n * jnp.mean(eg * n, axis=-1, keepdims=True)
    ) * inv
    return through, jnp.sum(grad * n, axis=0), jnp.sum(grad, axis=0)


def split_rows(a, count):
    row_count, rows, width = a.shape
    part = rows // count
    moved = a.reshape(row_count, count, part, width).transpose(1, 0, 2, 3)
    return moved.reshape(count, row_count * part, width)


def join_rows(a, row_count):
    count, rows, width = a.shape
    part = rows // row_count
    moved = a.reshape(count, row_count, part, width).transpose(1, 0, 2, 3)
    return moved.reshape(row_count, count * part, width)


def per_head(values, width):
    lanes = values[..., :HEADS]
    return jnp.repeat(lanes, width // HEADS, axis=-1)


def head_sums(values):
    rows, width = values.shape
    lane = jnp.arange(LANES)
    head = jnp.arange(width) // (width // HEADS)
    place = ((lane[None, :] % HEADS == head[:, None]) & (lane[None, :] < 3 * HEADS)).astype(jnp.bfloat16)
    top = values.astype(jnp.bfloat16)
    rest = (values - top.astype(jnp.float32)).astype(jnp.bfloat16)
    return nn(top, place) + nn(rest, place)


def body(
    inputs,
    global_inputs,
    lengths,
    first_gain,
    first_shift,
    qkv_weight,
    out_weight,
    second_gain,
    second_shift,
    inner_weight,
    inner_bias,
    outer_weight,
    output_cotangent,
    global_cotangent,
):
    f32, bf16 = jnp.float32, jnp.bfloat16
    row_count, block_len, width = inputs.shape
    half = block_len // 2
    global_count = global_inputs.shape[1]
    rows = block_len + global_count
    inner_width = inner_weight.shape[1]
    count = lax.axis_size("seq")
    me = lax.axis_index("seq")
    after = lax.rem(me + 1, count)
    back = [(i, (i - 1) % count) for i in range(count)]
    forth = [(i, (i + 1) % count) for i in range(count)]
    token_rows = row_count * block_len
    share = global_count // count
    own_rows = row_count * share

    next_inputs = lax.ppermute(inputs[:, :half], "seq", back)
    next_cotangent = lax.ppermute(output_cotangent[:, :half], "seq", back)
    block = jnp.concatenate([inputs[:, half:], next_inputs], axis=1)
    spots = jnp.arange(half, dtype=jnp.int32)
    positions = jnp.concatenate([me * block_len + half + spots, after * block_len + spots])
    valid = positions[None, :] < lengths[:, None]

    kind = jnp.arange(LANES)[None, None, :] - TYPE0
    key_half = (jnp.arange(block_len) // half)[None, :, None]
    last = me == count - 1
    hidden_key = jnp.logical_not(valid)[:, :, None] | (last & (kind < 2) & (kind != key_half))
    token_marks = jnp.where(hidden_key & (kind >= 0) & (kind < 3), NEG, 0.0)
    global_marks = jnp.where((kind == 2) & (me != 0), NEG, 0.0)
    global_marks = jnp.broadcast_to(global_marks, (row_count, global_count, LANES))
    kaug = jnp.concatenate([token_marks, global_marks], axis=1).astype(bf16)

    states = jnp.concatenate([block, global_inputs], axis=1)
    n_first, inv_first = norm_parts(states.astype(f32))
    normed = (n_first * first_gain + first_shift).astype(bf16)
    qkv = nn(normed.reshape(row_count * rows, width), qkv_weight).astype(bf16)
    qkv = qkv.reshape(row_count, rows, 3 * width)

    mixed, lse = attend(qkv, kaug, half)
    part_mixed, part_lse = spread(
        [split_rows(mixed[:, block_len:], count), split_rows(lse[:, block_len:], count)], count, False, 0
    )
    highest = jnp.max(part_lse, axis=0)
    part_weight = jnp.exp(part_lse - highest)
    total = jnp.sum(part_weight, axis=0)
    global_lse = highest + jnp.log(total)
    global_mixed = jnp.sum(per_head(part_weight / total, width) * part_mixed.astype(f32), axis=0)

    own_globals = lax.dynamic_slice_in_dim(global_inputs, me * share, share, axis=1)
    own_global_cot = lax.dynamic_slice_in_dim(global_cotangent, me * share, share, axis=1)
    tokens = jnp.concatenate(
        [block.reshape(token_rows, width), own_globals.reshape(own_rows, width)]
    ).astype(f32)
    cot_block = jnp.concatenate([output_cotangent[:, half:], next_cotangent], axis=1)
    cot_block = jnp.where(valid[:, :, None], cot_block, 0)
    cotangent = jnp.concatenate(
        [cot_block.reshape(token_rows, width), own_global_cot.reshape(own_rows, width)]
    )
    attended = jnp.concatenate(
        [mixed[:, :block_len].reshape(token_rows, width), global_mixed.astype(bf16)]
    )
    residual = tokens + nn(attended, out_weight)
    n_second, inv_second = norm_parts(residual)
    normed_second = (n_second * second_gain + second_shift).astype(bf16)
    inner = nn(normed_second, inner_weight) + inner_bias
    bell = jnp.exp(-0.5 * inner * inner)
    cdf = 0.5 * (1.0 + lax.erf(inner * (0.5 ** 0.5)))
    hidden = (inner * cdf).astype(bf16)
    final = residual + nn(hidden, outer_weight)
    hidden_grad = nt(cotangent, outer_weight)
    slope = cdf + inner * bell * ((0.5 / jnp.pi) ** 0.5)
    inner_grad = (hidden_grad * slope).astype(bf16)
    second_grad = nt(inner_grad, inner_weight)
    through, second_gain_grad, second_shift_grad = norm_back(second_grad, n_second, inv_second, second_gain)
    residual_grad = cotangent.astype(f32) + through
    projection_grad = residual_grad.astype(bf16)
    attended_grad = nt(projection_grad, out_weight).astype(bf16)
    delta = head_sums(attended_grad.astype(f32) * attended.astype(f32))
    outer_grad = tn(hidden, cotangent)
    inner_wgrad = tn(normed_second, inner_grad)
    bias_grad = jnp.sum(inner_grad.astype(f32), axis=0)
    out_grad = tn(attended, projection_grad)

    all_grad, all_lse, all_delta = spread(
        [attended_grad[token_rows:], global_lse, delta[token_rows:]], count, True, 1
    )
    block_grad = jnp.concatenate(
        [attended_grad[:token_rows].reshape(row_count, block_len, width), join_rows(all_grad, row_count)], axis=1
    )
    block_lse = jnp.concatenate([lse[:, :block_len], join_rows(all_lse, row_count)], axis=1)
    block_delta = jnp.concatenate(
        [delta[:token_rows].reshape(row_count, block_len, LANES), join_rows(all_delta, row_count)], axis=1
    )
    dqkv = jnp.concatenate(attend_back(qkv, block_grad, block_lse, block_delta, kaug, half, rows), axis=-1)
    (part_dqkv,) = spread([split_rows(dqkv[:, block_len:], count)], count, False, 2)
    global_dqkv = jnp.sum(part_dqkv.astype(f32), axis=0).astype(bf16)
    qkv_grad = jnp.concatenate([dqkv[:, :block_len].reshape(token_rows, 3 * width), global_dqkv])

    first_grad = nt(qkv_grad, qkv_weight)
    n_tokens, inv_tokens = norm_parts(tokens)
    through, first_gain_grad, first_shift_grad = norm_back(first_grad, n_tokens, inv_tokens, first_gain)
    input_grad = (residual_grad + through).astype(bf16)
    normed_tokens = (n_tokens * first_gain + first_shift).astype(bf16)
    qkv_wgrad = tn(normed_tokens, qkv_grad)

    layer = final[:token_rows].reshape(row_count, block_len, width)
    layer = jnp.where(valid[:, :, None], layer, 0.0).astype(bf16)
    grad_block = input_grad[:token_rows].reshape(row_count, block_len, width)
    layer_output = jnp.concatenate([lax.ppermute(layer[:, half:], "seq", forth), layer[:, :half]], axis=1)
    input_out = jnp.concatenate(
        [lax.ppermute(grad_block[:, half:], "seq", forth), grad_block[:, :half]], axis=1
    )
    global_final, global_grad = spread(
        [final[token_rows:].astype(bf16), input_grad[token_rows:]], count, True, 3
    )

    def shares(a):
        return a.reshape(count, a.shape[0] // count, -1)

    strips = inner_width // width
    inner_part = inner_wgrad.reshape(count, width // count, strips, width).transpose(0, 2, 1, 3)
    qkv_part = qkv_wgrad.reshape(count, width // count, 3, width).transpose(0, 2, 1, 3)
    small = jnp.concatenate(
        [
            shares(first_gain_grad),
            shares(first_shift_grad),
            shares(second_gain_grad),
            shares(second_shift_grad),
            shares(bias_grad),
        ],
        axis=1,
    )
    small = small.reshape(count, 1, -1)
    stacked = jnp.concatenate(
        [
            inner_part.reshape(count, -1, width).astype(bf16),
            shares(outer_grad).astype(bf16),
            shares(out_grad).astype(bf16),
            qkv_part.reshape(count, -1, width).astype(bf16),
        ],
        axis=1,
    )
    stacked = lax.psum_scatter(stacked, "seq", scatter_dimension=0, tiled=True)
    stacked = lax.psum(stacked, "batch")[0].astype(f32)
    small = lax.psum_scatter(small, "seq", scatter_dimension=0, tiled=True)
    small = lax.psum(small, "batch").reshape(-1)
    part = width // count
    first_rows = strips * part
    outer_rows = inner_width // count
    inner_out = stacked[:first_rows].reshape(strips, part, width).transpose(1, 0, 2).reshape(part, inner_width)
    at = first_rows + outer_rows
    outer_out = stacked[first_rows:at]
    out_out = stacked[at:at + part]
    qkv_out = stacked[at + part:].reshape(3, part, width).transpose(1, 0, 2).reshape(part, 3 * width)
    return (
        layer_output,
        join_rows(global_final, row_count),
        input_out,
        join_rows(global_grad, row_count),
        small[:part],
        small[part:2 * part],
        qkv_out,
        out_out,
        small[2 * part:3 * part],
        small[3 * part:4 * part],
        inner_out,
        small[4 * part:],
        outer_out,
    )


def solution(mesh):
    rows = P("batch", "seq", None)
    globals_at = P("batch", None, None)
    return jax.shard_map(
        body,
        mesh=mesh,
        in_specs=(rows, globals_at, P("batch")) + (P(),) * 9 + (rows, globals_at),
        out_specs=(
            rows,
            globals_at,
            rows,
            globals_at,
            P("seq"),
            P("seq"),
            P("seq", None),
            P("seq", None),
            P("seq"),
            P("seq"),
            P("seq", None),
            P("seq"),
            P("seq", None),
        ),
        check_vma=False,
    )
```

```python
import functools
import jax
import jax.numpy as jnp
from jax import lax
from jax.experimental import pallas as pl
from jax.experimental.pallas import tpu as pltpu
from jax.sharding import PartitionSpec as P

HEADS = 12
NEG = -1e30
LANES = 128
TYPE0 = 3 * HEADS

def nt(a, b):
    return lax.dot_general(a, b, (((1,), (1,)), ((), ())), preferred_element_type=jnp.float32)

def tn(a, b):
    return lax.dot_general(a, b, (((0,), (0,)), ((), ())), preferred_element_type=jnp.float32)

def nn(a, b):
    return jnp.dot(a, b, preferred_element_type=jnp.float32)


def type_marks(rows, half, lane, row):
    kind = jnp.where(row < half, TYPE0, jnp.where(row < 2 * half, TYPE0 + 1, TYPE0 + 2))
    return (lane == kind)


def attend_kernel(half, scale, tq, q_ref, k_ref, v_ref, kaug_ref, o_ref, lse_ref):
    pair = pl.program_id(1)
    rows = q_ref.shape[1]
    zero = jnp.zeros((), jnp.bfloat16)
    k, v = k_ref[0], v_ref[0]
    kaug = kaug_ref[0]
    lane_all = lax.broadcasted_iota(jnp.int32, (rows, LANES), 1)
    low_all = lane_all < LANES // 2
    one = jnp.ones((), jnp.bfloat16)
    kx, vx = [], []
    for sel in (low_all, jnp.logical_not(low_all)):
        kx.append(jnp.concatenate([jnp.where(sel, k, zero), kaug], axis=1))
        vx.append(jnp.concatenate([jnp.where(sel, v, zero), jnp.where(sel, one, zero)], axis=1))
    for start in range(0, rows, tq):
        lane = lax.broadcasted_iota(jnp.int32, (tq, LANES), 1)
        row = lax.broadcasted_iota(jnp.int32, (tq, LANES), 0) + start
        low = lane < LANES // 2
        qaug = jnp.where(type_marks(rows, half, lane, row), one, zero)
        q = (q_ref[0, start:start + tq].astype(jnp.float32) * scale).astype(jnp.bfloat16)
        qx = jnp.concatenate([q, qaug], axis=1)
        acc = None
        peaks = []
        for a in (0, 1):
            s = nt(qx, kx[a])
            peak = jnp.max(s, axis=1, keepdims=True)
            p = jnp.exp(s - peak).astype(jnp.bfloat16)
            part = nn(p, vx[a])
            acc = part if acc is None else acc + part
            peaks.append(peak)
        total = acc[:, LANES:]
        o_ref[0, start:start + tq] = (acc[:, :LANES] / total).astype(jnp.bfloat16)
        lse = jnp.where(low, peaks[0], peaks[1]) + jnp.log(total)
        first, second = lse[:, 0:1], lse[:, LANES // 2:LANES // 2 + 1]
        prev = jnp.where(pair == 0, 0.0, lse_ref[0, start:start + tq])
        head = lax.rem(lane, HEADS)
        inside = lane < 3 * HEADS
        kept = jnp.where(inside & (head == 2 * pair), first, prev)
        lse_ref[0, start:start + tq] = jnp.where(inside & (head == 2 * pair + 1), second, kept)


def attend(qkv, kaug, half, tq=320):
    row_count, rows, cols = qkv.shape
    width = cols // 3
    pairs = width // LANES
    scale = (width // HEADS) ** (-0.5)
    spec = lambda off: pl.BlockSpec((1, rows, LANES), lambda r, p: (r, 0, off + p))
    return pl.pallas_call(
        functools.partial(attend_kernel, half, scale, tq),
        grid=(row_count, pairs),
        in_specs=[spec(0), spec(pairs), spec(2 * pairs), pl.BlockSpec((1, rows, LANES), lambda r, p: (r, 0, 0))],
        out_specs=[spec(0), pl.BlockSpec((1, rows, LANES), lambda r, p: (r, 0, 0))],
        out_shape=[
            jax.ShapeDtypeStruct((row_count, rows, width), jnp.bfloat16),
            jax.ShapeDtypeStruct((row_count, rows, LANES), jnp.float32),
        ],
        compiler_params=pltpu.CompilerParams(vmem_limit_bytes=48 * 1024 * 1024),
        name="attend",
    )(qkv, qkv, qkv, kaug)


def three_parts(values, lane):
    top = values.astype(jnp.bfloat16)
    rest = values - top.astype(jnp.float32)
    mid = rest.astype(jnp.bfloat16)
    low = (rest - mid.astype(jnp.float32)).astype(jnp.bfloat16)
    zero = jnp.zeros((), jnp.bfloat16)
    return jnp.where(lane < HEADS, top, jnp.where(lane < 2 * HEADS, mid, jnp.where(lane < 3 * HEADS, low, zero)))


def attend_back_kernel(half, scale, tk, q_ref, k_ref, v_ref, g_ref, lse_ref, delta_ref, kaug_ref, dq_ref, dk_ref, dv_ref):
    pair = pl.program_id(1)
    rows = q_ref.shape[1]
    zero = jnp.zeros((), jnp.bfloat16)
    one = jnp.ones((), jnp.bfloat16)
    lane = lax.broadcasted_iota(jnp.int32, (rows, LANES), 1)
    row = lax.broadcasted_iota(jnp.int32, (rows, LANES), 0)
    low = lane < LANES // 2
    q = (q_ref[0].astype(jnp.float32) * scale).astype(jnp.bfloat16)
    g = g_ref[0]
    qaug = jnp.where(type_marks(rows, half, lane, row), one, three_parts(lse_ref[0], lane))
    gaug = three_parts(delta_ref[0], lane)
    qx = jnp.concatenate([q, qaug], axis=1)
    gx = jnp.concatenate([g, gaug], axis=1)
    sels = (low, jnp.logical_not(low))
    qh = [jnp.where(sel, q, zero) for sel in sels]
    gh = [jnp.where(sel, g, zero) for sel in sels]
    dq = None
    for start in range(0, rows, tk):
        lane_k = lax.broadcasted_iota(jnp.int32, (tk, LANES), 1)
        low_k = lane_k < LANES // 2
        head = lax.rem(lane_k, HEADS)
        inside = lane_k < 3 * HEADS
        k = k_ref[0, start:start + tk]
        v = v_ref[0, start:start + tk]
        kaug = kaug_ref[0, start:start + tk]
        dk = dv = None
        for a, sel in ((0, low_k), (1, jnp.logical_not(low_k))):
            marks = inside & (head == 2 * pair + a)
            kh = jnp.where(sel, k, zero)
            kx = jnp.concatenate([kh, jnp.where(marks, -one, kaug)], axis=1)
            vx = jnp.concatenate([jnp.where(sel, v, zero), jnp.where(marks, -one, zero)], axis=1)
            p = jnp.exp(nt(kx, qx))
            ds = (p * nt(vx, gx)).astype(jnp.bfloat16)
            part_v = nn(p.astype(jnp.bfloat16), gh[a])
            part_k = nn(ds, qh[a])
            part_q = tn(ds, kh)
            dv = part_v if dv is None else dv + part_v
            dk = part_k if dk is None else dk + part_k
            dq = part_q if dq is None else dq + part_q
        dk_ref[0, start:start + tk] = dk.astype(jnp.bfloat16)
        dv_ref[0, start:start + tk] = dv.astype(jnp.bfloat16)
    dq_ref[0] = (dq * scale).astype(jnp.bfloat16)


def attend_back(qkv, grad, lse, delta, kaug, half, tk=320):
    row_count, rows, cols = qkv.shape
    width = cols // 3
    pairs = width // LANES
    scale = (width // HEADS) ** (-0.5)
    spec = lambda off: pl.BlockSpec((1, rows, LANES), lambda r, p: (r, 0, off + p))
    whole = pl.BlockSpec((1, rows, LANES), lambda r, p: (r, 0, 0))
    out = jax.ShapeDtypeStruct((row_count, rows, width), jnp.bfloat16)
    return pl.pallas_call(
        functools.partial(attend_back_kernel, half, scale, tk),
        grid=(row_count, pairs),
        in_specs=[spec(0), spec(pairs), spec(2 * pairs), spec(0), whole, whole, whole],
        out_specs=[spec(0)] * 3,
        out_shape=[out] * 3,
        compiler_params=pltpu.CompilerParams(vmem_limit_bytes=48 * 1024 * 1024),
        name="attend_back",
    )(qkv, qkv, qkv, grad, lse, delta, kaug)


EPS = 1e-05
MESH_ID = pl.DeviceIdType.MESH


def spread_kernel(count, sizes, same, *refs):
    ins, outs = refs[:sizes], refs[sizes:2 * sizes]
    send, recv, local = refs[2 * sizes:]
    me = lax.axis_index("seq")
    barrier = pltpu.get_barrier_semaphore()
    for step in range(1, count):
        pl.semaphore_signal(
            barrier, inc=1, device_id={"seq": lax.rem(me + step, count)}, device_id_type=MESH_ID
        )
    pl.semaphore_wait(barrier, count - 1)
    own = []
    for n in range(sizes):
        copy = pltpu.make_async_copy(ins[n] if same else ins[n].at[me], outs[n].at[me], local.at[n])
        copy.start()
        own.append(copy)
    copies = []
    for step in range(1, count):
        peer = lax.rem(me + step, count)
        for n in range(sizes):
            copy = pltpu.make_async_remote_copy(
                src_ref=ins[n] if same else ins[n].at[peer],
                dst_ref=outs[n].at[me],
                send_sem=send.at[n, step],
                recv_sem=recv.at[n, step],
                device_id={"seq": peer},
                device_id_type=MESH_ID,
            )
            copy.start()
            copies.append(copy)
    for copy in own:
        copy.wait()
    for copy in copies:
        copy.wait()


def spread(arrays, count, same, collective_id):
    sizes = len(arrays)
    shapes = [(count,) + a.shape if same else a.shape for a in arrays]
    vmem = pl.BlockSpec(memory_space=pltpu.VMEM)
    return pl.pallas_call(
        functools.partial(spread_kernel, count, sizes, same),
        in_specs=[vmem] * sizes,
        out_specs=[vmem] * sizes,
        out_shape=[jax.ShapeDtypeStruct(s, a.dtype) for s, a in zip(shapes, arrays)],
        scratch_shapes=[
            pltpu.SemaphoreType.DMA((sizes, count)),
            pltpu.SemaphoreType.DMA((sizes, count)),
            pltpu.SemaphoreType.DMA((sizes,)),
        ],
        compiler_params=pltpu.CompilerParams(
            collective_id=collective_id, has_side_effects=True, vmem_limit_bytes=32 * 1024 * 1024
        ),
        name="spread",
    )(*arrays)


def seat():
    s, b = lax.axis_index("seq"), lax.axis_index("batch")
    return lax.div(s, 2), lax.rem(s, 2), lax.div(b, 2), lax.rem(b, 2)


class Fold:
    def __init__(self, depth, batches, own, got, bufs, done, send, recv, local):
        self.depth, self.batches = depth, batches
        self.own, self.got, self.bufs, self.done = own, got, bufs, done
        self.send, self.recv, self.local = send, recv, local
        self.z, self.x, self.y, self.c = seat()
        self.pending = []
        self.slots = 0

    def peer(self, dz=0, dx=0, dy=0, dc=0):
        z = lax.rem(self.z + dz, self.depth)
        x = 1 - self.x if dx else self.x
        y = 1 - self.y if dy else self.y
        c = 1 - self.c if dc else self.c
        return {"seq": 2 * z + x, "batch": 2 * y + c}

    def greet(self):
        barrier = pltpu.get_barrier_semaphore()
        peers = [self.peer(dx=1), self.peer(dy=1), self.peer(dc=1)]
        peers += [self.peer(dz=d) for d in range(1, self.depth)]
        for to in peers:
            pl.semaphore_signal(barrier, inc=1, device_id=to, device_id_type=MESH_ID)
        pl.semaphore_wait(barrier, len(peers))

    def copy(self, src, dst, to):
        slot = self.slots
        self.slots += 1
        moved = pltpu.make_async_remote_copy(
            src_ref=src, dst_ref=dst, send_sem=self.send.at[slot], recv_sem=self.recv.at[slot],
            device_id=to, device_id_type=MESH_ID,
        )
        self.pending.append(moved)
        return moved

    def lanes(self, part, y=None):
        if y is None:
            return pl.ds(part * 256, 256)
        return pl.ds(pl.multiple_of(part * 256 + y * 128, 128), 128)

    def plan(self, n):
        r0, r1, pieces = self.batches[n]
        rows = pl.ds(r0, r1 - r0)
        own, got, done, bufs = self.own, self.got, self.done, self.bufs
        z, x, y, c = self.z, self.x, self.y, self.c
        px, py, pc = 1 - x, 1 - y, 1 - c
        a1, a2, a3, b1, b2, b3, c1, c2, c3 = bufs
        others = [(d, lax.rem(z + d, self.depth)) for d in range(1, self.depth)]
        stages = []

        mine, core = [], []
        for k, (take, at, count) in enumerate(pieces):
            mine.append(pltpu.make_async_copy(take(c), own.at[:, :, pl.ds(at, count)], self.local.at[n, k]))
            core.append(self.copy(take(pc), got.at[:, :, pl.ds(at, count)], self.peer(dc=1)))

        def core_done():
            for copy in mine:
                copy.wait()
            for copy in core:
                copy.wait_recv()

            def add(i, carry):
                for j in range(2):
                    total = own[i, j, rows].astype(jnp.float32) + got[i, j, rows].astype(jnp.float32)
                    own[i, j, rows] = total.astype(jnp.bfloat16)
                return carry

            lax.fori_loop(0, self.depth, add, 0)

        stages.append((mine + core, core_done))

        def merge(at, piece):
            total = own[at].astype(jnp.float32) + piece.astype(jnp.float32)
            own[at] = total.astype(jnp.bfloat16)

        s_a1 = [self.copy(own.at[:, px, rows, self.lanes(0)], a1.at[:, rows], self.peer(dx=1))]
        s_b1 = [self.copy(own.at[:, :, rows, self.lanes(1, py)], b1.at[:, :, rows], self.peer(dy=1))]
        s_c1 = [
            self.copy(own.at[to, :, rows, self.lanes(2)], c1.at[d - 1, :, rows], self.peer(dz=d)) for d, to in others
        ]

        def first_done():
            for copy in s_a1 + s_b1:
                copy.wait_recv()

            def add(i, carry):
                merge((i, x, rows, self.lanes(0)), a1[i, rows])
                for j in range(2):
                    merge((i, j, rows, self.lanes(1, y)), b1[i, j, rows])
                return carry

            lax.fori_loop(0, self.depth, add, 0)

        stages.append((s_a1 + s_b1 + s_c1, first_done))

        s_a2 = [self.copy(own.at[:, x, rows, self.lanes(0, py)], a2.at[:, rows], self.peer(dy=1))]
        s_b2 = [self.copy(own.at[:, px, rows, self.lanes(1, y)], b2.at[:, rows], self.peer(dx=1))]

        def second_done():
            for copy in s_c1:
                copy.wait_recv()
            for j in range(2):
                total = own[z, j, rows, self.lanes(2)].astype(jnp.float32)
                for d, _ in others:
                    total = total + c1[d - 1, j, rows].astype(jnp.float32)
                own[z, j, rows, self.lanes(2)] = total.astype(jnp.bfloat16)
            for copy in s_a2 + s_b2:
                copy.wait_recv()

            def add(i, carry):
                merge((i, x, rows, self.lanes(0, y)), a2[i, rows])
                merge((i, x, rows, self.lanes(1, y)), b2[i, rows])
                return carry

            lax.fori_loop(0, self.depth, add, 0)

        stages.append((s_a2 + s_b2, second_done))

        s_c2 = [self.copy(own.at[z, px, rows, self.lanes(2)], c2.at[rows], self.peer(dx=1))]
        s_3 = []
        for part, buf in ((0, a3), (1, b3)):
            s_3 += [
                self.copy(own.at[to, x, rows, self.lanes(part, y)], buf.at[d - 1, rows], self.peer(dz=d))
                for d, to in others
            ]

        def third_done():
            for copy in s_c2:
                copy.wait_recv()
            merge((z, x, rows, self.lanes(2)), c2[rows])

        stages.append((s_c2 + s_3, third_done))

        s_c3 = [self.copy(own.at[z, x, rows, self.lanes(2, py)], c3.at[rows], self.peer(dy=1))]

        def fourth_done():
            for copy in s_3 + s_c3:
                copy.wait_recv()
            for part, buf in ((0, a3), (1, b3)):
                total = own[z, x, rows, self.lanes(part, y)].astype(jnp.float32)
                for d, _ in others:
                    total = total + buf[d - 1, rows].astype(jnp.float32)
                done[c, rows, self.lanes(part, y)] = total.astype(jnp.bfloat16)
            total = own[z, x, rows, self.lanes(2, y)].astype(jnp.float32) + c3[rows].astype(jnp.float32)
            done[c, rows, self.lanes(2, y)] = total.astype(jnp.bfloat16)

        stages.append((s_c3, fourth_done))

        s_y = [
            self.copy(done.at[c, rows, self.lanes(part, y)], done.at[c, rows, self.lanes(part, y)], self.peer(dy=1))
            for part in range(3)
        ]

        def fifth_done():
            for copy in s_y:
                copy.wait_recv()

        stages.append((s_y, fifth_done))
        s_last = [self.copy(done.at[c, rows], done.at[c, rows], self.peer(dc=1))]

        def sixth_done():
            for copy in s_last:
                copy.wait_recv()

        stages.append((s_last, sixth_done))
        return stages

    def finish(self):
        for copy in self.pending:
            copy.wait_send()


def fold_scratch(depth, rows, batches, copies):
    vmem = lambda *shape: pltpu.VMEM(shape, jnp.bfloat16)
    far = depth - 1
    return [
        vmem(depth, 2, rows, 768),
        vmem(depth, 2, rows, 768),
        vmem(depth, rows, 256),
        vmem(depth, rows, 128),
        vmem(far, rows, 128),
        vmem(depth, 2, rows, 128),
        vmem(depth, rows, 128),
        vmem(far, rows, 128),
        vmem(far, 2, rows, 256),
        vmem(rows, 256),
        vmem(rows, 128),
        vmem(2, rows, 768),
        pltpu.SemaphoreType.DMA((copies,)),
        pltpu.SemaphoreType.DMA((copies,)),
        pltpu.SemaphoreType.DMA((batches, 8)),
    ]


def fold_kernel(depth, inner, outer, out, qkv, small, inner_o, outer_o, out_o, qkv_o, small_o, *scratch):
    own, got = scratch[:2]
    bufs = scratch[2:11]
    done, send, recv, local = scratch[11:]
    part = inner.shape[3]
    half_part = part // 2
    outer_half = outer.shape[3]
    strips = inner.shape[0] // 2
    batches, at = [], 0

    def batch(pieces):
        nonlocal at
        start, listed = at, []
        for take, count in pieces:
            listed.append((take, at, count))
            at += count
        batches.append((start, at, listed))

    batch([(lambda c, j=j: inner.at[c * strips + j], part) for j in range(strips)])
    batch([(lambda c: outer.at[:, :, c], outer_half)])
    batch(
        [(lambda c: out.at[:, :, c], half_part)]
        + [(lambda c, j=j: qkv.at[j, :, :, c], half_part) for j in range(3)]
        + [(lambda c: small.at[:, :, c], small.shape[3])]
    )
    fold = Fold(depth, batches, own, got, bufs, done, send, recv, local)
    plans = [fold.plan(n) for n in range(len(batches))]
    fold.greet()
    steps = len(plans[0])
    for tick in range(steps + len(plans) - 1):
        for n, plan in enumerate(plans):
            if 0 <= tick - n < steps:
                if tick - n > 0:
                    plan[tick - n - 1][1]()
                for copy in plan[tick - n][0]:
                    copy.start()
        n = tick - steps + 1
        if n >= 0:
            plans[n][-1][1]()
    fold.finish()

    f32 = jnp.float32
    width = out_o.shape[1]
    for c in range(2):
        for j in range(strips):
            inner_o[:, pl.ds((c * strips + j) * width, width)] = done[c, pl.ds(j * part, part)].astype(f32)
        base = strips * part
        outer_o[pl.ds(c * outer_half, outer_half)] = done[c, pl.ds(base, outer_half)].astype(f32)
        base += outer_half
        out_o[pl.ds(c * half_part, half_part)] = done[c, pl.ds(base, half_part)].astype(f32)
        for j in range(3):
            base += half_part
            qkv_o[pl.ds(c * half_part, half_part), pl.ds(j * width, width)] = done[c, pl.ds(base, half_part)].astype(f32)
    small_o[...] = done[0, pl.ds(base + half_part, small_o.shape[0])].astype(f32)


def fold_grads(inner, outer, out, qkv, small, count):
    depth = count // 2
    strips, width, _ = inner.shape
    part = width // count
    outer_rows = outer.shape[0] // count
    inner = inner.reshape(strips, depth, 2, part, width)
    outer = outer.reshape(depth, 2, 2, outer_rows // 2, width)
    out = out.reshape(depth, 2, 2, part // 2, width)
    qkv = qkv.reshape(3, depth, 2, 2, part // 2, width)
    small = small.reshape(depth, 2, 2, -1, width)
    small_rows = small.shape[3]
    rows = strips // 2 * part + outer_rows // 2 + 2 * part + small_rows
    hbm = pl.BlockSpec(memory_space=pl.ANY)
    vmem = pl.BlockSpec(memory_space=pltpu.VMEM)
    f32 = jnp.float32
    return pl.pallas_call(
        functools.partial(fold_kernel, depth),
        in_specs=[hbm] * 5,
        out_specs=[vmem] * 5,
        out_shape=[
            jax.ShapeDtypeStruct((part, strips * width), f32),
            jax.ShapeDtypeStruct((outer_rows, width), f32),
            jax.ShapeDtypeStruct((part, width), f32),
            jax.ShapeDtypeStruct((part, 3 * width), f32),
            jax.ShapeDtypeStruct((small_rows, width), f32),
        ],
        scratch_shapes=fold_scratch(depth, rows, 3, 96),
        compiler_params=pltpu.CompilerParams(
            collective_id=8, has_side_effects=True, vmem_limit_bytes=56 * 1024 * 1024
        ),
        name="fold",
    )(inner, outer, out, qkv, small)


def wgrad_kernel(a_ref, b_ref, o_ref):
    o_ref[...] = tn(a_ref[...], b_ref[...]).astype(o_ref.dtype).reshape(o_ref.shape)


def wgrad(a, b, strip):
    rows, a_cols = a.shape
    b_cols = b.shape[1]
    split_a = a_cols > b_cols
    strips = max(a_cols, b_cols) // strip
    fixed = lambda n: (0, 0)
    moving = lambda n: (0, n)
    return pl.pallas_call(
        wgrad_kernel,
        grid=(strips,),
        in_specs=[
            pl.BlockSpec((rows, strip), moving if split_a else fixed),
            pl.BlockSpec((rows, strip), fixed if split_a else moving),
        ],
        out_specs=pl.BlockSpec((1, strip, strip), lambda n: (n, 0, 0)),
        out_shape=jax.ShapeDtypeStruct((strips, strip, strip), jnp.bfloat16),
        compiler_params=pltpu.CompilerParams(vmem_limit_bytes=40 * 1024 * 1024),
        name="wgrad",
    )(a, b)


def norm_parts(values):
    average = jnp.mean(values, axis=-1, keepdims=True)
    centred = values - average
    variance = jnp.mean(centred * centred, axis=-1, keepdims=True)
    inv = lax.rsqrt(variance + EPS)
    return centred * inv, inv


def norm_back(grad, n, inv, gain):
    eg = grad * gain
    through = (
        eg - jnp.mean(eg, axis=-1, keepdims=True) - n * jnp.mean(eg * n, axis=-1, keepdims=True)
    ) * inv
    return through, jnp.sum(grad * n, axis=0), jnp.sum(grad, axis=0)


def split_rows(a, count):
    row_count, rows, width = a.shape
    part = rows // count
    moved = a.reshape(row_count, count, part, width).transpose(1, 0, 2, 3)
    return moved.reshape(count, row_count * part, width)


def join_rows(a, row_count):
    count, rows, width = a.shape
    part = rows // row_count
    moved = a.reshape(count, row_count, part, width).transpose(1, 0, 2, 3)
    return moved.reshape(row_count, count * part, width)


def per_head(values, width):
    lanes = values[..., :HEADS]
    return jnp.repeat(lanes, width // HEADS, axis=-1)


def head_sums(values):
    rows, width = values.shape
    lane = jnp.arange(LANES)
    head = jnp.arange(width) // (width // HEADS)
    place = ((lane[None, :] % HEADS == head[:, None]) & (lane[None, :] < 3 * HEADS)).astype(jnp.bfloat16)
    top = values.astype(jnp.bfloat16)
    rest = (values - top.astype(jnp.float32)).astype(jnp.bfloat16)
    return nn(top, place) + nn(rest, place)


def reduce_share(a):
    a = lax.psum_scatter(a, "seq", scatter_dimension=0, tiled=True)
    return lax.psum(a.astype(jnp.bfloat16), "batch").astype(jnp.float32)


def body(
    inputs,
    global_inputs,
    lengths,
    first_gain,
    first_shift,
    qkv_weight,
    out_weight,
    second_gain,
    second_shift,
    inner_weight,
    inner_bias,
    outer_weight,
    output_cotangent,
    global_cotangent,
):
    f32, bf16 = jnp.float32, jnp.bfloat16
    row_count, block_len, width = inputs.shape
    half = block_len // 2
    global_count = global_inputs.shape[1]
    rows = block_len + global_count
    inner_width = inner_weight.shape[1]
    count = lax.axis_size("seq")
    me = lax.axis_index("seq")
    after = lax.rem(me + 1, count)
    back = [(i, (i - 1) % count) for i in range(count)]
    forth = [(i, (i + 1) % count) for i in range(count)]
    token_rows = row_count * block_len
    share = global_count // count
    own_rows = row_count * share

    next_inputs = lax.ppermute(inputs[:, :half], "seq", back)
    next_cotangent = lax.ppermute(output_cotangent[:, :half], "seq", back)
    block = jnp.concatenate([inputs[:, half:], next_inputs], axis=1)
    spots = jnp.arange(half, dtype=jnp.int32)
    positions = jnp.concatenate([me * block_len + half + spots, after * block_len + spots])
    valid = positions[None, :] < lengths[:, None]

    kind = jnp.arange(LANES)[None, None, :] - TYPE0
    key_half = (jnp.arange(block_len) // half)[None, :, None]
    last = me == count - 1
    hidden_key = jnp.logical_not(valid)[:, :, None] | (last & (kind < 2) & (kind != key_half))
    token_marks = jnp.where(hidden_key & (kind >= 0) & (kind < 3), NEG, 0.0)
    global_marks = jnp.where((kind == 2) & (me != 0), NEG, 0.0)
    global_marks = jnp.broadcast_to(global_marks, (row_count, global_count, LANES))
    kaug = jnp.concatenate([token_marks, global_marks], axis=1).astype(bf16)

    states = jnp.concatenate([block, global_inputs], axis=1)
    n_first, inv_first = norm_parts(states.astype(f32))
    normed = (n_first * first_gain + first_shift).astype(bf16)
    qkv = nn(normed.reshape(row_count * rows, width), qkv_weight).astype(bf16)
    qkv = qkv.reshape(row_count, rows, 3 * width)

    mixed, lse = attend(qkv, kaug, half)
    part_mixed, part_lse = spread(
        [split_rows(mixed[:, block_len:], count), split_rows(lse[:, block_len:], count)], count, False, 0
    )
    highest = jnp.max(part_lse, axis=0)
    part_weight = jnp.exp(part_lse - highest)
    total = jnp.sum(part_weight, axis=0)
    global_lse = highest + jnp.log(total)
    global_mixed = jnp.sum(per_head(part_weight / total, width) * part_mixed.astype(f32), axis=0)

    own_globals = lax.dynamic_slice_in_dim(global_inputs, me * share, share, axis=1)
    own_global_cot = lax.dynamic_slice_in_dim(global_cotangent, me * share, share, axis=1)
    tokens = jnp.concatenate(
        [block.reshape(token_rows, width), own_globals.reshape(own_rows, width)]
    ).astype(f32)
    cot_block = jnp.concatenate([output_cotangent[:, half:], next_cotangent], axis=1)
    cot_block = jnp.where(valid[:, :, None], cot_block, 0)
    cotangent = jnp.concatenate(
        [cot_block.reshape(token_rows, width), own_global_cot.reshape(own_rows, width)]
    )
    attended = jnp.concatenate(
        [mixed[:, :block_len].reshape(token_rows, width), global_mixed.astype(bf16)]
    )
    residual = tokens + nn(attended, out_weight)
    n_second, inv_second = norm_parts(residual)
    normed_second = (n_second * second_gain + second_shift).astype(bf16)
    inner = nn(normed_second, inner_weight) + inner_bias
    bell = jnp.exp(-0.5 * inner * inner)
    cdf = 0.5 * (1.0 + lax.erf(inner * (0.5 ** 0.5)))
    hidden = (inner * cdf).astype(bf16)
    final = residual + nn(hidden, outer_weight)
    hidden_grad = nt(cotangent, outer_weight)
    slope = cdf + inner * bell * ((0.5 / jnp.pi) ** 0.5)
    inner_grad = (hidden_grad * slope).astype(bf16)
    second_grad = nt(inner_grad, inner_weight)
    through, second_gain_grad, second_shift_grad = norm_back(second_grad, n_second, inv_second, second_gain)
    residual_grad = cotangent.astype(f32) + through
    projection_grad = residual_grad.astype(bf16)
    attended_grad = nt(projection_grad, out_weight).astype(bf16)
    delta = head_sums(attended_grad.astype(f32) * attended.astype(f32))
    outer_grad = wgrad(hidden, cotangent, width)
    inner_wgrad = wgrad(normed_second, inner_grad, width)
    bias_grad = jnp.sum(inner_grad.astype(f32), axis=0)
    out_grad = wgrad(attended, projection_grad, width)

    all_grad, all_lse, all_delta = spread(
        [attended_grad[token_rows:], global_lse, delta[token_rows:]], count, True, 1
    )
    block_grad = jnp.concatenate(
        [attended_grad[:token_rows].reshape(row_count, block_len, width), join_rows(all_grad, row_count)], axis=1
    )
    block_lse = jnp.concatenate([lse[:, :block_len], join_rows(all_lse, row_count)], axis=1)
    block_delta = jnp.concatenate(
        [delta[:token_rows].reshape(row_count, block_len, LANES), join_rows(all_delta, row_count)], axis=1
    )
    dqkv = jnp.concatenate(attend_back(qkv, block_grad, block_lse, block_delta, kaug, half, rows), axis=-1)
    (part_dqkv,) = spread([split_rows(dqkv[:, block_len:], count)], count, False, 2)
    global_dqkv = jnp.sum(part_dqkv.astype(f32), axis=0).astype(bf16)
    qkv_grad = jnp.concatenate([dqkv[:, :block_len].reshape(token_rows, 3 * width), global_dqkv])

    first_grad = nt(qkv_grad, qkv_weight)
    n_tokens, inv_tokens = norm_parts(tokens)
    through, first_gain_grad, first_shift_grad = norm_back(first_grad, n_tokens, inv_tokens, first_gain)
    input_grad = (residual_grad + through).astype(bf16)
    normed_tokens = (n_tokens * first_gain + first_shift).astype(bf16)
    qkv_wgrad = wgrad(normed_tokens, qkv_grad, width)

    layer = final[:token_rows].reshape(row_count, block_len, width)
    layer = jnp.where(valid[:, :, None], layer, 0.0).astype(bf16)
    grad_block = input_grad[:token_rows].reshape(row_count, block_len, width)
    layer_output = jnp.concatenate([lax.ppermute(layer[:, half:], "seq", forth), layer[:, :half]], axis=1)
    input_out = jnp.concatenate(
        [lax.ppermute(grad_block[:, half:], "seq", forth), grad_block[:, :half]], axis=1
    )
    global_final, global_grad = spread(
        [final[token_rows:].astype(bf16), input_grad[token_rows:]], count, True, 3
    )

    def shares(a):
        return a.reshape(count, a.shape[0] // count)

    part = width // count
    small = jnp.concatenate(
        [
            shares(first_gain_grad),
            shares(first_shift_grad),
            shares(second_gain_grad),
            shares(second_shift_grad),
            shares(bias_grad),
        ],
        axis=1,
    )
    if count == 8 and lax.axis_size("batch") == 4:
        small = jnp.pad(small.astype(bf16)[:, None, :], ((0, 0), (0, 31), (0, 0)))
        inner_out, outer_out, out_out, qkv_out, small = fold_grads(
            inner_wgrad, outer_grad.reshape(inner_width, width), out_grad[0], qkv_wgrad, small, count
        )
        small = small[0]
    else:
        inner_out = reduce_share(inner_wgrad.transpose(1, 0, 2).reshape(width, -1))
        outer_out = reduce_share(outer_grad.reshape(inner_width, width))
        out_out = reduce_share(out_grad[0])
        qkv_out = reduce_share(qkv_wgrad.transpose(1, 0, 2).reshape(width, -1))
        small = reduce_share(small)[0]
    return (
        layer_output,
        join_rows(global_final, row_count),
        input_out,
        join_rows(global_grad, row_count),
        small[:part],
        small[part:2 * part],
        qkv_out,
        out_out,
        small[2 * part:3 * part],
        small[3 * part:4 * part],
        inner_out,
        small[4 * part:],
        outer_out,
    )


def solution(mesh):
    rows = P("batch", "seq", None)
    globals_at = P("batch", None, None)
    return jax.shard_map(
        body,
        mesh=mesh,
        in_specs=(rows, globals_at, P("batch")) + (P(),) * 9 + (rows, globals_at),
        out_specs=(
            rows,
            globals_at,
            rows,
            globals_at,
            P("seq"),
            P("seq"),
            P("seq", None),
            P("seq", None),
            P("seq"),
            P("seq"),
            P("seq", None),
            P("seq"),
            P("seq", None),
        ),
        check_vma=False,
    )
```

```python
import functools
import jax
import jax.numpy as jnp
from jax import lax
from jax.experimental import pallas as pl
from jax.experimental.pallas import tpu as pltpu
from jax.sharding import PartitionSpec as P

HEADS = 12
NEG = -1e30
LANES = 128
TYPE0 = 3 * HEADS

def nt(a, b):
    return lax.dot_general(a, b, (((1,), (1,)), ((), ())), preferred_element_type=jnp.float32)

def tn(a, b):
    return lax.dot_general(a, b, (((0,), (0,)), ((), ())), preferred_element_type=jnp.float32)

def nn(a, b):
    return jnp.dot(a, b, preferred_element_type=jnp.float32)


def type_marks(rows, half, lane, row):
    kind = jnp.where(row < half, TYPE0, jnp.where(row < 2 * half, TYPE0 + 1, TYPE0 + 2))
    return (lane == kind)


def attend_kernel(half, scale, tq, q_ref, k_ref, v_ref, kaug_ref, o_ref, lse_ref):
    pair = pl.program_id(1)
    rows = q_ref.shape[1]
    zero = jnp.zeros((), jnp.bfloat16)
    k, v = k_ref[0], v_ref[0]
    kaug = kaug_ref[0]
    lane_all = lax.broadcasted_iota(jnp.int32, (rows, LANES), 1)
    low_all = lane_all < LANES // 2
    one = jnp.ones((), jnp.bfloat16)
    kx, vx = [], []
    for sel in (low_all, jnp.logical_not(low_all)):
        kx.append(jnp.concatenate([jnp.where(sel, k, zero), kaug], axis=1))
        vx.append(jnp.concatenate([jnp.where(sel, v, zero), jnp.where(sel, one, zero)], axis=1))
    for start in range(0, rows, tq):
        lane = lax.broadcasted_iota(jnp.int32, (tq, LANES), 1)
        row = lax.broadcasted_iota(jnp.int32, (tq, LANES), 0) + start
        low = lane < LANES // 2
        qaug = jnp.where(type_marks(rows, half, lane, row), one, zero)
        q = (q_ref[0, start:start + tq].astype(jnp.float32) * scale).astype(jnp.bfloat16)
        qx = jnp.concatenate([q, qaug], axis=1)
        acc = None
        peaks = []
        for a in (0, 1):
            s = nt(qx, kx[a])
            peak = jnp.max(s, axis=1, keepdims=True)
            p = jnp.exp(s - peak).astype(jnp.bfloat16)
            part = nn(p, vx[a])
            acc = part if acc is None else acc + part
            peaks.append(peak)
        total = acc[:, LANES:]
        o_ref[0, start:start + tq] = (acc[:, :LANES] / total).astype(jnp.bfloat16)
        lse = jnp.where(low, peaks[0], peaks[1]) + jnp.log(total)
        first, second = lse[:, 0:1], lse[:, LANES // 2:LANES // 2 + 1]
        prev = jnp.where(pair == 0, 0.0, lse_ref[0, start:start + tq])
        head = lax.rem(lane, HEADS)
        inside = lane < 3 * HEADS
        kept = jnp.where(inside & (head == 2 * pair), first, prev)
        lse_ref[0, start:start + tq] = jnp.where(inside & (head == 2 * pair + 1), second, kept)


def attend(qkv, kaug, half, tq=320):
    row_count, rows, cols = qkv.shape
    width = cols // 3
    pairs = width // LANES
    scale = (width // HEADS) ** (-0.5)
    spec = lambda off: pl.BlockSpec((1, rows, LANES), lambda r, p: (r, 0, off + p))
    return pl.pallas_call(
        functools.partial(attend_kernel, half, scale, tq),
        grid=(row_count, pairs),
        in_specs=[spec(0), spec(pairs), spec(2 * pairs), pl.BlockSpec((1, rows, LANES), lambda r, p: (r, 0, 0))],
        out_specs=[spec(0), pl.BlockSpec((1, rows, LANES), lambda r, p: (r, 0, 0))],
        out_shape=[
            jax.ShapeDtypeStruct((row_count, rows, width), jnp.bfloat16),
            jax.ShapeDtypeStruct((row_count, rows, LANES), jnp.float32),
        ],
        compiler_params=pltpu.CompilerParams(vmem_limit_bytes=48 * 1024 * 1024),
        name="attend",
    )(qkv, qkv, qkv, kaug)


def three_parts(values, lane):
    top = values.astype(jnp.bfloat16)
    rest = values - top.astype(jnp.float32)
    mid = rest.astype(jnp.bfloat16)
    low = (rest - mid.astype(jnp.float32)).astype(jnp.bfloat16)
    zero = jnp.zeros((), jnp.bfloat16)
    return jnp.where(lane < HEADS, top, jnp.where(lane < 2 * HEADS, mid, jnp.where(lane < 3 * HEADS, low, zero)))


def attend_back_step(half, scale, tk, *refs):
    attend_back_kernel(half, scale, tk, pl.program_id(1), *refs)


def attend_back_kernel(
    half, scale, tk, pair, q_ref, k_ref, v_ref, g_ref, lse_ref, delta_ref, kaug_ref, dq_ref, dk_ref, dv_ref
):
    rows = q_ref.shape[1]
    zero = jnp.zeros((), jnp.bfloat16)
    one = jnp.ones((), jnp.bfloat16)
    lane = lax.broadcasted_iota(jnp.int32, (rows, LANES), 1)
    row = lax.broadcasted_iota(jnp.int32, (rows, LANES), 0)
    low = lane < LANES // 2
    q = (q_ref[0].astype(jnp.float32) * scale).astype(jnp.bfloat16)
    g = g_ref[0]
    qaug = jnp.where(type_marks(rows, half, lane, row), one, three_parts(lse_ref[0], lane))
    gaug = three_parts(delta_ref[0], lane)
    qx = jnp.concatenate([q, qaug], axis=1)
    gx = jnp.concatenate([g, gaug], axis=1)
    sels = (low, jnp.logical_not(low))
    qh = [jnp.where(sel, q, zero) for sel in sels]
    gh = [jnp.where(sel, g, zero) for sel in sels]
    dq = None
    for start in range(0, rows, tk):
        lane_k = lax.broadcasted_iota(jnp.int32, (tk, LANES), 1)
        low_k = lane_k < LANES // 2
        head = lax.rem(lane_k, HEADS)
        inside = lane_k < 3 * HEADS
        k = k_ref[0, start:start + tk]
        v = v_ref[0, start:start + tk]
        kaug = kaug_ref[0, start:start + tk]
        dk = dv = None
        for a, sel in ((0, low_k), (1, jnp.logical_not(low_k))):
            marks = inside & (head == 2 * pair + a)
            kh = jnp.where(sel, k, zero)
            kx = jnp.concatenate([kh, jnp.where(marks, -one, kaug)], axis=1)
            vx = jnp.concatenate([jnp.where(sel, v, zero), jnp.where(marks, -one, zero)], axis=1)
            p = jnp.exp(nt(kx, qx))
            ds = (p * nt(vx, gx)).astype(jnp.bfloat16)
            part_v = nn(p.astype(jnp.bfloat16), gh[a])
            part_k = nn(ds, qh[a])
            part_q = tn(ds, kh)
            dv = part_v if dv is None else dv + part_v
            dk = part_k if dk is None else dk + part_k
            dq = part_q if dq is None else dq + part_q
        dk_ref[0, start:start + tk] = dk.astype(jnp.bfloat16)
        dv_ref[0, start:start + tk] = dv.astype(jnp.bfloat16)
    dq_ref[0] = (dq * scale).astype(jnp.bfloat16)


def attend_back(qkv, grad, lse, delta, kaug, half, tk=320):
    row_count, rows, cols = qkv.shape
    width = cols // 3
    pairs = width // LANES
    scale = (width // HEADS) ** (-0.5)
    spec = lambda off: pl.BlockSpec((1, rows, LANES), lambda r, p: (r, 0, off + p))
    whole = pl.BlockSpec((1, rows, LANES), lambda r, p: (r, 0, 0))
    out = jax.ShapeDtypeStruct((row_count, rows, width), jnp.bfloat16)
    return pl.pallas_call(
        functools.partial(attend_back_step, half, scale, tk),
        grid=(row_count, pairs),
        in_specs=[spec(0), spec(pairs), spec(2 * pairs), spec(0), whole, whole, whole],
        out_specs=[spec(0)] * 3,
        out_shape=[out] * 3,
        compiler_params=pltpu.CompilerParams(vmem_limit_bytes=48 * 1024 * 1024),
        name="attend_back",
    )(qkv, qkv, qkv, grad, lse, delta, kaug)


EPS = 1e-05
MESH_ID = pl.DeviceIdType.MESH


def spread_kernel(count, sizes, same, *refs):
    ins, outs = refs[:sizes], refs[sizes:2 * sizes]
    send, recv, local = refs[2 * sizes:]
    me = lax.axis_index("seq")
    barrier = pltpu.get_barrier_semaphore()
    for step in range(1, count):
        pl.semaphore_signal(
            barrier, inc=1, device_id={"seq": lax.rem(me + step, count)}, device_id_type=MESH_ID
        )
    pl.semaphore_wait(barrier, count - 1)
    own = []
    for n in range(sizes):
        copy = pltpu.make_async_copy(ins[n] if same else ins[n].at[me], outs[n].at[me], local.at[n])
        copy.start()
        own.append(copy)
    copies = []
    for step in range(1, count):
        peer = lax.rem(me + step, count)
        for n in range(sizes):
            copy = pltpu.make_async_remote_copy(
                src_ref=ins[n] if same else ins[n].at[peer],
                dst_ref=outs[n].at[me],
                send_sem=send.at[n, step],
                recv_sem=recv.at[n, step],
                device_id={"seq": peer},
                device_id_type=MESH_ID,
            )
            copy.start()
            copies.append(copy)
    for copy in own:
        copy.wait()
    for copy in copies:
        copy.wait()


def spread(arrays, count, same, collective_id):
    sizes = len(arrays)
    shapes = [(count,) + a.shape if same else a.shape for a in arrays]
    vmem = pl.BlockSpec(memory_space=pltpu.VMEM)
    return pl.pallas_call(
        functools.partial(spread_kernel, count, sizes, same),
        in_specs=[vmem] * sizes,
        out_specs=[vmem] * sizes,
        out_shape=[jax.ShapeDtypeStruct(s, a.dtype) for s, a in zip(shapes, arrays)],
        scratch_shapes=[
            pltpu.SemaphoreType.DMA((sizes, count)),
            pltpu.SemaphoreType.DMA((sizes, count)),
            pltpu.SemaphoreType.DMA((sizes,)),
        ],
        compiler_params=pltpu.CompilerParams(
            collective_id=collective_id, has_side_effects=True, vmem_limit_bytes=32 * 1024 * 1024
        ),
        name="spread",
    )(*arrays)


def seat():
    s, b = lax.axis_index("seq"), lax.axis_index("batch")
    return lax.div(s, 2), lax.rem(s, 2), lax.div(b, 2), lax.rem(b, 2)


def peer(depth, place, dz=0, dx=0, dy=0, dc=0):
    z, x, y, c = place
    z = lax.rem(z + dz, depth) if dz else z
    x = 1 - x if dx else x
    y = 1 - y if dy else y
    c = 1 - c if dc else c
    return {"seq": 2 * z + x, "batch": 2 * y + c}


def fold_peers(depth, place):
    peers = [peer(depth, place, dx=1), peer(depth, place, dy=1), peer(depth, place, dc=1)]
    return peers + [peer(depth, place, dz=d) for d in range(1, depth)]


PARTS = ((0, 384), (384, 256), (640, 128))


class Fold:
    def __init__(self, depth, pieces, bufs, sems):
        self.depth, self.pieces = depth, pieces
        self.own, self.got, self.a1, self.a2, self.a3, self.b1, self.b2, self.b3, self.c1, self.c2, self.c3, self.done = bufs
        self.send, self.recv, self.local = sems
        self.place = seat()
        self.rows = sum(count for _, count in pieces)
        self.sent = []
        self.build()

    @staticmethod
    def scratch(depth, rows, width, pieces):
        vmem = lambda *shape: pltpu.VMEM(shape, jnp.bfloat16)
        far, half = depth - 1, rows // 2
        (_, a), (_, b), (_, c) = PARTS
        bufs = [
            vmem(depth, 2, rows, width),
            vmem(depth, 2, rows, width),
            vmem(depth, rows, a),
            vmem(depth, half, a),
            vmem(far, half, a),
            vmem(depth, 2, half, b),
            vmem(depth, half, b),
            vmem(far, half, b),
            vmem(far, 2, rows, c),
            vmem(rows, c),
            vmem(half, c),
            vmem(2, rows, width),
        ]
        copies = pieces + 3 * (depth - 1) + 8
        return bufs + [
            pltpu.SemaphoreType.DMA((copies,)),
            pltpu.SemaphoreType.DMA((copies,)),
            pltpu.SemaphoreType.DMA((pieces,)),
        ]

    def copy(self, src, dst, **to):
        slot = len(self.sent)
        moved = pltpu.make_async_remote_copy(
            src_ref=src, dst_ref=dst, send_sem=self.send.at[slot], recv_sem=self.recv.at[slot],
            device_id=peer(self.depth, self.place, **to), device_id_type=MESH_ID,
        )
        self.sent.append(moved)
        return moved

    def build(self):
        depth, own, got, done = self.depth, self.own, self.got, self.done
        z, x, y, c = self.place
        px = 1 - x
        far = [(d, lax.rem(z + d, depth)) for d in range(1, depth)]
        half = self.rows // 2
        mine = pl.ds(pl.multiple_of(y * half, 16), half)
        theirs = pl.ds(pl.multiple_of((1 - y) * half, 16), half)
        la, lb, lc = (pl.ds(at, count) for at, count in PARTS)
        at, self.keep, core = 0, [], []
        for n, (take, count) in enumerate(self.pieces):
            rows = pl.ds(at, count)
            self.keep.append(pltpu.make_async_copy(take(c), own.at[:, :, rows], self.local.at[n]))
            core.append(self.copy(take(1 - c), got.at[:, :, rows], dc=1))
            at += count
        a1 = self.copy(own.at[:, px, :, la], self.a1, dx=1)
        b1 = self.copy(own.at[:, :, theirs, lb], self.b1, dy=1)
        c1 = [self.copy(own.at[to, :, :, lc], self.c1.at[d - 1], dz=d) for d, to in far]
        a2 = self.copy(own.at[:, x, theirs, la], self.a2, dy=1)
        b2 = self.copy(own.at[:, px, mine, lb], self.b2, dx=1)
        c2 = self.copy(own.at[z, px, :, lc], self.c2, dx=1)
        a3 = [self.copy(own.at[to, x, mine, la], self.a3.at[d - 1], dz=d) for d, to in far]
        b3 = [self.copy(own.at[to, x, mine, lb], self.b3.at[d - 1], dz=d) for d, to in far]
        c3 = self.copy(own.at[z, x, theirs, lc], self.c3, dy=1)
        y4 = self.copy(done.at[c, mine], done.at[c, mine], dy=1)
        c5 = self.copy(done.at[c], done.at[c], dc=1)
        self.starts = [self.keep + core, [a1, b1] + c1, [c2, a2, b2], [c3] + a3 + b3, [y4], [c5], []]

        def total(at, pieces):
            value = own[at].astype(jnp.float32)
            for piece in pieces:
                value = value + piece.astype(jnp.float32)
            return value.astype(jnp.bfloat16)

        def each(step):
            def run(i, carry):
                step(i)
                return carry

            lax.fori_loop(0, depth, run, 0)

        def core_done():
            for copy in self.keep:
                copy.wait()
            for copy in core:
                copy.wait_recv()

            def step(i):
                for j in range(2):
                    own[i, j] = total((i, j), [got[i, j]])

            each(step)

        def first_done():
            for copy in c1:
                copy.wait_recv()
            for j in range(2):
                own[z, j, :, lc] = total((z, j, slice(None), lc), [self.c1[d - 1, j] for d, _ in far])
            a1.wait_recv()
            b1.wait_recv()

            def step(i):
                own[i, x, :, la] = total((i, x, slice(None), la), [self.a1[i]])
                for j in range(2):
                    own[i, j, mine, lb] = total((i, j, mine, lb), [self.b1[i, j]])

            each(step)

        def second_done():
            c2.wait_recv()
            own[z, x, :, lc] = total((z, x, slice(None), lc), [self.c2[...]])
            a2.wait_recv()
            b2.wait_recv()

            def step(i):
                own[i, x, mine, la] = total((i, x, mine, la), [self.a2[i]])
                own[i, x, mine, lb] = total((i, x, mine, lb), [self.b2[i]])

            each(step)

        def third_done():
            c3.wait_recv()
            done[c, mine, lc] = total((z, x, mine, lc), [self.c3[...]])
            for copy in a3 + b3:
                copy.wait_recv()
            done[c, mine, la] = total((z, x, mine, la), [self.a3[d - 1] for d, _ in far])
            done[c, mine, lb] = total((z, x, mine, lb), [self.b3[d - 1] for d, _ in far])

        self.ends = [core_done, first_done, second_done, third_done, y4.wait_recv, c5.wait_recv, None]

    def stage(self, n):
        if n > 0:
            self.ends[n - 1]()
        for copy in self.starts[n]:
            copy.start()

    def finish(self):
        for copy in self.sent:
            copy.wait_send()


def greet(peers):
    barrier = pltpu.get_barrier_semaphore()
    for to in peers:
        pl.semaphore_signal(barrier, inc=1, device_id=to, device_id_type=MESH_ID)
    pl.semaphore_wait(barrier, len(peers))


def outer_views(outer, depth):
    half = outer.shape[0] // (4 * depth)
    return outer.reshape(depth, 2, 2, half, outer.shape[1])


def strip_views(strips, depth):
    count, width, _ = strips.shape
    return strips.reshape(count, depth, 2, width // (2 * depth), width)


def big_pieces(inner, outer):
    strips = inner.shape[0] // 2
    first = [(lambda c, j=j: inner.at[c * strips + j], inner.shape[3]) for j in range(strips)]
    return first, [(lambda c: outer.at[:, :, c], outer.shape[3])]


def write_big(first, second, inner_o, outer_o):
    width = outer_o.shape[1]
    part = inner_o.shape[0]
    half = outer_o.shape[0] // 2
    strips = inner_o.shape[1] // width // 2
    for c in range(2):
        for j in range(strips):
            inner_o[:, pl.ds((c * strips + j) * width, width)] = first.done[c, pl.ds(j * part, part)].astype(jnp.float32)
        outer_o[pl.ds(c * half, half)] = second.done[c].astype(jnp.float32)


class Exchange:
    def __init__(self, count, send, recv):
        self.count, self.send, self.recv = count, send, recv
        self.me = lax.axis_index("seq")

    def all(self, src, dst, start=True):
        copies = []
        for step in range(1, self.count):
            to = lax.rem(self.me + step, self.count)
            copies.append(
                pltpu.make_async_remote_copy(
                    src_ref=src(to), dst_ref=dst(self.me), send_sem=self.send.at[step], recv_sem=self.recv.at[step],
                    device_id={"seq": to}, device_id_type=MESH_ID,
                )
            )
        return copies


def begin(copies):
    for copy in copies:
        copy.start()


def end(copies):
    for copy in copies:
        copy.wait()


def seq_peers(count):
    me = lax.axis_index("seq")
    return [{"seq": lax.rem(me + step, count)} for step in range(1, count)]


def sum_rows(values):
    rows, width = values.shape
    return jnp.sum(values.reshape(rows // 8, 8, width), axis=0)


TILE = 256
FOLD_TICKS = {
    0: ((0, 0), (1, 0)),
    3: ((0, 1),),
    5: ((1, 1),),
    8: ((0, 2),),
    10: ((0, 3),),
    12: ((1, 2),),
    13: ((0, 4),),
    14: ((1, 3),),
    15: ((0, 5),),
    17: ((1, 4), (0, 6)),
    18: ((2, 0),),
    19: ((1, 5),),
    20: ((2, 1), (3, 0), (1, 6)),
    21: ((3, 1), (2, 2), (3, 2), (2, 3), (3, 3), (2, 4), (3, 4), (2, 5), (3, 5), (2, 6), (3, 6)),
}


def rear_kernel(
    depth, half, scale, pairs, fold_sizes,
    q_ref, k_ref, v_ref, g_ref, lse_ref, delta_ref, kaug_ref,
    x_ref, res_ref, gx_ref, gres_ref, gout_ref, weight_ref, gain_ref, shift_ref, vectors_ref,
    inner, outer, out,
    igrad_o, gout_o, ggrad_o, inner_o, outer_o, out_o, qkv_o, small_o,
    dqkv, normed, gnormed, gdqkv, parts, sums, qkv_src, small_src, foreign, kept, ggrad,
    send, recv, local, *scratch,
):
    count = 2 * depth
    step = pl.program_id(0)
    place = seat()
    me = lax.axis_index("seq")
    row_count = dqkv.shape[0]
    block_len = normed.shape[1]
    width = normed.shape[2]
    share = gx_ref.shape[1]
    attn = row_count * pairs
    sources = big_pieces(inner, outer) + (
        [(lambda c: out.at[:, :, c], out.shape[3]), (lambda c: qkv_src.at[0, :, :, c], out.shape[3])],
        [(lambda c, j=j: qkv_src.at[j, :, :, c], out.shape[3]) for j in (1, 2)]
        + [(lambda c: small_src, small_src.shape[2])],
    )
    folds, at = [], 0
    for pieces, size in zip(sources, fold_sizes):
        folds.append(Fold(depth, pieces, scratch[at:at + 12], scratch[at + 12:at + 15]))
        at += 15

    to_all = lambda n: Exchange(count, send.at[n], recv.at[n])
    gout_copies = to_all(0).all(lambda to: gout_ref, lambda m: gout_o.at[:, m])
    part_copies = [
        to_all(1 + r).all(
            lambda to: dqkv.at[r, pl.ds(pl.multiple_of(block_len + share * to, 16), share)], lambda m: parts.at[m, r]
        )
        for r in range(row_count)
    ]
    base = 1 + row_count
    ggrad_copies = to_all(base).all(lambda to: ggrad, lambda m: ggrad_o.at[:, m])
    following = lax.rem(me + 1, count)
    home = [
        pltpu.make_async_remote_copy(
            src_ref=foreign.at[r], dst_ref=igrad_o.at[r, pl.ds(0, half)], send_sem=send.at[base + 1, r],
            recv_sem=recv.at[base + 1, r], device_id={"seq": following}, device_id_type=MESH_ID,
        )
        for r in range(row_count)
    ]
    keep = [
        pltpu.make_async_copy(kept.at[r], igrad_o.at[r, pl.ds(half, half)], local.at[2 + r]) for r in range(row_count)
    ]
    own_gout = pltpu.make_async_copy(gout_ref, gout_o.at[:, me], local.at[0])
    own_ggrad = pltpu.make_async_copy(ggrad, ggrad_o.at[:, me], local.at[1])

    @pl.when(step == 0)
    def _():
        greet(seq_peers(count) + [peer(depth, place, dy=1), peer(depth, place, dc=1)])
        begin(gout_copies + [own_gout])
        sums[...] = jnp.zeros_like(sums)

    for t, todo in FOLD_TICKS.items():
        if t < 21:

            @pl.when(step == t)
            def _():
                for f, n in todo:
                    folds[f].stage(n)

    @pl.when(step < attn)
    def _():
        r, p = lax.div(step, pairs), lax.rem(step, pairs)
        spots = [pl.ds(pl.multiple_of(j * width + p * LANES, LANES), LANES) for j in range(3)]
        attend_back_kernel(
            half, scale, 320, p, q_ref, k_ref, v_ref, g_ref, lse_ref, delta_ref, kaug_ref,
            *(dqkv.at[pl.ds(r, 1), :, spot] for spot in spots),
        )

    for r in range(row_count):

        @pl.when(step == (r + 1) * pairs - 1)
        def _():
            begin(part_copies[r])

    gain, shift = gain_ref[...], shift_ref[...]

    def norm_rows(x, grad, dq):
        x = x.astype(jnp.float32)
        centred = x - jnp.mean(x, axis=-1, keepdims=True)
        inv = lax.rsqrt(jnp.mean(centred * centred, axis=-1, keepdims=True) + EPS)
        n = centred * inv
        first = nt(dq, weight_ref[...])
        eg = first * gain
        through = (eg - jnp.mean(eg, axis=-1, keepdims=True) - n * jnp.mean(eg * n, axis=-1, keepdims=True)) * inv
        sums[0] += sum_rows(first * n)
        sums[1] += sum_rows(first)
        return (grad + through).astype(jnp.bfloat16), (n * gain + shift).astype(jnp.bfloat16)

    for tile in range(2 * row_count):
        r, h = tile % row_count, 1 - tile // row_count

        @pl.when(step == attn + tile)
        def _():
            rows = pl.ds(h * half, half)
            grad, n = norm_rows(x_ref[...], res_ref[...], dqkv[r, rows])
            normed[r, rows] = n
            if h == 1:
                foreign[r] = grad
                home[r].start()
            else:
                kept[r] = grad
                keep[r].start()

    after = attn + 2 * row_count

    @pl.when(step == after)
    def _():
        for r in range(row_count):
            for copy in part_copies[r]:
                copy.wait_recv()
        for r in range(row_count):
            total = dqkv[r, pl.ds(pl.multiple_of(block_len + share * me, 16), share)].astype(jnp.float32)
            for s in range(1, count):
                total = total + parts[lax.rem(me + s, count), r].astype(jnp.float32)
            gdqkv[r] = total.astype(jnp.bfloat16)
        rows = row_count * share
        grad, n = norm_rows(
            gx_ref[...].reshape(rows, width), gres_ref[...].reshape(rows, width), gdqkv[...].reshape(rows, 3 * width)
        )
        ggrad[...] = grad.reshape(row_count, share, width)
        gnormed[...] = n
        begin(ggrad_copies + [own_ggrad])
        lines = [jnp.sum(sums[n], axis=0, keepdims=True) for n in range(2)]
        block = jnp.concatenate(lines + [vectors_ref[...], jnp.zeros((small_src.shape[2] - 8, width), jnp.float32)])
        block = block.astype(jnp.bfloat16)
        for i in range(depth):
            for j in range(2):
                small_src[i, j] = block

    for j in range(3):

        @pl.when(step == after + 1 + j)
        def _():
            strip = pl.ds(j * width, width)
            total = tn(gnormed[...], gdqkv[:, :, strip].reshape(row_count * share, width))
            for r in range(row_count):
                total = total + tn(normed[r], dqkv[r, pl.ds(0, block_len), strip])
            qkv_src[j] = total.astype(jnp.bfloat16).reshape(qkv_src.shape[1:])

    @pl.when(step == after + 4)
    def _():
        write_big(folds[0], folds[1], inner_o, outer_o)
        for f, n in FOLD_TICKS[21]:
            folds[f].stage(n)
        part = out_o.shape[0]
        f32 = jnp.float32
        for c in range(2):
            rows = pl.ds(c * part // 2, part // 2)
            first, second = pl.ds(0, part // 2), pl.ds(part // 2, part // 2)
            out_o[rows] = folds[2].done[c, first].astype(f32)
            for j, (fold, spot) in enumerate(((folds[2], second), (folds[3], first), (folds[3], second))):
                qkv_o[rows, pl.ds(j * width, width)] = fold.done[c, spot].astype(f32)
        small_o[...] = folds[3].done[0, pl.ds(part, small_o.shape[0])].astype(f32)
        for fold in folds:
            fold.finish()
        own_gout.wait()
        own_ggrad.wait()
        end(keep + gout_copies + ggrad_copies + home)
        for copies in part_copies:
            for copy in copies:
                copy.wait_send()


def rear(
    qkv, grad, lse, delta, kaug, tokens, res_grad, own_globals, own_res, own_out,
    weight, gain, shift, vectors, inner, outer, out, half, count,
):
    row_count, rows, cols = qkv.shape
    width = cols // 3
    pairs = width // LANES
    depth = count // 2
    block_len = 2 * half
    global_count = rows - block_len
    share = global_count // count
    part = width // count
    scale = (width // HEADS) ** (-0.5)
    attn = row_count * pairs
    f32, bf16 = jnp.float32, jnp.bfloat16
    row_of = lambda t: jnp.minimum(t, attn - 1) // pairs
    pair_of = lambda t: jnp.minimum(t, attn - 1) % pairs
    spec = lambda off: pl.BlockSpec((1, rows, LANES), lambda t: (row_of(t), 0, off + pair_of(t)))
    whole = pl.BlockSpec((1, rows, LANES), lambda t: (row_of(t), 0, 0))

    def tile_of(t):
        n = jnp.clip(t - attn, 0, 2 * row_count - 1)
        return n % row_count * 2 + 1 - n // row_count, 0

    fixed = lambda a: pl.BlockSpec(a.shape, lambda t: (0,) * a.ndim, pipeline_mode=pl.Buffered(1))
    tile = pl.BlockSpec((half, width), tile_of)
    hbm = pl.BlockSpec(memory_space=pl.ANY)
    own_globals, own_res, own_out = (a.reshape(row_count, share, width) for a in (own_globals, own_res, own_out))
    outs = [
        jax.ShapeDtypeStruct((row_count, block_len, width), bf16),
        jax.ShapeDtypeStruct((row_count, count, share, width), bf16),
        jax.ShapeDtypeStruct((row_count, count, share, width), bf16),
        jax.ShapeDtypeStruct((part, 4 * width), f32),
        jax.ShapeDtypeStruct((4 * part, width), f32),
        jax.ShapeDtypeStruct((part, width), f32),
        jax.ShapeDtypeStruct((part, 3 * width), f32),
        jax.ShapeDtypeStruct((8, width), f32),
    ]
    fold_sizes = ((2 * part, 2), (2 * part, 1), (part, 2), (part + 32, 3))
    folds = []
    for size, pieces in fold_sizes:
        folds += Fold.scratch(depth, size, width, pieces)
    vmem = pltpu.VMEM
    kinds = 3 + row_count
    inputs = (gain, shift, vectors)
    return pl.pallas_call(
        functools.partial(rear_kernel, depth, half, scale, pairs, fold_sizes),
        grid=(attn + 2 * row_count + 5,),
        in_specs=[spec(0), spec(pairs), spec(2 * pairs), spec(0), whole, whole, whole]
        + [tile, tile, fixed(own_globals), fixed(own_res), fixed(own_out), fixed(weight)]
        + [fixed(a) for a in inputs]
        + [hbm] * 3,
        out_specs=[hbm] * 3 + [pl.BlockSpec(memory_space=pltpu.VMEM)] * 5,
        out_shape=outs,
        scratch_shapes=[
            vmem((row_count, rows, cols), bf16),
            vmem((row_count, block_len, width), bf16),
            vmem((row_count * share, width), bf16),
            vmem((row_count, share, cols), bf16),
            vmem((count, row_count, share, cols), bf16),
            vmem((2, 8, width), f32),
            vmem((3, depth, 2, 2, part // 2, width), bf16),
            vmem((depth, 2, 32, width), bf16),
            vmem((row_count, half, width), bf16),
            vmem((row_count, half, width), bf16),
            vmem((row_count, share, width), bf16),
            pltpu.SemaphoreType.DMA((kinds, count)),
            pltpu.SemaphoreType.DMA((kinds, count)),
            pltpu.SemaphoreType.DMA((2 + row_count,)),
        ]
        + folds,
        compiler_params=pltpu.CompilerParams(
            collective_id=9, has_side_effects=True, vmem_limit_bytes=64 * 1024 * 1024
        ),
        name="rear",
    )(
        qkv, qkv, qkv, grad, lse, delta, kaug, tokens, res_grad, own_globals, own_res, own_out, weight, *inputs,
        strip_views(inner, depth), outer_views(outer, depth), out.reshape(depth, 2, 2, part // 2, width),
    )


def wgrad_kernel(a_ref, b_ref, o_ref):
    o_ref[...] = tn(a_ref[...], b_ref[...]).astype(o_ref.dtype).reshape(o_ref.shape)


def wgrad(a, b, strip):
    rows, a_cols = a.shape
    b_cols = b.shape[1]
    split_a = a_cols > b_cols
    strips = max(a_cols, b_cols) // strip
    fixed = lambda n: (0, 0)
    moving = lambda n: (0, n)
    return pl.pallas_call(
        wgrad_kernel,
        grid=(strips,),
        in_specs=[
            pl.BlockSpec((rows, strip), moving if split_a else fixed),
            pl.BlockSpec((rows, strip), fixed if split_a else moving),
        ],
        out_specs=pl.BlockSpec((1, strip, strip), lambda n: (n, 0, 0)),
        out_shape=jax.ShapeDtypeStruct((strips, strip, strip), jnp.bfloat16),
        compiler_params=pltpu.CompilerParams(vmem_limit_bytes=40 * 1024 * 1024),
        name="wgrad",
    )(a, b)


def norm_parts(values):
    average = jnp.mean(values, axis=-1, keepdims=True)
    centred = values - average
    variance = jnp.mean(centred * centred, axis=-1, keepdims=True)
    inv = lax.rsqrt(variance + EPS)
    return centred * inv, inv


def norm_back(grad, n, inv, gain):
    eg = grad * gain
    through = (
        eg - jnp.mean(eg, axis=-1, keepdims=True) - n * jnp.mean(eg * n, axis=-1, keepdims=True)
    ) * inv
    return through, jnp.sum(grad * n, axis=0), jnp.sum(grad, axis=0)


def split_rows(a, count):
    row_count, rows, width = a.shape
    part = rows // count
    moved = a.reshape(row_count, count, part, width).transpose(1, 0, 2, 3)
    return moved.reshape(count, row_count * part, width)


def join_rows(a, row_count):
    count, rows, width = a.shape
    part = rows // row_count
    moved = a.reshape(count, row_count, part, width).transpose(1, 0, 2, 3)
    return moved.reshape(row_count, count * part, width)


def per_head(values, width):
    lanes = values[..., :HEADS]
    return jnp.repeat(lanes, width // HEADS, axis=-1)


def head_sums(values):
    rows, width = values.shape
    lane = jnp.arange(LANES)
    head = jnp.arange(width) // (width // HEADS)
    place = ((lane[None, :] % HEADS == head[:, None]) & (lane[None, :] < 3 * HEADS)).astype(jnp.bfloat16)
    top = values.astype(jnp.bfloat16)
    rest = (values - top.astype(jnp.float32)).astype(jnp.bfloat16)
    return nn(top, place) + nn(rest, place)


def reduce_share(a):
    a = lax.psum_scatter(a, "seq", scatter_dimension=0, tiled=True)
    return lax.psum(a.astype(jnp.bfloat16), "batch").astype(jnp.float32)


def body(
    inputs,
    global_inputs,
    lengths,
    first_gain,
    first_shift,
    qkv_weight,
    out_weight,
    second_gain,
    second_shift,
    inner_weight,
    inner_bias,
    outer_weight,
    output_cotangent,
    global_cotangent,
):
    f32, bf16 = jnp.float32, jnp.bfloat16
    row_count, block_len, width = inputs.shape
    half = block_len // 2
    global_count = global_inputs.shape[1]
    rows = block_len + global_count
    inner_width = inner_weight.shape[1]
    count = lax.axis_size("seq")
    me = lax.axis_index("seq")
    after = lax.rem(me + 1, count)
    back = [(i, (i - 1) % count) for i in range(count)]
    forth = [(i, (i + 1) % count) for i in range(count)]
    token_rows = row_count * block_len
    share = global_count // count
    own_rows = row_count * share

    next_inputs = lax.ppermute(inputs[:, :half], "seq", back)
    next_cotangent = lax.ppermute(output_cotangent[:, :half], "seq", back)
    block = jnp.concatenate([inputs[:, half:], next_inputs], axis=1)
    spots = jnp.arange(half, dtype=jnp.int32)
    positions = jnp.concatenate([me * block_len + half + spots, after * block_len + spots])
    valid = positions[None, :] < lengths[:, None]

    kind = jnp.arange(LANES)[None, None, :] - TYPE0
    key_half = (jnp.arange(block_len) // half)[None, :, None]
    last = me == count - 1
    hidden_key = jnp.logical_not(valid)[:, :, None] | (last & (kind < 2) & (kind != key_half))
    token_marks = jnp.where(hidden_key & (kind >= 0) & (kind < 3), NEG, 0.0)
    global_marks = jnp.where((kind == 2) & (me != 0), NEG, 0.0)
    global_marks = jnp.broadcast_to(global_marks, (row_count, global_count, LANES))
    kaug = jnp.concatenate([token_marks, global_marks], axis=1).astype(bf16)

    states = jnp.concatenate([block, global_inputs], axis=1)
    n_first, inv_first = norm_parts(states.astype(f32))
    normed = (n_first * first_gain + first_shift).astype(bf16)
    qkv = nn(normed.reshape(row_count * rows, width), qkv_weight).astype(bf16)
    qkv = qkv.reshape(row_count, rows, 3 * width)

    mixed, lse = attend(qkv, kaug, half)
    part_mixed, part_lse = spread(
        [split_rows(mixed[:, block_len:], count), split_rows(lse[:, block_len:], count)], count, False, 0
    )
    highest = jnp.max(part_lse, axis=0)
    part_weight = jnp.exp(part_lse - highest)
    total = jnp.sum(part_weight, axis=0)
    global_lse = highest + jnp.log(total)
    global_mixed = jnp.sum(per_head(part_weight / total, width) * part_mixed.astype(f32), axis=0)

    own_globals = lax.dynamic_slice_in_dim(global_inputs, me * share, share, axis=1)
    own_global_cot = lax.dynamic_slice_in_dim(global_cotangent, me * share, share, axis=1)
    tokens_in = block.reshape(token_rows, width)
    tokens = jnp.concatenate([tokens_in, own_globals.reshape(own_rows, width)]).astype(f32)
    cot_block = jnp.concatenate([output_cotangent[:, half:], next_cotangent], axis=1)
    cot_block = jnp.where(valid[:, :, None], cot_block, 0)
    cotangent = jnp.concatenate(
        [cot_block.reshape(token_rows, width), own_global_cot.reshape(own_rows, width)]
    )
    attended = jnp.concatenate(
        [mixed[:, :block_len].reshape(token_rows, width), global_mixed.astype(bf16)]
    )
    residual = tokens + nn(attended, out_weight)
    n_second, inv_second = norm_parts(residual)
    normed_second = (n_second * second_gain + second_shift).astype(bf16)
    inner = nn(normed_second, inner_weight) + inner_bias
    bell = jnp.exp(-0.5 * inner * inner)
    cdf = 0.5 * (1.0 + lax.erf(inner * (0.5 ** 0.5)))
    hidden = (inner * cdf).astype(bf16)
    final = residual + nn(hidden, outer_weight)
    hidden_grad = nt(cotangent, outer_weight)
    slope = cdf + inner * bell * ((0.5 / jnp.pi) ** 0.5)
    inner_grad = (hidden_grad * slope).astype(bf16)
    second_grad = nt(inner_grad, inner_weight)
    through, second_gain_grad, second_shift_grad = norm_back(second_grad, n_second, inv_second, second_gain)
    residual_grad = cotangent.astype(f32) + through
    projection_grad = residual_grad.astype(bf16)
    attended_grad = nt(projection_grad, out_weight).astype(bf16)
    delta = head_sums(attended_grad.astype(f32) * attended.astype(f32))
    outer_grad = wgrad(hidden, cotangent, width)
    inner_wgrad = wgrad(normed_second, inner_grad, width)
    bias_grad = jnp.sum(inner_grad.astype(f32), axis=0)
    out_grad = wgrad(attended, projection_grad, width)

    all_grad, all_lse, all_delta = spread(
        [attended_grad[token_rows:], global_lse, delta[token_rows:]], count, True, 1
    )
    block_grad = jnp.concatenate(
        [attended_grad[:token_rows].reshape(row_count, block_len, width), join_rows(all_grad, row_count)], axis=1
    )
    block_lse = jnp.concatenate([lse[:, :block_len], join_rows(all_lse, row_count)], axis=1)
    block_delta = jnp.concatenate(
        [delta[:token_rows].reshape(row_count, block_len, LANES), join_rows(all_delta, row_count)], axis=1
    )
    layer = final[:token_rows].reshape(row_count, block_len, width)
    layer = jnp.where(valid[:, :, None], layer, 0.0).astype(bf16)
    layer_output = jnp.concatenate([lax.ppermute(layer[:, half:], "seq", forth), layer[:, :half]], axis=1)
    own_out = final[token_rows:].astype(bf16)
    part = width // count
    if count == 8 and lax.axis_size("batch") == 4:
        vectors = jnp.concatenate([second_gain_grad, second_shift_grad, bias_grad]).reshape(6, width)
        input_out, global_out, global_grad, inner_out, outer_out, out_out, qkv_out, small = rear(
            qkv, block_grad, block_lse, block_delta, kaug, tokens_in, residual_grad, own_globals, residual_grad[token_rows:],
            own_out, qkv_weight, first_gain[None], first_shift[None], vectors, inner_wgrad,
            outer_grad.reshape(inner_width, width), out_grad[0], half, count,
        )
        global_out = global_out.reshape(row_count, global_count, width)
        global_grad = global_grad.reshape(row_count, global_count, width)
        cut = lambda a: lax.dynamic_slice_in_dim(a, me * (a.shape[0] // count), a.shape[0] // count)
        vectors_out = [cut(small[n]) for n in range(4)] + [cut(small[4:].reshape(-1))]
        return (
            layer_output, global_out, input_out, global_grad, vectors_out[0], vectors_out[1], qkv_out, out_out,
            vectors_out[2], vectors_out[3], inner_out, vectors_out[4], outer_out,
        )
    dqkv = jnp.concatenate(attend_back(qkv, block_grad, block_lse, block_delta, kaug, half, rows), axis=-1)
    (part_dqkv,) = spread([split_rows(dqkv[:, block_len:], count)], count, False, 2)
    global_dqkv = jnp.sum(part_dqkv.astype(f32), axis=0).astype(bf16)
    qkv_grad = jnp.concatenate([dqkv[:, :block_len].reshape(token_rows, 3 * width), global_dqkv])

    first_grad = nt(qkv_grad, qkv_weight)
    n_tokens, inv_tokens = norm_parts(tokens)
    through, first_gain_grad, first_shift_grad = norm_back(first_grad, n_tokens, inv_tokens, first_gain)
    input_grad = (residual_grad + through).astype(bf16)
    normed_tokens = (n_tokens * first_gain + first_shift).astype(bf16)
    qkv_wgrad = wgrad(normed_tokens, qkv_grad, width)

    grad_block = input_grad[:token_rows].reshape(row_count, block_len, width)
    input_out = jnp.concatenate(
        [lax.ppermute(grad_block[:, half:], "seq", forth), grad_block[:, :half]], axis=1
    )
    global_final, global_grad = spread([own_out, input_grad[token_rows:]], count, True, 3)

    def shares(a):
        return a.reshape(count, a.shape[0] // count)

    small = jnp.concatenate(
        [
            shares(first_gain_grad),
            shares(first_shift_grad),
            shares(second_gain_grad),
            shares(second_shift_grad),
            shares(bias_grad),
        ],
        axis=1,
    )
    inner_out = reduce_share(inner_wgrad.transpose(1, 0, 2).reshape(width, -1))
    outer_out = reduce_share(outer_grad.reshape(inner_width, width))
    out_out = reduce_share(out_grad[0])
    qkv_out = reduce_share(qkv_wgrad.transpose(1, 0, 2).reshape(width, -1))
    small = reduce_share(small)[0]
    return (
        layer_output,
        join_rows(global_final, row_count),
        input_out,
        join_rows(global_grad, row_count),
        small[:part],
        small[part:2 * part],
        qkv_out,
        out_out,
        small[2 * part:3 * part],
        small[3 * part:4 * part],
        inner_out,
        small[4 * part:],
        outer_out,
    )


def solution(mesh):
    rows = P("batch", "seq", None)
    globals_at = P("batch", None, None)
    return jax.shard_map(
        body,
        mesh=mesh,
        in_specs=(rows, globals_at, P("batch")) + (P(),) * 9 + (rows, globals_at),
        out_specs=(
            rows,
            globals_at,
            rows,
            globals_at,
            P("seq"),
            P("seq"),
            P("seq", None),
            P("seq", None),
            P("seq"),
            P("seq"),
            P("seq", None),
            P("seq"),
            P("seq", None),
        ),
        check_vma=False,
    )
```

```python
import functools
import math

import jax
import jax.numpy as jnp
from jax import lax
from jax.experimental import pallas as pl
from jax.experimental.pallas import tpu as pltpu
from jax.sharding import PartitionSpec as P

HEADS = 12
NEG = -1e30
LANES = 128
TYPE0 = 3 * HEADS

def nt(a, b):
    return lax.dot_general(a, b, (((1,), (1,)), ((), ())), preferred_element_type=jnp.float32)

def tn(a, b):
    return lax.dot_general(a, b, (((0,), (0,)), ((), ())), preferred_element_type=jnp.float32)

def nn(a, b):
    return jnp.dot(a, b, preferred_element_type=jnp.float32)


def type_marks(rows, half, lane, row):
    kind = jnp.where(row < half, TYPE0, jnp.where(row < 2 * half, TYPE0 + 1, TYPE0 + 2))
    return (lane == kind)


def attend_kernel(half, scale, tq, q_ref, k_ref, v_ref, kaug_ref, o_ref, lse_ref):
    pair = pl.program_id(1)
    rows = q_ref.shape[1]
    zero = jnp.zeros((), jnp.bfloat16)
    k, v = k_ref[0], v_ref[0]
    kaug = kaug_ref[0]
    lane_all = lax.broadcasted_iota(jnp.int32, (rows, LANES), 1)
    low_all = lane_all < LANES // 2
    one = jnp.ones((), jnp.bfloat16)
    kx, vx = [], []
    for sel in (low_all, jnp.logical_not(low_all)):
        kx.append(jnp.concatenate([jnp.where(sel, k, zero), kaug], axis=1))
        vx.append(jnp.concatenate([jnp.where(sel, v, zero), jnp.where(sel, one, zero)], axis=1))
    for start in range(0, rows, tq):
        lane = lax.broadcasted_iota(jnp.int32, (tq, LANES), 1)
        row = lax.broadcasted_iota(jnp.int32, (tq, LANES), 0) + start
        low = lane < LANES // 2
        qaug = jnp.where(type_marks(rows, half, lane, row), one, zero)
        q = (q_ref[0, start:start + tq].astype(jnp.float32) * scale).astype(jnp.bfloat16)
        qx = jnp.concatenate([q, qaug], axis=1)
        acc = None
        peaks = []
        for a in (0, 1):
            s = nt(qx, kx[a])
            peak = jnp.max(s, axis=1, keepdims=True)
            p = jnp.exp(s - peak).astype(jnp.bfloat16)
            part = nn(p, vx[a])
            acc = part if acc is None else acc + part
            peaks.append(peak)
        total = acc[:, LANES:]
        o_ref[0, start:start + tq] = (acc[:, :LANES] / total).astype(jnp.bfloat16)
        lse = jnp.where(low, peaks[0], peaks[1]) + jnp.log(total)
        first, second = lse[:, 0:1], lse[:, LANES // 2:LANES // 2 + 1]
        prev = jnp.where(pair == 0, 0.0, lse_ref[0, start:start + tq])
        head = lax.rem(lane, HEADS)
        inside = lane < 3 * HEADS
        kept = jnp.where(inside & (head == 2 * pair), first, prev)
        lse_ref[0, start:start + tq] = jnp.where(inside & (head == 2 * pair + 1), second, kept)


def attend(qkv, kaug, half, tq=320):
    row_count, rows, cols = qkv.shape
    width = cols // 3
    pairs = width // LANES
    scale = (width // HEADS) ** (-0.5)
    spec = lambda off: pl.BlockSpec((1, rows, LANES), lambda r, p: (r, 0, off + p))
    return pl.pallas_call(
        functools.partial(attend_kernel, half, scale, tq),
        grid=(row_count, pairs),
        in_specs=[spec(0), spec(pairs), spec(2 * pairs), pl.BlockSpec((1, rows, LANES), lambda r, p: (r, 0, 0))],
        out_specs=[spec(0), pl.BlockSpec((1, rows, LANES), lambda r, p: (r, 0, 0))],
        out_shape=[
            jax.ShapeDtypeStruct((row_count, rows, width), jnp.bfloat16),
            jax.ShapeDtypeStruct((row_count, rows, LANES), jnp.float32),
        ],
        compiler_params=pltpu.CompilerParams(vmem_limit_bytes=48 * 1024 * 1024),
        name="attend",
    )(qkv, qkv, qkv, kaug)


def three_parts(values, lane):
    top = values.astype(jnp.bfloat16)
    rest = values - top.astype(jnp.float32)
    mid = rest.astype(jnp.bfloat16)
    low = (rest - mid.astype(jnp.float32)).astype(jnp.bfloat16)
    zero = jnp.zeros((), jnp.bfloat16)
    return jnp.where(lane < HEADS, top, jnp.where(lane < 2 * HEADS, mid, jnp.where(lane < 3 * HEADS, low, zero)))


def attend_back_step(half, scale, tk, q_ref, k_ref, v_ref, g_ref, lse_ref, delta_ref, *refs):
    attend_back_kernel(
        half, scale, tk, pl.program_id(1), q_ref, k_ref, v_ref, g_ref[0], lse_ref[0], delta_ref[0], *refs
    )


def attend_back_kernel(half, scale, tk, pair, q_ref, k_ref, v_ref, g, lse, delta, kaug_ref, dq_ref, dk_ref, dv_ref):
    rows = q_ref.shape[1]
    zero = jnp.zeros((), jnp.bfloat16)
    one = jnp.ones((), jnp.bfloat16)
    lane = lax.broadcasted_iota(jnp.int32, (rows, LANES), 1)
    row = lax.broadcasted_iota(jnp.int32, (rows, LANES), 0)
    low = lane < LANES // 2
    q = (q_ref[0].astype(jnp.float32) * scale).astype(jnp.bfloat16)
    qaug = jnp.where(type_marks(rows, half, lane, row), one, three_parts(lse, lane))
    gaug = three_parts(delta, lane)
    qx = jnp.concatenate([q, qaug], axis=1)
    gx = jnp.concatenate([g, gaug], axis=1)
    sels = (low, jnp.logical_not(low))
    qh = [jnp.where(sel, q, zero) for sel in sels]
    gh = [jnp.where(sel, g, zero) for sel in sels]
    dq = None
    for start in range(0, rows, tk):
        lane_k = lax.broadcasted_iota(jnp.int32, (tk, LANES), 1)
        low_k = lane_k < LANES // 2
        head = lax.rem(lane_k, HEADS)
        inside = lane_k < 3 * HEADS
        k = k_ref[0, start:start + tk]
        v = v_ref[0, start:start + tk]
        kaug = kaug_ref[0, start:start + tk]
        dk = dv = None
        for a, sel in ((0, low_k), (1, jnp.logical_not(low_k))):
            marks = inside & (head == 2 * pair + a)
            kh = jnp.where(sel, k, zero)
            kx = jnp.concatenate([kh, jnp.where(marks, -one, kaug)], axis=1)
            vx = jnp.concatenate([jnp.where(sel, v, zero), jnp.where(marks, -one, zero)], axis=1)
            p = jnp.exp(nt(kx, qx))
            ds = (p * nt(vx, gx)).astype(jnp.bfloat16)
            part_v = nn(p.astype(jnp.bfloat16), gh[a])
            part_k = nn(ds, qh[a])
            part_q = tn(ds, kh)
            dv = part_v if dv is None else dv + part_v
            dk = part_k if dk is None else dk + part_k
            dq = part_q if dq is None else dq + part_q
        dk_ref[0, start:start + tk] = dk.astype(jnp.bfloat16)
        dv_ref[0, start:start + tk] = dv.astype(jnp.bfloat16)
    dq_ref[0] = (dq * scale).astype(jnp.bfloat16)


def attend_back(qkv, grad, lse, delta, kaug, half, tk=320):
    row_count, rows, cols = qkv.shape
    width = cols // 3
    pairs = width // LANES
    scale = (width // HEADS) ** (-0.5)
    spec = lambda off: pl.BlockSpec((1, rows, LANES), lambda r, p: (r, 0, off + p))
    whole = pl.BlockSpec((1, rows, LANES), lambda r, p: (r, 0, 0))
    out = jax.ShapeDtypeStruct((row_count, rows, width), jnp.bfloat16)
    return pl.pallas_call(
        functools.partial(attend_back_step, half, scale, tk),
        grid=(row_count, pairs),
        in_specs=[spec(0), spec(pairs), spec(2 * pairs), spec(0), whole, whole, whole],
        out_specs=[spec(0)] * 3,
        out_shape=[out] * 3,
        compiler_params=pltpu.CompilerParams(vmem_limit_bytes=48 * 1024 * 1024),
        name="attend_back",
    )(qkv, qkv, qkv, grad, lse, delta, kaug)


EPS = 1e-05
MESH_ID = pl.DeviceIdType.MESH


def spread_kernel(count, sizes, same, *refs):
    ins, outs = refs[:sizes], refs[sizes:2 * sizes]
    send, recv, local = refs[2 * sizes:]
    me = lax.axis_index("seq")
    barrier = pltpu.get_barrier_semaphore()
    for step in range(1, count):
        pl.semaphore_signal(
            barrier, inc=1, device_id={"seq": lax.rem(me + step, count)}, device_id_type=MESH_ID
        )
    pl.semaphore_wait(barrier, count - 1)
    own = []
    for n in range(sizes):
        copy = pltpu.make_async_copy(ins[n] if same else ins[n].at[me], outs[n].at[me], local.at[n])
        copy.start()
        own.append(copy)
    copies = []
    for step in range(1, count):
        peer = lax.rem(me + step, count)
        for n in range(sizes):
            copy = pltpu.make_async_remote_copy(
                src_ref=ins[n] if same else ins[n].at[peer],
                dst_ref=outs[n].at[me],
                send_sem=send.at[n, step],
                recv_sem=recv.at[n, step],
                device_id={"seq": peer},
                device_id_type=MESH_ID,
            )
            copy.start()
            copies.append(copy)
    for copy in own:
        copy.wait()
    for copy in copies:
        copy.wait()


def spread(arrays, count, same, collective_id):
    sizes = len(arrays)
    shapes = [(count,) + a.shape if same else a.shape for a in arrays]
    vmem = pl.BlockSpec(memory_space=pltpu.VMEM)
    return pl.pallas_call(
        functools.partial(spread_kernel, count, sizes, same),
        in_specs=[vmem] * sizes,
        out_specs=[vmem] * sizes,
        out_shape=[jax.ShapeDtypeStruct(s, a.dtype) for s, a in zip(shapes, arrays)],
        scratch_shapes=[
            pltpu.SemaphoreType.DMA((sizes, count)),
            pltpu.SemaphoreType.DMA((sizes, count)),
            pltpu.SemaphoreType.DMA((sizes,)),
        ],
        compiler_params=pltpu.CompilerParams(
            collective_id=collective_id, has_side_effects=True, vmem_limit_bytes=32 * 1024 * 1024
        ),
        name="spread",
    )(*arrays)


SEQ_BITS = (("z1", 4), ("z0", 2), ("x", 1))
BATCH_BITS = (("y", 2), ("c", 1))


class Place:
    def __init__(self):
        self.spot, self.step = {}, {}
        for name, bits in (("seq", SEQ_BITS), ("batch", BATCH_BITS)):
            index = lax.axis_index(name)
            for axis, weight in bits:
                bit = lax.rem(lax.div(index, weight), 2)
                self.spot[axis] = bit
                self.step[axis] = {name: index + weight * (1 - 2 * bit)}

    def __getitem__(self, axis):
        return self.spot[axis]

    def partner(self, axis):
        return self.step[axis]

    def greet(self, others=()):
        barrier = pltpu.get_barrier_semaphore()
        peers = list(self.step.values()) + list(others)
        for to in peers:
            pl.semaphore_signal(barrier, inc=1, device_id=to, device_id_type=MESH_ID)
        pl.semaphore_wait(barrier, len(peers))


def remote(src, dst, send, recv, to):
    return pltpu.make_async_remote_copy(
        src_ref=src, dst_ref=dst, send_sem=send, recv_sem=recv, device_id=to, device_id_type=MESH_ID
    )


class Halve:
    def __init__(self, place, own, lanes, order, bufs, send, recv, first, stages=None):
        self.place, self.own, self.order = place, own, order
        self.lanes = pl.ds(*lanes)
        self.half = own.shape[3] // 2
        stages = range(len(order)) if stages is None else stages
        self.bufs = dict(zip(stages, bufs))
        self.copies = {
            n: remote(
                own.at[self.region(n, False)], self.bufs[n], send.at[first + n], recv.at[first + n], place.partner(order[n])
            )
            for n in stages
        }

    @staticmethod
    def buffers(rows, width, order, stages=None, dtype=jnp.bfloat16):
        shapes = []
        for n in range(len(order)) if stages is None else stages:
            left = [axis for axis, _ in SEQ_BITS if axis not in order[:n + 1]]
            shapes.append((2,) * len(left) + (rows // 2 if "y" in order[:n + 1] else rows, width))
        return [pltpu.VMEM(shape, dtype) for shape in shapes]

    def region(self, n, mine, free=(), piece=None):
        free = list(free)
        at = []
        for axis, _ in SEQ_BITS:
            if axis in self.order[:n]:
                at.append(self.place[axis])
            elif axis == self.order[n]:
                at.append(self.place[axis] if mine else 1 - self.place[axis])
            else:
                at.append(free.pop(0) if free else slice(None))
        first, count = 0, self.own.shape[3]
        if "y" in self.order[:n + 1]:
            y = self.place["y"]
            y = y if mine or self.order[n] != "y" else 1 - y
            first, count = y * self.half, self.half
        if piece is not None:
            first, count = first + piece[0], piece[1]
        rows = pl.ds(pl.multiple_of(first, 16), count)
        return (*at, rows, self.lanes)

    def start(self, n):
        self.copies[n].start()

    def finish(self, n):
        self.copies[n].wait_recv()
        buf = self.bufs[n]
        dims = len(buf.shape) - 2
        count = buf.shape[-2]
        piece = math.gcd(count, 48)
        pieces = count // piece

        def add(i, carry):
            block, row = lax.div(i, pieces), lax.rem(i, pieces) * piece
            free = [lax.rem(lax.div(block, 2 ** (dims - 1 - d)), 2) for d in range(dims)]
            at = self.region(n, True, free, (row, piece))
            more = buf[(*free, pl.ds(pl.multiple_of(row, 16), piece), slice(None))]
            self.own[at] = (self.own[at].astype(jnp.float32) + more.astype(jnp.float32)).astype(self.own.dtype)
            return carry

        lax.fori_loop(0, 2 ** dims * pieces, add, 0)


class Gather:
    order = ("z1", "z0", "x")

    def __init__(self, place, buf, send, recv):
        self.copies = []
        for n, axis in enumerate(self.order):
            at = tuple(slice(None) if other in self.order[:n] else place[other] for other, _ in SEQ_BITS)
            self.copies.append(remote(buf.at[at], buf.at[at], send.at[n], recv.at[n], place.partner(axis)))

    def stage(self, n):
        if n > 0:
            self.copies[n - 1].wait_recv()
        if n < 3:
            self.copies[n].start()

    def finish(self):
        for copy in self.copies:
            copy.wait_send()


PARTS = (
    ((0, 256), ("x", "y", "z0", "z1")),
    ((256, 256), ("y", "x", "z0", "z1")),
    ((512, 256), ("z0", "z1", "x", "y")),
)


class Fold:
    EARLY, LATE = (0, 1), (2, 3)

    def __init__(self, place, pieces, refs, source=None, stages=(0, 1, 2, 3)):
        self.place = place
        c, y = place["c"], place["y"]
        if stages == self.LATE:
            self.own, self.done, send, recv, *bufs = refs
            self.got = local = None
        elif source is None:
            self.own, self.done, *refs = refs
        else:
            self.own, self.done = source.at[:, :, :, c], None
        if stages != self.LATE:
            self.got, send, recv, local, *bufs = refs
        own, got, done = self.own, self.got, self.done
        rows = own.shape[3]
        half = rows // 2
        self.mine = pl.ds(pl.multiple_of(y * half, 16), half)
        at, self.keep, self.core = 0, [], []
        if stages == self.LATE:
            pieces = ()
        if source is not None:
            self.core.append(remote(source.at[:, :, :, 1 - c], got, send.at[0], recv.at[0], place.partner("c")))
            pieces = ()
        for n, (take, count) in enumerate(pieces):
            spot = pl.ds(at, count)
            self.keep.append(pltpu.make_async_copy(take(c), own.at[:, :, :, spot], local.at[n]))
            self.core.append(
                remote(take(1 - c), got.at[:, :, :, spot], send.at[n], recv.at[n], place.partner("c"))
            )
            at += count
        first = len(self.core)
        self.parts = []
        for n, (lanes, order) in enumerate(PARTS):
            own_bufs = bufs[len(stages) * n:len(stages) * (n + 1)]
            self.parts.append(Halve(place, own, lanes, order, own_bufs, send, recv, first + 4 * n, stages))
        first += 12
        if done is None:
            return
        self.across = remote(
            done.at[c, self.mine], done.at[c, self.mine], send.at[first], recv.at[first], place.partner("y")
        )
        self.back = remote(done.at[c], done.at[c], send.at[first + 1], recv.at[first + 1], place.partner("c"))

    @staticmethod
    def scratch(rows, width, pieces, sourced=False, stages=(0, 1, 2, 3)):
        vmem = lambda *shape: pltpu.VMEM(shape, jnp.bfloat16)
        refs = [] if sourced else [vmem(2, 2, 2, rows, width), vmem(2, rows, width)]
        if stages != Fold.LATE:
            refs.append(vmem(2, 2, 2, rows, width))
        refs += [
            pltpu.SemaphoreType.DMA((pieces + 14,)),
            pltpu.SemaphoreType.DMA((pieces + 14,)),
        ]
        if stages != Fold.LATE:
            refs.append(pltpu.SemaphoreType.DMA((pieces,)))
        for (_, count), order in PARTS:
            refs += Halve.buffers(rows, count, order, stages)
        return refs

    def stage(self, n):
        if n == 0:
            for copy in self.keep + self.core:
                copy.start()
        elif n == 1:
            for copy in self.keep:
                copy.wait()
            for copy in self.core:
                copy.wait_recv()

            piece = math.gcd(self.got.shape[3], 48)
            pieces = self.got.shape[3] // piece

            def add(i, carry):
                block = lax.div(i, pieces)
                rows = pl.ds(pl.multiple_of(lax.rem(i, pieces) * piece, 16), piece)
                at = (*(lax.rem(lax.div(block, w), 2) for _, w in SEQ_BITS), rows)
                total = self.own[at].astype(jnp.float32) + self.got[at].astype(jnp.float32)
                self.own[at] = total.astype(jnp.bfloat16)
                return carry

            lax.fori_loop(0, 8 * pieces, add, 0)
            for part in self.parts:
                part.start(0)
        elif n < 5:
            for part in self.parts:
                part.finish(n - 2)
                part.start(n - 1)
        elif n == 5:
            for part in self.parts:
                part.finish(3)
            at = tuple(self.place[axis] for axis, _ in SEQ_BITS)
            self.done[self.place["c"], self.mine] = self.own[(*at, self.mine)]
            self.across.start()
        elif n == 6:
            self.across.wait_recv()
            self.back.start()
        else:
            self.back.wait_recv()

    def held(self):
        z1, z0, x = (self.place[axis] for axis, _ in SEQ_BITS)
        a, b, c = (lanes[1] for lanes, _ in PARTS)
        return (slice(None), slice(None), x, self.mine, pl.ds(0, a + b)), (
            z1, z0, slice(None), slice(None), pl.ds(a + b, c)
        )

    def resume(self, ab, last):
        first, second = self.held()
        self.own[first] = ab[...]
        self.own[second] = last[...]
        for part in self.parts:
            part.start(2)

    def finish(self):
        for copy in self.core + [self.across, self.back]:
            copy.wait_send()
        for part in self.parts:
            for copy in part.copies.values():
                copy.wait_send()


class Sum:
    order = ("c", "x", "y", "z0", "z1")

    def __init__(self, place, value, got, send, recv):
        self.value, self.got = value, got
        self.copies = [
            remote(value.at[n], got.at[n], send.at[n], recv.at[n], place.partner(axis))
            for n, axis in enumerate(self.order)
        ]

    def stage(self, n):
        if n > 0:
            self.copies[n - 1].wait_recv()
            self.value[n] = self.value[n - 1] + self.got[n - 1]
        if n < 5:
            self.copies[n].start()

    def finish(self):
        for copy in self.copies:
            copy.wait_send()


def share_views(a, count):
    *lead, rows, width = a.shape
    return a.reshape(*lead, 2, 2, 2, rows // count, width)


def half_views(a, count):
    *lead, rows, width = a.shape
    return a.reshape(*lead, 2, 2, 2, 2, rows // (2 * count), width)


def write_big(first, second, inner_o, outer_o):
    width = outer_o.shape[1]
    part = inner_o.shape[0]
    half = outer_o.shape[0] // 2
    strips = inner_o.shape[1] // width // 2
    for c in range(2):
        for j in range(strips):
            inner_o[:, pl.ds((c * strips + j) * width, width)] = first.done[c, pl.ds(j * part, part)].astype(jnp.float32)
        outer_o[pl.ds(c * half, half)] = second.done[c].astype(jnp.float32)


def begin(copies):
    for copy in copies:
        copy.start()


def sum_rows(values):
    rows, width = values.shape
    return jnp.sum(values.reshape(rows // 8, 8, width), axis=0)


def ticks(plan, folds, step):
    for t, todo in plan.items():

        @pl.when(step == t)
        def _():
            for f, n in todo:
                folds[f].stage(n)


REAR_TICKS = {
    0: ((0, 0),),
    2: ((0, 1),),
    3: ((3, 4),),
    5: ((3, 5),),
    6: ((0, 2),),
    7: ((3, 6),),
    8: ((3, 7),),
    10: ((0, 3),),
    13: ((0, 4),),
    14: ((1, 0),),
    15: ((0, 5),),
    16: ((1, 1), (2, 0)),
    17: ((0, 6),),
    18: ((2, 1), (0, 7)),
    19: ((1, 2),),
    20: ((2, 2),),
}
REAR_END = (
    (5, 1), (4, 1), (1, 3), (5, 2), (4, 2), (2, 3), (5, 3), (1, 4), (4, 3), (5, 4), (2, 4), (5, 5), (1, 5), (2, 5), (1, 6),
    (2, 6), (1, 7), (2, 7),
)
SPREAD_TICKS = {15: 0, 17: 1, 20: 2}


def rear_kernel(
    half, scale, pairs, fold_refs,
    q_ref, k_ref, v_ref, g_ref, lse_ref, delta_ref, kaug_ref,
    x_ref, res_ref, gg_ref, glse_ref, gdelta_ref, gx_ref, gres_ref, normed_ref, globals_ref, weight_ref, gain_ref,
    vectors_ref, outer_ab_ref, outer_c_ref, inner, out,
    igrad_o, ggrad_o, inner_o, outer_o, out_o, qkv_o, small_o,
    dqkv, gfirst, sums, qkv_src, grads, ggrad, value, got,
    send, recv, local, *scratch,
):
    step = pl.program_id(0)
    place = Place()
    me = lax.axis_index("seq")
    count = lax.axis_size("seq")
    row_count, rows, cols = dqkv.shape
    block_len = 2 * half
    width = cols // 3
    share = gx_ref.shape[1]
    attn = row_count * pairs
    strips = inner.shape[0] // 2
    part_rows = inner.shape[4]
    half_part = part_rows // 2
    sources = (
        [(lambda c, j=j: inner.at[c * strips + j], part_rows) for j in range(strips)],
        [(lambda c: out.at[:, :, :, c], half_part), (lambda c: qkv_src.at[0, :, :, :, c], half_part)],
        [(lambda c, j=j: qkv_src.at[j, :, :, :, c], half_part) for j in (1, 2)],
    )
    folds, at = [], 0
    for pieces, size in zip(sources, fold_refs[:3]):
        folds.append(Fold(place, pieces, scratch[at:at + size]))
        at += size
    folds.append(Fold(place, (), scratch[at:at + fold_refs[3]], None, Fold.LATE))
    at += fold_refs[3]
    spread = Halve(place, gfirst, (0, width), ("x", "z0", "z1"), scratch[at:], send.at[0], recv.at[0], 0)
    gather = Gather(place, ggrad, send.at[row_count], recv.at[row_count])
    small = Sum(place, value, got, send.at[row_count + 1], recv.at[row_count + 1])
    following = {"seq": lax.rem(me + 1, count)}
    before = {"seq": lax.rem(me + count - 1, count)}
    home = [
        remote(
            grads.at[1, r], igrad_o.at[r, pl.ds(0, half)], send.at[row_count + 2, r], recv.at[row_count + 2, r], following
        )
        for r in range(row_count)
    ]
    keep = [
        pltpu.make_async_copy(grads.at[0, r], igrad_o.at[r, pl.ds(half, half)], local.at[r]) for r in range(row_count)
    ]

    @pl.when(step == 0)
    def _():
        place.greet([following, before])
        sums[...] = jnp.zeros_like(sums)
        folds[3].resume(outer_ab_ref, outer_c_ref)

    ticks(REAR_TICKS, folds, step)

    @pl.when(step < attn)
    def _():
        r, p = lax.div(step, pairs), lax.rem(step, pairs)
        spots = [pl.ds(pl.multiple_of(j * width + p * LANES, LANES), LANES) for j in range(3)]
        lane = pl.ds(pl.multiple_of(p * LANES, LANES), LANES)
        wide = lambda a, b: jnp.concatenate([a, b.reshape(rows - block_len, LANES)], axis=0)
        attend_back_kernel(
            half, scale, 320, p, q_ref, k_ref, v_ref, wide(g_ref[...], gg_ref[:, :, :, r, :, lane]),
            wide(lse_ref[0], glse_ref[:, :, :, r]), wide(delta_ref[...], gdelta_ref[:, :, :, r]), kaug_ref,
            *(dqkv.at[pl.ds(r, 1), :, spot] for spot in spots),
        )

    strip_at = step - (attn + 1)

    @pl.when((strip_at >= 0) & (strip_at < 3))
    def _():
        strip = pl.ds(pl.multiple_of(strip_at * width, width), width)
        total = tn(normed_ref[0], dqkv[0, :, strip])
        for r in range(1, row_count):
            total = total + tn(normed_ref[r], dqkv[r, :, strip])
        qkv_src[strip_at] = total.astype(jnp.bfloat16).reshape(qkv_src.shape[1:])

    for t, n in SPREAD_TICKS.items():

        @pl.when(step == t)
        def _():
            spread.finish(n)
            if n < 2:
                spread.start(n + 1)

    gain = gain_ref[...]

    def stats(x):
        centred = x - jnp.mean(x, axis=-1, keepdims=True)
        inv = lax.rsqrt(jnp.mean(centred * centred, axis=-1, keepdims=True) + EPS)
        return centred * inv, inv

    def add_sums(first, n):
        sums[0] += sum_rows(first * n)
        sums[1] += sum_rows(first)

    def through(first, n, inv):
        eg = first * gain
        return (eg - jnp.mean(eg, axis=-1, keepdims=True) - n * jnp.mean(eg * n, axis=-1, keepdims=True)) * inv

    @pl.when(step == attn)
    def _():
        own = pl.ds(block_len, rows - block_len)
        partial = jnp.concatenate([dqkv[r, own] for r in range(row_count)], axis=0)
        first = nt(partial, weight_ref[...])
        n, _ = stats(globals_ref[...].astype(jnp.float32).reshape(first.shape))
        add_sums(first, n)
        first = first.astype(jnp.bfloat16).reshape(row_count, 2, 2, 2, share, width)
        for r in range(row_count):
            gfirst[:, :, :, pl.ds(r * share, share)] = first[r]
        spread.start(0)

    tiles = attn + 4
    tile = step - tiles

    @pl.when((tile >= 0) & (tile < 2 * row_count))
    def _():
        r, h = lax.rem(tile, row_count), 1 - lax.div(tile, row_count)
        spot = pl.ds(pl.multiple_of(h * half, half), half)
        first = nt(dqkv[r, spot], weight_ref[...])
        n, inv = stats(x_ref[...].astype(jnp.float32))
        add_sums(first, n)
        grads[h, r] = (res_ref[...] + through(first, n, inv)).astype(jnp.bfloat16)

    for r in range(row_count):

        @pl.when(tile == r)
        def _():
            home[r].start()

        @pl.when(tile == row_count + r)
        def _():
            keep[r].start()

    after = tiles + 2 * row_count

    @pl.when(step == after)
    def _():
        lines = [jnp.sum(sums[n], axis=0, keepdims=True) for n in range(2)]
        value[0] = jnp.concatenate(lines + [vectors_ref[...]])
        small.stage(0)
        own_rows = row_count * share
        at = tuple(place[axis] for axis, _ in SEQ_BITS)
        n, inv = stats(gx_ref[...].astype(jnp.float32).reshape(own_rows, width))
        grad = gres_ref[...].reshape(own_rows, width) + through(gfirst[at].astype(jnp.float32), n, inv)
        ggrad[at] = grad.astype(jnp.bfloat16).reshape(row_count, share, width)
        gather.stage(0)

    @pl.when(step == after + 1)
    def _():
        write_big(folds[0], folds[3], inner_o, outer_o)
        leave = pltpu.make_async_copy(ggrad, ggrad_o, local.at[row_count])
        movers = folds + [gather, small]
        for f, n in REAR_END:
            movers[f].stage(n)
            if (f, n) == (4, 3):
                leave.start()
        small_o[...] = value[5]
        f32 = jnp.float32
        for c in range(2):
            spot = pl.ds(c * half_part, half_part)
            first, second = pl.ds(0, half_part), pl.ds(half_part, half_part)
            out_o[spot] = folds[1].done[c, first].astype(f32)
            for j, (fold, lines) in enumerate(((folds[1], second), (folds[2], first), (folds[2], second))):
                qkv_o[spot, pl.ds(j * width, width)] = fold.done[c, lines].astype(f32)
        for fold in folds:
            fold.finish()
        gather.finish()
        small.finish()
        for copy in spread.copies.values():
            copy.wait_send()
        for copy in keep + home + [leave]:
            copy.wait()


def rear(
    qkv, grad, lse, delta, kaug, tokens, res_grad, global_grad, global_lse, global_delta, own_globals, own_res, normed,
    globals_in, weight, gain, vectors, outer_ab, outer_c, inner, out, half, count,
):
    row_count, rows, cols = qkv.shape
    width = cols // 3
    pairs = width // LANES
    block_len = 2 * half
    global_count = rows - block_len
    share = global_count // count
    part = width // count
    scale = (width // HEADS) ** (-0.5)
    attn = row_count * pairs
    f32, bf16 = jnp.float32, jnp.bfloat16
    row_of = lambda t: jnp.minimum(t, attn - 1) // pairs
    pair_of = lambda t: jnp.minimum(t, attn - 1) % pairs
    spec = lambda off: pl.BlockSpec((1, rows, LANES), lambda t: (row_of(t), 0, off + pair_of(t)))
    whole = pl.BlockSpec((1, rows, LANES), lambda t: (row_of(t), 0, 0))

    def tile_of(t):
        n = jnp.clip(t - attn - 4, 0, 2 * row_count - 1)
        return n % row_count * 2 + 1 - n // row_count, 0

    fixed = lambda a: pl.BlockSpec(a.shape, lambda t: (0,) * a.ndim, pipeline_mode=pl.Buffered(1))
    tile = pl.BlockSpec((half, width), tile_of)
    hbm = pl.BlockSpec(memory_space=pl.ANY)
    outs = [
        jax.ShapeDtypeStruct((row_count, block_len, width), bf16),
        jax.ShapeDtypeStruct((2, 2, 2, row_count, share, width), bf16),
        jax.ShapeDtypeStruct((part, 4 * width), f32),
        jax.ShapeDtypeStruct((4 * part, width), f32),
        jax.ShapeDtypeStruct((part, width), f32),
        jax.ShapeDtypeStruct((part, 3 * width), f32),
        jax.ShapeDtypeStruct((8, width), f32),
    ]
    folds, sizes = [], []
    for size, pieces in ((2 * part, 2), (part, 2), (part, 2)):
        refs = Fold.scratch(size, width, pieces)
        folds += refs
        sizes.append(len(refs))
    refs = Fold.scratch(2 * part, width, 0, False, Fold.LATE)
    folds += refs
    sizes.append(len(refs))
    vmem = pltpu.VMEM
    kinds = 4 + row_count
    fixeds = (
        global_grad, global_lse, global_delta, own_globals, own_res, normed, globals_in, weight, gain, vectors,
        outer_ab, outer_c,
    )
    return pl.pallas_call(
        functools.partial(rear_kernel, half, scale, pairs, tuple(sizes)),
        grid=(attn + 4 + 2 * row_count + 2,),
        in_specs=[spec(0), spec(pairs), spec(2 * pairs)]
        + [pl.BlockSpec((block_len, LANES), lambda t: (row_of(t), pair_of(t)))]
        + [pl.BlockSpec((1, block_len, LANES), lambda t: (row_of(t), 0, 0))]
        + [pl.BlockSpec((block_len, LANES), lambda t: (row_of(t), 0)), whole]
        + [tile, tile]
        + [fixed(a) for a in fixeds]
        + [hbm] * 2,
        out_specs=[hbm] * 2 + [pl.BlockSpec(memory_space=pltpu.VMEM)] * 5,
        out_shape=outs,
        scratch_shapes=[
            vmem((row_count, rows, cols), bf16),
            vmem((2, 2, 2, row_count * share, width), bf16),
            vmem((2, 8, width), f32),
            vmem((3, 2, 2, 2, 2, part // 2, width), bf16),
            vmem((2, row_count, half, width), bf16),
            vmem((2, 2, 2, row_count, share, width), bf16),
            vmem((6, 8, width), f32),
            vmem((5, 8, width), f32),
            pltpu.SemaphoreType.DMA((kinds, 5)),
            pltpu.SemaphoreType.DMA((kinds, 5)),
            pltpu.SemaphoreType.DMA((1 + row_count,)),
        ]
        + folds
        + Halve.buffers(row_count * share, width, ("x", "z0", "z1")),
        compiler_params=pltpu.CompilerParams(
            collective_id=9, has_side_effects=True, vmem_limit_bytes=64 * 1024 * 1024
        ),
        name="rear",
    )(
        qkv, qkv, qkv, grad, lse, delta, kaug, tokens, res_grad, *fixeds,
        share_views(inner, count), half_views(out, count),
    )


def cdf_bell(v):
    bell = jnp.exp(-0.5 * v * v)
    t = 1.0 / (1.0 + (0.3275911 * 0.5 ** 0.5) * jnp.abs(v))
    poly = t * (
        0.127414796 + t * (-0.142248368 + t * (0.7107068705 + t * (-0.7265760135 + t * 0.5307027145)))
    )
    tail = poly * bell
    return jnp.where(v < 0, tail, 1.0 - tail), bell


MID_TICKS = {9: 0, 11: 1, 14: 2}
MID_GATHERS = {6: (0, 1), 8: (0, 2), 10: (0, 3), 11: (1, 1), 12: (1, 2), 13: (1, 3)}


def mid_kernel(
    half, fold_refs,
    lengths, x_ref, mixed_ref, cot_ref, gx_ref, gcot_ref, out_w, inner_w, outer_w, bias_ref, gain_ref, shift_ref, heads_ref,
    mixed_all, lse_all,
    layer_o, res_o, grad_o, delta_o, gres_o, gout_o, ggrad_o, glse_o, gdelta_o, inner_o, outer_ab_o, outer_c_o, out_o,
    vectors_o,
    hidden, slope, normed, cot, att, proj, residual, outer_src, sums, bias_sums, layers,
    gout, ggrad, glse, gdelta, part_mixed, part_lse, send, recv, local, *scratch,
):
    f32, bf16 = jnp.float32, jnp.bfloat16
    step = pl.program_id(0)
    place = Place()
    me = lax.axis_index("seq")
    count = lax.axis_size("seq")
    row_count, share = gx_ref.shape[:2]
    block_len = 2 * half
    tokens = row_count * block_len
    own_rows = row_count * share
    width = gx_ref.shape[2]
    strips = inner_w.shape[1] // width
    tiles = 2 * row_count
    fold = Fold(place, None, scratch, outer_src, Fold.EARLY)
    following = {"seq": lax.rem(me + 1, count)}
    at = tuple(place[axis] for axis, _ in SEQ_BITS)

    def parts(m, to, r, n):
        rows = pl.ds(pl.multiple_of(block_len + share * to, 16), share)
        return (
            (mixed_all.at[r, rows], part_mixed.at[m, r]) if n == 0 else (lse_all.at[r, rows], part_lse.at[m, r])
        )

    part_copies, part_own = [], []
    for r in range(row_count):
        for n in range(2):
            src, dst = parts(me, me, r, n)
            part_own.append(pltpu.make_async_copy(src, dst, local.at[2 * r + n]))
            for other in range(1, count):
                to = lax.rem(me + other, count)
                src, dst = parts(me, to, r, n)
                part_copies.append(remote(src, dst, send.at[2 * r + n, other], recv.at[2 * r + n, other], {"seq": to}))
    base = 2 * row_count
    gathers = [
        Gather(place, buf, send.at[base + n], recv.at[base + n]) for n, buf in enumerate((gout, ggrad, glse, gdelta))
    ]
    leaves = [
        pltpu.make_async_copy(buf, o, local.at[base + n])
        for n, (buf, o) in enumerate(((gout, gout_o), (ggrad, ggrad_o), (glse, glse_o), (gdelta, gdelta_o)))
    ]
    base += 4
    home = [
        remote(layers.at[1, r], layer_o.at[r, pl.ds(0, half)], send.at[base, r], recv.at[base, r], following)
        for r in range(row_count)
    ]
    keep = [
        pltpu.make_async_copy(layers.at[0, r], layer_o.at[r, pl.ds(half, half)], local.at[base + r]) for r in range(row_count)
    ]
    gain, shift = gain_ref[...], shift_ref[...]

    @pl.when(step == 0)
    def _():
        place.greet([{"seq": lax.rem(me + other, count)} for other in range(1, count)])
        begin(part_own + part_copies)
        sums[...] = jnp.zeros_like(sums)
        bias_sums[...] = jnp.zeros_like(bias_sums)

    def stats(values):
        centred = values - jnp.mean(values, axis=-1, keepdims=True)
        inv = lax.rsqrt(jnp.mean(centred * centred, axis=-1, keepdims=True) + EPS)
        return centred * inv, inv

    def forward(x, attended, rows):
        att[rows] = attended
        total = x.astype(f32) + nn(attended, out_w[...])
        residual[rows] = total
        n, _ = stats(total)
        second = (n * gain + shift).astype(bf16)
        normed[rows] = second

        def run(j, total):
            strip = pl.ds(pl.multiple_of(j * width, width), width)
            inner = nn(second, inner_w[:, strip]) + bias_ref[:, strip]
            cdf, bell = cdf_bell(inner)
            active = (inner * cdf).astype(bf16)
            hidden[rows, strip] = active
            slope[rows, strip] = (cdf + inner * bell * ((0.5 / math.pi) ** 0.5)).astype(bf16)
            return total + nn(active, outer_w[strip, :])

        return lax.fori_loop(0, strips, run, total)

    def backward(cotangent, rows):
        def run(j, total):
            strip = pl.ds(pl.multiple_of(j * width, width), width)
            grad = (nt(cotangent, outer_w[strip, :]) * slope[rows, strip].astype(f32)).astype(bf16)
            slope[rows, strip] = grad
            bias_sums[j] += sum_rows(grad.astype(f32))
            return total + nt(grad, inner_w[:, strip])

        second_grad = lax.fori_loop(0, strips, run, jnp.zeros(cotangent.shape, f32))
        n, inv = stats(residual[rows])
        eg = second_grad * gain
        through = (eg - jnp.mean(eg, axis=-1, keepdims=True) - n * jnp.mean(eg * n, axis=-1, keepdims=True)) * inv
        sums[0] += sum_rows(second_grad * n)
        sums[1] += sum_rows(second_grad)
        res = cotangent.astype(f32) + through
        projected = res.astype(bf16)
        proj[rows] = projected
        grad = nt(projected, out_w[...]).astype(bf16)
        product = grad.astype(f32) * att[rows].astype(f32)
        top = product.astype(bf16)
        rest = (product - top.astype(f32)).astype(bf16)
        return res, grad, nn(top, heads_ref[...]) + nn(rest, heads_ref[...])

    @pl.when(step < tiles)
    def _():
        r, h = lax.rem(step, row_count), 1 - lax.div(step, row_count)
        rows = pl.ds(pl.multiple_of((2 * r + h) * half, half), half)
        owner = lax.rem(me + h, count)
        spot = owner * block_len + (1 - h) * half + lax.broadcasted_iota(jnp.int32, (half, width), 0)
        valid = spot < lengths[r]
        cot[rows] = jnp.where(valid, cot_ref[...].astype(f32), 0.0).astype(bf16)
        final = forward(x_ref[...], mixed_ref[0], rows)
        layers[h, r] = jnp.where(valid, final, 0.0).astype(bf16)

    back = step - (tiles + 2 + strips)

    @pl.when((back >= 0) & (back < tiles))
    def _():
        r, h = lax.rem(back, row_count), 1 - lax.div(back, row_count)
        rows = pl.ds(pl.multiple_of((2 * r + h) * half, half), half)
        res, grad, delta = backward(cot[rows], rows)
        res_o[...] = res
        grad_o[...] = grad
        delta_o[...] = delta

    for r in range(row_count):

        @pl.when(step == r)
        def _():
            home[r].start()

        @pl.when(step == row_count + r)
        def _():
            keep[r].start()

    last = pl.ds(tokens, own_rows)

    @pl.when(step == tiles)
    def _():
        for copy in part_own:
            copy.wait()
        for copy in part_copies:
            copy.wait_recv()
        peak = jnp.max(part_lse[...], axis=0)
        shares = jnp.exp(part_lse[...] - peak)
        total = jnp.sum(shares, axis=0)
        lse = peak + jnp.log(total)
        glse[at] = lse
        shares = (shares / total).reshape(count * own_rows, LANES)
        lane = lax.broadcasted_iota(jnp.int32, shares.shape, 1)
        shares = jnp.where(lane < HEADS, shares, 0.0)
        top = shares.astype(bf16)
        rest = (shares - top.astype(f32)).astype(bf16)
        wide = nt(top, heads_ref[...]) + nt(rest, heads_ref[...])
        mixed = wide * part_mixed[...].reshape(count * own_rows, width).astype(f32)
        mixed = jnp.sum(mixed.reshape(count, own_rows, width), axis=0).astype(bf16)
        cot[last] = gcot_ref[...].reshape(own_rows, width)
        final = forward(gx_ref[...].reshape(own_rows, width), mixed, last)
        gout[at] = final.astype(bf16).reshape(row_count, share, width)
        gathers[0].stage(0)

    strip_at = step - (tiles + 1)

    @pl.when((strip_at >= 0) & (strip_at < strips))
    def _():
        strip = pl.ds(pl.multiple_of(strip_at * width, width), width)
        grad = tn(hidden[:, strip], cot[...]).astype(bf16)
        outer_src[lax.div(strip_at, 2), lax.rem(strip_at, 2)] = grad.reshape(outer_src.shape[2:])

    for t, (kind, n) in MID_GATHERS.items():

        @pl.when(step == t)
        def _():
            chosen = range(1, 4) if kind else range(1)
            for g in chosen:
                gathers[g].stage(n)
                if n == 3:
                    leaves[g].start()

    for t, n in MID_TICKS.items():

        @pl.when(step == t)
        def _():
            fold.stage(n)

    after = 2 * tiles + 1 + strips

    @pl.when(step == tiles + 1 + strips)
    def _():
        res, grad, delta = backward(cot[last], last)
        gres_o[...] = res.reshape(row_count, share, width)
        ggrad[at] = grad.reshape(row_count, share, width)
        gdelta[at] = delta.reshape(row_count, share, LANES)
        for gather in gathers[1:]:
            gather.stage(0)

    inner_at = step - (after + 1)

    @pl.when((inner_at >= 0) & (inner_at < strips))
    def _():
        strip = pl.ds(pl.multiple_of(inner_at * width, width), width)
        inner_o[0] = tn(normed[...], slope[:, strip]).astype(bf16)

    @pl.when(step == after + 1 + strips)
    def _():
        out_o[...] = tn(att[...], proj[...]).astype(bf16)
        lines = [jnp.sum(sums[n], axis=0, keepdims=True) for n in range(2)]
        lines += [jnp.sum(bias_sums[n], axis=0, keepdims=True) for n in range(strips)]
        vectors_o[...] = jnp.concatenate(lines)
        for part in fold.parts:
            part.finish(1)
        first, second = fold.held()
        outer_ab_o[...] = fold.own[first]
        outer_c_o[...] = fold.own[second]
        for copy in fold.core:
            copy.wait_send()
        for part in fold.parts:
            for copy in part.copies.values():
                copy.wait_send()
        for gather in gathers:
            gather.finish()
        for copy in part_copies:
            copy.wait_send()
        for copy in keep + home + leaves:
            copy.wait()


def mid(
    lengths, tokens, mixed, lse, cotangent, own_globals, own_cot, out_weight, inner_weight, outer_weight, bias, gain, shift,
    half, count,
):
    f32, bf16 = jnp.float32, jnp.bfloat16
    row_count, rows, width = mixed.shape
    block_len = 2 * half
    share = (rows - block_len) // count
    own_rows = row_count * share
    inner_width = inner_weight.shape[1]
    strips = inner_width // width
    part = width // count
    tiles = 2 * row_count
    total = row_count * block_len + own_rows
    lane, head = jnp.arange(LANES), jnp.arange(width) // (width // HEADS)
    heads = ((lane[None, :] % HEADS == head[:, None]) & (lane[None, :] < 3 * HEADS)).astype(bf16)

    def tile_at(first):
        def place(t):
            n = jnp.clip(t - first, 0, tiles - 1)
            return n % row_count, 1 - n // row_count

        return place

    forward_at, back_at = tile_at(0), tile_at(tiles + 2 + strips)

    def flat(where, cols):
        def index(t):
            r, h = where(t)
            return 2 * r + h, 0

        return pl.BlockSpec((half, cols), index)

    fixed = lambda a: pl.BlockSpec(a.shape, lambda t: (0,) * a.ndim, pipeline_mode=pl.Buffered(1))
    whole = lambda *shape: pl.BlockSpec(shape, lambda t: (0,) * len(shape))
    hbm = pl.BlockSpec(memory_space=pl.ANY)
    fixeds = (own_globals, own_cot, out_weight, inner_weight, outer_weight, bias[None], gain[None], shift[None], heads)
    shared = (2, 2, 2, row_count, share)
    after = 2 * tiles + 2 + strips
    of = jax.ShapeDtypeStruct
    outs = [
        of((row_count, block_len, width), bf16),
        of((row_count * block_len, width), f32),
        of((row_count * block_len, width), bf16),
        of((row_count * block_len, LANES), f32),
        of((row_count, share, width), f32),
        of((*shared, width), bf16),
        of((*shared, width), bf16),
        of((*shared, LANES), f32),
        of((*shared, LANES), f32),
        of((strips, width, width), bf16),
        of((2, 2, strips * part // 4, 512), bf16),
        of((2, strips * part // 2, 256), bf16),
        of((width, width), bf16),
        of((2 + strips, width), f32),
    ]
    vmem = pltpu.VMEM
    fold = Fold.scratch(strips * part // 2, width, 1, True, Fold.EARLY)
    kinds = 2 * row_count + 5
    return pl.pallas_call(
        functools.partial(mid_kernel, half, len(fold)),
        grid=(after + strips + 1,),
        in_specs=[
            pl.BlockSpec(memory_space=pltpu.SMEM),
            flat(forward_at, width),
            pl.BlockSpec((1, half, width), lambda t: (*forward_at(t), 0)),
            flat(forward_at, width),
        ]
        + [fixed(a) for a in fixeds]
        + [hbm] * 2,
        out_specs=[
            hbm,
            flat(back_at, width),
            flat(back_at, width),
            flat(back_at, LANES),
            whole(row_count, share, width),
            hbm,
            hbm,
            hbm,
            hbm,
            pl.BlockSpec((1, width, width), lambda t: (jnp.clip(t - after, 0, strips - 1), 0, 0)),
            whole(*outs[10].shape),
            whole(*outs[11].shape),
            whole(width, width),
            whole(2 + strips, width),
        ],
        out_shape=outs,
        scratch_shapes=[
            vmem((total, inner_width), bf16),
            vmem((total, inner_width), bf16),
            vmem((total, width), bf16),
            vmem((total, width), bf16),
            vmem((total, width), bf16),
            vmem((total, width), bf16),
            vmem((total, width), f32),
            vmem((2, 2, 2, 2, strips * part // 2, width), bf16),
            vmem((2, 8, width), f32),
            vmem((strips, 8, width), f32),
            vmem((2, row_count, half, width), bf16),
            vmem((*shared, width), bf16),
            vmem((*shared, width), bf16),
            vmem((*shared, LANES), f32),
            vmem((*shared, LANES), f32),
            vmem((count, row_count, share, width), bf16),
            vmem((count, row_count, share, LANES), f32),
            pltpu.SemaphoreType.DMA((kinds, count)),
            pltpu.SemaphoreType.DMA((kinds, count)),
            pltpu.SemaphoreType.DMA((kinds + row_count,)),
        ]
        + fold,
        compiler_params=pltpu.CompilerParams(
            collective_id=10, has_side_effects=True, vmem_limit_bytes=64 * 1024 * 1024
        ),
        name="mid",
    )(lengths, tokens, mixed, cotangent, *fixeds, mixed, lse)


def wgrad_kernel(a_ref, b_ref, o_ref):
    o_ref[...] = tn(a_ref[...], b_ref[...]).astype(o_ref.dtype).reshape(o_ref.shape)


def wgrad(a, b, strip):
    rows, a_cols = a.shape
    b_cols = b.shape[1]
    split_a = a_cols > b_cols
    strips = max(a_cols, b_cols) // strip
    fixed = lambda n: (0, 0)
    moving = lambda n: (0, n)
    return pl.pallas_call(
        wgrad_kernel,
        grid=(strips,),
        in_specs=[
            pl.BlockSpec((rows, strip), moving if split_a else fixed),
            pl.BlockSpec((rows, strip), fixed if split_a else moving),
        ],
        out_specs=pl.BlockSpec((1, strip, strip), lambda n: (n, 0, 0)),
        out_shape=jax.ShapeDtypeStruct((strips, strip, strip), jnp.bfloat16),
        compiler_params=pltpu.CompilerParams(vmem_limit_bytes=40 * 1024 * 1024),
        name="wgrad",
    )(a, b)


def norm_parts(values):
    average = jnp.mean(values, axis=-1, keepdims=True)
    centred = values - average
    variance = jnp.mean(centred * centred, axis=-1, keepdims=True)
    inv = lax.rsqrt(variance + EPS)
    return centred * inv, inv


def norm_back(grad, n, inv, gain):
    eg = grad * gain
    through = (
        eg - jnp.mean(eg, axis=-1, keepdims=True) - n * jnp.mean(eg * n, axis=-1, keepdims=True)
    ) * inv
    return through, jnp.sum(grad * n, axis=0), jnp.sum(grad, axis=0)


def split_rows(a, count):
    row_count, rows, width = a.shape
    part = rows // count
    moved = a.reshape(row_count, count, part, width).transpose(1, 0, 2, 3)
    return moved.reshape(count, row_count * part, width)


def join_rows(a, row_count):
    count, rows, width = a.shape
    part = rows // row_count
    moved = a.reshape(count, row_count, part, width).transpose(1, 0, 2, 3)
    return moved.reshape(row_count, count * part, width)


def per_head(values, width):
    lanes = values[..., :HEADS]
    return jnp.repeat(lanes, width // HEADS, axis=-1)


def head_sums(values):
    rows, width = values.shape
    lane = jnp.arange(LANES)
    head = jnp.arange(width) // (width // HEADS)
    place = ((lane[None, :] % HEADS == head[:, None]) & (lane[None, :] < 3 * HEADS)).astype(jnp.bfloat16)
    top = values.astype(jnp.bfloat16)
    rest = (values - top.astype(jnp.float32)).astype(jnp.bfloat16)
    return nn(top, place) + nn(rest, place)


def reduce_share(a):
    a = lax.psum_scatter(a, "seq", scatter_dimension=0, tiled=True)
    return lax.psum(a.astype(jnp.bfloat16), "batch").astype(jnp.float32)


def body(
    inputs,
    global_inputs,
    lengths,
    first_gain,
    first_shift,
    qkv_weight,
    out_weight,
    second_gain,
    second_shift,
    inner_weight,
    inner_bias,
    outer_weight,
    output_cotangent,
    global_cotangent,
):
    f32, bf16 = jnp.float32, jnp.bfloat16
    row_count, block_len, width = inputs.shape
    half = block_len // 2
    global_count = global_inputs.shape[1]
    rows = block_len + global_count
    inner_width = inner_weight.shape[1]
    count = lax.axis_size("seq")
    me = lax.axis_index("seq")
    after = lax.rem(me + 1, count)
    back = [(i, (i - 1) % count) for i in range(count)]
    forth = [(i, (i + 1) % count) for i in range(count)]
    token_rows = row_count * block_len
    share = global_count // count
    own_rows = row_count * share

    next_inputs = lax.ppermute(inputs[:, :half], "seq", back)
    next_cotangent = lax.ppermute(output_cotangent[:, :half], "seq", back)
    block = jnp.concatenate([inputs[:, half:], next_inputs], axis=1)
    spots = jnp.arange(half, dtype=jnp.int32)
    positions = jnp.concatenate([me * block_len + half + spots, after * block_len + spots])
    valid = positions[None, :] < lengths[:, None]

    kind = jnp.arange(LANES)[None, None, :] - TYPE0
    key_half = (jnp.arange(block_len) // half)[None, :, None]
    last = me == count - 1
    hidden_key = jnp.logical_not(valid)[:, :, None] | (last & (kind < 2) & (kind != key_half))
    token_marks = jnp.where(hidden_key & (kind >= 0) & (kind < 3), NEG, 0.0)
    global_marks = jnp.where((kind == 2) & (me != 0), NEG, 0.0)
    global_marks = jnp.broadcast_to(global_marks, (row_count, global_count, LANES))
    kaug = jnp.concatenate([token_marks, global_marks], axis=1).astype(bf16)

    states = jnp.concatenate([block, global_inputs], axis=1)
    n_first, inv_first = norm_parts(states.astype(f32))
    normed = (n_first * first_gain + first_shift).astype(bf16)
    qkv = nn(normed.reshape(row_count * rows, width), qkv_weight).astype(bf16)
    qkv = qkv.reshape(row_count, rows, 3 * width)

    mixed, lse = attend(qkv, kaug, half)
    own_globals = lax.dynamic_slice_in_dim(global_inputs, me * share, share, axis=1)
    own_global_cot = lax.dynamic_slice_in_dim(global_cotangent, me * share, share, axis=1)
    tokens_in = block.reshape(token_rows, width)
    cot_block = jnp.concatenate([output_cotangent[:, half:], next_cotangent], axis=1)
    if count == 8 and lax.axis_size("batch") == 4:
        (
            layer_output, residual_grad, block_grad, block_delta, own_res, global_out, global_grad, global_lse, global_delta,
            inner_wgrad, outer_ab, outer_c, out_grad, vectors,
        ) = mid(
            lengths, tokens_in, mixed, lse, cot_block.reshape(token_rows, width), own_globals, own_global_cot, out_weight,
            inner_weight, outer_weight, inner_bias, second_gain, second_shift, half, count,
        )
        input_out, global_grad, inner_out, outer_out, out_out, qkv_out, small = rear(
            qkv, block_grad, lse, block_delta, kaug, tokens_in, residual_grad, global_grad, global_lse, global_delta,
            own_globals, own_res, normed, global_inputs, qkv_weight, first_gain[None], vectors, outer_ab, outer_c, inner_wgrad,
            out_grad, half, count,
        )
        cut = lambda a: lax.dynamic_slice_in_dim(a, me * (a.shape[0] // count), a.shape[0] // count)
        vectors_out = [cut(small[n]) for n in range(4)] + [cut(small[4:].reshape(-1))]
        joined = lambda a: join_rows(a.reshape(count, own_rows, width), row_count)
        return (
            layer_output, joined(global_out), input_out, joined(global_grad), vectors_out[0], vectors_out[1], qkv_out,
            out_out, vectors_out[2], vectors_out[3], inner_out, vectors_out[4], outer_out,
        )

    part_mixed, part_lse = spread(
        [split_rows(mixed[:, block_len:], count), split_rows(lse[:, block_len:], count)], count, False, 0
    )
    highest = jnp.max(part_lse, axis=0)
    part_weight = jnp.exp(part_lse - highest)
    total = jnp.sum(part_weight, axis=0)
    global_lse = highest + jnp.log(total)
    global_mixed = jnp.sum(per_head(part_weight / total, width) * part_mixed.astype(f32), axis=0)

    tokens = jnp.concatenate([tokens_in, own_globals.reshape(own_rows, width)]).astype(f32)
    cot_block = jnp.where(valid[:, :, None], cot_block, 0)
    cotangent = jnp.concatenate(
        [cot_block.reshape(token_rows, width), own_global_cot.reshape(own_rows, width)]
    )
    attended = jnp.concatenate(
        [mixed[:, :block_len].reshape(token_rows, width), global_mixed.astype(bf16)]
    )
    residual = tokens + nn(attended, out_weight)
    n_second, inv_second = norm_parts(residual)
    normed_second = (n_second * second_gain + second_shift).astype(bf16)
    inner = nn(normed_second, inner_weight) + inner_bias
    bell = jnp.exp(-0.5 * inner * inner)
    cdf = 0.5 * (1.0 + lax.erf(inner * (0.5 ** 0.5)))
    hidden = (inner * cdf).astype(bf16)
    final = residual + nn(hidden, outer_weight)
    hidden_grad = nt(cotangent, outer_weight)
    slope = cdf + inner * bell * ((0.5 / jnp.pi) ** 0.5)
    inner_grad = (hidden_grad * slope).astype(bf16)
    second_grad = nt(inner_grad, inner_weight)
    through, second_gain_grad, second_shift_grad = norm_back(second_grad, n_second, inv_second, second_gain)
    residual_grad = cotangent.astype(f32) + through
    projection_grad = residual_grad.astype(bf16)
    attended_grad = nt(projection_grad, out_weight).astype(bf16)
    delta = head_sums(attended_grad.astype(f32) * attended.astype(f32))
    outer_grad = wgrad(hidden, cotangent, width)
    inner_wgrad = wgrad(normed_second, inner_grad, width)
    bias_grad = jnp.sum(inner_grad.astype(f32), axis=0)
    out_grad = wgrad(attended, projection_grad, width)

    all_grad, all_lse, all_delta = spread(
        [attended_grad[token_rows:], global_lse, delta[token_rows:]], count, True, 1
    )
    block_grad = jnp.concatenate(
        [attended_grad[:token_rows].reshape(row_count, block_len, width), join_rows(all_grad, row_count)], axis=1
    )
    block_lse = jnp.concatenate([lse[:, :block_len], join_rows(all_lse, row_count)], axis=1)
    block_delta = jnp.concatenate(
        [delta[:token_rows].reshape(row_count, block_len, LANES), join_rows(all_delta, row_count)], axis=1
    )
    layer = final[:token_rows].reshape(row_count, block_len, width)
    layer = jnp.where(valid[:, :, None], layer, 0.0).astype(bf16)
    layer_output = jnp.concatenate([lax.ppermute(layer[:, half:], "seq", forth), layer[:, :half]], axis=1)
    own_out = final[token_rows:].astype(bf16)
    part = width // count
    dqkv = jnp.concatenate(attend_back(qkv, block_grad, block_lse, block_delta, kaug, half, rows), axis=-1)
    (part_dqkv,) = spread([split_rows(dqkv[:, block_len:], count)], count, False, 2)
    global_dqkv = jnp.sum(part_dqkv.astype(f32), axis=0).astype(bf16)
    qkv_grad = jnp.concatenate([dqkv[:, :block_len].reshape(token_rows, 3 * width), global_dqkv])

    first_grad = nt(qkv_grad, qkv_weight)
    n_tokens, inv_tokens = norm_parts(tokens)
    through, first_gain_grad, first_shift_grad = norm_back(first_grad, n_tokens, inv_tokens, first_gain)
    input_grad = (residual_grad + through).astype(bf16)
    normed_tokens = (n_tokens * first_gain + first_shift).astype(bf16)
    qkv_wgrad = wgrad(normed_tokens, qkv_grad, width)

    grad_block = input_grad[:token_rows].reshape(row_count, block_len, width)
    input_out = jnp.concatenate(
        [lax.ppermute(grad_block[:, half:], "seq", forth), grad_block[:, :half]], axis=1
    )
    global_final, global_grad = spread([own_out, input_grad[token_rows:]], count, True, 3)

    def shares(a):
        return a.reshape(count, a.shape[0] // count)

    small = jnp.concatenate(
        [
            shares(first_gain_grad),
            shares(first_shift_grad),
            shares(second_gain_grad),
            shares(second_shift_grad),
            shares(bias_grad),
        ],
        axis=1,
    )
    inner_out = reduce_share(inner_wgrad.transpose(1, 0, 2).reshape(width, -1))
    outer_out = reduce_share(outer_grad.reshape(inner_width, width))
    out_out = reduce_share(out_grad[0])
    qkv_out = reduce_share(qkv_wgrad.transpose(1, 0, 2).reshape(width, -1))
    small = reduce_share(small)[0]
    return (
        layer_output,
        join_rows(global_final, row_count),
        input_out,
        join_rows(global_grad, row_count),
        small[:part],
        small[part:2 * part],
        qkv_out,
        out_out,
        small[2 * part:3 * part],
        small[3 * part:4 * part],
        inner_out,
        small[4 * part:],
        outer_out,
    )


def solution(mesh):
    rows = P("batch", "seq", None)
    globals_at = P("batch", None, None)
    return jax.shard_map(
        body,
        mesh=mesh,
        in_specs=(rows, globals_at, P("batch")) + (P(),) * 9 + (rows, globals_at),
        out_specs=(
            rows,
            globals_at,
            rows,
            globals_at,
            P("seq"),
            P("seq"),
            P("seq", None),
            P("seq", None),
            P("seq"),
            P("seq"),
            P("seq", None),
            P("seq"),
            P("seq", None),
        ),
        check_vma=False,
    )
```

```python
import functools
import math

import jax
import jax.numpy as jnp
from jax import lax
from jax.experimental import pallas as pl
from jax.experimental.pallas import tpu as pltpu
from jax.sharding import PartitionSpec as P

HEADS = 12
NEG = -1e30
LANES = 128
TYPE0 = 3 * HEADS

def nt(a, b):
    return lax.dot_general(a, b, (((1,), (1,)), ((), ())), preferred_element_type=jnp.float32)

def tn(a, b):
    return lax.dot_general(a, b, (((0,), (0,)), ((), ())), preferred_element_type=jnp.float32)

def nn(a, b):
    return jnp.dot(a, b, preferred_element_type=jnp.float32)


def type_marks(rows, half, lane, row):
    kind = jnp.where(row < half, TYPE0, jnp.where(row < 2 * half, TYPE0 + 1, TYPE0 + 2))
    return (lane == kind)


def attend_step(half, scale, tq, *refs):
    attend_kernel(half, scale, tq, pl.program_id(1), *refs)


def attend_kernel(half, scale, tq, pair, q_ref, k_ref, v_ref, kaug_ref, o_ref, lse_ref):
    rows = q_ref.shape[1]
    zero = jnp.zeros((), jnp.bfloat16)
    k, v = k_ref[0], v_ref[0]
    kaug = kaug_ref[0]
    lane_all = lax.broadcasted_iota(jnp.int32, (rows, LANES), 1)
    low_all = lane_all < LANES // 2
    one = jnp.ones((), jnp.bfloat16)
    kx, vx = [], []
    for sel in (low_all, jnp.logical_not(low_all)):
        kx.append(jnp.concatenate([jnp.where(sel, k, zero), kaug], axis=1))
        vx.append(jnp.concatenate([jnp.where(sel, v, zero), jnp.where(sel, one, zero)], axis=1))
    for start in range(0, rows, tq):
        lane = lax.broadcasted_iota(jnp.int32, (tq, LANES), 1)
        row = lax.broadcasted_iota(jnp.int32, (tq, LANES), 0) + start
        low = lane < LANES // 2
        qaug = jnp.where(type_marks(rows, half, lane, row), one, zero)
        q = (q_ref[0, start:start + tq].astype(jnp.float32) * scale).astype(jnp.bfloat16)
        qx = jnp.concatenate([q, qaug], axis=1)
        acc = None
        peaks = []
        for a in (0, 1):
            s = nt(qx, kx[a])
            peak = jnp.max(s, axis=1, keepdims=True)
            p = jnp.exp(s - peak).astype(jnp.bfloat16)
            part = nn(p, vx[a])
            acc = part if acc is None else acc + part
            peaks.append(peak)
        total = acc[:, LANES:]
        o_ref[0, start:start + tq] = (acc[:, :LANES] / total).astype(jnp.bfloat16)
        lse = jnp.where(low, peaks[0], peaks[1]) + jnp.log(total)
        first, second = lse[:, 0:1], lse[:, LANES // 2:LANES // 2 + 1]
        prev = jnp.where(pair == 0, 0.0, lse_ref[0, start:start + tq])
        head = lax.rem(lane, HEADS)
        inside = lane < 3 * HEADS
        kept = jnp.where(inside & (head == 2 * pair), first, prev)
        lse_ref[0, start:start + tq] = jnp.where(inside & (head == 2 * pair + 1), second, kept)


def attend(qkv, kaug, half, tq=320):
    row_count, rows, cols = qkv.shape
    width = cols // 3
    pairs = width // LANES
    scale = (width // HEADS) ** (-0.5)
    spec = lambda off: pl.BlockSpec((1, rows, LANES), lambda r, p: (r, 0, off + p))
    return pl.pallas_call(
        functools.partial(attend_step, half, scale, tq),
        grid=(row_count, pairs),
        in_specs=[spec(0), spec(pairs), spec(2 * pairs), pl.BlockSpec((1, rows, LANES), lambda r, p: (r, 0, 0))],
        out_specs=[spec(0), pl.BlockSpec((1, rows, LANES), lambda r, p: (r, 0, 0))],
        out_shape=[
            jax.ShapeDtypeStruct((row_count, rows, width), jnp.bfloat16),
            jax.ShapeDtypeStruct((row_count, rows, LANES), jnp.float32),
        ],
        compiler_params=pltpu.CompilerParams(vmem_limit_bytes=48 * 1024 * 1024),
        name="attend",
    )(qkv, qkv, qkv, kaug)


def three_parts(values, lane):
    top = values.astype(jnp.bfloat16)
    rest = values - top.astype(jnp.float32)
    mid = rest.astype(jnp.bfloat16)
    low = (rest - mid.astype(jnp.float32)).astype(jnp.bfloat16)
    zero = jnp.zeros((), jnp.bfloat16)
    return jnp.where(lane < HEADS, top, jnp.where(lane < 2 * HEADS, mid, jnp.where(lane < 3 * HEADS, low, zero)))


def attend_back_step(half, scale, tk, q_ref, k_ref, v_ref, g_ref, lse_ref, delta_ref, *refs):
    attend_back_kernel(
        half, scale, tk, pl.program_id(1), q_ref, k_ref, v_ref, g_ref[0], lse_ref[0], delta_ref[0], *refs
    )


def attend_back_kernel(half, scale, tk, pair, q_ref, k_ref, v_ref, g, lse, delta, kaug_ref, dq_ref, dk_ref, dv_ref):
    rows = q_ref.shape[1]
    zero = jnp.zeros((), jnp.bfloat16)
    one = jnp.ones((), jnp.bfloat16)
    lane = lax.broadcasted_iota(jnp.int32, (rows, LANES), 1)
    row = lax.broadcasted_iota(jnp.int32, (rows, LANES), 0)
    low = lane < LANES // 2
    q = (q_ref[0].astype(jnp.float32) * scale).astype(jnp.bfloat16)
    qaug = jnp.where(type_marks(rows, half, lane, row), one, three_parts(lse, lane))
    gaug = three_parts(delta, lane)
    qx = jnp.concatenate([q, qaug], axis=1)
    gx = jnp.concatenate([g, gaug], axis=1)
    sels = (low, jnp.logical_not(low))
    qh = [jnp.where(sel, q, zero) for sel in sels]
    gh = [jnp.where(sel, g, zero) for sel in sels]
    dq = None
    for start in range(0, rows, tk):
        lane_k = lax.broadcasted_iota(jnp.int32, (tk, LANES), 1)
        low_k = lane_k < LANES // 2
        head = lax.rem(lane_k, HEADS)
        inside = lane_k < 3 * HEADS
        k = k_ref[0, start:start + tk]
        v = v_ref[0, start:start + tk]
        kaug = kaug_ref[0, start:start + tk]
        dk = dv = None
        for a, sel in ((0, low_k), (1, jnp.logical_not(low_k))):
            marks = inside & (head == 2 * pair + a)
            kh = jnp.where(sel, k, zero)
            kx = jnp.concatenate([kh, jnp.where(marks, -one, kaug)], axis=1)
            vx = jnp.concatenate([jnp.where(sel, v, zero), jnp.where(marks, -one, zero)], axis=1)
            p = jnp.exp(nt(kx, qx))
            ds = (p * nt(vx, gx)).astype(jnp.bfloat16)
            part_v = nn(p.astype(jnp.bfloat16), gh[a])
            part_k = nn(ds, qh[a])
            part_q = tn(ds, kh)
            dv = part_v if dv is None else dv + part_v
            dk = part_k if dk is None else dk + part_k
            dq = part_q if dq is None else dq + part_q
        dk_ref[0, start:start + tk] = dk.astype(jnp.bfloat16)
        dv_ref[0, start:start + tk] = dv.astype(jnp.bfloat16)
    dq_ref[0] = (dq * scale).astype(jnp.bfloat16)


def attend_back(qkv, grad, lse, delta, kaug, half, tk=320):
    row_count, rows, cols = qkv.shape
    width = cols // 3
    pairs = width // LANES
    scale = (width // HEADS) ** (-0.5)
    spec = lambda off: pl.BlockSpec((1, rows, LANES), lambda r, p: (r, 0, off + p))
    whole = pl.BlockSpec((1, rows, LANES), lambda r, p: (r, 0, 0))
    out = jax.ShapeDtypeStruct((row_count, rows, width), jnp.bfloat16)
    return pl.pallas_call(
        functools.partial(attend_back_step, half, scale, tk),
        grid=(row_count, pairs),
        in_specs=[spec(0), spec(pairs), spec(2 * pairs), spec(0), whole, whole, whole],
        out_specs=[spec(0)] * 3,
        out_shape=[out] * 3,
        compiler_params=pltpu.CompilerParams(vmem_limit_bytes=48 * 1024 * 1024),
        name="attend_back",
    )(qkv, qkv, qkv, grad, lse, delta, kaug)


EPS = 1e-05
MESH_ID = pl.DeviceIdType.MESH


def spread_kernel(count, sizes, same, *refs):
    ins, outs = refs[:sizes], refs[sizes:2 * sizes]
    send, recv, local = refs[2 * sizes:]
    me = lax.axis_index("seq")
    barrier = pltpu.get_barrier_semaphore()
    for step in range(1, count):
        pl.semaphore_signal(
            barrier, inc=1, device_id={"seq": lax.rem(me + step, count)}, device_id_type=MESH_ID
        )
    pl.semaphore_wait(barrier, count - 1)
    own = []
    for n in range(sizes):
        copy = pltpu.make_async_copy(ins[n] if same else ins[n].at[me], outs[n].at[me], local.at[n])
        copy.start()
        own.append(copy)
    copies = []
    for step in range(1, count):
        peer = lax.rem(me + step, count)
        for n in range(sizes):
            copy = pltpu.make_async_remote_copy(
                src_ref=ins[n] if same else ins[n].at[peer],
                dst_ref=outs[n].at[me],
                send_sem=send.at[n, step],
                recv_sem=recv.at[n, step],
                device_id={"seq": peer},
                device_id_type=MESH_ID,
            )
            copy.start()
            copies.append(copy)
    for copy in own:
        copy.wait()
    for copy in copies:
        copy.wait()


def spread(arrays, count, same, collective_id):
    sizes = len(arrays)
    shapes = [(count,) + a.shape if same else a.shape for a in arrays]
    vmem = pl.BlockSpec(memory_space=pltpu.VMEM)
    return pl.pallas_call(
        functools.partial(spread_kernel, count, sizes, same),
        in_specs=[vmem] * sizes,
        out_specs=[vmem] * sizes,
        out_shape=[jax.ShapeDtypeStruct(s, a.dtype) for s, a in zip(shapes, arrays)],
        scratch_shapes=[
            pltpu.SemaphoreType.DMA((sizes, count)),
            pltpu.SemaphoreType.DMA((sizes, count)),
            pltpu.SemaphoreType.DMA((sizes,)),
        ],
        compiler_params=pltpu.CompilerParams(
            collective_id=collective_id, has_side_effects=True, vmem_limit_bytes=32 * 1024 * 1024
        ),
        name="spread",
    )(*arrays)


SEQ_BITS = (("z1", 4), ("z0", 2), ("x", 1))
BATCH_BITS = (("y", 2), ("c", 1))


class Place:
    def __init__(self):
        self.spot, self.step = {}, {}
        for name, bits in (("seq", SEQ_BITS), ("batch", BATCH_BITS)):
            index = lax.axis_index(name)
            for axis, weight in bits:
                bit = lax.rem(lax.div(index, weight), 2)
                self.spot[axis] = bit
                self.step[axis] = {name: index + weight * (1 - 2 * bit)}

    def __getitem__(self, axis):
        return self.spot[axis]

    def partner(self, axis):
        return self.step[axis]

    def greet(self, others=()):
        barrier = pltpu.get_barrier_semaphore()
        peers = list(self.step.values()) + list(others)
        for to in peers:
            pl.semaphore_signal(barrier, inc=1, device_id=to, device_id_type=MESH_ID)
        pl.semaphore_wait(barrier, len(peers))


def remote(src, dst, send, recv, to):
    return pltpu.make_async_remote_copy(
        src_ref=src, dst_ref=dst, send_sem=send, recv_sem=recv, device_id=to, device_id_type=MESH_ID
    )


class Halve:
    def __init__(self, place, own, lanes, order, bufs, send, recv, first, stages=None):
        self.place, self.own, self.order = place, own, order
        self.lanes = pl.ds(*lanes)
        self.half = own.shape[3] // 2
        stages = range(len(order)) if stages is None else stages
        self.bufs = dict(zip(stages, bufs))
        self.send, self.recv, self.first = send, recv, first

    def copy(self, n):
        at = self.first + n
        return remote(
            self.own.at[self.region(n, False)], self.bufs[n], self.send.at[at], self.recv.at[at],
            self.place.partner(self.order[n]),
        )

    @staticmethod
    def buffers(rows, width, order, stages=None, dtype=jnp.bfloat16):
        shapes = []
        for n in range(len(order)) if stages is None else stages:
            left = [axis for axis, _ in SEQ_BITS if axis not in order[:n + 1]]
            shapes.append((2,) * len(left) + (rows // 2 if "y" in order[:n + 1] else rows, width))
        return [pltpu.VMEM(shape, dtype) for shape in shapes]

    def region(self, n, mine, free=(), piece=None):
        free = list(free)
        at = []
        for axis, _ in SEQ_BITS:
            if axis in self.order[:n]:
                at.append(self.place[axis])
            elif axis == self.order[n]:
                at.append(self.place[axis] if mine else 1 - self.place[axis])
            else:
                at.append(free.pop(0) if free else slice(None))
        first, count = 0, self.own.shape[3]
        if "y" in self.order[:n + 1]:
            y = self.place["y"]
            y = y if mine or self.order[n] != "y" else 1 - y
            first, count = y * self.half, self.half
        if piece is not None:
            first, count = first + piece[0], piece[1]
        rows = pl.ds(pl.multiple_of(first, 16), count)
        return (*at, rows, self.lanes)

    def start(self, n):
        self.copy(n).start()

    def sent(self):
        for n in self.bufs:
            self.copy(n).wait_send()

    def finish(self, n):
        self.copy(n).wait_recv()
        buf = self.bufs[n]
        dims = len(buf.shape) - 2
        count = buf.shape[-2]
        piece = math.gcd(count, 48)
        pieces = count // piece

        def add(i, carry):
            block, row = lax.div(i, pieces), lax.rem(i, pieces) * piece
            free = [lax.rem(lax.div(block, 2 ** (dims - 1 - d)), 2) for d in range(dims)]
            at = self.region(n, True, free, (row, piece))
            self.own[at] = self.own[at] + buf[(*free, pl.ds(pl.multiple_of(row, 16), piece), slice(None))]
            return carry

        lax.fori_loop(0, 2 ** dims * pieces, add, 0)


class Gather:
    order = ("z1", "z0", "x")

    def __init__(self, place, buf, send, recv):
        self.place, self.buf, self.send, self.recv = place, buf, send, recv

    def copy(self, n):
        done = self.order[:n]
        at = (slice(None), *(slice(None) if axis in done else self.place[axis] for axis, _ in SEQ_BITS))
        block = self.buf.at[at]
        return remote(block, block, self.send.at[n], self.recv.at[n], self.place.partner(self.order[n]))

    def stage(self, n):
        if n > 0:
            self.copy(n - 1).wait_recv()
        if n < 3:
            self.copy(n).start()

    def finish(self):
        for n in range(3):
            self.copy(n).wait_send()


PARTS = (
    ((0, 256), ("x", "y", "z0", "z1")),
    ((256, 256), ("y", "x", "z0", "z1")),
    ((512, 256), ("z0", "z1", "x", "y")),
)


class Fold:
    EARLY, LATE = (0, 1), (2, 3)

    def __init__(self, place, pieces, refs, source=None, stages=(0, 1, 2, 3)):
        self.place = place
        c, y = place["c"], place["y"]
        if stages == self.LATE:
            self.own, self.done, send, recv, *bufs = refs
            self.got = local = None
        elif source is None:
            self.own, self.done, *refs = refs
        else:
            self.own, self.done = source.at[:, :, :, c], None
        if stages != self.LATE:
            self.got, send, recv, local, *bufs = refs
        own, got, done = self.own, self.got, self.done
        rows = own.shape[3]
        half = rows // 2
        self.mine = pl.ds(pl.multiple_of(y * half, 16), half)
        self.pieces, self.source, self.done = pieces, source, done
        self.sems = send, recv, local
        first = 1 if source is not None else len(pieces)
        self.first = first + 12
        self.parts = []
        for n, (lanes, order) in enumerate(PARTS):
            own_bufs = bufs[len(stages) * n:len(stages) * (n + 1)]
            self.parts.append(Halve(place, own, lanes, order, own_bufs, send, recv, first + 4 * n, stages))

    def keep(self):
        at, copies = 0, []
        if self.source is None:
            for n, (take, count) in enumerate(self.pieces):
                spot = self.own.at[:, :, :, pl.ds(at, count)]
                copies.append(pltpu.make_async_copy(take(self.place["c"]), spot, self.sems[2].at[n]))
                at += count
        return copies

    def core(self):
        send, recv, _ = self.sems
        to, c = self.place.partner("c"), 1 - self.place["c"]
        if self.source is not None:
            return [remote(self.source.at[:, :, :, c], self.got, send.at[0], recv.at[0], to)]
        at, copies = 0, []
        for n, (take, count) in enumerate(self.pieces):
            copies.append(remote(take(c), self.got.at[:, :, :, pl.ds(at, count)], send.at[n], recv.at[n], to))
            at += count
        return copies

    def across(self):
        send, recv, _ = self.sems
        spot = self.done.at[self.place["c"], self.mine]
        return remote(spot, spot, send.at[self.first], recv.at[self.first], self.place.partner("y"))

    def back(self):
        send, recv, _ = self.sems
        spot = self.done.at[self.place["c"]]
        return remote(spot, spot, send.at[self.first + 1], recv.at[self.first + 1], self.place.partner("c"))

    @staticmethod
    def scratch(rows, width, pieces, sourced=False, stages=(0, 1, 2, 3)):
        vmem = lambda *shape: pltpu.VMEM(shape, jnp.bfloat16)
        refs = [] if sourced else [vmem(2, 2, 2, rows, width), vmem(2, rows, width)]
        if stages != Fold.LATE:
            refs.append(vmem(2, 2, 2, rows, width))
        refs += [
            pltpu.SemaphoreType.DMA((pieces + 14,)),
            pltpu.SemaphoreType.DMA((pieces + 14,)),
        ]
        if stages != Fold.LATE:
            refs.append(pltpu.SemaphoreType.DMA((pieces,)))
        for (_, count), order in PARTS:
            refs += Halve.buffers(rows, count, order, stages)
        return refs

    def stage(self, n):
        if n == 0:
            for copy in self.keep() + self.core():
                copy.start()
        elif n == 1:
            for copy in self.keep():
                copy.wait()
            for copy in self.core():
                copy.wait_recv()

            piece = math.gcd(self.got.shape[3], 48)
            pieces = self.got.shape[3] // piece

            def add(i, carry):
                block = lax.div(i, pieces)
                rows = pl.ds(pl.multiple_of(lax.rem(i, pieces) * piece, 16), piece)
                at = (*(lax.rem(lax.div(block, w), 2) for _, w in SEQ_BITS), rows)
                self.own[at] = self.own[at] + self.got[at]
                return carry

            lax.fori_loop(0, 8 * pieces, add, 0)
            for part in self.parts:
                part.start(0)
        elif n < 5:
            for part in self.parts:
                part.finish(n - 2)
                part.start(n - 1)
        elif n == 5:
            for part in self.parts:
                part.finish(3)
            at = tuple(self.place[axis] for axis, _ in SEQ_BITS)
            self.done[self.place["c"], self.mine] = self.own[(*at, self.mine)]
            self.across().start()
        elif n == 6:
            self.across().wait_recv()
            self.back().start()
        else:
            self.back().wait_recv()

    def held(self):
        z1, z0, x = (self.place[axis] for axis, _ in SEQ_BITS)
        a, b, c = (lanes[1] for lanes, _ in PARTS)
        return (slice(None), slice(None), x, self.mine, pl.ds(0, a + b)), (
            z1, z0, slice(None), slice(None), pl.ds(a + b, c)
        )

    def resume(self):
        for part in self.parts:
            part.start(2)

    def finish(self):
        copies = self.core()
        if self.done is not None:
            copies = copies + [self.across(), self.back()]
        for copy in copies:
            copy.wait_send()
        for part in self.parts:
            part.sent()


class Sum:
    order = ("c", "x", "y", "z0", "z1")

    def __init__(self, place, value, got, send, recv):
        self.place, self.value, self.got, self.send, self.recv = place, value, got, send, recv

    def copy(self, n):
        to = self.place.partner(self.order[n])
        return remote(self.value.at[n], self.got.at[n], self.send.at[n], self.recv.at[n], to)

    def stage(self, n):
        if n > 0:
            self.copy(n - 1).wait_recv()
            self.value[n] = self.value[n - 1] + self.got[n - 1]
        if n < 5:
            self.copy(n).start()

    def finish(self):
        for n in range(5):
            self.copy(n).wait_send()


def share_views(a, count):
    *lead, rows, width = a.shape
    return a.reshape(*lead, 2, 2, 2, rows // count, width)


def half_views(a, count):
    *lead, rows, width = a.shape
    return a.reshape(*lead, 2, 2, 2, 2, rows // (2 * count), width)


def fetch(sources, targets, sems, first=0):
    return [pltpu.make_async_copy(s, t, sems.at[first + n]) for n, (s, t) in enumerate(zip(sources, targets))]


def finish_kernel(
    inner, late, keys, outer, small, layer, igrad, gout, ggrad,
    inner_o, outer_o, out_o, qkv_o, fg_o, fs_o, sg_o, ss_o, bias_o, layer_o, igrad_o, gout_o, ggrad_o, sems,
):
    f32 = jnp.float32
    me = lax.axis_index("seq")
    copies = fetch((layer, igrad, gout, ggrad), (layer_o, igrad_o, gout_o, ggrad_o), sems)
    begin(copies)
    width = outer_o.shape[1]
    part = inner_o.shape[0]
    strips = inner.shape[1] // part
    half = outer.shape[1]
    for c in range(2):
        for j in range(strips):
            inner_o[:, pl.ds((c * strips + j) * width, width)] = inner[c, pl.ds(j * part, part)].astype(f32)
        outer_o[pl.ds(c * half, half)] = outer[c].astype(f32)
        spot = pl.ds(c * part // 2, part // 2)
        first, second = pl.ds(0, part // 2), pl.ds(part // 2, part // 2)
        out_o[spot] = late[c, first].astype(f32)
        for j, (ref, lines) in enumerate(((late, second), (keys, first), (keys, second))):
            qkv_o[spot, pl.ds(j * width, width)] = ref[c, lines].astype(f32)
    values = small[...]
    turned = pltpu.roll(values, lax.rem(width - part * me, width), 1)
    for n, ref in enumerate((fg_o, fs_o, sg_o, ss_o)):
        ref[...] = turned[n:n + 1, :part]
    wide = bias_o.shape[1]
    per = width // wide
    row = small[pl.ds(4 + lax.div(me, per), 1)]
    spots = [row[:, n * wide:(n + 1) * wide] for n in range(per)]
    chosen = spots[0]
    for n in range(1, per):
        chosen = jnp.where(lax.rem(me, per) == n, spots[n], chosen)
    bias_o[...] = chosen
    for copy in copies:
        copy.wait()


def finish(inner, late, keys, outer, small, layer, igrad, gout, ggrad):
    width = small.shape[1]
    part = late.shape[1]
    bias = 2 * outer.shape[1]
    vmem, hbm = pl.BlockSpec(memory_space=pltpu.VMEM), pl.BlockSpec(memory_space=pl.ANY)
    shapes = [(part, 2 * inner.shape[1] // part * width), (bias, width), (part, width), (part, 3 * width)]
    shapes += [(1, part)] * 4 + [(1, bias)]
    moved = [layer, igrad, gout, ggrad]
    return pl.pallas_call(
        finish_kernel,
        in_specs=[vmem] * 9,
        out_specs=[vmem] * 9 + [hbm] * 4,
        out_shape=[jax.ShapeDtypeStruct(s, jnp.float32) for s in shapes]
        + [jax.ShapeDtypeStruct(a.shape, a.dtype) for a in moved],
        scratch_shapes=[pltpu.SemaphoreType.DMA((4,))],
        compiler_params=pltpu.CompilerParams(vmem_limit_bytes=60 * 1024 * 1024),
        name="finish",
    )(inner, late, keys, outer, small, *moved)


def begin(copies):
    for copy in copies:
        copy.start()


def sum_rows(values):
    rows, width = values.shape
    return jnp.sum(values.reshape(rows // 8, 8, width), axis=0)


def ticks(plan, folds, step):
    for t, todo in plan.items():

        @pl.when(step == t)
        def _():
            for f, n in todo:
                folds[f].stage(n)


TILE_AT = ((6, 0, 1), (7, 0, 0), (15, 1, 1), (19, 1, 0))
GLOBALS_AT, STRIPS_AT, OWN_AT = 14, 16, 20
REAR_TICKS = {
    0: ((0, 0),),
    2: ((0, 1),),
    3: ((3, 4),),
    5: ((3, 5),),
    6: ((0, 2),),
    7: ((3, 6),),
    8: ((3, 7),),
    11: ((0, 3),),
    14: ((0, 4),),
    16: ((0, 5),),
    17: ((1, 0),),
    18: ((0, 6),),
    19: ((1, 1), (2, 0), (0, 7)),
}
REAR_END = (
    (2, 1), (5, 1), (1, 2), (4, 1), (2, 2), (1, 3), (5, 2), (4, 2), (2, 3), (5, 3), (1, 4), (4, 3), (5, 4), (2, 4), (5, 5), (1, 5), (2, 5), (1, 6),
    (2, 6), (1, 7), (2, 7),
)
SPREAD_TICKS = {17: 0, 18: 1, 20: 2}


def rear_kernel(
    half, scale, pairs, fold_refs,
    q_ref, k_ref, v_ref, g_ref, lse_ref, delta_ref, kaug_ref,
    x_ref, next_x_ref, res_ref, gg_in, glse_in, gdelta_in, outer_ab, outer_c, gres_in, globals_in, weight_in, gain_in, vectors_in,
    normed_in, inner, out,
    igrad_o, ggrad_o, inner_o, late_o, keys_o, outer_o, small_o,
    gg_ref, glse_ref, gdelta_ref, gres_ref, globals_ref, weight_ref, gain_ref, vectors_ref, normed_ref,
    dqkv, gfirst, sums, qkv_src, grads, ggrad, value, got,
    send, recv, local, *scratch,
):
    step = pl.program_id(0)
    place = Place()
    me = lax.axis_index("seq")
    count = lax.axis_size("seq")
    row_count, rows, cols = dqkv.shape
    block_len = 2 * half
    width = cols // 3
    share = gres_ref.shape[1]
    attn = row_count * pairs
    strips = inner.shape[0] // 2
    part_rows = inner.shape[4]
    half_part = part_rows // 2
    sources = (
        [(lambda c, j=j: inner.at[c * strips + j], part_rows) for j in range(strips)],
        [(lambda c: out.at[:, :, :, c], half_part), (lambda c: qkv_src.at[0, :, :, :, c], half_part)],
        [(lambda c, j=j: qkv_src.at[j, :, :, :, c], half_part) for j in (1, 2)],
    )
    folds, at = [], 0
    for pieces, size in zip(sources, fold_refs[:3]):
        folds.append(Fold(place, pieces, scratch[at:at + size]))
        at += size
    folds.append(Fold(place, (), scratch[at:at + fold_refs[3]], None, Fold.LATE))
    at += fold_refs[3]
    spread = Halve(place, gfirst, (0, width), ("x", "z0", "z1"), scratch[at:], send.at[0], recv.at[0], 0)
    gather = Gather(place, ggrad, send.at[row_count], recv.at[row_count])
    small = Sum(place, value, got, send.at[row_count + 1], recv.at[row_count + 1])
    following = {"seq": lax.rem(me + 1, count)}
    before = {"seq": lax.rem(me + count - 1, count)}
    held = folds[3].held()
    early = lambda: fetch(
        (gg_in, glse_in, gdelta_in, outer_ab, outer_c),
        (gg_ref, glse_ref, gdelta_ref, folds[3].own.at[held[0]], folds[3].own.at[held[1]]), local,
    )
    later = lambda: fetch(
        (gres_in, globals_in, weight_in, gain_in, vectors_in),
        (gres_ref, globals_ref, weight_ref, gain_ref.at[0], vectors_ref), local, 5,
    )
    latest = lambda: fetch((normed_in,), (normed_ref,), local, 11)

    def home(r):
        sems = send.at[row_count + 2, r], recv.at[row_count + 2, r]
        return remote(grads.at[1, r], igrad_o.at[r, pl.ds(0, half)], *sems, following)

    def keep(r):
        return pltpu.make_async_copy(grads.at[0, r], igrad_o.at[r, pl.ds(half, half)], local.at[12 + r])

    @pl.when(step == 0)
    def _():
        begin(early() + later() + latest())
        place.greet([following, before])
        sums[...] = jnp.zeros_like(sums)
        for copy in early():
            copy.wait()
        folds[3].resume()

    ticks(REAR_TICKS, folds, step)

    @pl.when((step < pairs) | ((step >= pairs + 2) & (step < attn + 2)))
    def _():
        r = jnp.where(step < pairs, 0, 1)
        p = step - r * (pairs + 2)
        spots = [pl.ds(pl.multiple_of(j * width + p * LANES, LANES), LANES) for j in range(3)]
        lane = pl.ds(pl.multiple_of(p * LANES, LANES), LANES)
        wide = lambda a, b: jnp.concatenate([a, b.reshape(rows - block_len, LANES)], axis=0)
        attend_back_kernel(
            half, scale, 320, p, q_ref, k_ref, v_ref, wide(g_ref[...], gg_ref[r, :, :, :, :, lane]),
            wide(lse_ref[0], glse_ref[r]), wide(delta_ref[...], gdelta_ref[r]), kaug_ref,
            *(dqkv.at[pl.ds(r, 1), :, spot] for spot in spots),
        )

    for t, n in SPREAD_TICKS.items():

        @pl.when(step == t)
        def _():
            spread.finish(n)
            if n < 2:
                spread.start(n + 1)

    @pl.when(step == TILE_AT[0][0])
    def _():
        for copy in later():
            copy.wait()

    @pl.when(step == STRIPS_AT)
    def _():
        for copy in latest():
            copy.wait()


    strip_at = step - STRIPS_AT

    @pl.when((strip_at >= 0) & (strip_at < 3))
    def _():
        strip = pl.ds(pl.multiple_of(strip_at * width, width), width)
        total = tn(normed_ref[0], dqkv[0, :, strip])
        for r in range(1, row_count):
            total = total + tn(normed_ref[r], dqkv[r, :, strip])
        qkv_src[strip_at] = total.astype(jnp.bfloat16).reshape(qkv_src.shape[1:])

    def stats(x):
        centred = x - jnp.mean(x, axis=-1, keepdims=True)
        inv = lax.rsqrt(jnp.mean(centred * centred, axis=-1, keepdims=True) + EPS)
        return centred * inv, inv

    def add_sums(first, n):
        sums[0] += sum_rows(first * n)
        sums[1] += sum_rows(first)

    def through(first, n, inv):
        eg = first * gain_ref[...]
        return (eg - jnp.mean(eg, axis=-1, keepdims=True) - n * jnp.mean(eg * n, axis=-1, keepdims=True)) * inv

    @pl.when(step == GLOBALS_AT)
    def _():
        own = pl.ds(block_len, rows - block_len)
        partial = jnp.concatenate([dqkv[r, own] for r in range(row_count)], axis=0)
        first = nt(partial, weight_ref[...])
        n, _ = stats(globals_ref[...].astype(jnp.float32).reshape(first.shape))
        add_sums(first, n)
        first = first.astype(jnp.bfloat16).reshape(row_count, 2, 2, 2, share, width)
        for r in range(row_count):
            gfirst[:, :, :, pl.ds(r * share, share)] = first[r]
        spread.start(0)

    @pl.when(functools.reduce(jnp.logical_or, [step == t for t, _, _ in TILE_AT]))
    def _():
        r = jnp.where(step < pairs + 2, 0, 1)
        h = jnp.where((step == TILE_AT[0][0]) | (step == TILE_AT[2][0]), 1, 0)
        first = nt(dqkv[r, pl.ds(pl.multiple_of(h * half, half), half)], weight_ref[...])
        n, inv = stats(jnp.where(h == 0, x_ref[0].astype(jnp.float32), next_x_ref[0].astype(jnp.float32)))
        add_sums(first, n)
        grads[h, r] = (res_ref[...] + through(first, n, inv)).astype(jnp.bfloat16)

    for t, r, h in TILE_AT:

        @pl.when(step == t)
        def _():
            (home if h else keep)(r).start()

    @pl.when(step == OWN_AT)
    def _():
        lines = [jnp.sum(sums[n], axis=0, keepdims=True) for n in range(2)]
        value[0] = jnp.concatenate(lines + [vectors_ref[...]])
        small.stage(0)
        own_rows = row_count * share
        at = tuple(place[axis] for axis, _ in SEQ_BITS)
        held = pl.ds(pl.multiple_of(share * me, 16), share)
        n, inv = stats(globals_ref[:, held].astype(jnp.float32).reshape(own_rows, width))
        grad = gres_ref[...].reshape(own_rows, width) + through(gfirst[at].astype(jnp.float32), n, inv)
        ggrad[(slice(None), *at)] = grad.astype(jnp.bfloat16).reshape(row_count, share, width)
        gather.stage(0)

    @pl.when(step == OWN_AT + 1)
    def _():
        leaves = fetch(
            (folds[0].done, folds[3].done, ggrad, folds[1].done, folds[2].done, value.at[5]),
            (inner_o, outer_o, ggrad_o, late_o, keys_o, small_o), local, 12 + row_count,
        )
        begin(leaves[:2])
        movers = folds + [gather, small]
        for f, n in REAR_END:
            movers[f].stage(n)
        begin(leaves[2:])
        for fold in folds:
            fold.finish()
        gather.finish()
        small.finish()
        spread.sent()
        for r in range(row_count):
            keep(r).wait()
            home(r).wait()
        for copy in leaves:
            copy.wait()


def rear(
    qkv, grad, lse, delta, kaug, inputs, next_x, res_grad, global_grad, global_lse, global_delta, own_res, normed,
    globals_in, weight, gain, vectors, outer_ab, outer_c, inner, out, half, count,
):
    row_count, rows, cols = qkv.shape
    width = cols // 3
    pairs = width // LANES
    block_len = 2 * half
    global_count = rows - block_len
    share = global_count // count
    part = width // count
    scale = (width // HEADS) ** (-0.5)
    attn = row_count * pairs
    f32, bf16 = jnp.float32, jnp.bfloat16
    turn = lambda t: jnp.where(t < pairs, t, jnp.clip(t - 2, pairs, attn - 1))
    row_of = lambda t: turn(t) // pairs
    pair_of = lambda t: turn(t) % pairs
    spec = lambda off: pl.BlockSpec((1, rows, LANES), lambda t: (row_of(t), 0, off + pair_of(t)))
    whole = pl.BlockSpec((1, rows, LANES), lambda t: (row_of(t), 0, 0))

    def tile_of(t):
        (a, _, _), (b, _, _), (c, _, _), _ = TILE_AT
        return jnp.where(t <= a, 1, jnp.where(t <= b, 0, jnp.where(t <= c, 3, 2))), 0

    tile = pl.BlockSpec((half, width), tile_of)
    hbm = pl.BlockSpec(memory_space=pl.ANY)
    outs = [
        jax.ShapeDtypeStruct((row_count, block_len, width), bf16),
        jax.ShapeDtypeStruct((row_count, 2, 2, 2, share, width), bf16),
        jax.ShapeDtypeStruct((2, 2 * part, width), bf16),
        jax.ShapeDtypeStruct((2, part, width), bf16),
        jax.ShapeDtypeStruct((2, part, width), bf16),
        jax.ShapeDtypeStruct((2, 2 * part, width), bf16),
        jax.ShapeDtypeStruct((8, width), f32),
    ]
    folds, sizes = [], []
    for size, pieces in ((2 * part, 2), (part, 2), (part, 2)):
        refs = Fold.scratch(size, width, pieces)
        folds += refs
        sizes.append(len(refs))
    refs = Fold.scratch(2 * part, width, 0, False, Fold.LATE)
    folds += refs
    sizes.append(len(refs))
    vmem = pltpu.VMEM
    kinds = 4 + row_count
    early = (global_grad, global_lse, global_delta)
    later = (own_res, globals_in, weight, gain, vectors, normed)
    return pl.pallas_call(
        functools.partial(rear_kernel, half, scale, pairs, tuple(sizes)),
        grid=(OWN_AT + 2,),
        in_specs=[spec(0), spec(pairs), spec(2 * pairs)]
        + [pl.BlockSpec((block_len, LANES), lambda t: (row_of(t), pair_of(t)))]
        + [pl.BlockSpec((1, block_len, LANES), lambda t: (row_of(t), 0, 0))]
        + [pl.BlockSpec((block_len, LANES), lambda t: (row_of(t), 0)), whole]
        + [
            pl.BlockSpec((1, half, width), lambda t: (jnp.where(t <= TILE_AT[1][0], 0, 1), 1, 0)),
            pl.BlockSpec((1, half, width), lambda t: (jnp.where(t <= TILE_AT[0][0], 0, 1), 0, 0)),
            tile,
        ]
        + [hbm] * 13,
        out_specs=[hbm] * 7,
        out_shape=outs,
        scratch_shapes=[vmem(a.shape if a.ndim > 1 else (1, *a.shape), a.dtype) for a in early + later]
        + [
            vmem((row_count, rows, cols), bf16),
            vmem((2, 2, 2, row_count * share, width), bf16),
            vmem((2, 8, width), f32),
            vmem((3, 2, 2, 2, 2, part // 2, width), bf16),
            vmem((2, row_count, half, width), bf16),
            vmem((row_count, 2, 2, 2, share, width), bf16),
            vmem((6, 8, width), f32),
            vmem((5, 8, width), f32),
            pltpu.SemaphoreType.DMA((kinds, 5)),
            pltpu.SemaphoreType.DMA((kinds, 5)),
            pltpu.SemaphoreType.DMA((18 + row_count,)),
        ]
        + folds
        + Halve.buffers(row_count * share, width, ("x", "z0", "z1")),
        compiler_params=pltpu.CompilerParams(
            collective_id=9, has_side_effects=True, vmem_limit_bytes=64 * 1024 * 1024
        ),
        name="rear",
    )(
        qkv, qkv, qkv, grad, lse, delta, kaug, inputs, next_x, res_grad, *early, outer_ab, outer_c, *later,
        share_views(inner, count), half_views(out, count),
    )


def cdf_bell(v):
    bell = jnp.exp(-0.5 * v * v)
    t = 1.0 / (1.0 + (0.3275911 * 0.5 ** 0.5) * jnp.abs(v))
    poly = t * (
        0.127414796 + t * (-0.142248368 + t * (0.7107068705 + t * (-0.7265760135 + t * 0.5307027145)))
    )
    tail = poly * bell
    return jnp.where(v < 0, tail, 1.0 - tail), bell


MID_TICKS = {9: 0, 11: 1, 14: 2}
MID_GATHERS = {6: (0, 1), 8: (0, 2), 10: (0, 3), 11: (1, 1), 12: (1, 2), 13: (1, 3)}


def mid_kernel(
    half, fold_refs,
    lengths, x_ref, next_x_ref, mixed_ref, cot_ref, next_cot_ref, gain_in, shift_in, bias_in, out_in, inner_in, outer_in, gx_in, gcot_in,
    mixed_all, lse_all,
    layer_o, res_o, grad_o, delta_o, gres_o, gout_o, ggrad_o, glse_o, gdelta_o, inner_o, outer_ab_o, outer_c_o, out_o,
    vectors_o,
    gain_ref, shift_ref, bias_ref, out_w, inner_w, outer_w, gx_ref, gcot_ref, heads_ref,
    hidden, slope, normed, cot, att, proj, residual, outer_src, sums, bias_sums, layers,
    gout, ggrad, glse, gdelta, part_mixed, part_lse, send, recv, local, *scratch,
):
    f32, bf16 = jnp.float32, jnp.bfloat16
    step = pl.program_id(0)
    place = Place()
    me = lax.axis_index("seq")
    count = lax.axis_size("seq")
    row_count, share = gx_ref.shape[:2]
    block_len = 2 * half
    tokens = row_count * block_len
    own_rows = row_count * share
    width = gx_ref.shape[2]
    strips = inner_w.shape[1] // width
    tiles = 2 * row_count
    fold = Fold(place, None, scratch, outer_src, Fold.EARLY)
    held = pl.ds(pl.multiple_of(share * me, 16), share)
    following = {"seq": lax.rem(me + 1, count)}
    at = tuple(place[axis] for axis, _ in SEQ_BITS)

    def parts(m, to, r, n):
        rows = pl.ds(pl.multiple_of(block_len + share * to, 16), share)
        return (
            (mixed_all.at[r, rows], part_mixed.at[m, r]) if n == 0 else (lse_all.at[r, rows], part_lse.at[m, r])
        )

    def part_copies():
        copies = []
        for r in range(row_count):
            for n in range(2):
                for other in range(1, count):
                    to = lax.rem(me + other, count)
                    src, dst = parts(me, to, r, n)
                    sems = send.at[2 * r + n, other], recv.at[2 * r + n, other]
                    copies.append(remote(src, dst, *sems, {"seq": to}))
        return copies

    def part_own():
        return [
            pltpu.make_async_copy(*parts(me, me, r, n), local.at[2 * r + n]) for r in range(row_count) for n in range(2)
        ]

    base = 2 * row_count
    gathers = [
        Gather(place, buf, send.at[base + n], recv.at[base + n]) for n, buf in enumerate((gout, ggrad, glse, gdelta))
    ]
    leaves = lambda: fetch((gout, ggrad, glse, gdelta), (gout_o, ggrad_o, glse_o, gdelta_o), local, base)
    ends = base + 4

    def home(r):
        return remote(layers.at[1, r], layer_o.at[r, pl.ds(0, half)], send.at[ends, r], recv.at[ends, r], following)

    def keep(r):
        return pltpu.make_async_copy(layers.at[0, r], layer_o.at[r, pl.ds(half, half)], local.at[ends + r])

    loads = lambda: fetch(
        (gain_in, shift_in, bias_in, out_in, inner_in, outer_in, gx_in.at[:, held], gcot_in.at[:, held]),
        (gain_ref.at[0], shift_ref.at[0], bias_ref.at[0], out_w, inner_w, outer_w, gx_ref, gcot_ref), local, ends + row_count,
    )

    @pl.when(step == 0)
    def _():
        begin(loads())
        place.greet([{"seq": lax.rem(me + other, count)} for other in range(1, count)])
        begin(part_own() + part_copies())
        lane = lax.broadcasted_iota(jnp.int32, (width, LANES), 1)
        head = lax.div(lax.broadcasted_iota(jnp.int32, (width, LANES), 0), width // HEADS)
        chosen = jnp.where(lane < 3 * HEADS, lax.rem(lane, HEADS), -1) == head
        heads_ref[...] = jnp.where(chosen, 1.0, 0.0).astype(bf16)
        sums[...] = jnp.zeros_like(sums)
        bias_sums[...] = jnp.zeros_like(bias_sums)
        for copy in loads():
            copy.wait()

    def stats(values):
        centred = values - jnp.mean(values, axis=-1, keepdims=True)
        inv = lax.rsqrt(jnp.mean(centred * centred, axis=-1, keepdims=True) + EPS)
        return centred * inv, inv

    def forward(x, attended, rows):
        att[rows] = attended
        total = x.astype(f32) + nn(attended, out_w[...])
        residual[rows] = total
        n, _ = stats(total)
        second = (n * gain_ref[...] + shift_ref[...]).astype(bf16)
        normed[rows] = second

        def run(j, total):
            strip = pl.ds(pl.multiple_of(j * width, width), width)
            inner = nn(second, inner_w[:, strip]) + bias_ref[:, strip]
            cdf, bell = cdf_bell(inner)
            active = (inner * cdf).astype(bf16)
            hidden[rows, strip] = active
            slope[rows, strip] = (cdf + inner * bell * ((0.5 / math.pi) ** 0.5)).astype(bf16)
            return total + nn(active, outer_w[strip, :])

        return lax.fori_loop(0, strips, run, total)

    def backward(cotangent, rows):
        def run(j, total):
            strip = pl.ds(pl.multiple_of(j * width, width), width)
            grad = (nt(cotangent, outer_w[strip, :]) * slope[rows, strip].astype(f32)).astype(bf16)
            slope[rows, strip] = grad
            bias_sums[j] += sum_rows(grad.astype(f32))
            return total + nt(grad, inner_w[:, strip])

        second_grad = lax.fori_loop(0, strips, run, jnp.zeros(cotangent.shape, f32))
        n, inv = stats(residual[rows])
        eg = second_grad * gain_ref[...]
        through = (eg - jnp.mean(eg, axis=-1, keepdims=True) - n * jnp.mean(eg * n, axis=-1, keepdims=True)) * inv
        sums[0] += sum_rows(second_grad * n)
        sums[1] += sum_rows(second_grad)
        res = cotangent.astype(f32) + through
        projected = res.astype(bf16)
        proj[rows] = projected
        grad = nt(projected, out_w[...]).astype(bf16)
        product = grad.astype(f32) * att[rows].astype(f32)
        top = product.astype(bf16)
        rest = (product - top.astype(f32)).astype(bf16)
        return res, grad, nn(top, heads_ref[...]) + nn(rest, heads_ref[...])

    @pl.when(step < tiles)
    def _():
        r, h = lax.rem(step, row_count), 1 - lax.div(step, row_count)
        rows = pl.ds(pl.multiple_of((2 * r + h) * half, half), half)
        owner = lax.rem(me + h, count)
        spot = owner * block_len + (1 - h) * half + lax.broadcasted_iota(jnp.int32, (half, width), 0)
        valid = spot < lengths[r]
        pick = lambda a, b: jnp.where(h == 0, a[0].astype(f32), b[0].astype(f32))
        cot[rows] = jnp.where(valid, pick(cot_ref, next_cot_ref), 0.0).astype(bf16)
        final = forward(pick(x_ref, next_x_ref), mixed_ref[0], rows)
        layers[h, r] = jnp.where(valid, final, 0.0).astype(bf16)

    back = step - (tiles + 2 + strips)

    @pl.when((back >= 0) & (back < tiles))
    def _():
        r, h = lax.rem(back, row_count), 1 - lax.div(back, row_count)
        rows = pl.ds(pl.multiple_of((2 * r + h) * half, half), half)
        res, grad, delta = backward(cot[rows], rows)
        res_o[...] = res
        grad_o[...] = grad
        delta_o[...] = delta

    for r in range(row_count):

        @pl.when(step == r)
        def _():
            home(r).start()

        @pl.when(step == row_count + r)
        def _():
            keep(r).start()

    last = pl.ds(tokens, own_rows)

    @pl.when(step == tiles)
    def _():
        for copy in part_own():
            copy.wait()
        for copy in part_copies():
            copy.wait_recv()
        peak = jnp.max(part_lse[...], axis=0)
        shares = jnp.exp(part_lse[...] - peak)
        total = jnp.sum(shares, axis=0)
        lse = peak + jnp.log(total)
        glse[(slice(None), *at)] = lse
        shares = (shares / total).reshape(count * own_rows, LANES)
        lane = lax.broadcasted_iota(jnp.int32, shares.shape, 1)
        shares = jnp.where(lane < HEADS, shares, 0.0)
        top = shares.astype(bf16)
        rest = (shares - top.astype(f32)).astype(bf16)
        wide = nt(top, heads_ref[...]) + nt(rest, heads_ref[...])
        mixed = wide * part_mixed[...].reshape(count * own_rows, width).astype(f32)
        mixed = jnp.sum(mixed.reshape(count, own_rows, width), axis=0).astype(bf16)
        cot[last] = gcot_ref[...].reshape(own_rows, width)
        final = forward(gx_ref[...].reshape(own_rows, width), mixed, last)
        gout[(slice(None), *at)] = final.astype(bf16).reshape(row_count, share, width)
        gathers[0].stage(0)

    strip_at = step - (tiles + 1)

    @pl.when((strip_at >= 0) & (strip_at < strips))
    def _():
        strip = pl.ds(pl.multiple_of(strip_at * width, width), width)
        grad = tn(hidden[:, strip], cot[...]).astype(bf16)
        outer_src[lax.div(strip_at, 2), lax.rem(strip_at, 2)] = grad.reshape(outer_src.shape[2:])

    for t, (kind, n) in MID_GATHERS.items():

        @pl.when(step == t)
        def _():
            chosen = range(1, 4) if kind else range(1)
            for g in chosen:
                gathers[g].stage(n)
                if n == 3:
                    leaves()[g].start()

    for t, n in MID_TICKS.items():

        @pl.when(step == t)
        def _():
            fold.stage(n)

    after = 2 * tiles + 1 + strips

    @pl.when(step == tiles + 1 + strips)
    def _():
        res, grad, delta = backward(cot[last], last)
        gres_o[...] = res.reshape(row_count, share, width)
        ggrad[(slice(None), *at)] = grad.reshape(row_count, share, width)
        gdelta[(slice(None), *at)] = delta.reshape(row_count, share, LANES)
        for gather in gathers[1:]:
            gather.stage(0)

    inner_at = step - (after + 1)

    @pl.when((inner_at >= 0) & (inner_at < strips))
    def _():
        strip = pl.ds(pl.multiple_of(inner_at * width, width), width)
        inner_o[0] = tn(normed[...], slope[:, strip]).astype(bf16)

    @pl.when(step == after + 1 + strips)
    def _():
        out_o[...] = tn(att[...], proj[...]).astype(bf16)
        lines = [jnp.sum(sums[n], axis=0, keepdims=True) for n in range(2)]
        lines += [jnp.sum(bias_sums[n], axis=0, keepdims=True) for n in range(strips)]
        vectors_o[...] = jnp.concatenate(lines)
        for part in fold.parts:
            part.finish(1)
        first, second = fold.held()
        outer_ab_o[...] = fold.own[first]
        outer_c_o[...] = fold.own[second]
        fold.finish()
        for gather in gathers:
            gather.finish()
        for copy in part_copies():
            copy.wait_send()
        for r in range(row_count):
            keep(r).wait()
            home(r).wait()
        for copy in leaves():
            copy.wait()


def mid(
    lengths, inputs, next_x, mixed, lse, cotangent, next_cot, globals_in, global_cot, out_weight, inner_weight, outer_weight, bias, gain, shift,
    half, count,
):
    f32, bf16 = jnp.float32, jnp.bfloat16
    row_count, rows, width = mixed.shape
    block_len = 2 * half
    share = (rows - block_len) // count
    own_rows = row_count * share
    inner_width = inner_weight.shape[1]
    strips = inner_width // width
    part = width // count
    tiles = 2 * row_count
    total = row_count * block_len + own_rows

    def tile_at(first):
        def place(t):
            n = jnp.clip(t - first, 0, tiles - 1)
            return n % row_count, 1 - n // row_count

        return place

    forward_at, back_at = tile_at(0), tile_at(tiles + 2 + strips)

    def flat(where, cols):
        def index(t):
            r, h = where(t)
            return 2 * r + h, 0

        return pl.BlockSpec((half, cols), index)

    own_spec = pl.BlockSpec((1, half, width), lambda t: (jnp.clip(t - row_count, 0, row_count - 1), 1, 0))
    next_spec = pl.BlockSpec((1, half, width), lambda t: (jnp.clip(t, 0, row_count - 1), 0, 0))
    whole = lambda *shape: pl.BlockSpec(shape, lambda t: (0,) * len(shape))
    hbm = pl.BlockSpec(memory_space=pl.ANY)
    fixeds = (gain, shift, bias, out_weight, inner_weight, outer_weight, globals_in, global_cot)
    shared = (row_count, 2, 2, 2, share)
    after = 2 * tiles + 2 + strips
    of = jax.ShapeDtypeStruct
    outs = [
        of((row_count, block_len, width), bf16),
        of((row_count * block_len, width), f32),
        of((row_count * block_len, width), bf16),
        of((row_count * block_len, LANES), f32),
        of((row_count, share, width), f32),
        of((*shared, width), bf16),
        of((*shared, width), bf16),
        of((*shared, LANES), f32),
        of((*shared, LANES), f32),
        of((strips, width, width), bf16),
        of((2, 2, strips * part // 4, 512), bf16),
        of((2, strips * part // 2, 256), bf16),
        of((width, width), bf16),
        of((2 + strips, width), f32),
    ]
    vmem = pltpu.VMEM
    fold = Fold.scratch(strips * part // 2, width, 1, True, Fold.EARLY)
    kinds = 2 * row_count + 5
    return pl.pallas_call(
        functools.partial(mid_kernel, half, len(fold)),
        grid=(after + strips + 1,),
        in_specs=[
            pl.BlockSpec(memory_space=pltpu.SMEM),
            own_spec,
            next_spec,
            pl.BlockSpec((1, half, width), lambda t: (*forward_at(t), 0)),
            own_spec,
            next_spec,
        ]
        + [hbm] * (len(fixeds) + 2),
        out_specs=[
            hbm,
            flat(back_at, width),
            flat(back_at, width),
            flat(back_at, LANES),
            whole(row_count, share, width),
            hbm,
            hbm,
            hbm,
            hbm,
            pl.BlockSpec((1, width, width), lambda t: (jnp.clip(t - after, 0, strips - 1), 0, 0)),
            whole(*outs[10].shape),
            whole(*outs[11].shape),
            whole(width, width),
            whole(2 + strips, width),
        ],
        out_shape=outs,
        scratch_shapes=[vmem((1, a.shape[0]), f32) for a in fixeds[:3]]
        + [vmem(a.shape, bf16) for a in fixeds[3:6]]
        + [vmem((row_count, share, width), bf16)] * 2
        + [
            vmem((width, LANES), bf16),
            vmem((total, inner_width), bf16),
            vmem((total, inner_width), bf16),
            vmem((total, width), bf16),
            vmem((total, width), bf16),
            vmem((total, width), bf16),
            vmem((total, width), bf16),
            vmem((total, width), f32),
            vmem((2, 2, 2, 2, strips * part // 2, width), bf16),
            vmem((2, 8, width), f32),
            vmem((strips, 8, width), f32),
            vmem((2, row_count, half, width), bf16),
            vmem((*shared, width), bf16),
            vmem((*shared, width), bf16),
            vmem((*shared, LANES), f32),
            vmem((*shared, LANES), f32),
            vmem((count, row_count, share, width), bf16),
            vmem((count, row_count, share, LANES), f32),
            pltpu.SemaphoreType.DMA((kinds, count)),
            pltpu.SemaphoreType.DMA((kinds, count)),
            pltpu.SemaphoreType.DMA((kinds + row_count + len(fixeds),)),
        ]
        + fold,
        compiler_params=pltpu.CompilerParams(
            collective_id=10, has_side_effects=True, vmem_limit_bytes=64 * 1024 * 1024
        ),
        name="mid",
    )(lengths, inputs, next_x, mixed, cotangent, next_cot, *fixeds, mixed, lse)


def key_marks(me, count, length, half, rows):
    lane = lax.broadcasted_iota(jnp.int32, (rows, LANES), 1)
    row = lax.broadcasted_iota(jnp.int32, (rows, LANES), 0)
    kind = lane - TYPE0
    side = jnp.where(row < half, 0, 1)
    owner = lax.rem(me + side, count)
    position = owner * (2 * half) + jnp.where(row < half, row + half, row - half)
    apart = (me == count - 1) & (kind < 2) & (kind != side)
    of_token = jnp.where((position >= length) | apart, NEG, 0.0)
    of_global = jnp.where((kind == 2) & (me != 0), NEG, 0.0)
    marks = jnp.where(row < 2 * half, of_token, of_global)
    return jnp.where((kind >= 0) & (kind < 3), marks, 0.0).astype(jnp.bfloat16)


def head_kernel(
    half, scale, pairs, tq,
    lengths, inputs, cotangent, globals_in, gain_in, shift_in, weight_in,
    next_x, next_cot, qkv_o, mixed_o, lse_o, normed_o, kaug_o,
    gain, shift, weight, xs, qkv, mixed, lse, normed, kaug, send, recv, local,
):
    bf16, f32 = jnp.bfloat16, jnp.float32
    step = pl.program_id(0)
    me, count = lax.axis_index("seq"), lax.axis_size("seq")
    row_count, rows, width = xs.shape
    block_len = 2 * half
    previous = {"seq": lax.rem(me + count - 1, count)}
    following = {"seq": lax.rem(me + 1, count)}
    lower, upper, tail = pl.ds(0, half), pl.ds(half, half), pl.ds(block_len, rows - block_len)
    turns = [row_count + 1 + r * (pairs + 1) for r in range(row_count)]

    def arrive(r):
        return remote(inputs.at[r, lower], xs.at[r, upper], send.at[0, r], recv.at[0, r], previous)

    def arrive_cot(r):
        return remote(cotangent.at[r, lower], next_cot.at[r], send.at[1, r], recv.at[1, r], previous)

    def loads():
        own = [(inputs.at[r, upper], xs.at[r, lower]) for r in range(row_count)]
        own += [(globals_in.at[r], xs.at[r, tail]) for r in range(row_count)]
        own += [(gain_in, gain.at[0]), (shift_in, shift.at[0]), (weight_in, weight)]
        return fetch(*zip(*own), local)

    def leaves(r):
        pairs_of = ((qkv, qkv_o), (mixed, mixed_o), (lse, lse_o), (normed, normed_o), (kaug, kaug_o))
        moved = [(a.at[r], b.at[r]) for a, b in pairs_of] + [(xs.at[r, upper], next_x.at[r])]
        return fetch(*zip(*moved), local, 16 + 8 * r)

    def project(x):
        x = x.astype(f32)
        centred = x - jnp.mean(x, axis=-1, keepdims=True)
        inv = lax.rsqrt(jnp.mean(centred * centred, axis=-1, keepdims=True) + EPS)
        n = (centred * inv * gain[...] + shift[...]).astype(bf16)
        return n, nn(n, weight[...]).astype(bf16)

    @pl.when(step == 0)
    def _():
        begin(loads())
        barrier = pltpu.get_barrier_semaphore()
        for to in (previous, following):
            pl.semaphore_signal(barrier, inc=1, device_id=to, device_id_type=MESH_ID)
        pl.semaphore_wait(barrier, 2)
        begin([arrive(r) for r in range(row_count)])
        for r in range(row_count):
            kaug[r] = key_marks(me, count, lengths[r], half, rows)
        for copy in loads():
            copy.wait()

    for r in range(row_count):

        @pl.when(step == turns[r])
        def _():
            arrive(r).wait_recv()

    first = turns[0]
    is_turn = functools.reduce(jnp.logical_or, [step == t for t in turns])

    @pl.when((step < row_count) | is_turn)
    def _():
        h = jnp.where(step < row_count, 0, 1)
        r = jnp.where(step < row_count, step, lax.div(step - first, pairs + 1))
        spot = pl.ds(pl.multiple_of(h * half, half), half)
        normed[r, spot], qkv[r, spot] = project(xs[r, spot])

    @pl.when(step == row_count)
    def _():
        n, p = project(jnp.concatenate([xs[r, tail] for r in range(row_count)], axis=0))
        many = rows - block_len
        for r in range(row_count):
            normed[r, tail] = n[r * many:(r + 1) * many]
            qkv[r, tail] = p[r * many:(r + 1) * many]

    @pl.when(step == first + 1)
    def _():
        begin([arrive_cot(r) for r in range(row_count)])

    @pl.when((step > first) & jnp.logical_not(is_turn))
    def _():
        r, p = lax.div(step - first, pairs + 1), lax.rem(step - first, pairs + 1) - 1
        lane = lambda j: pl.ds(pl.multiple_of(j * width + p * LANES, LANES), LANES)
        row = pl.ds(r, 1)
        attend_kernel(
            half, scale, tq, p, qkv.at[row, :, lane(0)], qkv.at[row, :, lane(1)], qkv.at[row, :, lane(2)], kaug.at[row],
            mixed.at[row, :, lane(0)], lse.at[row],
        )

    for r in range(row_count):

        @pl.when(step == turns[r] + pairs)
        def _():
            begin(leaves(r))

    @pl.when(step == turns[-1] + pairs)
    def _():
        for r in range(row_count):
            for copy in leaves(r):
                copy.wait()
            arrive(r).wait_send()
            arrive_cot(r).wait()


def head(lengths, inputs, cotangent, globals_in, gain, shift, weight, tq):
    bf16, f32 = jnp.bfloat16, jnp.float32
    row_count, block_len, width = inputs.shape
    half = block_len // 2
    rows = block_len + globals_in.shape[1]
    pairs = width // LANES
    scale = (width // HEADS) ** (-0.5)
    hbm = pl.BlockSpec(memory_space=pl.ANY)
    of, vmem = jax.ShapeDtypeStruct, pltpu.VMEM
    results = [
        ((row_count, rows, 3 * width), bf16),
        ((row_count, rows, width), bf16),
        ((row_count, rows, LANES), f32),
        ((row_count, rows, width), bf16),
        ((row_count, rows, LANES), bf16),
    ]
    return pl.pallas_call(
        functools.partial(head_kernel, half, scale, pairs, tq),
        grid=(row_count + 1 + row_count * (pairs + 1),),
        in_specs=[pl.BlockSpec(memory_space=pltpu.SMEM)] + [hbm] * 6,
        out_specs=[hbm] * 7,
        out_shape=[of((row_count, half, width), bf16)] * 2 + [of(*r) for r in results],
        scratch_shapes=[
            vmem((1, width), f32),
            vmem((1, width), f32),
            vmem(weight.shape, bf16),
            vmem((row_count, rows, width), bf16),
        ]
        + [vmem(*r) for r in results]
        + [
            pltpu.SemaphoreType.DMA((2, row_count)),
            pltpu.SemaphoreType.DMA((2, row_count)),
            pltpu.SemaphoreType.DMA((16 + 8 * row_count,)),
        ],
        compiler_params=pltpu.CompilerParams(
            collective_id=11, has_side_effects=True, vmem_limit_bytes=60 * 1024 * 1024
        ),
        name="head",
    )(lengths, inputs, cotangent, globals_in, gain, shift, weight)


def wgrad_kernel(a_ref, b_ref, o_ref):
    o_ref[...] = tn(a_ref[...], b_ref[...]).astype(o_ref.dtype).reshape(o_ref.shape)


def wgrad(a, b, strip):
    rows, a_cols = a.shape
    b_cols = b.shape[1]
    split_a = a_cols > b_cols
    strips = max(a_cols, b_cols) // strip
    fixed = lambda n: (0, 0)
    moving = lambda n: (0, n)
    return pl.pallas_call(
        wgrad_kernel,
        grid=(strips,),
        in_specs=[
            pl.BlockSpec((rows, strip), moving if split_a else fixed),
            pl.BlockSpec((rows, strip), fixed if split_a else moving),
        ],
        out_specs=pl.BlockSpec((1, strip, strip), lambda n: (n, 0, 0)),
        out_shape=jax.ShapeDtypeStruct((strips, strip, strip), jnp.bfloat16),
        compiler_params=pltpu.CompilerParams(vmem_limit_bytes=40 * 1024 * 1024),
        name="wgrad",
    )(a, b)


def norm_parts(values):
    average = jnp.mean(values, axis=-1, keepdims=True)
    centred = values - average
    variance = jnp.mean(centred * centred, axis=-1, keepdims=True)
    inv = lax.rsqrt(variance + EPS)
    return centred * inv, inv


def norm_back(grad, n, inv, gain):
    eg = grad * gain
    through = (
        eg - jnp.mean(eg, axis=-1, keepdims=True) - n * jnp.mean(eg * n, axis=-1, keepdims=True)
    ) * inv
    return through, jnp.sum(grad * n, axis=0), jnp.sum(grad, axis=0)


def split_rows(a, count):
    row_count, rows, width = a.shape
    part = rows // count
    moved = a.reshape(row_count, count, part, width).transpose(1, 0, 2, 3)
    return moved.reshape(count, row_count * part, width)


def join_rows(a, row_count):
    count, rows, width = a.shape
    part = rows // row_count
    moved = a.reshape(count, row_count, part, width).transpose(1, 0, 2, 3)
    return moved.reshape(row_count, count * part, width)


def per_head(values, width):
    lanes = values[..., :HEADS]
    return jnp.repeat(lanes, width // HEADS, axis=-1)


def head_sums(values):
    rows, width = values.shape
    lane = jnp.arange(LANES)
    head = jnp.arange(width) // (width // HEADS)
    place = ((lane[None, :] % HEADS == head[:, None]) & (lane[None, :] < 3 * HEADS)).astype(jnp.bfloat16)
    top = values.astype(jnp.bfloat16)
    rest = (values - top.astype(jnp.float32)).astype(jnp.bfloat16)
    return nn(top, place) + nn(rest, place)


def reduce_share(a):
    a = lax.psum_scatter(a, "seq", scatter_dimension=0, tiled=True)
    return lax.psum(a.astype(jnp.bfloat16), "batch").astype(jnp.float32)


def body(
    inputs,
    global_inputs,
    lengths,
    first_gain,
    first_shift,
    qkv_weight,
    out_weight,
    second_gain,
    second_shift,
    inner_weight,
    inner_bias,
    outer_weight,
    output_cotangent,
    global_cotangent,
):
    f32, bf16 = jnp.float32, jnp.bfloat16
    row_count, block_len, width = inputs.shape
    half = block_len // 2
    global_count = global_inputs.shape[1]
    rows = block_len + global_count
    inner_width = inner_weight.shape[1]
    count = lax.axis_size("seq")
    me = lax.axis_index("seq")
    after = lax.rem(me + 1, count)
    back = [(i, (i - 1) % count) for i in range(count)]
    forth = [(i, (i + 1) % count) for i in range(count)]
    token_rows = row_count * block_len
    share = global_count // count
    own_rows = row_count * share

    if count == 8 and lax.axis_size("batch") == 4:
        next_x, next_cot, qkv, mixed, lse, normed, kaug = head(
            lengths, inputs, output_cotangent, global_inputs, first_gain, first_shift, qkv_weight, 320
        )
        (
            layer_output, residual_grad, block_grad, block_delta, own_res, global_out, global_grad, global_lse, global_delta,
            inner_wgrad, outer_ab, outer_c, out_grad, vectors,
        ) = mid(
            lengths, inputs, next_x, mixed, lse, output_cotangent, next_cot, global_inputs, global_cotangent, out_weight, inner_weight,
            outer_weight, inner_bias, second_gain, second_shift, half, count,
        )
        input_out, global_grad, *reduced = rear(
            qkv, block_grad, lse, block_delta, kaug, inputs, next_x, residual_grad, global_grad, global_lse, global_delta,
            own_res, normed, global_inputs, qkv_weight, first_gain, vectors, outer_ab, outer_c, inner_wgrad,
            out_grad, half, count,
        )
        joined = lambda a: a.reshape(row_count, global_count, width)
        inner_out, outer_out, out_out, qkv_out, *lines, layer_output, input_out, global_out, global_grad = finish(
            *reduced, layer_output, input_out, joined(global_out), joined(global_grad)
        )
        fg, fs, sg, ss, bias = (line.reshape(-1) for line in lines)
        return (
            layer_output, global_out, input_out, global_grad, fg, fs, qkv_out, out_out, sg, ss, inner_out, bias, outer_out,
        )

    own_globals = lax.dynamic_slice_in_dim(global_inputs, me * share, share, axis=1)
    own_global_cot = lax.dynamic_slice_in_dim(global_cotangent, me * share, share, axis=1)
    next_inputs = lax.ppermute(inputs[:, :half], "seq", back)
    next_cotangent = lax.ppermute(output_cotangent[:, :half], "seq", back)
    block = jnp.concatenate([inputs[:, half:], next_inputs], axis=1)
    spots = jnp.arange(half, dtype=jnp.int32)
    positions = jnp.concatenate([me * block_len + half + spots, after * block_len + spots])
    valid = positions[None, :] < lengths[:, None]

    kind = jnp.arange(LANES)[None, None, :] - TYPE0
    key_half = (jnp.arange(block_len) // half)[None, :, None]
    last = me == count - 1
    hidden_key = jnp.logical_not(valid)[:, :, None] | (last & (kind < 2) & (kind != key_half))
    token_marks = jnp.where(hidden_key & (kind >= 0) & (kind < 3), NEG, 0.0)
    global_marks = jnp.where((kind == 2) & (me != 0), NEG, 0.0)
    global_marks = jnp.broadcast_to(global_marks, (row_count, global_count, LANES))
    kaug = jnp.concatenate([token_marks, global_marks], axis=1).astype(bf16)

    states = jnp.concatenate([block, global_inputs], axis=1)
    n_first, inv_first = norm_parts(states.astype(f32))
    normed = (n_first * first_gain + first_shift).astype(bf16)
    qkv = nn(normed.reshape(row_count * rows, width), qkv_weight).astype(bf16)
    qkv = qkv.reshape(row_count, rows, 3 * width)

    mixed, lse = attend(qkv, kaug, half)
    tokens_in = block.reshape(token_rows, width)
    cot_block = jnp.concatenate([output_cotangent[:, half:], next_cotangent], axis=1)
    part_mixed, part_lse = spread(
        [split_rows(mixed[:, block_len:], count), split_rows(lse[:, block_len:], count)], count, False, 0
    )
    highest = jnp.max(part_lse, axis=0)
    part_weight = jnp.exp(part_lse - highest)
    total = jnp.sum(part_weight, axis=0)
    global_lse = highest + jnp.log(total)
    global_mixed = jnp.sum(per_head(part_weight / total, width) * part_mixed.astype(f32), axis=0)

    tokens = jnp.concatenate([tokens_in, own_globals.reshape(own_rows, width)]).astype(f32)
    cot_block = jnp.where(valid[:, :, None], cot_block, 0)
    cotangent = jnp.concatenate(
        [cot_block.reshape(token_rows, width), own_global_cot.reshape(own_rows, width)]
    )
    attended = jnp.concatenate(
        [mixed[:, :block_len].reshape(token_rows, width), global_mixed.astype(bf16)]
    )
    residual = tokens + nn(attended, out_weight)
    n_second, inv_second = norm_parts(residual)
    normed_second = (n_second * second_gain + second_shift).astype(bf16)
    inner = nn(normed_second, inner_weight) + inner_bias
    bell = jnp.exp(-0.5 * inner * inner)
    cdf = 0.5 * (1.0 + lax.erf(inner * (0.5 ** 0.5)))
    hidden = (inner * cdf).astype(bf16)
    final = residual + nn(hidden, outer_weight)
    hidden_grad = nt(cotangent, outer_weight)
    slope = cdf + inner * bell * ((0.5 / jnp.pi) ** 0.5)
    inner_grad = (hidden_grad * slope).astype(bf16)
    second_grad = nt(inner_grad, inner_weight)
    through, second_gain_grad, second_shift_grad = norm_back(second_grad, n_second, inv_second, second_gain)
    residual_grad = cotangent.astype(f32) + through
    projection_grad = residual_grad.astype(bf16)
    attended_grad = nt(projection_grad, out_weight).astype(bf16)
    delta = head_sums(attended_grad.astype(f32) * attended.astype(f32))
    outer_grad = wgrad(hidden, cotangent, width)
    inner_wgrad = wgrad(normed_second, inner_grad, width)
    bias_grad = jnp.sum(inner_grad.astype(f32), axis=0)
    out_grad = wgrad(attended, projection_grad, width)

    all_grad, all_lse, all_delta = spread(
        [attended_grad[token_rows:], global_lse, delta[token_rows:]], count, True, 1
    )
    block_grad = jnp.concatenate(
        [attended_grad[:token_rows].reshape(row_count, block_len, width), join_rows(all_grad, row_count)], axis=1
    )
    block_lse = jnp.concatenate([lse[:, :block_len], join_rows(all_lse, row_count)], axis=1)
    block_delta = jnp.concatenate(
        [delta[:token_rows].reshape(row_count, block_len, LANES), join_rows(all_delta, row_count)], axis=1
    )
    layer = final[:token_rows].reshape(row_count, block_len, width)
    layer = jnp.where(valid[:, :, None], layer, 0.0).astype(bf16)
    layer_output = jnp.concatenate([lax.ppermute(layer[:, half:], "seq", forth), layer[:, :half]], axis=1)
    own_out = final[token_rows:].astype(bf16)
    part = width // count
    dqkv = jnp.concatenate(attend_back(qkv, block_grad, block_lse, block_delta, kaug, half, rows), axis=-1)
    (part_dqkv,) = spread([split_rows(dqkv[:, block_len:], count)], count, False, 2)
    global_dqkv = jnp.sum(part_dqkv.astype(f32), axis=0).astype(bf16)
    qkv_grad = jnp.concatenate([dqkv[:, :block_len].reshape(token_rows, 3 * width), global_dqkv])

    first_grad = nt(qkv_grad, qkv_weight)
    n_tokens, inv_tokens = norm_parts(tokens)
    through, first_gain_grad, first_shift_grad = norm_back(first_grad, n_tokens, inv_tokens, first_gain)
    input_grad = (residual_grad + through).astype(bf16)
    normed_tokens = (n_tokens * first_gain + first_shift).astype(bf16)
    qkv_wgrad = wgrad(normed_tokens, qkv_grad, width)

    grad_block = input_grad[:token_rows].reshape(row_count, block_len, width)
    input_out = jnp.concatenate(
        [lax.ppermute(grad_block[:, half:], "seq", forth), grad_block[:, :half]], axis=1
    )
    global_final, global_grad = spread([own_out, input_grad[token_rows:]], count, True, 3)

    def shares(a):
        return a.reshape(count, a.shape[0] // count)

    small = jnp.concatenate(
        [
            shares(first_gain_grad),
            shares(first_shift_grad),
            shares(second_gain_grad),
            shares(second_shift_grad),
            shares(bias_grad),
        ],
        axis=1,
    )
    inner_out = reduce_share(inner_wgrad.transpose(1, 0, 2).reshape(width, -1))
    outer_out = reduce_share(outer_grad.reshape(inner_width, width))
    out_out = reduce_share(out_grad[0])
    qkv_out = reduce_share(qkv_wgrad.transpose(1, 0, 2).reshape(width, -1))
    small = reduce_share(small)[0]
    return (
        layer_output,
        join_rows(global_final, row_count),
        input_out,
        join_rows(global_grad, row_count),
        small[:part],
        small[part:2 * part],
        qkv_out,
        out_out,
        small[2 * part:3 * part],
        small[3 * part:4 * part],
        inner_out,
        small[4 * part:],
        outer_out,
    )


def solution(mesh):
    rows = P("batch", "seq", None)
    globals_at = P("batch", None, None)
    return jax.shard_map(
        body,
        mesh=mesh,
        in_specs=(rows, globals_at, P("batch")) + (P(),) * 9 + (rows, globals_at),
        out_specs=(
            rows,
            globals_at,
            rows,
            globals_at,
            P("seq"),
            P("seq"),
            P("seq", None),
            P("seq", None),
            P("seq"),
            P("seq"),
            P("seq", None),
            P("seq"),
            P("seq", None),
        ),
        check_vma=False,
    )
```

```python
import functools
import math

import jax
import jax.numpy as jnp
from jax import lax
from jax.experimental import pallas as pl
from jax.experimental.pallas import tpu as pltpu
from jax.sharding import PartitionSpec as P

HEADS = 12
NEG = -1e30
LANES = 128
TYPE0 = 3 * HEADS

def nt(a, b):
    return lax.dot_general(a, b, (((1,), (1,)), ((), ())), preferred_element_type=jnp.float32)

def tn(a, b):
    return lax.dot_general(a, b, (((0,), (0,)), ((), ())), preferred_element_type=jnp.float32)

def nn(a, b):
    return jnp.dot(a, b, preferred_element_type=jnp.float32)


def type_marks(rows, half, lane, row):
    kind = jnp.where(row < half, TYPE0, jnp.where(row < 2 * half, TYPE0 + 1, TYPE0 + 2))
    return (lane == kind)


def attend_step(half, scale, tq, *refs):
    attend_kernel(half, scale, tq, pl.program_id(1), *refs)


def attend_kernel(half, scale, tq, pair, q_ref, k_ref, v_ref, kaug_ref, o_ref, lse_ref):
    rows = q_ref.shape[1]
    zero = jnp.zeros((), jnp.bfloat16)
    k, v = k_ref[0], v_ref[0]
    kaug = kaug_ref[0]
    lane_all = lax.broadcasted_iota(jnp.int32, (rows, LANES), 1)
    low_all = lane_all < LANES // 2
    one = jnp.ones((), jnp.bfloat16)
    kx, vx = [], []
    for sel in (low_all, jnp.logical_not(low_all)):
        kx.append(jnp.concatenate([jnp.where(sel, k, zero), kaug], axis=1))
        vx.append(jnp.concatenate([jnp.where(sel, v, zero), jnp.where(sel, one, zero)], axis=1))
    vx = jnp.concatenate(vx, axis=0)
    for start in range(0, rows, tq):
        lane = lax.broadcasted_iota(jnp.int32, (tq, LANES), 1)
        row = lax.broadcasted_iota(jnp.int32, (tq, LANES), 0) + start
        low = lane < LANES // 2
        qaug = jnp.where(type_marks(rows, half, lane, row), one, zero)
        q = (q_ref[0, start:start + tq].astype(jnp.float32) * scale).astype(jnp.bfloat16)
        qx = jnp.concatenate([q, qaug], axis=1)
        probs, peaks = [], []
        for a in (0, 1):
            s = nt(qx, kx[a])
            peak = jnp.max(s, axis=1, keepdims=True)
            probs.append(jnp.exp(s - peak).astype(jnp.bfloat16))
            peaks.append(peak)
        acc = nn(jnp.concatenate(probs, axis=1), vx)
        total = acc[:, LANES:]
        o_ref[0, start:start + tq] = (acc[:, :LANES] / total).astype(jnp.bfloat16)
        lse = jnp.where(low, peaks[0], peaks[1]) + jnp.log(total)
        first, second = lse[:, 0:1], lse[:, LANES // 2:LANES // 2 + 1]
        prev = jnp.where(pair == 0, 0.0, lse_ref[0, start:start + tq])
        head = lax.rem(lane, HEADS)
        inside = lane < 3 * HEADS
        kept = jnp.where(inside & (head == 2 * pair), first, prev)
        lse_ref[0, start:start + tq] = jnp.where(inside & (head == 2 * pair + 1), second, kept)


def attend(qkv, kaug, half, tq=320):
    row_count, rows, cols = qkv.shape
    width = cols // 3
    pairs = width // LANES
    scale = (width // HEADS) ** (-0.5)
    spec = lambda off: pl.BlockSpec((1, rows, LANES), lambda r, p: (r, 0, off + p))
    return pl.pallas_call(
        functools.partial(attend_step, half, scale, tq),
        grid=(row_count, pairs),
        in_specs=[spec(0), spec(pairs), spec(2 * pairs), pl.BlockSpec((1, rows, LANES), lambda r, p: (r, 0, 0))],
        out_specs=[spec(0), pl.BlockSpec((1, rows, LANES), lambda r, p: (r, 0, 0))],
        out_shape=[
            jax.ShapeDtypeStruct((row_count, rows, width), jnp.bfloat16),
            jax.ShapeDtypeStruct((row_count, rows, LANES), jnp.float32),
        ],
        compiler_params=pltpu.CompilerParams(vmem_limit_bytes=48 * 1024 * 1024),
        name="attend",
    )(qkv, qkv, qkv, kaug)


def three_parts(values, lane):
    top = values.astype(jnp.bfloat16)
    rest = values - top.astype(jnp.float32)
    mid = rest.astype(jnp.bfloat16)
    low = (rest - mid.astype(jnp.float32)).astype(jnp.bfloat16)
    zero = jnp.zeros((), jnp.bfloat16)
    return jnp.where(lane < HEADS, top, jnp.where(lane < 2 * HEADS, mid, jnp.where(lane < 3 * HEADS, low, zero)))


def attend_back_step(half, scale, tk, q_ref, k_ref, v_ref, g_ref, lse_ref, delta_ref, *refs):
    attend_back_kernel(
        half, scale, tk, pl.program_id(1), q_ref, k_ref, v_ref, g_ref[0], lse_ref[0], delta_ref[0], *refs
    )


def attend_back_kernel(half, scale, tk, pair, q_ref, k_ref, v_ref, g, lse, delta, kaug_ref, dq_ref, dk_ref, dv_ref):
    rows = q_ref.shape[1]
    zero = jnp.zeros((), jnp.bfloat16)
    one = jnp.ones((), jnp.bfloat16)
    lane = lax.broadcasted_iota(jnp.int32, (rows, LANES), 1)
    row = lax.broadcasted_iota(jnp.int32, (rows, LANES), 0)
    low = lane < LANES // 2
    q = (q_ref[0].astype(jnp.float32) * scale).astype(jnp.bfloat16)
    qaug = jnp.where(type_marks(rows, half, lane, row), one, three_parts(lse, lane))
    gaug = three_parts(delta, lane)
    qx = jnp.concatenate([q, qaug], axis=1)
    gx = jnp.concatenate([g, gaug], axis=1)
    sels = (low, jnp.logical_not(low))
    qh = jnp.concatenate([jnp.where(sel, q, zero) for sel in sels], axis=0)
    gh = jnp.concatenate([jnp.where(sel, g, zero) for sel in sels], axis=0)
    dq = None
    for start in range(0, rows, tk):
        lane_k = lax.broadcasted_iota(jnp.int32, (tk, LANES), 1)
        low_k = lane_k < LANES // 2
        head = lax.rem(lane_k, HEADS)
        inside = lane_k < 3 * HEADS
        k = k_ref[0, start:start + tk]
        v = v_ref[0, start:start + tk]
        kaug = kaug_ref[0, start:start + tk]
        probs, grads, keys = [], [], []
        for a, sel in ((0, low_k), (1, jnp.logical_not(low_k))):
            marks = inside & (head == 2 * pair + a)
            keys.append(jnp.where(sel, k, zero))
            kx = jnp.concatenate([keys[a], jnp.where(marks, -one, kaug)], axis=1)
            vx = jnp.concatenate([jnp.where(sel, v, zero), jnp.where(marks, -one, zero)], axis=1)
            p = jnp.exp(nt(kx, qx))
            grads.append((p * nt(vx, gx)).astype(jnp.bfloat16))
            probs.append(p.astype(jnp.bfloat16))
        dv_ref[0, start:start + tk] = nn(jnp.concatenate(probs, axis=1), gh).astype(jnp.bfloat16)
        dk_ref[0, start:start + tk] = nn(jnp.concatenate(grads, axis=1), qh).astype(jnp.bfloat16)
        part = tn(jnp.concatenate(grads, axis=0), jnp.concatenate(keys, axis=0))
        dq = part if dq is None else dq + part
    dq_ref[0] = (dq * scale).astype(jnp.bfloat16)


def attend_back(qkv, grad, lse, delta, kaug, half, tk=320):
    row_count, rows, cols = qkv.shape
    width = cols // 3
    pairs = width // LANES
    scale = (width // HEADS) ** (-0.5)
    spec = lambda off: pl.BlockSpec((1, rows, LANES), lambda r, p: (r, 0, off + p))
    whole = pl.BlockSpec((1, rows, LANES), lambda r, p: (r, 0, 0))
    out = jax.ShapeDtypeStruct((row_count, rows, width), jnp.bfloat16)
    return pl.pallas_call(
        functools.partial(attend_back_step, half, scale, tk),
        grid=(row_count, pairs),
        in_specs=[spec(0), spec(pairs), spec(2 * pairs), spec(0), whole, whole, whole],
        out_specs=[spec(0)] * 3,
        out_shape=[out] * 3,
        compiler_params=pltpu.CompilerParams(vmem_limit_bytes=48 * 1024 * 1024),
        name="attend_back",
    )(qkv, qkv, qkv, grad, lse, delta, kaug)


EPS = 1e-05
MESH_ID = pl.DeviceIdType.MESH


def spread_kernel(count, sizes, same, *refs):
    ins, outs = refs[:sizes], refs[sizes:2 * sizes]
    send, recv, local = refs[2 * sizes:]
    me = lax.axis_index("seq")
    barrier = pltpu.get_barrier_semaphore()
    for step in range(1, count):
        pl.semaphore_signal(
            barrier, inc=1, device_id={"seq": lax.rem(me + step, count)}, device_id_type=MESH_ID
        )
    pl.semaphore_wait(barrier, count - 1)
    own = []
    for n in range(sizes):
        copy = pltpu.make_async_copy(ins[n] if same else ins[n].at[me], outs[n].at[me], local.at[n])
        copy.start()
        own.append(copy)
    copies = []
    for step in range(1, count):
        peer = lax.rem(me + step, count)
        for n in range(sizes):
            copy = pltpu.make_async_remote_copy(
                src_ref=ins[n] if same else ins[n].at[peer],
                dst_ref=outs[n].at[me],
                send_sem=send.at[n, step],
                recv_sem=recv.at[n, step],
                device_id={"seq": peer},
                device_id_type=MESH_ID,
            )
            copy.start()
            copies.append(copy)
    for copy in own:
        copy.wait()
    for copy in copies:
        copy.wait()


def spread(arrays, count, same, collective_id):
    sizes = len(arrays)
    shapes = [(count,) + a.shape if same else a.shape for a in arrays]
    vmem = pl.BlockSpec(memory_space=pltpu.VMEM)
    return pl.pallas_call(
        functools.partial(spread_kernel, count, sizes, same),
        in_specs=[vmem] * sizes,
        out_specs=[vmem] * sizes,
        out_shape=[jax.ShapeDtypeStruct(s, a.dtype) for s, a in zip(shapes, arrays)],
        scratch_shapes=[
            pltpu.SemaphoreType.DMA((sizes, count)),
            pltpu.SemaphoreType.DMA((sizes, count)),
            pltpu.SemaphoreType.DMA((sizes,)),
        ],
        compiler_params=pltpu.CompilerParams(
            collective_id=collective_id, has_side_effects=True, vmem_limit_bytes=32 * 1024 * 1024
        ),
        name="spread",
    )(*arrays)


SEQ_BITS = (("z1", 4), ("z0", 2), ("x", 1))
BATCH_BITS = (("y", 2), ("c", 1))


class Place:
    def __init__(self):
        self.spot, self.step = {}, {}
        for name, bits in (("seq", SEQ_BITS), ("batch", BATCH_BITS)):
            index = lax.axis_index(name)
            for axis, weight in bits:
                bit = lax.rem(lax.div(index, weight), 2)
                self.spot[axis] = bit
                self.step[axis] = {name: index + weight * (1 - 2 * bit)}

    def __getitem__(self, axis):
        return self.spot[axis]

    def partner(self, axis):
        return self.step[axis]

    def greet(self, others=()):
        barrier = pltpu.get_barrier_semaphore()
        peers = list(self.step.values()) + list(others)
        for to in peers:
            pl.semaphore_signal(barrier, inc=1, device_id=to, device_id_type=MESH_ID)
        pl.semaphore_wait(barrier, len(peers))


def remote(src, dst, send, recv, to):
    return pltpu.make_async_remote_copy(
        src_ref=src, dst_ref=dst, send_sem=send, recv_sem=recv, device_id=to, device_id_type=MESH_ID
    )


class Halve:
    def __init__(self, place, own, lanes, order, bufs, send, recv, first, stages=None):
        self.place, self.own, self.order = place, own, order
        self.lanes = pl.ds(*lanes)
        self.half = own.shape[3] // 2
        stages = range(len(order)) if stages is None else stages
        self.bufs = dict(zip(stages, bufs))
        self.send, self.recv, self.first = send, recv, first

    def copy(self, n):
        at = self.first + n
        return remote(
            self.own.at[self.region(n, False)], self.bufs[n], self.send.at[at], self.recv.at[at],
            self.place.partner(self.order[n]),
        )

    @staticmethod
    def buffers(rows, width, order, stages=None, dtype=jnp.bfloat16):
        shapes = []
        for n in range(len(order)) if stages is None else stages:
            left = [axis for axis, _ in SEQ_BITS if axis not in order[:n + 1]]
            shapes.append((2,) * len(left) + (rows // 2 if "y" in order[:n + 1] else rows, width))
        return [pltpu.VMEM(shape, dtype) for shape in shapes]

    def region(self, n, mine, free=(), piece=None):
        free = list(free)
        at = []
        for axis, _ in SEQ_BITS:
            if axis in self.order[:n]:
                at.append(self.place[axis])
            elif axis == self.order[n]:
                at.append(self.place[axis] if mine else 1 - self.place[axis])
            else:
                at.append(free.pop(0) if free else slice(None))
        first, count = 0, self.own.shape[3]
        if "y" in self.order[:n + 1]:
            y = self.place["y"]
            y = y if mine or self.order[n] != "y" else 1 - y
            first, count = y * self.half, self.half
        if piece is not None:
            first, count = first + piece[0], piece[1]
        rows = pl.ds(pl.multiple_of(first, 16), count)
        return (*at, rows, self.lanes)

    def start(self, n):
        self.copy(n).start()

    def sent(self):
        for n in self.bufs:
            self.copy(n).wait_send()

    def finish(self, n):
        self.copy(n).wait_recv()
        buf = self.bufs[n]
        dims = len(buf.shape) - 2
        count = buf.shape[-2]
        piece = math.gcd(count, 48)
        pieces = count // piece

        def add(i, carry):
            block, row = lax.div(i, pieces), lax.rem(i, pieces) * piece
            free = [lax.rem(lax.div(block, 2 ** (dims - 1 - d)), 2) for d in range(dims)]
            at = self.region(n, True, free, (row, piece))
            self.own[at] = self.own[at] + buf[(*free, pl.ds(pl.multiple_of(row, 16), piece), slice(None))]
            return carry

        lax.fori_loop(0, 2 ** dims * pieces, add, 0)


class Gather:
    order = ("z1", "z0", "x")

    def __init__(self, place, buf, send, recv):
        self.place, self.buf, self.send, self.recv = place, buf, send, recv

    def copy(self, n):
        done = self.order[:n]
        at = (slice(None), *(slice(None) if axis in done else self.place[axis] for axis, _ in SEQ_BITS))
        block = self.buf.at[at]
        return remote(block, block, self.send.at[n], self.recv.at[n], self.place.partner(self.order[n]))

    def stage(self, n):
        if n > 0:
            self.copy(n - 1).wait_recv()
        if n < 3:
            self.copy(n).start()

    def finish(self):
        for n in range(3):
            self.copy(n).wait_send()


PARTS = (
    ((0, 256), ("x", "y", "z0", "z1")),
    ((256, 384), ("y", "x", "z0", "z1")),
    ((640, 128), ("z0", "z1", "x", "y")),
)


class Fold:
    EARLY, LATE = (0, 1), (2, 3)

    def __init__(self, place, pieces, refs, source=None, stages=(0, 1, 2, 3)):
        self.place = place
        c, y = place["c"], place["y"]
        if stages == self.LATE:
            self.own, self.done, send, recv, *bufs = refs
            self.got = local = None
        elif source is None:
            self.own, self.done, *refs = refs
        else:
            self.own, self.done = source.at[:, :, :, c], None
        if stages != self.LATE:
            self.got, send, recv, local, *bufs = refs
        own, got, done = self.own, self.got, self.done
        rows = own.shape[3]
        half = rows // 2
        self.mine = pl.ds(pl.multiple_of(y * half, 16), half)
        self.pieces, self.source, self.done = pieces, source, done
        self.sems = send, recv, local
        first = 1 if source is not None else len(pieces)
        self.first = first + 12
        self.parts = []
        for n, (lanes, order) in enumerate(PARTS):
            own_bufs = bufs[len(stages) * n:len(stages) * (n + 1)]
            self.parts.append(Halve(place, own, lanes, order, own_bufs, send, recv, first + 4 * n, stages))

    def keep(self):
        at, copies = 0, []
        if self.source is None:
            for n, (take, count) in enumerate(self.pieces):
                spot = self.own.at[:, :, :, pl.ds(at, count)]
                copies.append(pltpu.make_async_copy(take(self.place["c"]), spot, self.sems[2].at[n]))
                at += count
        return copies

    def core(self):
        send, recv, _ = self.sems
        to, c = self.place.partner("c"), 1 - self.place["c"]
        if self.source is not None:
            return [remote(self.source.at[:, :, :, c], self.got, send.at[0], recv.at[0], to)]
        at, copies = 0, []
        for n, (take, count) in enumerate(self.pieces):
            copies.append(remote(take(c), self.got.at[:, :, :, pl.ds(at, count)], send.at[n], recv.at[n], to))
            at += count
        return copies

    def across(self):
        send, recv, _ = self.sems
        spot = self.done.at[self.place["c"], self.mine]
        return remote(spot, spot, send.at[self.first], recv.at[self.first], self.place.partner("y"))

    def back(self):
        send, recv, _ = self.sems
        spot = self.done.at[self.place["c"]]
        return remote(spot, spot, send.at[self.first + 1], recv.at[self.first + 1], self.place.partner("c"))

    @staticmethod
    def scratch(rows, width, pieces, sourced=False, stages=(0, 1, 2, 3)):
        vmem = lambda *shape: pltpu.VMEM(shape, jnp.bfloat16)
        refs = [] if sourced else [vmem(2, 2, 2, rows, width), vmem(2, rows, width)]
        if stages != Fold.LATE:
            refs.append(vmem(2, 2, 2, rows, width))
        refs += [
            pltpu.SemaphoreType.DMA((pieces + 14,)),
            pltpu.SemaphoreType.DMA((pieces + 14,)),
        ]
        if stages != Fold.LATE:
            refs.append(pltpu.SemaphoreType.DMA((pieces,)))
        for (_, count), order in PARTS:
            refs += Halve.buffers(rows, count, order, stages)
        return refs

    def stage(self, n):
        if n == 0:
            for copy in self.keep() + self.core():
                copy.start()
        elif n == 1:
            for copy in self.keep():
                copy.wait()
            for copy in self.core():
                copy.wait_recv()

            piece = math.gcd(self.got.shape[3], 48)
            pieces = self.got.shape[3] // piece

            def add(i, carry):
                block = lax.div(i, pieces)
                rows = pl.ds(pl.multiple_of(lax.rem(i, pieces) * piece, 16), piece)
                at = (*(lax.rem(lax.div(block, w), 2) for _, w in SEQ_BITS), rows)
                self.own[at] = self.own[at] + self.got[at]
                return carry

            lax.fori_loop(0, 8 * pieces, add, 0)
            for part in self.parts:
                part.start(0)
        elif n < 5:
            for part in self.parts:
                part.finish(n - 2)
                part.start(n - 1)
        elif n == 5:
            for part in self.parts:
                part.finish(3)
            at = tuple(self.place[axis] for axis, _ in SEQ_BITS)
            self.done[self.place["c"], self.mine] = self.own[(*at, self.mine)]
            self.across().start()
        elif n == 6:
            self.across().wait_recv()
            self.back().start()
        else:
            self.back().wait_recv()

    def held(self):
        z1, z0, x = (self.place[axis] for axis, _ in SEQ_BITS)
        a, b, c = (lanes[1] for lanes, _ in PARTS)
        return (slice(None), slice(None), x, self.mine, pl.ds(0, a + b)), (
            z1, z0, slice(None), slice(None), pl.ds(a + b, c)
        )

    def resume(self):
        for part in self.parts:
            part.start(2)

    def finish(self):
        copies = self.core()
        if self.done is not None:
            copies = copies + [self.across(), self.back()]
        for copy in copies:
            copy.wait_send()
        for part in self.parts:
            part.sent()


class Sum:
    order = ("c", "x", "y", "z0", "z1")

    def __init__(self, place, value, got, send, recv):
        self.place, self.value, self.got, self.send, self.recv = place, value, got, send, recv

    def copy(self, n):
        to = self.place.partner(self.order[n])
        return remote(self.value.at[n], self.got.at[n], self.send.at[n], self.recv.at[n], to)

    def stage(self, n):
        if n > 0:
            self.copy(n - 1).wait_recv()
            self.value[n] = self.value[n - 1] + self.got[n - 1]
        if n < 5:
            self.copy(n).start()

    def finish(self):
        for n in range(5):
            self.copy(n).wait_send()


def share_views(a, count):
    *lead, rows, width = a.shape
    return a.reshape(*lead, 2, 2, 2, rows // count, width)


def half_views(a, count):
    *lead, rows, width = a.shape
    return a.reshape(*lead, 2, 2, 2, 2, rows // (2 * count), width)


def fetch(sources, targets, sems, first=0):
    return [pltpu.make_async_copy(s, t, sems.at[first + n]) for n, (s, t) in enumerate(zip(sources, targets))]


def finish_kernel(
    inner, out, queries, keys, outer, small, layer, igrad, gout, ggrad,
    inner_o, outer_o, out_o, qkv_o, fg_o, fs_o, sg_o, ss_o, bias_o, layer_o, igrad_o, gout_o, ggrad_o, sems,
):
    f32 = jnp.float32
    me = lax.axis_index("seq")
    copies = fetch((layer, igrad, gout, ggrad), (layer_o, igrad_o, gout_o, ggrad_o), sems)
    begin(copies)
    width = outer_o.shape[1]
    part = inner_o.shape[0]
    strips = inner.shape[1] // part
    half = outer.shape[1]
    for c in range(2):
        for j in range(strips):
            inner_o[:, pl.ds((c * strips + j) * width, width)] = inner[c, pl.ds(j * part, part)].astype(f32)
        outer_o[pl.ds(c * half, half)] = outer[c].astype(f32)
        spot = pl.ds(c * part // 2, part // 2)
        first, second = pl.ds(0, part // 2), pl.ds(part // 2, part // 2)
        out_o[spot] = out[c, first].astype(f32)
        for j, (ref, lines) in enumerate(((queries, first), (keys, first), (keys, second))):
            qkv_o[spot, pl.ds(j * width, width)] = ref[c, lines].astype(f32)
    values = small[...]
    turned = pltpu.roll(values, lax.rem(width - part * me, width), 1)
    for n, ref in enumerate((fg_o, fs_o, sg_o, ss_o)):
        ref[...] = turned[n:n + 1, :part]
    wide = bias_o.shape[1]
    per = width // wide
    row = small[pl.ds(4 + lax.div(me, per), 1)]
    spots = [row[:, n * wide:(n + 1) * wide] for n in range(per)]
    chosen = spots[0]
    for n in range(1, per):
        chosen = jnp.where(lax.rem(me, per) == n, spots[n], chosen)
    bias_o[...] = chosen
    for copy in copies:
        copy.wait()


def finish(inner, out, queries, keys, outer, small, layer, igrad, gout, ggrad):
    width = small.shape[1]
    part = keys.shape[1]
    bias = 2 * outer.shape[1]
    vmem, hbm = pl.BlockSpec(memory_space=pltpu.VMEM), pl.BlockSpec(memory_space=pl.ANY)
    shapes = [(part, 2 * inner.shape[1] // part * width), (bias, width), (part, width), (part, 3 * width)]
    shapes += [(1, part)] * 4 + [(1, bias)]
    moved = [layer, igrad, gout, ggrad]
    return pl.pallas_call(
        finish_kernel,
        in_specs=[vmem] * 10,
        out_specs=[vmem] * 9 + [hbm] * 4,
        out_shape=[jax.ShapeDtypeStruct(s, jnp.float32) for s in shapes]
        + [jax.ShapeDtypeStruct(a.shape, a.dtype) for a in moved],
        scratch_shapes=[pltpu.SemaphoreType.DMA((4,))],
        compiler_params=pltpu.CompilerParams(vmem_limit_bytes=60 * 1024 * 1024),
        name="finish",
    )(inner, out, queries, keys, outer, small, *moved)


def begin(copies):
    for copy in copies:
        copy.start()


def sum_rows(values):
    rows, width = values.shape
    return jnp.sum(values.reshape(rows // 8, 8, width), axis=0)


def ticks(plan, folds, step):
    for t, todo in plan.items():

        @pl.when(step == t)
        def _():
            for f, n in todo:
                folds[f].stage(n)


TILE_AT = ((6, 0, 1), (7, 0, 0), (15, 1, 1), (19, 1, 0))
GLOBALS_AT, STRIPS_AT, LAST = 14, 16, 20
REAR_TICKS = {
    0: ((0, 0), (4, 0)),
    3: ((0, 1),),
    4: ((3, 4), (4, 1)),
    8: ((3, 5),),
    9: ((0, 2), (4, 2)),
    10: ((3, 6),),
    12: ((3, 7), (4, 3)),
    13: ((0, 3),),
    15: ((4, 4),),
    17: ((0, 4), (1, 0)),
    18: ((4, 5),),
    19: ((0, 5), (1, 1), (2, 0)),
}
REAR_END = (
    (7, 0), (5, 1), (2, 1), (7, 1), (1, 2), (4, 6), (0, 6), (5, 2), (6, 0), (2, 2), (7, 2), (1, 3), (0, 7), (4, 7), (6, 1),
    (2, 3), (7, 3), (1, 4), (6, 2), (2, 4), (7, 4), (1, 5), (6, 3), (2, 5), (7, 5), (1, 6), (2, 6), (1, 7), (2, 7),
)
SPREAD_AT = 18
LONE = 64


def rear_kernel(
    half, scale, pairs, fold_refs,
    q_ref, k_ref, v_ref, g_ref, lse_ref, delta_ref, kaug_ref,
    x_ref, next_x_ref, res_ref, gg_in, glse_in, gdelta_in, outer_ab, outer_c, gres_in, globals_in, weight_in, gain_in, vectors_in,
    normed_in, inner, out,
    igrad_o, ggrad_o, inner_o, out_o, queries_o, keys_o, outer_o, small_o,
    gg_ref, glse_ref, gdelta_ref, gres_ref, globals_ref, weight_ref, gain_ref, vectors_ref, normed_ref,
    dqkv, gfirst, sums, qkv_src, grads, ggrad, value, got,
    send, recv, local, *scratch,
):
    step = pl.program_id(0)
    place = Place()
    me = lax.axis_index("seq")
    count = lax.axis_size("seq")
    row_count, rows, cols = dqkv.shape
    block_len = 2 * half
    width = cols // 3
    share = gres_ref.shape[1]
    attn = row_count * pairs
    strips = inner.shape[0] // 2
    part_rows = inner.shape[4]
    half_part = part_rows // 2
    sources = (
        [(lambda c, j=j: inner.at[c * strips + j], part_rows) for j in range(strips)],
        [(lambda c: qkv_src.at[0, :, :, :, c], half_part)],
        [(lambda c, j=j: qkv_src.at[j, :, :, :, c], half_part) for j in (1, 2)],
    )
    folds, at = [], 0
    for pieces, size in zip(sources, fold_refs[:3]):
        folds.append(Fold(place, pieces, scratch[at:at + size]))
        at += size
    folds.append(Fold(place, (), scratch[at:at + fold_refs[3]], None, Fold.LATE))
    at += fold_refs[3]
    folds.append(Fold(place, [(lambda c: out.at[:, :, :, c], half_part)], scratch[at:at + fold_refs[4]]))
    at += fold_refs[4]
    spread = Halve(place, gfirst, (0, width), ("x", "z0", "z1"), scratch[at:], send.at[0], recv.at[0], 0)
    gather = Gather(place, ggrad, send.at[row_count], recv.at[row_count])
    small = Sum(place, value, got, send.at[row_count + 1], recv.at[row_count + 1])
    following = {"seq": lax.rem(me + 1, count)}
    before = {"seq": lax.rem(me + count - 1, count)}
    held = folds[3].held()
    early = lambda: fetch(
        (gg_in, glse_in, gdelta_in, outer_ab, outer_c),
        (gg_ref, glse_ref, gdelta_ref, folds[3].own.at[held[0]], folds[3].own.at[held[1]]), local,
    )
    later = lambda: fetch(
        (gres_in, globals_in, weight_in, gain_in, vectors_in),
        (gres_ref, globals_ref, weight_ref, gain_ref.at[0], vectors_ref), local, 5,
    )
    latest = lambda: fetch((normed_in,), (normed_ref,), local, 11)

    def home(r):
        sems = send.at[row_count + 2, r], recv.at[row_count + 2, r]
        return remote(grads.at[1, r], igrad_o.at[r, pl.ds(0, half)], *sems, following)

    def keep(r):
        return pltpu.make_async_copy(grads.at[0, r], igrad_o.at[r, pl.ds(half, half)], local.at[12 + r])

    @pl.when(step == 0)
    def _():
        begin(early() + later() + latest())
        place.greet([following, before])
        sums[...] = jnp.zeros_like(sums)
        for copy in early():
            copy.wait()
        folds[3].resume()

    ticks(REAR_TICKS, folds, step)

    @pl.when((step < pairs) | ((step >= pairs + 2) & (step < attn + 2)))
    def _():
        r = jnp.where(step < pairs, 0, 1)
        p = step - r * (pairs + 2)
        spots = [pl.ds(pl.multiple_of(j * width + p * LANES, LANES), LANES) for j in range(3)]
        lane = pl.ds(pl.multiple_of(p * LANES, LANES), LANES)
        wide = lambda a, b: jnp.concatenate([a, b.reshape(rows - block_len, LANES)], axis=0)
        attend_back_kernel(
            half, scale, 320, p, q_ref, k_ref, v_ref, wide(g_ref[...], gg_ref[r, :, :, :, :, lane]),
            wide(lse_ref[0], glse_ref[r]), wide(delta_ref[...], gdelta_ref[r]), kaug_ref,
            *(dqkv.at[pl.ds(r, 1), :, spot] for spot in spots),
        )

    def move_spread(n):
        spread.finish(n)
        if n < 2:
            spread.start(n + 1)

    @pl.when(step == SPREAD_AT)
    def _():
        move_spread(0)

    @pl.when(step == TILE_AT[0][0])
    def _():
        for copy in later():
            copy.wait()

    @pl.when(step == STRIPS_AT)
    def _():
        for copy in latest():
            copy.wait()


    strip_at = step - STRIPS_AT

    @pl.when((strip_at >= 0) & (strip_at < 3))
    def _():
        strip = pl.ds(pl.multiple_of(strip_at * width, width), width)
        total = tn(normed_ref[0], dqkv[0, :, strip])
        for r in range(1, row_count):
            total = total + tn(normed_ref[r], dqkv[r, :, strip])
        qkv_src[strip_at] = total.astype(jnp.bfloat16).reshape(qkv_src.shape[1:])

    def stats(x):
        centred = x - jnp.mean(x, axis=-1, keepdims=True)
        inv = lax.rsqrt(jnp.mean(centred * centred, axis=-1, keepdims=True) + EPS)
        return centred * inv, inv

    def add_sums(first, n):
        sums[0] += sum_rows(first * n)
        sums[1] += sum_rows(first)

    def through(first, n, inv):
        eg = first * gain_ref[...]
        return (eg - jnp.mean(eg, axis=-1, keepdims=True) - n * jnp.mean(eg * n, axis=-1, keepdims=True)) * inv

    @pl.when(step == GLOBALS_AT)
    def _():
        own = pl.ds(block_len, rows - block_len)
        partial = jnp.concatenate([dqkv[r, own] for r in range(row_count)], axis=0)
        first = nt(partial, weight_ref[...])
        n, _ = stats(globals_ref[...].astype(jnp.float32).reshape(first.shape))
        add_sums(first, n)
        first = first.astype(jnp.bfloat16).reshape(row_count, 2, 2, 2, share, width)
        for r in range(row_count):
            gfirst[:, :, :, pl.ds(r * share, share)] = first[r]
        spread.start(0)

    @pl.when(functools.reduce(jnp.logical_or, [step == t for t, _, _ in TILE_AT]))
    def _():
        r = jnp.where(step < pairs + 2, 0, 1)
        h = jnp.where((step == TILE_AT[0][0]) | (step == TILE_AT[2][0]), 1, 0)
        first = nt(dqkv[r, pl.ds(pl.multiple_of(h * half, half), half)], weight_ref[...])
        n, inv = stats(jnp.where(h == 0, x_ref[0].astype(jnp.float32), next_x_ref[0].astype(jnp.float32)))
        add_sums(first, n)
        grads[h, r] = (res_ref[...] + through(first, n, inv)).astype(jnp.bfloat16)

    for t, r, h in TILE_AT:

        @pl.when(step == t)
        def _():
            (home if h else keep)(r).start()

    def own_globals():
        own_rows = row_count * share
        at = tuple(place[axis] for axis, _ in SEQ_BITS)
        held = pl.ds(pl.multiple_of(share * me, 16), share)
        n, inv = stats(globals_ref[:, held].astype(jnp.float32).reshape(own_rows, width))
        grad = gres_ref[...].reshape(own_rows, width) + through(gfirst[at].astype(jnp.float32), n, inv)
        ggrad[(slice(None), *at)] = grad.astype(jnp.bfloat16).reshape(row_count, share, width)

    @pl.when(step == LAST)
    def _():
        lines = [jnp.sum(sums[n], axis=0, keepdims=True) for n in range(2)]
        value[0] = jnp.concatenate(lines + [vectors_ref[...]])
        leaves = fetch(
            (folds[0].done, folds[4].done, folds[1].done, folds[2].done, folds[3].done, value.at[5], ggrad),
            (inner_o, out_o, queries_o, keys_o, outer_o, small_o, ggrad_o), local, 12 + row_count,
        )
        ready = {(0, 7): 0, (4, 7): 1, (1, 7): 2, (2, 7): 3, (3, 7): 4, (7, 5): 5, (6, 3): 6}
        leaves[4].start()
        for f, n in REAR_END:
            if f == 5:
                move_spread(n)
                if n == 2:
                    own_globals()
            elif f == 6:
                gather.stage(n)
            elif f == 7:
                small.stage(n)
            else:
                folds[f].stage(n)
            if (f, n) in ready:
                leaves[ready[f, n]].start()
        for fold in folds:
            fold.finish()
        gather.finish()
        small.finish()
        spread.sent()
        for r in range(row_count):
            keep(r).wait()
            home(r).wait()
        for copy in leaves:
            copy.wait()


def rear(
    qkv, grad, lse, delta, kaug, inputs, next_x, res_grad, global_grad, global_lse, global_delta, own_res, normed,
    globals_in, weight, gain, vectors, outer_ab, outer_c, inner, out, half, count,
):
    row_count, rows, cols = qkv.shape
    width = cols // 3
    pairs = width // LANES
    block_len = 2 * half
    global_count = rows - block_len
    share = global_count // count
    part = width // count
    scale = (width // HEADS) ** (-0.5)
    attn = row_count * pairs
    f32, bf16 = jnp.float32, jnp.bfloat16
    turn = lambda t: jnp.where(t < pairs, t, jnp.clip(t - 2, pairs, attn - 1))
    row_of = lambda t: turn(t) // pairs
    pair_of = lambda t: turn(t) % pairs
    spec = lambda off: pl.BlockSpec((1, rows, LANES), lambda t: (row_of(t), 0, off + pair_of(t)))
    whole = pl.BlockSpec((1, rows, LANES), lambda t: (row_of(t), 0, 0))

    def tile_of(t):
        (a, _, _), (b, _, _), (c, _, _), _ = TILE_AT
        return jnp.where(t <= a, 1, jnp.where(t <= b, 0, jnp.where(t <= c, 3, 2))), 0

    tile = pl.BlockSpec((half, width), tile_of)
    hbm = pl.BlockSpec(memory_space=pl.ANY)
    outs = [
        jax.ShapeDtypeStruct((row_count, block_len, width), bf16),
        jax.ShapeDtypeStruct((row_count, 2, 2, 2, share, width), bf16),
        jax.ShapeDtypeStruct((2, 2 * part, width), bf16),
        jax.ShapeDtypeStruct((2, LONE, width), bf16),
        jax.ShapeDtypeStruct((2, LONE, width), bf16),
        jax.ShapeDtypeStruct((2, part, width), bf16),
        jax.ShapeDtypeStruct((2, 2 * part, width), bf16),
        jax.ShapeDtypeStruct((8, width), f32),
    ]
    folds, sizes = [], []
    for size, pieces in ((2 * part, 2), (LONE, 1), (part, 2)):
        refs = Fold.scratch(size, width, pieces)
        folds += refs
        sizes.append(len(refs))
    for refs in (Fold.scratch(2 * part, width, 0, False, Fold.LATE), Fold.scratch(LONE, width, 1)):
        folds += refs
        sizes.append(len(refs))
    vmem = pltpu.VMEM
    kinds = 4 + row_count
    early = (global_grad, global_lse, global_delta)
    later = (own_res, globals_in, weight, gain, vectors, normed)
    return pl.pallas_call(
        functools.partial(rear_kernel, half, scale, pairs, tuple(sizes)),
        grid=(LAST + 1,),
        in_specs=[spec(0), spec(pairs), spec(2 * pairs)]
        + [pl.BlockSpec((block_len, LANES), lambda t: (row_of(t), pair_of(t)))]
        + [pl.BlockSpec((1, block_len, LANES), lambda t: (row_of(t), 0, 0))]
        + [pl.BlockSpec((block_len, LANES), lambda t: (row_of(t), 0)), whole]
        + [
            pl.BlockSpec((1, half, width), lambda t: (jnp.where(t <= TILE_AT[1][0], 0, 1), 1, 0)),
            pl.BlockSpec((1, half, width), lambda t: (jnp.where(t <= TILE_AT[0][0], 0, 1), 0, 0)),
            tile,
        ]
        + [hbm] * 13,
        out_specs=[hbm] * 8,
        out_shape=outs,
        scratch_shapes=[vmem(a.shape if a.ndim > 1 else (1, *a.shape), a.dtype) for a in early + later]
        + [
            vmem((row_count, rows, cols), bf16),
            vmem((2, 2, 2, row_count * share, width), bf16),
            vmem((2, 8, width), f32),
            vmem((3, 2, 2, 2, 2, part // 2, width), bf16),
            vmem((2, row_count, half, width), bf16),
            vmem((row_count, 2, 2, 2, share, width), bf16),
            vmem((6, 8, width), f32),
            vmem((5, 8, width), f32),
            pltpu.SemaphoreType.DMA((kinds, 5)),
            pltpu.SemaphoreType.DMA((kinds, 5)),
            pltpu.SemaphoreType.DMA((20 + row_count,)),
        ]
        + folds
        + Halve.buffers(row_count * share, width, ("x", "z0", "z1")),
        compiler_params=pltpu.CompilerParams(
            collective_id=9, has_side_effects=True, vmem_limit_bytes=64 * 1024 * 1024
        ),
        name="rear",
    )(
        qkv, qkv, qkv, grad, lse, delta, kaug, inputs, next_x, res_grad, *early, outer_ab, outer_c, *later,
        share_views(inner, count), half_views(out, count),
    )


def cdf_bell(v):
    bell = jnp.exp(-0.5 * v * v)
    t = 1.0 / (1.0 + (0.3275911 * 0.5 ** 0.5) * jnp.abs(v))
    poly = t * (
        0.127414796 + t * (-0.142248368 + t * (0.7107068705 + t * (-0.7265760135 + t * 0.5307027145)))
    )
    tail = poly * bell
    return jnp.where(v < 0, tail, 1.0 - tail), bell


MID_TICKS = {9: 0, 11: 1, 14: 2}
MID_GATHERS = {6: (0, 1), 8: (0, 2), 10: (0, 3), 11: (1, 1), 12: (1, 2), 13: (1, 3)}


def mid_kernel(
    half, fold_refs,
    lengths, x_ref, next_x_ref, mixed_ref, cot_ref, next_cot_ref, gain_in, shift_in, bias_in, out_in, inner_in, outer_in, gx_in, gcot_in,
    mixed_all, lse_all,
    layer_o, res_o, grad_o, delta_o, gres_o, gout_o, ggrad_o, glse_o, gdelta_o, inner_o, outer_ab_o, outer_c_o, out_o,
    vectors_o,
    gain_ref, shift_ref, bias_ref, out_w, inner_w, outer_w, gx_ref, gcot_ref, heads_ref,
    hidden, slope, normed, cot, att, proj, residual, outer_src, sums, bias_sums, layers,
    gout, ggrad, glse, gdelta, part_mixed, part_lse, send, recv, local, *scratch,
):
    f32, bf16 = jnp.float32, jnp.bfloat16
    step = pl.program_id(0)
    place = Place()
    me = lax.axis_index("seq")
    count = lax.axis_size("seq")
    row_count, share = gx_ref.shape[:2]
    block_len = 2 * half
    tokens = row_count * block_len
    own_rows = row_count * share
    width = gx_ref.shape[2]
    strips = inner_w.shape[1] // width
    tiles = 2 * row_count
    fold = Fold(place, None, scratch, outer_src, Fold.EARLY)
    held = pl.ds(pl.multiple_of(share * me, 16), share)
    following = {"seq": lax.rem(me + 1, count)}
    at = tuple(place[axis] for axis, _ in SEQ_BITS)

    def parts(m, to, r, n):
        rows = pl.ds(pl.multiple_of(block_len + share * to, 16), share)
        return (
            (mixed_all.at[r, rows], part_mixed.at[m, r]) if n == 0 else (lse_all.at[r, rows], part_lse.at[m, r])
        )

    def part_copies():
        copies = []
        for r in range(row_count):
            for n in range(2):
                for other in range(1, count):
                    to = lax.rem(me + other, count)
                    src, dst = parts(me, to, r, n)
                    sems = send.at[2 * r + n, other], recv.at[2 * r + n, other]
                    copies.append(remote(src, dst, *sems, {"seq": to}))
        return copies

    def part_own():
        return [
            pltpu.make_async_copy(*parts(me, me, r, n), local.at[2 * r + n]) for r in range(row_count) for n in range(2)
        ]

    base = 2 * row_count
    gathers = [
        Gather(place, buf, send.at[base + n], recv.at[base + n]) for n, buf in enumerate((gout, ggrad, glse, gdelta))
    ]
    leaves = lambda: fetch((gout, ggrad, glse, gdelta), (gout_o, ggrad_o, glse_o, gdelta_o), local, base)
    ends = base + 4

    def home(r):
        return remote(layers.at[1, r], layer_o.at[r, pl.ds(0, half)], send.at[ends, r], recv.at[ends, r], following)

    def keep(r):
        return pltpu.make_async_copy(layers.at[0, r], layer_o.at[r, pl.ds(half, half)], local.at[ends + r])

    loads = lambda: fetch(
        (gain_in, shift_in, bias_in, out_in, inner_in, outer_in, gx_in.at[:, held], gcot_in.at[:, held]),
        (gain_ref.at[0], shift_ref.at[0], bias_ref.at[0], out_w, inner_w, outer_w, gx_ref, gcot_ref), local, ends + row_count,
    )

    @pl.when(step == 0)
    def _():
        begin(loads())
        place.greet([{"seq": lax.rem(me + other, count)} for other in range(1, count)])
        begin(part_own() + part_copies())
        lane = lax.broadcasted_iota(jnp.int32, (width, LANES), 1)
        head = lax.div(lax.broadcasted_iota(jnp.int32, (width, LANES), 0), width // HEADS)
        chosen = jnp.where(lane < 3 * HEADS, lax.rem(lane, HEADS), -1) == head
        heads_ref[...] = jnp.where(chosen, 1.0, 0.0).astype(bf16)
        sums[...] = jnp.zeros_like(sums)
        bias_sums[...] = jnp.zeros_like(bias_sums)
        for copy in loads():
            copy.wait()

    def stats(values):
        centred = values - jnp.mean(values, axis=-1, keepdims=True)
        inv = lax.rsqrt(jnp.mean(centred * centred, axis=-1, keepdims=True) + EPS)
        return centred * inv, inv

    def forward(x, attended, rows, unroll=True):
        att[rows] = attended
        total = x.astype(f32) + nn(attended, out_w[...])
        residual[rows] = total
        n, _ = stats(total)
        second = (n * gain_ref[...] + shift_ref[...]).astype(bf16)
        normed[rows] = second

        def run(j, total):
            strip = pl.ds(pl.multiple_of(j * width, width), width)
            inner = nn(second, inner_w[:, strip]) + bias_ref[:, strip]
            cdf, bell = cdf_bell(inner)
            active = (inner * cdf).astype(bf16)
            hidden[rows, strip] = active
            slope[rows, strip] = (cdf + inner * bell * ((0.5 / math.pi) ** 0.5)).astype(bf16)
            return total + nn(active, outer_w[strip, :])

        return lax.fori_loop(0, strips, run, total, unroll=unroll)

    def backward(cotangent, rows, unroll=True):
        def run(j, total):
            strip = pl.ds(pl.multiple_of(j * width, width), width)
            grad = (nt(cotangent, outer_w[strip, :]) * slope[rows, strip].astype(f32)).astype(bf16)
            slope[rows, strip] = grad
            bias_sums[j] += sum_rows(grad.astype(f32))
            return total + nt(grad, inner_w[:, strip])

        second_grad = lax.fori_loop(0, strips, run, jnp.zeros(cotangent.shape, f32), unroll=unroll)
        n, inv = stats(residual[rows])
        eg = second_grad * gain_ref[...]
        through = (eg - jnp.mean(eg, axis=-1, keepdims=True) - n * jnp.mean(eg * n, axis=-1, keepdims=True)) * inv
        sums[0] += sum_rows(second_grad * n)
        sums[1] += sum_rows(second_grad)
        res = cotangent.astype(f32) + through
        projected = res.astype(bf16)
        proj[rows] = projected
        grad = nt(projected, out_w[...]).astype(bf16)
        product = grad.astype(f32) * att[rows].astype(f32)
        top = product.astype(bf16)
        rest = (product - top.astype(f32)).astype(bf16)
        return res, grad, nn(top, heads_ref[...]) + nn(rest, heads_ref[...])

    @pl.when(step < tiles)
    def _():
        r, h = lax.rem(step, row_count), 1 - lax.div(step, row_count)
        rows = pl.ds(pl.multiple_of((2 * r + h) * half, half), half)
        owner = lax.rem(me + h, count)
        spot = owner * block_len + (1 - h) * half + lax.broadcasted_iota(jnp.int32, (half, width), 0)
        valid = spot < lengths[r]
        pick = lambda a, b: jnp.where(h == 0, a[0].astype(f32), b[0].astype(f32))
        cot[rows] = jnp.where(valid, pick(cot_ref, next_cot_ref), 0.0).astype(bf16)
        final = forward(pick(x_ref, next_x_ref), mixed_ref[0], rows)
        layers[h, r] = jnp.where(valid, final, 0.0).astype(bf16)

    back = step - (tiles + 2 + strips)

    @pl.when((back >= 0) & (back < tiles))
    def _():
        r, h = lax.rem(back, row_count), 1 - lax.div(back, row_count)
        rows = pl.ds(pl.multiple_of((2 * r + h) * half, half), half)
        res, grad, delta = backward(cot[rows], rows)
        res_o[...] = res
        grad_o[...] = grad
        delta_o[...] = delta

    for r in range(row_count):

        @pl.when(step == r)
        def _():
            home(r).start()

        @pl.when(step == row_count + r)
        def _():
            keep(r).start()

    last = pl.ds(tokens, own_rows)

    @pl.when(step == tiles)
    def _():
        for copy in part_own():
            copy.wait()
        for copy in part_copies():
            copy.wait_recv()
        peak = jnp.max(part_lse[...], axis=0)
        shares = jnp.exp(part_lse[...] - peak)
        total = jnp.sum(shares, axis=0)
        lse = peak + jnp.log(total)
        glse[(slice(None), *at)] = lse
        shares = (shares / total).reshape(count * own_rows, LANES)
        lane = lax.broadcasted_iota(jnp.int32, shares.shape, 1)
        shares = jnp.where(lane < HEADS, shares, 0.0)
        top = shares.astype(bf16)
        rest = (shares - top.astype(f32)).astype(bf16)
        wide = nt(top, heads_ref[...]) + nt(rest, heads_ref[...])
        mixed = wide * part_mixed[...].reshape(count * own_rows, width).astype(f32)
        mixed = jnp.sum(mixed.reshape(count, own_rows, width), axis=0).astype(bf16)
        cot[last] = gcot_ref[...].reshape(own_rows, width)
        final = forward(gx_ref[...].reshape(own_rows, width), mixed, last, False)
        gout[(slice(None), *at)] = final.astype(bf16).reshape(row_count, share, width)
        gathers[0].stage(0)

    strip_at = step - (tiles + 1)

    @pl.when((strip_at >= 0) & (strip_at < strips))
    def _():
        strip = pl.ds(pl.multiple_of(strip_at * width, width), width)
        grad = tn(hidden[:, strip], cot[...]).astype(bf16)
        outer_src[lax.div(strip_at, 2), lax.rem(strip_at, 2)] = grad.reshape(outer_src.shape[2:])

    for t, (kind, n) in MID_GATHERS.items():

        @pl.when(step == t)
        def _():
            chosen = range(1, 4) if kind else range(1)
            for g in chosen:
                gathers[g].stage(n)
                if n == 3:
                    leaves()[g].start()

    for t, n in MID_TICKS.items():

        @pl.when(step == t)
        def _():
            fold.stage(n)

    after = 2 * tiles + 1 + strips

    @pl.when(step == tiles + 1 + strips)
    def _():
        res, grad, delta = backward(cot[last], last, False)
        gres_o[...] = res.reshape(row_count, share, width)
        ggrad[(slice(None), *at)] = grad.reshape(row_count, share, width)
        gdelta[(slice(None), *at)] = delta.reshape(row_count, share, LANES)
        for gather in gathers[1:]:
            gather.stage(0)

    inner_at = step - (after + 1)

    @pl.when((inner_at >= 0) & (inner_at < strips))
    def _():
        strip = pl.ds(pl.multiple_of(inner_at * width, width), width)
        inner_o[0] = tn(normed[...], slope[:, strip]).astype(bf16)

    @pl.when(step == after + 1 + strips)
    def _():
        out_o[...] = tn(att[...], proj[...]).astype(bf16)
        lines = [jnp.sum(sums[n], axis=0, keepdims=True) for n in range(2)]
        lines += [jnp.sum(bias_sums[n], axis=0, keepdims=True) for n in range(strips)]
        vectors_o[...] = jnp.concatenate(lines)
        for part in fold.parts:
            part.finish(1)
        first, second = fold.held()
        outer_ab_o[...] = fold.own[first]
        outer_c_o[...] = fold.own[second]
        fold.finish()
        for gather in gathers:
            gather.finish()
        for copy in part_copies():
            copy.wait_send()
        for r in range(row_count):
            keep(r).wait()
            home(r).wait()
        for copy in leaves():
            copy.wait()


def mid(
    lengths, inputs, next_x, mixed, lse, cotangent, next_cot, globals_in, global_cot, out_weight, inner_weight, outer_weight, bias, gain, shift,
    half, count,
):
    f32, bf16 = jnp.float32, jnp.bfloat16
    row_count, rows, width = mixed.shape
    block_len = 2 * half
    share = (rows - block_len) // count
    own_rows = row_count * share
    inner_width = inner_weight.shape[1]
    strips = inner_width // width
    part = width // count
    tiles = 2 * row_count
    total = row_count * block_len + own_rows

    def tile_at(first):
        def place(t):
            n = jnp.clip(t - first, 0, tiles - 1)
            return n % row_count, 1 - n // row_count

        return place

    forward_at, back_at = tile_at(0), tile_at(tiles + 2 + strips)

    def flat(where, cols):
        def index(t):
            r, h = where(t)
            return 2 * r + h, 0

        return pl.BlockSpec((half, cols), index)

    own_spec = pl.BlockSpec((1, half, width), lambda t: (jnp.clip(t - row_count, 0, row_count - 1), 1, 0))
    next_spec = pl.BlockSpec((1, half, width), lambda t: (jnp.clip(t, 0, row_count - 1), 0, 0))
    whole = lambda *shape: pl.BlockSpec(shape, lambda t: (0,) * len(shape))
    hbm = pl.BlockSpec(memory_space=pl.ANY)
    fixeds = (gain, shift, bias, out_weight, inner_weight, outer_weight, globals_in, global_cot)
    shared = (row_count, 2, 2, 2, share)
    after = 2 * tiles + 2 + strips
    of = jax.ShapeDtypeStruct
    outs = [
        of((row_count, block_len, width), bf16),
        of((row_count * block_len, width), f32),
        of((row_count * block_len, width), bf16),
        of((row_count * block_len, LANES), f32),
        of((row_count, share, width), f32),
        of((*shared, width), bf16),
        of((*shared, width), bf16),
        of((*shared, LANES), f32),
        of((*shared, LANES), f32),
        of((strips, width, width), bf16),
        of((2, 2, strips * part // 4, 640), bf16),
        of((2, strips * part // 2, 128), bf16),
        of((width, width), bf16),
        of((2 + strips, width), f32),
    ]
    vmem = pltpu.VMEM
    fold = Fold.scratch(strips * part // 2, width, 1, True, Fold.EARLY)
    kinds = 2 * row_count + 5
    return pl.pallas_call(
        functools.partial(mid_kernel, half, len(fold)),
        grid=(after + strips + 1,),
        in_specs=[
            pl.BlockSpec(memory_space=pltpu.SMEM),
            own_spec,
            next_spec,
            pl.BlockSpec((1, half, width), lambda t: (*forward_at(t), 0)),
            own_spec,
            next_spec,
        ]
        + [hbm] * (len(fixeds) + 2),
        out_specs=[
            hbm,
            flat(back_at, width),
            flat(back_at, width),
            flat(back_at, LANES),
            whole(row_count, share, width),
            hbm,
            hbm,
            hbm,
            hbm,
            pl.BlockSpec((1, width, width), lambda t: (jnp.clip(t - after, 0, strips - 1), 0, 0)),
            whole(*outs[10].shape),
            whole(*outs[11].shape),
            whole(width, width),
            whole(2 + strips, width),
        ],
        out_shape=outs,
        scratch_shapes=[vmem((1, a.shape[0]), f32) for a in fixeds[:3]]
        + [vmem(a.shape, bf16) for a in fixeds[3:6]]
        + [vmem((row_count, share, width), bf16)] * 2
        + [
            vmem((width, LANES), bf16),
            vmem((total, inner_width), bf16),
            vmem((total, inner_width), bf16),
            vmem((total, width), bf16),
            vmem((total, width), bf16),
            vmem((total, width), bf16),
            vmem((total, width), bf16),
            vmem((total, width), f32),
            vmem((2, 2, 2, 2, strips * part // 2, width), bf16),
            vmem((2, 8, width), f32),
            vmem((strips, 8, width), f32),
            vmem((2, row_count, half, width), bf16),
            vmem((*shared, width), bf16),
            vmem((*shared, width), bf16),
            vmem((*shared, LANES), f32),
            vmem((*shared, LANES), f32),
            vmem((count, row_count, share, width), bf16),
            vmem((count, row_count, share, LANES), f32),
            pltpu.SemaphoreType.DMA((kinds, count)),
            pltpu.SemaphoreType.DMA((kinds, count)),
            pltpu.SemaphoreType.DMA((kinds + row_count + len(fixeds),)),
        ]
        + fold,
        compiler_params=pltpu.CompilerParams(
            collective_id=10, has_side_effects=True, vmem_limit_bytes=64 * 1024 * 1024
        ),
        name="mid",
    )(lengths, inputs, next_x, mixed, cotangent, next_cot, *fixeds, mixed, lse)


def key_marks(me, count, length, half, rows):
    lane = lax.broadcasted_iota(jnp.int32, (rows, LANES), 1)
    row = lax.broadcasted_iota(jnp.int32, (rows, LANES), 0)
    kind = lane - TYPE0
    side = jnp.where(row < half, 0, 1)
    owner = lax.rem(me + side, count)
    position = owner * (2 * half) + jnp.where(row < half, row + half, row - half)
    apart = (me == count - 1) & (kind < 2) & (kind != side)
    of_token = jnp.where((position >= length) | apart, NEG, 0.0)
    of_global = jnp.where((kind == 2) & (me != 0), NEG, 0.0)
    marks = jnp.where(row < 2 * half, of_token, of_global)
    return jnp.where((kind >= 0) & (kind < 3), marks, 0.0).astype(jnp.bfloat16)


def head_kernel(
    half, scale, pairs, tq,
    lengths, inputs, cotangent, globals_in, gain_in, shift_in, weight_in,
    next_x, next_cot, qkv_o, mixed_o, lse_o, normed_o, kaug_o,
    gain, shift, weight, xs, qkv, mixed, lse, normed, kaug, send, recv, local,
):
    bf16, f32 = jnp.bfloat16, jnp.float32
    step = pl.program_id(0)
    me, count = lax.axis_index("seq"), lax.axis_size("seq")
    row_count, rows, width = xs.shape
    block_len = 2 * half
    previous = {"seq": lax.rem(me + count - 1, count)}
    following = {"seq": lax.rem(me + 1, count)}
    lower, upper, tail = pl.ds(0, half), pl.ds(half, half), pl.ds(block_len, rows - block_len)
    turns = [row_count + 1 + r * (pairs + 1) for r in range(row_count)]

    def arrive(r):
        return remote(inputs.at[r, lower], xs.at[r, upper], send.at[0, r], recv.at[0, r], previous)

    def arrive_cot(r):
        return remote(cotangent.at[r, lower], next_cot.at[r], send.at[1, r], recv.at[1, r], previous)

    def loads():
        own = [(inputs.at[r, upper], xs.at[r, lower]) for r in range(row_count)]
        own += [(globals_in.at[r], xs.at[r, tail]) for r in range(row_count)]
        own += [(gain_in, gain.at[0]), (shift_in, shift.at[0]), (weight_in, weight)]
        return fetch(*zip(*own), local)

    def leaves(r):
        pairs_of = ((qkv, qkv_o), (mixed, mixed_o), (lse, lse_o), (normed, normed_o), (kaug, kaug_o))
        moved = [(a.at[r], b.at[r]) for a, b in pairs_of] + [(xs.at[r, upper], next_x.at[r])]
        return fetch(*zip(*moved), local, 16 + 8 * r)

    def project(x):
        x = x.astype(f32)
        centred = x - jnp.mean(x, axis=-1, keepdims=True)
        inv = lax.rsqrt(jnp.mean(centred * centred, axis=-1, keepdims=True) + EPS)
        n = (centred * inv * gain[...] + shift[...]).astype(bf16)
        return n, nn(n, weight[...]).astype(bf16)

    @pl.when(step == 0)
    def _():
        begin(loads())
        barrier = pltpu.get_barrier_semaphore()
        for to in (previous, following):
            pl.semaphore_signal(barrier, inc=1, device_id=to, device_id_type=MESH_ID)
        pl.semaphore_wait(barrier, 2)
        arrive(0).start()
        for r in range(row_count):
            kaug[r] = key_marks(me, count, lengths[r], half, rows)
        for copy in loads():
            copy.wait()

    for r in range(row_count):

        @pl.when(step == turns[r])
        def _():
            arrive(r).wait_recv()
            if r + 1 < row_count:
                arrive(r + 1).start()

    first = turns[0]
    is_turn = functools.reduce(jnp.logical_or, [step == t for t in turns])

    @pl.when((step < row_count) | is_turn)
    def _():
        h = jnp.where(step < row_count, 0, 1)
        r = jnp.where(step < row_count, step, lax.div(step - first, pairs + 1))
        spot = pl.ds(pl.multiple_of(h * half, half), half)
        normed[r, spot], qkv[r, spot] = project(xs[r, spot])

    @pl.when(step == row_count)
    def _():
        n, p = project(jnp.concatenate([xs[r, tail] for r in range(row_count)], axis=0))
        many = rows - block_len
        for r in range(row_count):
            normed[r, tail] = n[r * many:(r + 1) * many]
            qkv[r, tail] = p[r * many:(r + 1) * many]

    @pl.when(step == first + 4)
    def _():
        begin([arrive_cot(r) for r in range(row_count)])

    @pl.when((step > first) & jnp.logical_not(is_turn))
    def _():
        r, p = lax.div(step - first, pairs + 1), lax.rem(step - first, pairs + 1) - 1
        lane = lambda j: pl.ds(pl.multiple_of(j * width + p * LANES, LANES), LANES)
        row = pl.ds(r, 1)
        attend_kernel(
            half, scale, tq, p, qkv.at[row, :, lane(0)], qkv.at[row, :, lane(1)], qkv.at[row, :, lane(2)], kaug.at[row],
            mixed.at[row, :, lane(0)], lse.at[row],
        )

    for r in range(row_count):

        @pl.when(step == turns[r] + pairs)
        def _():
            begin(leaves(r))

    @pl.when(step == turns[-1] + pairs)
    def _():
        for r in range(row_count):
            for copy in leaves(r):
                copy.wait()
            arrive(r).wait_send()
            arrive_cot(r).wait()


def head(lengths, inputs, cotangent, globals_in, gain, shift, weight, tq):
    bf16, f32 = jnp.bfloat16, jnp.float32
    row_count, block_len, width = inputs.shape
    half = block_len // 2
    rows = block_len + globals_in.shape[1]
    pairs = width // LANES
    scale = (width // HEADS) ** (-0.5)
    hbm = pl.BlockSpec(memory_space=pl.ANY)
    of, vmem = jax.ShapeDtypeStruct, pltpu.VMEM
    results = [
        ((row_count, rows, 3 * width), bf16),
        ((row_count, rows, width), bf16),
        ((row_count, rows, LANES), f32),
        ((row_count, rows, width), bf16),
        ((row_count, rows, LANES), bf16),
    ]
    return pl.pallas_call(
        functools.partial(head_kernel, half, scale, pairs, tq),
        grid=(row_count + 1 + row_count * (pairs + 1),),
        in_specs=[pl.BlockSpec(memory_space=pltpu.SMEM)] + [hbm] * 6,
        out_specs=[hbm] * 7,
        out_shape=[of((row_count, half, width), bf16)] * 2 + [of(*r) for r in results],
        scratch_shapes=[
            vmem((1, width), f32),
            vmem((1, width), f32),
            vmem(weight.shape, bf16),
            vmem((row_count, rows, width), bf16),
        ]
        + [vmem(*r) for r in results]
        + [
            pltpu.SemaphoreType.DMA((2, row_count)),
            pltpu.SemaphoreType.DMA((2, row_count)),
            pltpu.SemaphoreType.DMA((16 + 8 * row_count,)),
        ],
        compiler_params=pltpu.CompilerParams(
            collective_id=11, has_side_effects=True, vmem_limit_bytes=60 * 1024 * 1024
        ),
        name="head",
    )(lengths, inputs, cotangent, globals_in, gain, shift, weight)


def wgrad_kernel(a_ref, b_ref, o_ref):
    o_ref[...] = tn(a_ref[...], b_ref[...]).astype(o_ref.dtype).reshape(o_ref.shape)


def wgrad(a, b, strip):
    rows, a_cols = a.shape
    b_cols = b.shape[1]
    split_a = a_cols > b_cols
    strips = max(a_cols, b_cols) // strip
    fixed = lambda n: (0, 0)
    moving = lambda n: (0, n)
    return pl.pallas_call(
        wgrad_kernel,
        grid=(strips,),
        in_specs=[
            pl.BlockSpec((rows, strip), moving if split_a else fixed),
            pl.BlockSpec((rows, strip), fixed if split_a else moving),
        ],
        out_specs=pl.BlockSpec((1, strip, strip), lambda n: (n, 0, 0)),
        out_shape=jax.ShapeDtypeStruct((strips, strip, strip), jnp.bfloat16),
        compiler_params=pltpu.CompilerParams(vmem_limit_bytes=40 * 1024 * 1024),
        name="wgrad",
    )(a, b)


def norm_parts(values):
    average = jnp.mean(values, axis=-1, keepdims=True)
    centred = values - average
    variance = jnp.mean(centred * centred, axis=-1, keepdims=True)
    inv = lax.rsqrt(variance + EPS)
    return centred * inv, inv


def norm_back(grad, n, inv, gain):
    eg = grad * gain
    through = (
        eg - jnp.mean(eg, axis=-1, keepdims=True) - n * jnp.mean(eg * n, axis=-1, keepdims=True)
    ) * inv
    return through, jnp.sum(grad * n, axis=0), jnp.sum(grad, axis=0)


def split_rows(a, count):
    row_count, rows, width = a.shape
    part = rows // count
    moved = a.reshape(row_count, count, part, width).transpose(1, 0, 2, 3)
    return moved.reshape(count, row_count * part, width)


def join_rows(a, row_count):
    count, rows, width = a.shape
    part = rows // row_count
    moved = a.reshape(count, row_count, part, width).transpose(1, 0, 2, 3)
    return moved.reshape(row_count, count * part, width)


def per_head(values, width):
    lanes = values[..., :HEADS]
    return jnp.repeat(lanes, width // HEADS, axis=-1)


def head_sums(values):
    rows, width = values.shape
    lane = jnp.arange(LANES)
    head = jnp.arange(width) // (width // HEADS)
    place = ((lane[None, :] % HEADS == head[:, None]) & (lane[None, :] < 3 * HEADS)).astype(jnp.bfloat16)
    top = values.astype(jnp.bfloat16)
    rest = (values - top.astype(jnp.float32)).astype(jnp.bfloat16)
    return nn(top, place) + nn(rest, place)


def reduce_share(a):
    a = lax.psum_scatter(a, "seq", scatter_dimension=0, tiled=True)
    return lax.psum(a.astype(jnp.bfloat16), "batch").astype(jnp.float32)


def body(
    inputs,
    global_inputs,
    lengths,
    first_gain,
    first_shift,
    qkv_weight,
    out_weight,
    second_gain,
    second_shift,
    inner_weight,
    inner_bias,
    outer_weight,
    output_cotangent,
    global_cotangent,
):
    f32, bf16 = jnp.float32, jnp.bfloat16
    row_count, block_len, width = inputs.shape
    half = block_len // 2
    global_count = global_inputs.shape[1]
    rows = block_len + global_count
    inner_width = inner_weight.shape[1]
    count = lax.axis_size("seq")
    me = lax.axis_index("seq")
    after = lax.rem(me + 1, count)
    back = [(i, (i - 1) % count) for i in range(count)]
    forth = [(i, (i + 1) % count) for i in range(count)]
    token_rows = row_count * block_len
    share = global_count // count
    own_rows = row_count * share

    if count == 8 and lax.axis_size("batch") == 4:
        next_x, next_cot, qkv, mixed, lse, normed, kaug = head(
            lengths, inputs, output_cotangent, global_inputs, first_gain, first_shift, qkv_weight, 320
        )
        (
            layer_output, residual_grad, block_grad, block_delta, own_res, global_out, global_grad, global_lse, global_delta,
            inner_wgrad, outer_ab, outer_c, out_grad, vectors,
        ) = mid(
            lengths, inputs, next_x, mixed, lse, output_cotangent, next_cot, global_inputs, global_cotangent, out_weight, inner_weight,
            outer_weight, inner_bias, second_gain, second_shift, half, count,
        )
        input_out, global_grad, *reduced = rear(
            qkv, block_grad, lse, block_delta, kaug, inputs, next_x, residual_grad, global_grad, global_lse, global_delta,
            own_res, normed, global_inputs, qkv_weight, first_gain, vectors, outer_ab, outer_c, inner_wgrad,
            out_grad, half, count,
        )
        joined = lambda a: a.reshape(row_count, global_count, width)
        inner_out, outer_out, out_out, qkv_out, *lines, layer_output, input_out, global_out, global_grad = finish(
            *reduced, layer_output, input_out, joined(global_out), joined(global_grad)
        )
        fg, fs, sg, ss, bias = (line.reshape(-1) for line in lines)
        return (
            layer_output, global_out, input_out, global_grad, fg, fs, qkv_out, out_out, sg, ss, inner_out, bias, outer_out,
        )

    own_globals = lax.dynamic_slice_in_dim(global_inputs, me * share, share, axis=1)
    own_global_cot = lax.dynamic_slice_in_dim(global_cotangent, me * share, share, axis=1)
    next_inputs = lax.ppermute(inputs[:, :half], "seq", back)
    next_cotangent = lax.ppermute(output_cotangent[:, :half], "seq", back)
    block = jnp.concatenate([inputs[:, half:], next_inputs], axis=1)
    spots = jnp.arange(half, dtype=jnp.int32)
    positions = jnp.concatenate([me * block_len + half + spots, after * block_len + spots])
    valid = positions[None, :] < lengths[:, None]

    kind = jnp.arange(LANES)[None, None, :] - TYPE0
    key_half = (jnp.arange(block_len) // half)[None, :, None]
    last = me == count - 1
    hidden_key = jnp.logical_not(valid)[:, :, None] | (last & (kind < 2) & (kind != key_half))
    token_marks = jnp.where(hidden_key & (kind >= 0) & (kind < 3), NEG, 0.0)
    global_marks = jnp.where((kind == 2) & (me != 0), NEG, 0.0)
    global_marks = jnp.broadcast_to(global_marks, (row_count, global_count, LANES))
    kaug = jnp.concatenate([token_marks, global_marks], axis=1).astype(bf16)

    states = jnp.concatenate([block, global_inputs], axis=1)
    n_first, inv_first = norm_parts(states.astype(f32))
    normed = (n_first * first_gain + first_shift).astype(bf16)
    qkv = nn(normed.reshape(row_count * rows, width), qkv_weight).astype(bf16)
    qkv = qkv.reshape(row_count, rows, 3 * width)

    mixed, lse = attend(qkv, kaug, half)
    tokens_in = block.reshape(token_rows, width)
    cot_block = jnp.concatenate([output_cotangent[:, half:], next_cotangent], axis=1)
    part_mixed, part_lse = spread(
        [split_rows(mixed[:, block_len:], count), split_rows(lse[:, block_len:], count)], count, False, 0
    )
    highest = jnp.max(part_lse, axis=0)
    part_weight = jnp.exp(part_lse - highest)
    total = jnp.sum(part_weight, axis=0)
    global_lse = highest + jnp.log(total)
    global_mixed = jnp.sum(per_head(part_weight / total, width) * part_mixed.astype(f32), axis=0)

    tokens = jnp.concatenate([tokens_in, own_globals.reshape(own_rows, width)]).astype(f32)
    cot_block = jnp.where(valid[:, :, None], cot_block, 0)
    cotangent = jnp.concatenate(
        [cot_block.reshape(token_rows, width), own_global_cot.reshape(own_rows, width)]
    )
    attended = jnp.concatenate(
        [mixed[:, :block_len].reshape(token_rows, width), global_mixed.astype(bf16)]
    )
    residual = tokens + nn(attended, out_weight)
    n_second, inv_second = norm_parts(residual)
    normed_second = (n_second * second_gain + second_shift).astype(bf16)
    inner = nn(normed_second, inner_weight) + inner_bias
    bell = jnp.exp(-0.5 * inner * inner)
    cdf = 0.5 * (1.0 + lax.erf(inner * (0.5 ** 0.5)))
    hidden = (inner * cdf).astype(bf16)
    final = residual + nn(hidden, outer_weight)
    hidden_grad = nt(cotangent, outer_weight)
    slope = cdf + inner * bell * ((0.5 / jnp.pi) ** 0.5)
    inner_grad = (hidden_grad * slope).astype(bf16)
    second_grad = nt(inner_grad, inner_weight)
    through, second_gain_grad, second_shift_grad = norm_back(second_grad, n_second, inv_second, second_gain)
    residual_grad = cotangent.astype(f32) + through
    projection_grad = residual_grad.astype(bf16)
    attended_grad = nt(projection_grad, out_weight).astype(bf16)
    delta = head_sums(attended_grad.astype(f32) * attended.astype(f32))
    outer_grad = wgrad(hidden, cotangent, width)
    inner_wgrad = wgrad(normed_second, inner_grad, width)
    bias_grad = jnp.sum(inner_grad.astype(f32), axis=0)
    out_grad = wgrad(attended, projection_grad, width)

    all_grad, all_lse, all_delta = spread(
        [attended_grad[token_rows:], global_lse, delta[token_rows:]], count, True, 1
    )
    block_grad = jnp.concatenate(
        [attended_grad[:token_rows].reshape(row_count, block_len, width), join_rows(all_grad, row_count)], axis=1
    )
    block_lse = jnp.concatenate([lse[:, :block_len], join_rows(all_lse, row_count)], axis=1)
    block_delta = jnp.concatenate(
        [delta[:token_rows].reshape(row_count, block_len, LANES), join_rows(all_delta, row_count)], axis=1
    )
    layer = final[:token_rows].reshape(row_count, block_len, width)
    layer = jnp.where(valid[:, :, None], layer, 0.0).astype(bf16)
    layer_output = jnp.concatenate([lax.ppermute(layer[:, half:], "seq", forth), layer[:, :half]], axis=1)
    own_out = final[token_rows:].astype(bf16)
    part = width // count
    dqkv = jnp.concatenate(attend_back(qkv, block_grad, block_lse, block_delta, kaug, half, rows), axis=-1)
    (part_dqkv,) = spread([split_rows(dqkv[:, block_len:], count)], count, False, 2)
    global_dqkv = jnp.sum(part_dqkv.astype(f32), axis=0).astype(bf16)
    qkv_grad = jnp.concatenate([dqkv[:, :block_len].reshape(token_rows, 3 * width), global_dqkv])

    first_grad = nt(qkv_grad, qkv_weight)
    n_tokens, inv_tokens = norm_parts(tokens)
    through, first_gain_grad, first_shift_grad = norm_back(first_grad, n_tokens, inv_tokens, first_gain)
    input_grad = (residual_grad + through).astype(bf16)
    normed_tokens = (n_tokens * first_gain + first_shift).astype(bf16)
    qkv_wgrad = wgrad(normed_tokens, qkv_grad, width)

    grad_block = input_grad[:token_rows].reshape(row_count, block_len, width)
    input_out = jnp.concatenate(
        [lax.ppermute(grad_block[:, half:], "seq", forth), grad_block[:, :half]], axis=1
    )
    global_final, global_grad = spread([own_out, input_grad[token_rows:]], count, True, 3)

    def shares(a):
        return a.reshape(count, a.shape[0] // count)

    small = jnp.concatenate(
        [
            shares(first_gain_grad),
            shares(first_shift_grad),
            shares(second_gain_grad),
            shares(second_shift_grad),
            shares(bias_grad),
        ],
        axis=1,
    )
    inner_out = reduce_share(inner_wgrad.transpose(1, 0, 2).reshape(width, -1))
    outer_out = reduce_share(outer_grad.reshape(inner_width, width))
    out_out = reduce_share(out_grad[0])
    qkv_out = reduce_share(qkv_wgrad.transpose(1, 0, 2).reshape(width, -1))
    small = reduce_share(small)[0]
    return (
        layer_output,
        join_rows(global_final, row_count),
        input_out,
        join_rows(global_grad, row_count),
        small[:part],
        small[part:2 * part],
        qkv_out,
        out_out,
        small[2 * part:3 * part],
        small[3 * part:4 * part],
        inner_out,
        small[4 * part:],
        outer_out,
    )


def solution(mesh):
    rows = P("batch", "seq", None)
    globals_at = P("batch", None, None)
    return jax.shard_map(
        body,
        mesh=mesh,
        in_specs=(rows, globals_at, P("batch")) + (P(),) * 9 + (rows, globals_at),
        out_specs=(
            rows,
            globals_at,
            rows,
            globals_at,
            P("seq"),
            P("seq"),
            P("seq", None),
            P("seq", None),
            P("seq"),
            P("seq"),
            P("seq", None),
            P("seq"),
            P("seq", None),
        ),
        check_vma=False,
    )
```

```python
import functools
import math

import jax
import jax.numpy as jnp
from jax import lax
from jax.experimental import pallas as pl
from jax.experimental.pallas import tpu as pltpu
from jax.sharding import PartitionSpec as P

HEADS = 12
NEG = -1e30
LANES = 128
TYPE0 = 3 * HEADS

def nt(a, b):
    return lax.dot_general(a, b, (((1,), (1,)), ((), ())), preferred_element_type=jnp.float32)

def tn(a, b):
    return lax.dot_general(a, b, (((0,), (0,)), ((), ())), preferred_element_type=jnp.float32)

def nn(a, b):
    return jnp.dot(a, b, preferred_element_type=jnp.float32)


def type_marks(rows, half, lane, row):
    kind = jnp.where(row < half, TYPE0, jnp.where(row < 2 * half, TYPE0 + 1, TYPE0 + 2))
    return (lane == kind)


def attend_step(half, scale, tq, *refs):
    attend_kernel(half, scale, tq, pl.program_id(1), *refs)


def attend_kernel(half, scale, tq, pair, q_ref, k_ref, v_ref, kaug_ref, o_ref, lse_ref):
    rows = q_ref.shape[1]
    zero = jnp.zeros((), jnp.bfloat16)
    k, v = k_ref[0], v_ref[0]
    kaug = kaug_ref[0]
    lane_all = lax.broadcasted_iota(jnp.int32, (rows, LANES), 1)
    low_all = lane_all < LANES // 2
    one = jnp.ones((), jnp.bfloat16)
    kx, vx = [], []
    for sel in (low_all, jnp.logical_not(low_all)):
        kx.append(jnp.concatenate([jnp.where(sel, k, zero), kaug], axis=1))
        vx.append(jnp.concatenate([jnp.where(sel, v, zero), jnp.where(sel, one, zero)], axis=1))
    vx = jnp.concatenate(vx, axis=0)
    for start in range(0, rows, tq):
        lane = lax.broadcasted_iota(jnp.int32, (tq, LANES), 1)
        row = lax.broadcasted_iota(jnp.int32, (tq, LANES), 0) + start
        low = lane < LANES // 2
        qaug = jnp.where(type_marks(rows, half, lane, row), one, zero)
        q = (q_ref[0, start:start + tq].astype(jnp.float32) * scale).astype(jnp.bfloat16)
        qx = jnp.concatenate([q, qaug], axis=1)
        probs, peaks = [], []
        for a in (0, 1):
            s = nt(qx, kx[a])
            peak = jnp.max(s, axis=1, keepdims=True)
            probs.append(jnp.exp(s - peak).astype(jnp.bfloat16))
            peaks.append(peak)
        acc = nn(jnp.concatenate(probs, axis=1), vx)
        total = acc[:, LANES:]
        o_ref[0, start:start + tq] = (acc[:, :LANES] / total).astype(jnp.bfloat16)
        lse = jnp.where(low, peaks[0], peaks[1]) + jnp.log(total)
        first, second = lse[:, 0:1], lse[:, LANES // 2:LANES // 2 + 1]
        prev = jnp.where(pair == 0, 0.0, lse_ref[0, start:start + tq])
        head = lax.rem(lane, HEADS)
        inside = lane < 3 * HEADS
        kept = jnp.where(inside & (head == 2 * pair), first, prev)
        lse_ref[0, start:start + tq] = jnp.where(inside & (head == 2 * pair + 1), second, kept)


def attend(qkv, kaug, half, tq=320):
    row_count, rows, cols = qkv.shape
    width = cols // 3
    pairs = width // LANES
    scale = (width // HEADS) ** (-0.5)
    spec = lambda off: pl.BlockSpec((1, rows, LANES), lambda r, p: (r, 0, off + p))
    return pl.pallas_call(
        functools.partial(attend_step, half, scale, tq),
        grid=(row_count, pairs),
        in_specs=[spec(0), spec(pairs), spec(2 * pairs), pl.BlockSpec((1, rows, LANES), lambda r, p: (r, 0, 0))],
        out_specs=[spec(0), pl.BlockSpec((1, rows, LANES), lambda r, p: (r, 0, 0))],
        out_shape=[
            jax.ShapeDtypeStruct((row_count, rows, width), jnp.bfloat16),
            jax.ShapeDtypeStruct((row_count, rows, LANES), jnp.float32),
        ],
        compiler_params=pltpu.CompilerParams(vmem_limit_bytes=48 * 1024 * 1024),
        name="attend",
    )(qkv, qkv, qkv, kaug)


def three_parts(values, lane):
    top = values.astype(jnp.bfloat16)
    rest = values - top.astype(jnp.float32)
    mid = rest.astype(jnp.bfloat16)
    low = (rest - mid.astype(jnp.float32)).astype(jnp.bfloat16)
    zero = jnp.zeros((), jnp.bfloat16)
    return jnp.where(lane < HEADS, top, jnp.where(lane < 2 * HEADS, mid, jnp.where(lane < 3 * HEADS, low, zero)))


def attend_back_step(half, scale, tk, q_ref, k_ref, v_ref, g_ref, lse_ref, delta_ref, *refs):
    attend_back_kernel(
        half, scale, tk, pl.program_id(1), q_ref, k_ref, v_ref, g_ref[0], lse_ref[0], delta_ref[0], *refs
    )


def attend_back_kernel(half, scale, tk, pair, q_ref, k_ref, v_ref, g, lse, delta, kaug_ref, dq_ref, dk_ref, dv_ref):
    rows = q_ref.shape[1]
    zero = jnp.zeros((), jnp.bfloat16)
    one = jnp.ones((), jnp.bfloat16)
    lane = lax.broadcasted_iota(jnp.int32, (rows, LANES), 1)
    row = lax.broadcasted_iota(jnp.int32, (rows, LANES), 0)
    low = lane < LANES // 2
    q = (q_ref[0].astype(jnp.float32) * scale).astype(jnp.bfloat16)
    qaug = jnp.where(type_marks(rows, half, lane, row), one, three_parts(lse, lane))
    gaug = three_parts(delta, lane)
    qx = jnp.concatenate([q, qaug], axis=1)
    gx = jnp.concatenate([g, gaug], axis=1)
    sels = (low, jnp.logical_not(low))
    qh = jnp.concatenate([jnp.where(sel, q, zero) for sel in sels], axis=0)
    gh = jnp.concatenate([jnp.where(sel, g, zero) for sel in sels], axis=0)
    dq = None
    for start in range(0, rows, tk):
        lane_k = lax.broadcasted_iota(jnp.int32, (tk, LANES), 1)
        low_k = lane_k < LANES // 2
        head = lax.rem(lane_k, HEADS)
        inside = lane_k < 3 * HEADS
        k = k_ref[0, start:start + tk]
        v = v_ref[0, start:start + tk]
        kaug = kaug_ref[0, start:start + tk]
        probs, grads, keys = [], [], []
        for a, sel in ((0, low_k), (1, jnp.logical_not(low_k))):
            marks = inside & (head == 2 * pair + a)
            keys.append(jnp.where(sel, k, zero))
            kx = jnp.concatenate([keys[a], jnp.where(marks, -one, kaug)], axis=1)
            vx = jnp.concatenate([jnp.where(sel, v, zero), jnp.where(marks, -one, zero)], axis=1)
            p = jnp.exp(nt(kx, qx))
            grads.append((p * nt(vx, gx)).astype(jnp.bfloat16))
            probs.append(p.astype(jnp.bfloat16))
        dv_ref[0, start:start + tk] = nn(jnp.concatenate(probs, axis=1), gh).astype(jnp.bfloat16)
        dk_ref[0, start:start + tk] = nn(jnp.concatenate(grads, axis=1), qh).astype(jnp.bfloat16)
        part = tn(jnp.concatenate(grads, axis=0), jnp.concatenate(keys, axis=0))
        dq = part if dq is None else dq + part
    dq_ref[0] = (dq * scale).astype(jnp.bfloat16)


def attend_back(qkv, grad, lse, delta, kaug, half, tk=320):
    row_count, rows, cols = qkv.shape
    width = cols // 3
    pairs = width // LANES
    scale = (width // HEADS) ** (-0.5)
    spec = lambda off: pl.BlockSpec((1, rows, LANES), lambda r, p: (r, 0, off + p))
    whole = pl.BlockSpec((1, rows, LANES), lambda r, p: (r, 0, 0))
    out = jax.ShapeDtypeStruct((row_count, rows, width), jnp.bfloat16)
    return pl.pallas_call(
        functools.partial(attend_back_step, half, scale, tk),
        grid=(row_count, pairs),
        in_specs=[spec(0), spec(pairs), spec(2 * pairs), spec(0), whole, whole, whole],
        out_specs=[spec(0)] * 3,
        out_shape=[out] * 3,
        compiler_params=pltpu.CompilerParams(vmem_limit_bytes=48 * 1024 * 1024),
        name="attend_back",
    )(qkv, qkv, qkv, grad, lse, delta, kaug)


EPS = 1e-05
MESH_ID = pl.DeviceIdType.MESH


def spread_kernel(count, sizes, same, *refs):
    ins, outs = refs[:sizes], refs[sizes:2 * sizes]
    send, recv, local = refs[2 * sizes:]
    me = lax.axis_index("seq")
    barrier = pltpu.get_barrier_semaphore()
    for step in range(1, count):
        pl.semaphore_signal(
            barrier, inc=1, device_id={"seq": lax.rem(me + step, count)}, device_id_type=MESH_ID
        )
    pl.semaphore_wait(barrier, count - 1)
    own = []
    for n in range(sizes):
        copy = pltpu.make_async_copy(ins[n] if same else ins[n].at[me], outs[n].at[me], local.at[n])
        copy.start()
        own.append(copy)
    copies = []
    for step in range(1, count):
        peer = lax.rem(me + step, count)
        for n in range(sizes):
            copy = pltpu.make_async_remote_copy(
                src_ref=ins[n] if same else ins[n].at[peer],
                dst_ref=outs[n].at[me],
                send_sem=send.at[n, step],
                recv_sem=recv.at[n, step],
                device_id={"seq": peer},
                device_id_type=MESH_ID,
            )
            copy.start()
            copies.append(copy)
    for copy in own:
        copy.wait()
    for copy in copies:
        copy.wait()


def spread(arrays, count, same, collective_id):
    sizes = len(arrays)
    shapes = [(count,) + a.shape if same else a.shape for a in arrays]
    vmem = pl.BlockSpec(memory_space=pltpu.VMEM)
    return pl.pallas_call(
        functools.partial(spread_kernel, count, sizes, same),
        in_specs=[vmem] * sizes,
        out_specs=[vmem] * sizes,
        out_shape=[jax.ShapeDtypeStruct(s, a.dtype) for s, a in zip(shapes, arrays)],
        scratch_shapes=[
            pltpu.SemaphoreType.DMA((sizes, count)),
            pltpu.SemaphoreType.DMA((sizes, count)),
            pltpu.SemaphoreType.DMA((sizes,)),
        ],
        compiler_params=pltpu.CompilerParams(
            collective_id=collective_id, has_side_effects=True, vmem_limit_bytes=32 * 1024 * 1024
        ),
        name="spread",
    )(*arrays)


SEQ_BITS = (("z1", 4), ("z0", 2), ("x", 1))
BATCH_BITS = (("y", 2), ("c", 1))


class Place:
    def __init__(self):
        self.spot, self.step = {}, {}
        for name, bits in (("seq", SEQ_BITS), ("batch", BATCH_BITS)):
            index = lax.axis_index(name)
            for axis, weight in bits:
                bit = lax.rem(lax.div(index, weight), 2)
                self.spot[axis] = bit
                self.step[axis] = {name: index + weight * (1 - 2 * bit)}

    def __getitem__(self, axis):
        return self.spot[axis]

    def partner(self, axis):
        return self.step[axis]

    def greet(self, others=()):
        barrier = pltpu.get_barrier_semaphore()
        peers = list(self.step.values()) + list(others)
        for to in peers:
            pl.semaphore_signal(barrier, inc=1, device_id=to, device_id_type=MESH_ID)
        pl.semaphore_wait(barrier, len(peers))


def remote(src, dst, send, recv, to):
    return pltpu.make_async_remote_copy(
        src_ref=src, dst_ref=dst, send_sem=send, recv_sem=recv, device_id=to, device_id_type=MESH_ID
    )


class Halve:
    def __init__(self, place, own, lanes, order, bufs, send, recv, first, stages=None):
        self.place, self.own, self.order = place, own, order
        self.lanes = pl.ds(*lanes)
        self.half = own.shape[3] // 2
        stages = range(len(order)) if stages is None else stages
        self.bufs = dict(zip(stages, bufs))
        self.send, self.recv, self.first = send, recv, first

    def copy(self, n):
        at = self.first + n
        return remote(
            self.own.at[self.region(n, False)], self.bufs[n], self.send.at[at], self.recv.at[at],
            self.place.partner(self.order[n]),
        )

    @staticmethod
    def buffers(rows, width, order, stages=None, dtype=jnp.bfloat16):
        shapes = []
        for n in range(len(order)) if stages is None else stages:
            left = [axis for axis, _ in SEQ_BITS if axis not in order[:n + 1]]
            shapes.append((2,) * len(left) + (rows // 2 if "y" in order[:n + 1] else rows, width))
        return [pltpu.VMEM(shape, dtype) for shape in shapes]

    def region(self, n, mine, free=(), piece=None):
        free = list(free)
        at = []
        for axis, _ in SEQ_BITS:
            if axis in self.order[:n]:
                at.append(self.place[axis])
            elif axis == self.order[n]:
                at.append(self.place[axis] if mine else 1 - self.place[axis])
            else:
                at.append(free.pop(0) if free else slice(None))
        first, count = 0, self.own.shape[3]
        if "y" in self.order[:n + 1]:
            y = self.place["y"]
            y = y if mine or self.order[n] != "y" else 1 - y
            first, count = y * self.half, self.half
        if piece is not None:
            first, count = first + piece[0], piece[1]
        rows = pl.ds(pl.multiple_of(first, 16), count)
        return (*at, rows, self.lanes)

    def start(self, n):
        self.copy(n).start()

    def sent(self):
        for n in self.bufs:
            self.copy(n).wait_send()

    def finish(self, n):
        self.copy(n).wait_recv()
        buf = self.bufs[n]
        dims = len(buf.shape) - 2
        count = buf.shape[-2]
        piece = math.gcd(count, 48)
        pieces = count // piece

        def add(i, carry):
            block, row = lax.div(i, pieces), lax.rem(i, pieces) * piece
            free = [lax.rem(lax.div(block, 2 ** (dims - 1 - d)), 2) for d in range(dims)]
            at = self.region(n, True, free, (row, piece))
            self.own[at] = self.own[at] + buf[(*free, pl.ds(pl.multiple_of(row, 16), piece), slice(None))]
            return carry

        lax.fori_loop(0, 2 ** dims * pieces, add, 0)


class Gather:
    order = ("z1", "z0", "x")

    def __init__(self, place, buf, send, recv):
        self.place, self.buf, self.send, self.recv = place, buf, send, recv

    def copy(self, n):
        done = self.order[:n]
        at = (slice(None), *(slice(None) if axis in done else self.place[axis] for axis, _ in SEQ_BITS))
        block = self.buf.at[at]
        return remote(block, block, self.send.at[n], self.recv.at[n], self.place.partner(self.order[n]))

    def stage(self, n):
        if n > 0:
            self.copy(n - 1).wait_recv()
        if n < 3:
            self.copy(n).start()

    def finish(self):
        for n in range(3):
            self.copy(n).wait_send()


PARTS = (
    ((0, 256), ("x", "y", "z0", "z1")),
    ((256, 384), ("y", "x", "z0", "z1")),
    ((640, 128), ("z0", "z1", "x", "y")),
)


class Fold:
    EARLY, LATE = (0, 1), (2, 3)

    def __init__(self, place, pieces, refs, source=None, stages=(0, 1, 2, 3)):
        self.place = place
        c, y = place["c"], place["y"]
        if stages == self.LATE:
            self.own, self.done, send, recv, *bufs = refs
            self.got = local = None
        elif source is None:
            self.own, self.done, *refs = refs
        else:
            self.own, self.done = source.at[:, :, :, c], None
        if stages != self.LATE:
            self.got, send, recv, local, *bufs = refs
        own, got, done = self.own, self.got, self.done
        rows = own.shape[3]
        half = rows // 2
        self.mine = pl.ds(pl.multiple_of(y * half, 16), half)
        self.pieces, self.source, self.done = pieces, source, done
        self.sems = send, recv, local
        first = 1 if source is not None else len(pieces)
        self.first = first + 12
        self.parts = []
        for n, (lanes, order) in enumerate(PARTS):
            own_bufs = bufs[len(stages) * n:len(stages) * (n + 1)]
            self.parts.append(Halve(place, own, lanes, order, own_bufs, send, recv, first + 4 * n, stages))

    def keep(self):
        at, copies = 0, []
        if self.source is None:
            for n, (take, count) in enumerate(self.pieces):
                spot = self.own.at[:, :, :, pl.ds(at, count)]
                copies.append(pltpu.make_async_copy(take(self.place["c"]), spot, self.sems[2].at[n]))
                at += count
        return copies

    def core(self):
        send, recv, _ = self.sems
        to, c = self.place.partner("c"), 1 - self.place["c"]
        if self.source is not None:
            return [remote(self.source.at[:, :, :, c], self.got, send.at[0], recv.at[0], to)]
        at, copies = 0, []
        for n, (take, count) in enumerate(self.pieces):
            copies.append(remote(take(c), self.got.at[:, :, :, pl.ds(at, count)], send.at[n], recv.at[n], to))
            at += count
        return copies

    def across(self):
        send, recv, _ = self.sems
        spot = self.done.at[self.place["c"], self.mine]
        return remote(spot, spot, send.at[self.first], recv.at[self.first], self.place.partner("y"))

    def back(self):
        send, recv, _ = self.sems
        spot = self.done.at[self.place["c"]]
        return remote(spot, spot, send.at[self.first + 1], recv.at[self.first + 1], self.place.partner("c"))

    @staticmethod
    def scratch(rows, width, pieces, sourced=False, stages=(0, 1, 2, 3)):
        vmem = lambda *shape: pltpu.VMEM(shape, jnp.bfloat16)
        refs = [] if sourced else [vmem(2, 2, 2, rows, width), vmem(2, rows, width)]
        if stages != Fold.LATE:
            refs.append(vmem(2, 2, 2, rows, width))
        refs += [
            pltpu.SemaphoreType.DMA((pieces + 14,)),
            pltpu.SemaphoreType.DMA((pieces + 14,)),
        ]
        if stages != Fold.LATE:
            refs.append(pltpu.SemaphoreType.DMA((pieces,)))
        for (_, count), order in PARTS:
            refs += Halve.buffers(rows, count, order, stages)
        return refs

    def stage(self, n):
        if n == 0:
            for copy in self.keep() + self.core():
                copy.start()
        elif n == 1:
            for copy in self.keep():
                copy.wait()
            for copy in self.core():
                copy.wait_recv()

            piece = math.gcd(self.got.shape[3], 48)
            pieces = self.got.shape[3] // piece

            def add(i, carry):
                block = lax.div(i, pieces)
                rows = pl.ds(pl.multiple_of(lax.rem(i, pieces) * piece, 16), piece)
                at = (*(lax.rem(lax.div(block, w), 2) for _, w in SEQ_BITS), rows)
                self.own[at] = self.own[at] + self.got[at]
                return carry

            lax.fori_loop(0, 8 * pieces, add, 0)
            for part in self.parts:
                part.start(0)
        elif n < 5:
            for part in self.parts:
                part.finish(n - 2)
                part.start(n - 1)
        elif n == 5:
            for part in self.parts:
                part.finish(3)
            at = tuple(self.place[axis] for axis, _ in SEQ_BITS)
            self.done[self.place["c"], self.mine] = self.own[(*at, self.mine)]
            self.across().start()
        elif n == 6:
            self.across().wait_recv()
            self.back().start()
        else:
            self.back().wait_recv()

    def held(self):
        z1, z0, x = (self.place[axis] for axis, _ in SEQ_BITS)
        a, b, c = (lanes[1] for lanes, _ in PARTS)
        return (slice(None), slice(None), x, self.mine, pl.ds(0, a + b)), (
            z1, z0, slice(None), slice(None), pl.ds(a + b, c)
        )

    def resume(self):
        for part in self.parts:
            part.start(2)

    def finish(self):
        copies = self.core()
        if self.done is not None:
            copies = copies + [self.across(), self.back()]
        for copy in copies:
            copy.wait_send()
        for part in self.parts:
            part.sent()


class Sum:
    order = ("c", "x", "y", "z0", "z1")

    def __init__(self, place, value, got, send, recv):
        self.place, self.value, self.got, self.send, self.recv = place, value, got, send, recv

    def copy(self, n):
        to = self.place.partner(self.order[n])
        return remote(self.value.at[n], self.got.at[n], self.send.at[n], self.recv.at[n], to)

    def stage(self, n):
        if n > 0:
            self.copy(n - 1).wait_recv()
            self.value[n] = self.value[n - 1] + self.got[n - 1]
        if n < 5:
            self.copy(n).start()

    def finish(self):
        for n in range(5):
            self.copy(n).wait_send()


def share_views(a, count):
    *lead, rows, width = a.shape
    return a.reshape(*lead, 2, 2, 2, rows // count, width)


def half_views(a, count):
    *lead, rows, width = a.shape
    return a.reshape(*lead, 2, 2, 2, 2, rows // (2 * count), width)


def fetch(sources, targets, sems, first=0):
    return [pltpu.make_async_copy(s, t, sems.at[first + n]) for n, (s, t) in enumerate(zip(sources, targets))]


def finish_kernel(
    inner_in, out_in, queries_in, keys_in, outer_in, small_in, layer, igrad, gout, ggrad,
    inner_o, outer_o, out_o, qkv_o, fg_o, fs_o, sg_o, ss_o, bias_o, layer_o, igrad_o, gout_o, ggrad_o,
    inner, out, queries, keys, outer, small, *scratch,
):
    *held, sems = scratch
    f32 = jnp.float32
    me = lax.axis_index("seq")
    moved = (layer, igrad, gout, ggrad)
    own = fetch(
        (inner_in, out_in, queries_in, keys_in, outer_in, small_in), (inner, out, queries, keys, outer, small), sems
    )
    into, away = fetch(moved, held, sems, 6), fetch(held, (layer_o, igrad_o, gout_o, ggrad_o), sems, 10)
    begin(own + into)
    width = outer_o.shape[1]
    part = inner_o.shape[0]
    strips = inner_o.shape[1] // width // 2
    half = outer.shape[1]
    for copy in own:
        copy.wait()
    for c in range(2):
        for j in range(strips):
            inner_o[:, pl.ds((c * strips + j) * width, width)] = inner[c, pl.ds(j * part, part)].astype(f32)
        outer_o[pl.ds(c * half, half)] = outer[c].astype(f32)
        spot = pl.ds(c * part // 2, part // 2)
        first, second = pl.ds(0, part // 2), pl.ds(part // 2, part // 2)
        out_o[spot] = out[c, first].astype(f32)
        for j, (ref, lines) in enumerate(((queries, first), (keys, first), (keys, second))):
            qkv_o[spot, pl.ds(j * width, width)] = ref[c, lines].astype(f32)
    for copy, onward in zip(into, away):
        copy.wait()
        onward.start()
    values = small[...]
    turned = pltpu.roll(values, lax.rem(width - part * me, width), 1)
    for n, ref in enumerate((fg_o, fs_o, sg_o, ss_o)):
        ref[...] = turned[n, :part]
    wide = bias_o.shape[0]
    per = width // wide
    row = small[pl.ds(4 + lax.div(me, per), 1)]
    spots = [row[0, n * wide:(n + 1) * wide] for n in range(per)]
    chosen = spots[0]
    for n in range(1, per):
        chosen = jnp.where(lax.rem(me, per) == n, spots[n], chosen)
    bias_o[...] = chosen
    for copy in away:
        copy.wait()


def finish(inner, out, queries, keys, outer, small, layer, igrad, gout, ggrad):
    width = small.shape[1]
    part = keys.shape[1]
    bias = 2 * outer.shape[1]
    vmem, hbm = pl.BlockSpec(memory_space=pltpu.VMEM), pl.BlockSpec(memory_space=pl.ANY)
    shapes = [(part, 4 * width), (bias, width), (part, width), (part, 3 * width)] + [(part,)] * 4 + [(bias,)]
    own, moved = [inner, out, queries, keys, outer, small], [layer, igrad, gout, ggrad]
    return pl.pallas_call(
        finish_kernel,
        in_specs=[hbm] * 10,
        out_specs=[vmem] * 9 + [hbm] * 4,
        out_shape=[jax.ShapeDtypeStruct(s, jnp.float32) for s in shapes]
        + [jax.ShapeDtypeStruct(a.shape, a.dtype) for a in moved],
        scratch_shapes=[pltpu.VMEM(a.shape, a.dtype) for a in own + moved] + [pltpu.SemaphoreType.DMA((14,))],
        compiler_params=pltpu.CompilerParams(vmem_limit_bytes=60 * 1024 * 1024),
        name="finish",
    )(*own, *moved)


def begin(copies):
    for copy in copies:
        copy.start()


def sum_rows(values):
    rows, width = values.shape
    return jnp.sum(values.reshape(rows // 8, 8, width), axis=0)


def ticks(plan, folds, step):
    for t, todo in plan.items():

        @pl.when(step == t)
        def _():
            for f, n in todo:
                folds[f].stage(n)


TILE_AT = ((6, 0, 1), (7, 0, 0), (15, 1, 1), (19, 1, 0))
GLOBALS_AT, STRIPS_AT, LAST = 14, 16, 20
REAR_TICKS = {
    0: ((0, 0), (4, 0)),
    3: ((0, 1),),
    4: ((3, 4), (4, 1)),
    8: ((3, 5),),
    9: ((0, 2), (4, 2)),
    10: ((3, 6),),
    12: ((3, 7), (4, 3)),
    13: ((0, 3),),
    15: ((4, 4),),
    17: ((0, 4), (1, 0)),
    18: ((4, 5),),
    19: ((0, 5), (1, 1), (2, 0)),
}
REAR_END = (
    (7, 0), (5, 1), (2, 1), (7, 1), (1, 2), (4, 6), (0, 6), (5, 2), (6, 0), (2, 2), (7, 2), (1, 3), (0, 7), (4, 7), (6, 1),
    (2, 3), (7, 3), (1, 4), (6, 2), (2, 4), (7, 4), (1, 5), (6, 3), (2, 5), (7, 5), (1, 6), (2, 6), (1, 7), (2, 7),
)
SPREAD_AT = 18
LONE = 64


def rear_kernel(
    half, scale, pairs, fold_refs,
    q_ref, k_ref, v_ref, g_ref, lse_ref, delta_ref, kaug_ref,
    x_ref, next_x_ref, res_ref, gg_in, glse_in, gdelta_in, outer_ab, outer_c, gres_in, globals_in, weight_in, gain_in, vectors_in,
    normed_in, inner, out,
    igrad_o, ggrad_o, inner_o, out_o, queries_o, keys_o, outer_o, small_o,
    gg_ref, glse_ref, gdelta_ref, gres_ref, globals_ref, weight_ref, gain_ref, vectors_ref, normed_ref,
    dqkv, gfirst, sums, qkv_src, grads, ggrad, value, got,
    send, recv, local, *scratch,
):
    step = pl.program_id(0)
    place = Place()
    me = lax.axis_index("seq")
    count = lax.axis_size("seq")
    row_count, rows, cols = dqkv.shape
    block_len = 2 * half
    width = cols // 3
    share = gres_ref.shape[1]
    attn = row_count * pairs
    strips = inner.shape[0] // 2
    part_rows = inner.shape[4]
    half_part = part_rows // 2
    sources = (
        [(lambda c, j=j: inner.at[c * strips + j], part_rows) for j in range(strips)],
        [(lambda c: qkv_src.at[0, :, :, :, c], half_part)],
        [(lambda c, j=j: qkv_src.at[j, :, :, :, c], half_part) for j in (1, 2)],
    )
    folds, at = [], 0
    for pieces, size in zip(sources, fold_refs[:3]):
        folds.append(Fold(place, pieces, scratch[at:at + size]))
        at += size
    folds.append(Fold(place, (), scratch[at:at + fold_refs[3]], None, Fold.LATE))
    at += fold_refs[3]
    folds.append(Fold(place, [(lambda c: out.at[:, :, :, c], half_part)], scratch[at:at + fold_refs[4]]))
    at += fold_refs[4]
    spread = Halve(place, gfirst, (0, width), ("x", "z0", "z1"), scratch[at:], send.at[0], recv.at[0], 0)
    gather = Gather(place, ggrad, send.at[row_count], recv.at[row_count])
    small = Sum(place, value, got, send.at[row_count + 1], recv.at[row_count + 1])
    following = {"seq": lax.rem(me + 1, count)}
    before = {"seq": lax.rem(me + count - 1, count)}
    held = folds[3].held()
    early = lambda: fetch(
        (gg_in, glse_in, gdelta_in, outer_ab, outer_c),
        (gg_ref, glse_ref, gdelta_ref, folds[3].own.at[held[0]], folds[3].own.at[held[1]]), local,
    )
    later = lambda: fetch(
        (gres_in, globals_in, weight_in, gain_in, vectors_in),
        (gres_ref, globals_ref, weight_ref, gain_ref.at[0], vectors_ref), local, 5,
    )
    latest = lambda: fetch((normed_in,), (normed_ref,), local, 11)

    def home(r):
        sems = send.at[row_count + 2, r], recv.at[row_count + 2, r]
        return remote(grads.at[1, r], igrad_o.at[r, pl.ds(0, half)], *sems, following)

    def keep(r):
        return pltpu.make_async_copy(grads.at[0, r], igrad_o.at[r, pl.ds(half, half)], local.at[12 + r])

    @pl.when(step == 0)
    def _():
        begin(early() + later() + latest())
        place.greet([following, before])
        sums[...] = jnp.zeros_like(sums)
        for copy in early():
            copy.wait()
        folds[3].resume()

    ticks(REAR_TICKS, folds, step)

    @pl.when((step < pairs) | ((step >= pairs + 2) & (step < attn + 2)))
    def _():
        r = jnp.where(step < pairs, 0, 1)
        p = step - r * (pairs + 2)
        spots = [pl.ds(pl.multiple_of(j * width + p * LANES, LANES), LANES) for j in range(3)]
        lane = pl.ds(pl.multiple_of(p * LANES, LANES), LANES)
        wide = lambda a, b: jnp.concatenate([a, b.reshape(rows - block_len, LANES)], axis=0)
        attend_back_kernel(
            half, scale, 320, p, q_ref, k_ref, v_ref, wide(g_ref[...], gg_ref[r, :, :, :, :, lane]),
            wide(lse_ref[0], glse_ref[r]), wide(delta_ref[...], gdelta_ref[r]), kaug_ref,
            *(dqkv.at[pl.ds(r, 1), :, spot] for spot in spots),
        )

    def move_spread(n):
        spread.finish(n)
        if n < 2:
            spread.start(n + 1)

    @pl.when(step == SPREAD_AT)
    def _():
        move_spread(0)

    @pl.when(step == TILE_AT[0][0])
    def _():
        for copy in later():
            copy.wait()

    @pl.when(step == STRIPS_AT)
    def _():
        for copy in latest():
            copy.wait()


    strip_at = step - STRIPS_AT

    @pl.when((strip_at >= 0) & (strip_at < 3))
    def _():
        strip = pl.ds(pl.multiple_of(strip_at * width, width), width)
        total = tn(normed_ref[0], dqkv[0, :, strip])
        for r in range(1, row_count):
            total = total + tn(normed_ref[r], dqkv[r, :, strip])
        qkv_src[strip_at] = total.astype(jnp.bfloat16).reshape(qkv_src.shape[1:])

    def stats(x):
        centred = x - jnp.mean(x, axis=-1, keepdims=True)
        inv = lax.rsqrt(jnp.mean(centred * centred, axis=-1, keepdims=True) + EPS)
        return centred * inv, inv

    def add_sums(first, n):
        sums[0] += sum_rows(first * n)
        sums[1] += sum_rows(first)

    def through(first, n, inv):
        eg = first * gain_ref[...]
        return (eg - jnp.mean(eg, axis=-1, keepdims=True) - n * jnp.mean(eg * n, axis=-1, keepdims=True)) * inv

    @pl.when(step == GLOBALS_AT)
    def _():
        own = pl.ds(block_len, rows - block_len)
        partial = jnp.concatenate([dqkv[r, own] for r in range(row_count)], axis=0)
        first = nt(partial, weight_ref[...])
        n, _ = stats(globals_ref[...].astype(jnp.float32).reshape(first.shape))
        add_sums(first, n)
        first = first.astype(jnp.bfloat16).reshape(row_count, 2, 2, 2, share, width)
        for r in range(row_count):
            gfirst[:, :, :, pl.ds(r * share, share)] = first[r]
        spread.start(0)

    @pl.when(functools.reduce(jnp.logical_or, [step == t for t, _, _ in TILE_AT]))
    def _():
        r = jnp.where(step < pairs + 2, 0, 1)
        h = jnp.where((step == TILE_AT[0][0]) | (step == TILE_AT[2][0]), 1, 0)
        first = nt(dqkv[r, pl.ds(pl.multiple_of(h * half, half), half)], weight_ref[...])
        n, inv = stats(jnp.where(h == 0, x_ref[0].astype(jnp.float32), next_x_ref[0].astype(jnp.float32)))
        add_sums(first, n)
        grads[h, r] = (res_ref[...] + through(first, n, inv)).astype(jnp.bfloat16)

    for t, r, h in TILE_AT:

        @pl.when(step == t)
        def _():
            (home if h else keep)(r).start()

    def own_globals():
        own_rows = row_count * share
        at = tuple(place[axis] for axis, _ in SEQ_BITS)
        held = pl.ds(pl.multiple_of(share * me, 16), share)
        n, inv = stats(globals_ref[:, held].astype(jnp.float32).reshape(own_rows, width))
        grad = gres_ref[...].reshape(own_rows, width) + through(gfirst[at].astype(jnp.float32), n, inv)
        ggrad[(slice(None), *at)] = grad.astype(jnp.bfloat16).reshape(row_count, share, width)

    @pl.when(step == LAST)
    def _():
        lines = [jnp.sum(sums[n], axis=0, keepdims=True) for n in range(2)]
        value[0] = jnp.concatenate(lines + [vectors_ref[...]])
        leaves = fetch(
            (folds[0].done, folds[4].done, folds[1].done, folds[2].done, folds[3].done, value.at[5], ggrad),
            (inner_o, out_o, queries_o, keys_o, outer_o, small_o, ggrad_o), local, 12 + row_count,
        )
        ready = {(0, 7): 0, (4, 7): 1, (1, 7): 2, (2, 7): 3, (3, 7): 4, (7, 5): 5, (6, 3): 6}
        leaves[4].start()
        for f, n in REAR_END:
            if f == 5:
                move_spread(n)
                if n == 2:
                    own_globals()
            elif f == 6:
                gather.stage(n)
            elif f == 7:
                small.stage(n)
            else:
                folds[f].stage(n)
            if (f, n) in ready:
                leaves[ready[f, n]].start()
        for fold in folds:
            fold.finish()
        gather.finish()
        small.finish()
        spread.sent()
        for r in range(row_count):
            keep(r).wait()
            home(r).wait()
        for copy in leaves:
            copy.wait()


def rear(
    qkv, grad, lse, delta, kaug, inputs, next_x, res_grad, global_grad, global_lse, global_delta, own_res, normed,
    globals_in, weight, gain, vectors, outer_ab, outer_c, inner, out, half, count,
):
    row_count, rows, cols = qkv.shape
    width = cols // 3
    pairs = width // LANES
    block_len = 2 * half
    global_count = rows - block_len
    share = global_count // count
    part = width // count
    scale = (width // HEADS) ** (-0.5)
    attn = row_count * pairs
    f32, bf16 = jnp.float32, jnp.bfloat16
    turn = lambda t: jnp.where(t < pairs, t, jnp.clip(t - 2, pairs, attn - 1))
    row_of = lambda t: turn(t) // pairs
    pair_of = lambda t: turn(t) % pairs
    spec = lambda off: pl.BlockSpec((1, rows, LANES), lambda t: (row_of(t), 0, off + pair_of(t)))
    whole = pl.BlockSpec((1, rows, LANES), lambda t: (row_of(t), 0, 0))

    def tile_of(t):
        (a, _, _), (b, _, _), (c, _, _), _ = TILE_AT
        return jnp.where(t <= a, 1, jnp.where(t <= b, 0, jnp.where(t <= c, 3, 2))), 0

    tile = pl.BlockSpec((half, width), tile_of)
    hbm = pl.BlockSpec(memory_space=pl.ANY)
    outs = [
        jax.ShapeDtypeStruct((row_count, block_len, width), bf16),
        jax.ShapeDtypeStruct((row_count, 2, 2, 2, share, width), bf16),
        jax.ShapeDtypeStruct((2, 2 * part, width), bf16),
        jax.ShapeDtypeStruct((2, LONE, width), bf16),
        jax.ShapeDtypeStruct((2, LONE, width), bf16),
        jax.ShapeDtypeStruct((2, part, width), bf16),
        jax.ShapeDtypeStruct((2, 2 * part, width), bf16),
        jax.ShapeDtypeStruct((8, width), f32),
    ]
    folds, sizes = [], []
    for size, pieces in ((2 * part, 2), (LONE, 1), (part, 2)):
        refs = Fold.scratch(size, width, pieces)
        folds += refs
        sizes.append(len(refs))
    for refs in (Fold.scratch(2 * part, width, 0, False, Fold.LATE), Fold.scratch(LONE, width, 1)):
        folds += refs
        sizes.append(len(refs))
    vmem = pltpu.VMEM
    kinds = 4 + row_count
    early = (global_grad, global_lse, global_delta)
    later = (own_res, globals_in, weight, gain, vectors, normed)
    return pl.pallas_call(
        functools.partial(rear_kernel, half, scale, pairs, tuple(sizes)),
        grid=(LAST + 1,),
        in_specs=[spec(0), spec(pairs), spec(2 * pairs)]
        + [pl.BlockSpec((block_len, LANES), lambda t: (row_of(t), pair_of(t)))]
        + [pl.BlockSpec((1, block_len, LANES), lambda t: (row_of(t), 0, 0))]
        + [pl.BlockSpec((block_len, LANES), lambda t: (row_of(t), 0)), whole]
        + [
            pl.BlockSpec((1, half, width), lambda t: (jnp.where(t <= TILE_AT[1][0], 0, 1), 1, 0)),
            pl.BlockSpec((1, half, width), lambda t: (jnp.where(t <= TILE_AT[0][0], 0, 1), 0, 0)),
            tile,
        ]
        + [hbm] * 13,
        out_specs=[hbm] * 8,
        out_shape=outs,
        scratch_shapes=[vmem(a.shape if a.ndim > 1 else (1, *a.shape), a.dtype) for a in early + later]
        + [
            vmem((row_count, rows, cols), bf16),
            vmem((2, 2, 2, row_count * share, width), bf16),
            vmem((2, 8, width), f32),
            vmem((3, 2, 2, 2, 2, part // 2, width), bf16),
            vmem((2, row_count, half, width), bf16),
            vmem((row_count, 2, 2, 2, share, width), bf16),
            vmem((6, 8, width), f32),
            vmem((5, 8, width), f32),
            pltpu.SemaphoreType.DMA((kinds, 5)),
            pltpu.SemaphoreType.DMA((kinds, 5)),
            pltpu.SemaphoreType.DMA((20 + row_count,)),
        ]
        + folds
        + Halve.buffers(row_count * share, width, ("x", "z0", "z1")),
        compiler_params=pltpu.CompilerParams(
            collective_id=9, has_side_effects=True, vmem_limit_bytes=64 * 1024 * 1024
        ),
        name="rear",
    )(
        qkv, qkv, qkv, grad, lse, delta, kaug, inputs, next_x, res_grad, *early, outer_ab, outer_c, *later,
        share_views(inner, count), half_views(out, count),
    )


def cdf_bell(v):
    bell = jnp.exp(-0.5 * v * v)
    t = 1.0 / (1.0 + (0.3275911 * 0.5 ** 0.5) * jnp.abs(v))
    poly = t * (
        0.127414796 + t * (-0.142248368 + t * (0.7107068705 + t * (-0.7265760135 + t * 0.5307027145)))
    )
    tail = poly * bell
    return jnp.where(v < 0, tail, 1.0 - tail), bell


STRIPS_FROM, BACK_FROM = 4, 8
MID_TICKS = {8: 0, 9: 1, 13: 2}
MID_GATHERS = {6: (0, 1), 8: (0, 2), 11: (0, 3), 10: (1, 1), 12: (1, 2), 15: (1, 3)}


def mid_kernel(
    half, fold_refs,
    lengths, x_ref, next_x_ref, mixed_ref, cot_ref, next_cot_ref, gain_in, shift_in, bias_in, out_in, inner_in, outer_in, gx_in, gcot_in,
    mixed_all, lse_all,
    layer_o, res_o, grad_o, delta_o, gres_o, gout_o, ggrad_o, glse_o, gdelta_o, inner_o, outer_ab_o, outer_c_o, out_o,
    vectors_o,
    gain_ref, shift_ref, bias_ref, out_w, inner_w, outer_w, gx_ref, gcot_ref, heads_ref,
    hidden, slope, normed, cot, att, proj, residual, outer_src, sums, bias_sums, layers,
    gout, ggrad, glse, gdelta, part_mixed, part_lse, send, recv, local, *scratch,
):
    f32, bf16 = jnp.float32, jnp.bfloat16
    step = pl.program_id(0)
    place = Place()
    me = lax.axis_index("seq")
    count = lax.axis_size("seq")
    row_count, share = gx_ref.shape[:2]
    block_len = 2 * half
    tokens = row_count * block_len
    own_rows = row_count * share
    width = gx_ref.shape[2]
    strips = inner_w.shape[1] // width
    tiles = 2 * row_count
    fold = Fold(place, None, scratch, outer_src, Fold.EARLY)
    held = pl.ds(pl.multiple_of(share * me, 16), share)
    following = {"seq": lax.rem(me + 1, count)}
    at = tuple(place[axis] for axis, _ in SEQ_BITS)

    def parts(m, to, r, n):
        rows = pl.ds(pl.multiple_of(block_len + share * to, 16), share)
        return (
            (mixed_all.at[r, rows], part_mixed.at[m, r]) if n == 0 else (lse_all.at[r, rows], part_lse.at[m, r])
        )

    def part_copies():
        copies = []
        for r in range(row_count):
            for n in range(2):
                for other in range(1, count):
                    to = lax.rem(me + other, count)
                    src, dst = parts(me, to, r, n)
                    sems = send.at[2 * r + n, other], recv.at[2 * r + n, other]
                    copies.append(remote(src, dst, *sems, {"seq": to}))
        return copies

    def part_own():
        return [
            pltpu.make_async_copy(*parts(me, me, r, n), local.at[2 * r + n]) for r in range(row_count) for n in range(2)
        ]

    base = 2 * row_count
    gathers = [
        Gather(place, buf, send.at[base + n], recv.at[base + n]) for n, buf in enumerate((gout, ggrad, glse, gdelta))
    ]
    leaves = lambda: fetch((gout, ggrad, glse, gdelta), (gout_o, ggrad_o, glse_o, gdelta_o), local, base)
    ends = base + 4

    def home(r):
        return remote(layers.at[1, r], layer_o.at[r, pl.ds(0, half)], send.at[ends, r], recv.at[ends, r], following)

    def keep(r):
        return pltpu.make_async_copy(layers.at[0, r], layer_o.at[r, pl.ds(half, half)], local.at[ends + r])

    loads = lambda: fetch(
        (gain_in, shift_in, bias_in, out_in, inner_in, outer_in, gx_in.at[:, held], gcot_in.at[:, held]),
        (gain_ref.at[0], shift_ref.at[0], bias_ref.at[0], out_w, inner_w, outer_w, gx_ref, gcot_ref), local, ends + row_count,
    )

    @pl.when(step == 0)
    def _():
        begin(loads())
        place.greet([{"seq": lax.rem(me + other, count)} for other in range(1, count)])
        begin(part_own() + part_copies())
        lane = lax.broadcasted_iota(jnp.int32, (width, LANES), 1)
        head = lax.div(lax.broadcasted_iota(jnp.int32, (width, LANES), 0), width // HEADS)
        chosen = jnp.where(lane < 3 * HEADS, lax.rem(lane, HEADS), -1) == head
        heads_ref[...] = jnp.where(chosen, 1.0, 0.0).astype(bf16)
        sums[...] = jnp.zeros_like(sums)
        bias_sums[...] = jnp.zeros_like(bias_sums)
        for copy in loads():
            copy.wait()

    def stats(values):
        centred = values - jnp.mean(values, axis=-1, keepdims=True)
        inv = lax.rsqrt(jnp.mean(centred * centred, axis=-1, keepdims=True) + EPS)
        return centred * inv, inv

    def forward(x, attended, rows, unroll=True):
        att[rows] = attended
        total = x.astype(f32) + nn(attended, out_w[...])
        residual[rows] = total
        n, _ = stats(total)
        second = (n * gain_ref[...] + shift_ref[...]).astype(bf16)
        normed[rows] = second

        def run(j, total):
            strip = pl.ds(pl.multiple_of(j * width, width), width)
            inner = nn(second, inner_w[:, strip]) + bias_ref[:, strip]
            cdf, bell = cdf_bell(inner)
            active = (inner * cdf).astype(bf16)
            hidden[rows, strip] = active
            slope[rows, strip] = (cdf + inner * bell * ((0.5 / math.pi) ** 0.5)).astype(bf16)
            return total + nn(active, outer_w[strip, :])

        return lax.fori_loop(0, strips, run, total, unroll=unroll)

    def backward(cotangent, rows, unroll=True):
        def run(j, total):
            strip = pl.ds(pl.multiple_of(j * width, width), width)
            grad = (nt(cotangent, outer_w[strip, :]) * slope[rows, strip].astype(f32)).astype(bf16)
            slope[rows, strip] = grad
            bias_sums[j] += sum_rows(grad.astype(f32))
            return total + nt(grad, inner_w[:, strip])

        second_grad = lax.fori_loop(0, strips, run, jnp.zeros(cotangent.shape, f32), unroll=unroll)
        n, inv = stats(residual[rows])
        eg = second_grad * gain_ref[...]
        through = (eg - jnp.mean(eg, axis=-1, keepdims=True) - n * jnp.mean(eg * n, axis=-1, keepdims=True)) * inv
        sums[0] += sum_rows(second_grad * n)
        sums[1] += sum_rows(second_grad)
        res = cotangent.astype(f32) + through
        projected = res.astype(bf16)
        proj[rows] = projected
        grad = nt(projected, out_w[...]).astype(bf16)
        product = grad.astype(f32) * att[rows].astype(f32)
        top = product.astype(bf16)
        rest = (product - top.astype(f32)).astype(bf16)
        return res, grad, nn(top, heads_ref[...]) + nn(rest, heads_ref[...])

    def turn(n):
        return lax.div(n, 2), jnp.where(n == 0, 1, 0)

    def is_valid(r, h):
        owner = lax.rem(me + h, count)
        spot = owner * block_len + (1 - h) * half + lax.broadcasted_iota(jnp.int32, (half, width), 0)
        return spot < lengths[r]

    @pl.when(step < tiles - 1)
    def _():
        r, h = turn(step)
        rows = pl.ds(pl.multiple_of((2 * r + h) * half, half), half)
        valid = is_valid(r, h)
        pick = lambda a, b: jnp.where(h == 0, a[0].astype(f32), b[0].astype(f32))
        cot[rows] = jnp.where(valid, pick(cot_ref, next_cot_ref), 0.0).astype(bf16)
        final = forward(pick(x_ref, next_x_ref), mixed_ref[0], rows)
        layers[h, r] = jnp.where(valid, final, 0.0).astype(bf16)

    back = step - (BACK_FROM + 1)

    @pl.when((back >= 0) & (back < tiles - 1))
    def _():
        r, h = turn(back)
        rows = pl.ds(pl.multiple_of((2 * r + h) * half, half), half)
        res, grad, delta = backward(cot[rows], rows)
        res_o[...] = res
        grad_o[...] = grad
        delta_o[...] = delta

    last_row = row_count - 1
    joint = pl.ds(tokens - half, half + own_rows)

    @pl.when(step == tiles - 1)
    def _():
        for copy in part_own():
            copy.wait()
        for copy in part_copies():
            copy.wait_recv()
        peak = jnp.max(part_lse[...], axis=0)
        shares = jnp.exp(part_lse[...] - peak)
        total = jnp.sum(shares, axis=0)
        lse = peak + jnp.log(total)
        glse[(slice(None), *at)] = lse
        shares = (shares / total).reshape(count * own_rows, LANES)
        lane = lax.broadcasted_iota(jnp.int32, shares.shape, 1)
        shares = jnp.where(lane < HEADS, shares, 0.0)
        top = shares.astype(bf16)
        rest = (shares - top.astype(f32)).astype(bf16)
        wide = nt(top, heads_ref[...]) + nt(rest, heads_ref[...])
        mixed = wide * part_mixed[...].reshape(count * own_rows, width).astype(f32)
        mixed = jnp.sum(mixed.reshape(count, own_rows, width), axis=0).astype(bf16)
        valid = is_valid(last_row, 1)
        local_cot = jnp.where(valid, next_cot_ref[0].astype(f32), 0.0).astype(bf16)
        cot[joint] = jnp.concatenate([local_cot, gcot_ref[...].reshape(own_rows, width)], axis=0)
        x = jnp.concatenate([next_x_ref[0], gx_ref[...].reshape(own_rows, width)], axis=0)
        final = forward(x, jnp.concatenate([mixed_ref[0], mixed], axis=0), joint, False)
        layers[1, last_row] = jnp.where(valid, final[:half], 0.0).astype(bf16)
        gout[(slice(None), *at)] = final[half:].astype(bf16).reshape(row_count, share, width)
        gathers[0].stage(0)

    @pl.when(step == 0)
    def _():
        home(0).start()

    for t, h, r in ((1, 0, 0), (2, 0, 1), (3, 1, 1)):

        @pl.when(step == t)
        def _():
            (home if h else keep)(r).start()

    strip_at = step - STRIPS_FROM

    @pl.when((strip_at >= 0) & (strip_at < strips))
    def _():
        strip = pl.ds(pl.multiple_of(strip_at * width, width), width)
        grad = tn(hidden[:, strip], cot[...]).astype(bf16)
        outer_src[lax.div(strip_at, 2), lax.rem(strip_at, 2)] = grad.reshape(outer_src.shape[2:])

    for t, (kind, n) in MID_GATHERS.items():

        @pl.when(step == t)
        def _():
            chosen = range(1, 4) if kind else range(1)
            for g in chosen:
                gathers[g].stage(n)
                if n == 3:
                    leaves()[g].start()

    for t, n in MID_TICKS.items():

        @pl.when(step == t)
        def _():
            fold.stage(n)

    after = BACK_FROM + tiles

    @pl.when(step == BACK_FROM)
    def _():
        res, grad, delta = backward(cot[joint], joint, False)
        res_o[...], gres_o[...] = res[:half], res[half:].reshape(row_count, share, width)
        grad_o[...], delta_o[...] = grad[:half], delta[:half]
        ggrad[(slice(None), *at)] = grad[half:].reshape(row_count, share, width)
        gdelta[(slice(None), *at)] = delta[half:].reshape(row_count, share, LANES)
        for gather in gathers[1:]:
            gather.stage(0)

    inner_at = step - after

    @pl.when((inner_at >= 0) & (inner_at < strips))
    def _():
        strip = pl.ds(pl.multiple_of(inner_at * width, width), width)
        inner_o[0] = tn(normed[...], slope[:, strip]).astype(bf16)

    @pl.when(step == after + strips)
    def _():
        out_o[...] = tn(att[...], proj[...]).astype(bf16)
        lines = [jnp.sum(sums[n], axis=0, keepdims=True) for n in range(2)]
        lines += [jnp.sum(bias_sums[n], axis=0, keepdims=True) for n in range(strips)]
        vectors_o[...] = jnp.concatenate(lines)
        for part in fold.parts:
            part.finish(1)
        first, second = fold.held()
        outer_ab_o[...] = fold.own[first]
        outer_c_o[...] = fold.own[second]
        fold.finish()
        for gather in gathers:
            gather.finish()
        for copy in part_copies():
            copy.wait_send()
        for r in range(row_count):
            keep(r).wait()
            home(r).wait()
        for copy in leaves():
            copy.wait()


def mid(
    lengths, inputs, next_x, mixed, lse, cotangent, next_cot, globals_in, global_cot, out_weight, inner_weight, outer_weight, bias, gain, shift,
    half, count,
):
    f32, bf16 = jnp.float32, jnp.bfloat16
    row_count, rows, width = mixed.shape
    block_len = 2 * half
    share = (rows - block_len) // count
    own_rows = row_count * share
    inner_width = inner_weight.shape[1]
    strips = inner_width // width
    part = width // count
    tiles = 2 * row_count
    total = row_count * block_len + own_rows

    def flat(cols):
        def index(t):
            n = t - BACK_FROM
            return jnp.where(n <= 0, 3, jnp.where(n == 1, 1, jnp.where(n == 2, 0, 2))), 0

        return pl.BlockSpec((half, cols), index)

    own_spec = pl.BlockSpec((1, half, width), lambda t: (jnp.where(t <= 1, 0, 1), 1, 0))
    next_spec = pl.BlockSpec((1, half, width), lambda t: (jnp.where(t <= 0, 0, 1), 0, 0))
    whole = lambda *shape: pl.BlockSpec(shape, lambda t: (0,) * len(shape))
    hbm = pl.BlockSpec(memory_space=pl.ANY)
    fixeds = (gain, shift, bias, out_weight, inner_weight, outer_weight, globals_in, global_cot)
    shared = (row_count, 2, 2, 2, share)
    after = BACK_FROM + tiles
    of = jax.ShapeDtypeStruct
    outs = [
        of((row_count, block_len, width), bf16),
        of((row_count * block_len, width), f32),
        of((row_count * block_len, width), bf16),
        of((row_count * block_len, LANES), f32),
        of((row_count, share, width), f32),
        of((*shared, width), bf16),
        of((*shared, width), bf16),
        of((*shared, LANES), f32),
        of((*shared, LANES), f32),
        of((strips, width, width), bf16),
        of((2, 2, strips * part // 4, 640), bf16),
        of((2, strips * part // 2, 128), bf16),
        of((width, width), bf16),
        of((2 + strips, width), f32),
    ]
    vmem = pltpu.VMEM
    fold = Fold.scratch(strips * part // 2, width, 1, True, Fold.EARLY)
    kinds = 2 * row_count + 5
    return pl.pallas_call(
        functools.partial(mid_kernel, half, len(fold)),
        grid=(after + strips + 1,),
        in_specs=[
            pl.BlockSpec(memory_space=pltpu.SMEM),
            own_spec,
            next_spec,
            pl.BlockSpec((1, half, width), lambda t: (jnp.where(t <= 1, 0, 1), jnp.where((t == 0) | (t >= 3), 1, 0), 0)),
            own_spec,
            next_spec,
        ]
        + [hbm] * (len(fixeds) + 2),
        out_specs=[
            hbm,
            flat(width),
            flat(width),
            flat(LANES),
            whole(row_count, share, width),
            hbm,
            hbm,
            hbm,
            hbm,
            pl.BlockSpec((1, width, width), lambda t: (jnp.clip(t - after, 0, strips - 1), 0, 0)),
            whole(*outs[10].shape),
            whole(*outs[11].shape),
            whole(width, width),
            whole(2 + strips, width),
        ],
        out_shape=outs,
        scratch_shapes=[vmem((1, a.shape[0]), f32) for a in fixeds[:3]]
        + [vmem(a.shape, bf16) for a in fixeds[3:6]]
        + [vmem((row_count, share, width), bf16)] * 2
        + [
            vmem((width, LANES), bf16),
            vmem((total, inner_width), bf16),
            vmem((total, inner_width), bf16),
            vmem((total, width), bf16),
            vmem((total, width), bf16),
            vmem((total, width), bf16),
            vmem((total, width), bf16),
            vmem((total, width), f32),
            vmem((2, 2, 2, 2, strips * part // 2, width), bf16),
            vmem((2, 8, width), f32),
            vmem((strips, 8, width), f32),
            vmem((2, row_count, half, width), bf16),
            vmem((*shared, width), bf16),
            vmem((*shared, width), bf16),
            vmem((*shared, LANES), f32),
            vmem((*shared, LANES), f32),
            vmem((count, row_count, share, width), bf16),
            vmem((count, row_count, share, LANES), f32),
            pltpu.SemaphoreType.DMA((kinds, count)),
            pltpu.SemaphoreType.DMA((kinds, count)),
            pltpu.SemaphoreType.DMA((kinds + row_count + len(fixeds),)),
        ]
        + fold,
        compiler_params=pltpu.CompilerParams(
            collective_id=10, has_side_effects=True, vmem_limit_bytes=64 * 1024 * 1024
        ),
        name="mid",
    )(lengths, inputs, next_x, mixed, cotangent, next_cot, *fixeds, mixed, lse)


def key_marks(me, count, length, half, rows):
    lane = lax.broadcasted_iota(jnp.int32, (rows, LANES), 1)
    row = lax.broadcasted_iota(jnp.int32, (rows, LANES), 0)
    kind = lane - TYPE0
    side = jnp.where(row < half, 0, 1)
    owner = lax.rem(me + side, count)
    position = owner * (2 * half) + jnp.where(row < half, row + half, row - half)
    apart = (me == count - 1) & (kind < 2) & (kind != side)
    of_token = jnp.where((position >= length) | apart, NEG, 0.0)
    of_global = jnp.where((kind == 2) & (me != 0), NEG, 0.0)
    marks = jnp.where(row < 2 * half, of_token, of_global)
    return jnp.where((kind >= 0) & (kind < 3), marks, 0.0).astype(jnp.bfloat16)


def head_kernel(
    half, scale, pairs, tq,
    lengths, inputs, cotangent, globals_in, gain_in, shift_in, weight_in,
    next_x, next_cot, qkv_o, mixed_o, lse_o, normed_o, kaug_o,
    gain, shift, weight, xs, qkv, mixed, lse, normed, kaug, send, recv, local,
):
    bf16, f32 = jnp.bfloat16, jnp.float32
    step = pl.program_id(0)
    me, count = lax.axis_index("seq"), lax.axis_size("seq")
    row_count, rows, width = xs.shape
    block_len = 2 * half
    previous = {"seq": lax.rem(me + count - 1, count)}
    following = {"seq": lax.rem(me + 1, count)}
    lower, upper, tail = pl.ds(0, half), pl.ds(half, half), pl.ds(block_len, rows - block_len)
    turns = [row_count + 1 + r * (pairs + 1) for r in range(row_count)]

    def arrive(r):
        return remote(inputs.at[r, lower], xs.at[r, upper], send.at[0, r], recv.at[0, r], previous)

    def arrive_cot(r):
        return remote(cotangent.at[r, lower], next_cot.at[r], send.at[1, r], recv.at[1, r], previous)

    def loads():
        own = [(inputs.at[r, upper], xs.at[r, lower]) for r in range(row_count)]
        own += [(globals_in.at[r], xs.at[r, tail]) for r in range(row_count)]
        own += [(gain_in, gain.at[0]), (shift_in, shift.at[0]), (weight_in, weight)]
        return fetch(*zip(*own), local)

    def leaves(r):
        pairs_of = ((qkv, qkv_o), (mixed, mixed_o), (lse, lse_o), (normed, normed_o), (kaug, kaug_o))
        moved = [(a.at[r], b.at[r]) for a, b in pairs_of] + [(xs.at[r, upper], next_x.at[r])]
        return fetch(*zip(*moved), local, 16 + 8 * r)

    def project(x):
        x = x.astype(f32)
        centred = x - jnp.mean(x, axis=-1, keepdims=True)
        inv = lax.rsqrt(jnp.mean(centred * centred, axis=-1, keepdims=True) + EPS)
        n = (centred * inv * gain[...] + shift[...]).astype(bf16)
        return n, nn(n, weight[...]).astype(bf16)

    @pl.when(step == 0)
    def _():
        begin(loads())
        barrier = pltpu.get_barrier_semaphore()
        for to in (previous, following):
            pl.semaphore_signal(barrier, inc=1, device_id=to, device_id_type=MESH_ID)
        pl.semaphore_wait(barrier, 2)
        arrive(0).start()
        for r in range(row_count):
            kaug[r] = key_marks(me, count, lengths[r], half, rows)
        for copy in loads():
            copy.wait()

    for r in range(row_count):

        @pl.when(step == turns[r])
        def _():
            arrive(r).wait_recv()
            if r + 1 < row_count:
                arrive(r + 1).start()

    first = turns[0]
    is_turn = functools.reduce(jnp.logical_or, [step == t for t in turns])

    @pl.when((step < row_count) | is_turn)
    def _():
        h = jnp.where(step < row_count, 0, 1)
        r = jnp.where(step < row_count, step, lax.div(step - first, pairs + 1))
        spot = pl.ds(pl.multiple_of(h * half, half), half)
        normed[r, spot], qkv[r, spot] = project(xs[r, spot])

    @pl.when(step == row_count)
    def _():
        n, p = project(jnp.concatenate([xs[r, tail] for r in range(row_count)], axis=0))
        many = rows - block_len
        for r in range(row_count):
            normed[r, tail] = n[r * many:(r + 1) * many]
            qkv[r, tail] = p[r * many:(r + 1) * many]

    @pl.when(step == first + 4)
    def _():
        begin([arrive_cot(r) for r in range(row_count)])

    @pl.when((step > first) & jnp.logical_not(is_turn))
    def _():
        r, p = lax.div(step - first, pairs + 1), lax.rem(step - first, pairs + 1) - 1
        lane = lambda j: pl.ds(pl.multiple_of(j * width + p * LANES, LANES), LANES)
        row = pl.ds(r, 1)
        attend_kernel(
            half, scale, tq, p, qkv.at[row, :, lane(0)], qkv.at[row, :, lane(1)], qkv.at[row, :, lane(2)], kaug.at[row],
            mixed.at[row, :, lane(0)], lse.at[row],
        )

    for r in range(row_count):

        @pl.when(step == turns[r] + pairs)
        def _():
            begin(leaves(r))

    @pl.when(step == turns[-1] + pairs)
    def _():
        for r in range(row_count):
            for copy in leaves(r):
                copy.wait()
            arrive(r).wait_send()
            arrive_cot(r).wait()


def head(lengths, inputs, cotangent, globals_in, gain, shift, weight, tq):
    bf16, f32 = jnp.bfloat16, jnp.float32
    row_count, block_len, width = inputs.shape
    half = block_len // 2
    rows = block_len + globals_in.shape[1]
    pairs = width // LANES
    scale = (width // HEADS) ** (-0.5)
    hbm = pl.BlockSpec(memory_space=pl.ANY)
    of, vmem = jax.ShapeDtypeStruct, pltpu.VMEM
    results = [
        ((row_count, rows, 3 * width), bf16),
        ((row_count, rows, width), bf16),
        ((row_count, rows, LANES), f32),
        ((row_count, rows, width), bf16),
        ((row_count, rows, LANES), bf16),
    ]
    return pl.pallas_call(
        functools.partial(head_kernel, half, scale, pairs, tq),
        grid=(row_count + 1 + row_count * (pairs + 1),),
        in_specs=[pl.BlockSpec(memory_space=pltpu.SMEM)] + [hbm] * 6,
        out_specs=[hbm] * 7,
        out_shape=[of((row_count, half, width), bf16)] * 2 + [of(*r) for r in results],
        scratch_shapes=[
            vmem((1, width), f32),
            vmem((1, width), f32),
            vmem(weight.shape, bf16),
            vmem((row_count, rows, width), bf16),
        ]
        + [vmem(*r) for r in results]
        + [
            pltpu.SemaphoreType.DMA((2, row_count)),
            pltpu.SemaphoreType.DMA((2, row_count)),
            pltpu.SemaphoreType.DMA((16 + 8 * row_count,)),
        ],
        compiler_params=pltpu.CompilerParams(
            collective_id=11, has_side_effects=True, vmem_limit_bytes=60 * 1024 * 1024
        ),
        name="head",
    )(lengths, inputs, cotangent, globals_in, gain, shift, weight)


def wgrad_kernel(a_ref, b_ref, o_ref):
    o_ref[...] = tn(a_ref[...], b_ref[...]).astype(o_ref.dtype).reshape(o_ref.shape)


def wgrad(a, b, strip):
    rows, a_cols = a.shape
    b_cols = b.shape[1]
    split_a = a_cols > b_cols
    strips = max(a_cols, b_cols) // strip
    fixed = lambda n: (0, 0)
    moving = lambda n: (0, n)
    return pl.pallas_call(
        wgrad_kernel,
        grid=(strips,),
        in_specs=[
            pl.BlockSpec((rows, strip), moving if split_a else fixed),
            pl.BlockSpec((rows, strip), fixed if split_a else moving),
        ],
        out_specs=pl.BlockSpec((1, strip, strip), lambda n: (n, 0, 0)),
        out_shape=jax.ShapeDtypeStruct((strips, strip, strip), jnp.bfloat16),
        compiler_params=pltpu.CompilerParams(vmem_limit_bytes=40 * 1024 * 1024),
        name="wgrad",
    )(a, b)


def norm_parts(values):
    average = jnp.mean(values, axis=-1, keepdims=True)
    centred = values - average
    variance = jnp.mean(centred * centred, axis=-1, keepdims=True)
    inv = lax.rsqrt(variance + EPS)
    return centred * inv, inv


def norm_back(grad, n, inv, gain):
    eg = grad * gain
    through = (
        eg - jnp.mean(eg, axis=-1, keepdims=True) - n * jnp.mean(eg * n, axis=-1, keepdims=True)
    ) * inv
    return through, jnp.sum(grad * n, axis=0), jnp.sum(grad, axis=0)


def split_rows(a, count):
    row_count, rows, width = a.shape
    part = rows // count
    moved = a.reshape(row_count, count, part, width).transpose(1, 0, 2, 3)
    return moved.reshape(count, row_count * part, width)


def join_rows(a, row_count):
    count, rows, width = a.shape
    part = rows // row_count
    moved = a.reshape(count, row_count, part, width).transpose(1, 0, 2, 3)
    return moved.reshape(row_count, count * part, width)


def per_head(values, width):
    lanes = values[..., :HEADS]
    return jnp.repeat(lanes, width // HEADS, axis=-1)


def head_sums(values):
    rows, width = values.shape
    lane = jnp.arange(LANES)
    head = jnp.arange(width) // (width // HEADS)
    place = ((lane[None, :] % HEADS == head[:, None]) & (lane[None, :] < 3 * HEADS)).astype(jnp.bfloat16)
    top = values.astype(jnp.bfloat16)
    rest = (values - top.astype(jnp.float32)).astype(jnp.bfloat16)
    return nn(top, place) + nn(rest, place)


def reduce_share(a):
    a = lax.psum_scatter(a, "seq", scatter_dimension=0, tiled=True)
    return lax.psum(a.astype(jnp.bfloat16), "batch").astype(jnp.float32)


def body(
    inputs,
    global_inputs,
    lengths,
    first_gain,
    first_shift,
    qkv_weight,
    out_weight,
    second_gain,
    second_shift,
    inner_weight,
    inner_bias,
    outer_weight,
    output_cotangent,
    global_cotangent,
):
    f32, bf16 = jnp.float32, jnp.bfloat16
    row_count, block_len, width = inputs.shape
    half = block_len // 2
    global_count = global_inputs.shape[1]
    rows = block_len + global_count
    inner_width = inner_weight.shape[1]
    count = lax.axis_size("seq")
    me = lax.axis_index("seq")
    after = lax.rem(me + 1, count)
    back = [(i, (i - 1) % count) for i in range(count)]
    forth = [(i, (i + 1) % count) for i in range(count)]
    token_rows = row_count * block_len
    share = global_count // count
    own_rows = row_count * share

    if count == 8 and lax.axis_size("batch") == 4:
        next_x, next_cot, qkv, mixed, lse, normed, kaug = head(
            lengths, inputs, output_cotangent, global_inputs, first_gain, first_shift, qkv_weight, 320
        )
        (
            layer_output, residual_grad, block_grad, block_delta, own_res, global_out, global_grad, global_lse, global_delta,
            inner_wgrad, outer_ab, outer_c, out_grad, vectors,
        ) = mid(
            lengths, inputs, next_x, mixed, lse, output_cotangent, next_cot, global_inputs, global_cotangent, out_weight, inner_weight,
            outer_weight, inner_bias, second_gain, second_shift, half, count,
        )
        input_out, global_grad, *reduced = rear(
            qkv, block_grad, lse, block_delta, kaug, inputs, next_x, residual_grad, global_grad, global_lse, global_delta,
            own_res, normed, global_inputs, qkv_weight, first_gain, vectors, outer_ab, outer_c, inner_wgrad,
            out_grad, half, count,
        )
        joined = lambda a: a.reshape(row_count, global_count, width)
        inner_out, outer_out, out_out, qkv_out, *lines, layer_output, input_out, global_out, global_grad = finish(
            *reduced, layer_output, input_out, joined(global_out), joined(global_grad)
        )
        fg, fs, sg, ss, bias = lines
        return (
            layer_output, global_out, input_out, global_grad, fg, fs, qkv_out, out_out, sg, ss, inner_out, bias, outer_out,
        )

    own_globals = lax.dynamic_slice_in_dim(global_inputs, me * share, share, axis=1)
    own_global_cot = lax.dynamic_slice_in_dim(global_cotangent, me * share, share, axis=1)
    next_inputs = lax.ppermute(inputs[:, :half], "seq", back)
    next_cotangent = lax.ppermute(output_cotangent[:, :half], "seq", back)
    block = jnp.concatenate([inputs[:, half:], next_inputs], axis=1)
    spots = jnp.arange(half, dtype=jnp.int32)
    positions = jnp.concatenate([me * block_len + half + spots, after * block_len + spots])
    valid = positions[None, :] < lengths[:, None]

    kind = jnp.arange(LANES)[None, None, :] - TYPE0
    key_half = (jnp.arange(block_len) // half)[None, :, None]
    last = me == count - 1
    hidden_key = jnp.logical_not(valid)[:, :, None] | (last & (kind < 2) & (kind != key_half))
    token_marks = jnp.where(hidden_key & (kind >= 0) & (kind < 3), NEG, 0.0)
    global_marks = jnp.where((kind == 2) & (me != 0), NEG, 0.0)
    global_marks = jnp.broadcast_to(global_marks, (row_count, global_count, LANES))
    kaug = jnp.concatenate([token_marks, global_marks], axis=1).astype(bf16)

    states = jnp.concatenate([block, global_inputs], axis=1)
    n_first, inv_first = norm_parts(states.astype(f32))
    normed = (n_first * first_gain + first_shift).astype(bf16)
    qkv = nn(normed.reshape(row_count * rows, width), qkv_weight).astype(bf16)
    qkv = qkv.reshape(row_count, rows, 3 * width)

    mixed, lse = attend(qkv, kaug, half)
    tokens_in = block.reshape(token_rows, width)
    cot_block = jnp.concatenate([output_cotangent[:, half:], next_cotangent], axis=1)
    part_mixed, part_lse = spread(
        [split_rows(mixed[:, block_len:], count), split_rows(lse[:, block_len:], count)], count, False, 0
    )
    highest = jnp.max(part_lse, axis=0)
    part_weight = jnp.exp(part_lse - highest)
    total = jnp.sum(part_weight, axis=0)
    global_lse = highest + jnp.log(total)
    global_mixed = jnp.sum(per_head(part_weight / total, width) * part_mixed.astype(f32), axis=0)

    tokens = jnp.concatenate([tokens_in, own_globals.reshape(own_rows, width)]).astype(f32)
    cot_block = jnp.where(valid[:, :, None], cot_block, 0)
    cotangent = jnp.concatenate(
        [cot_block.reshape(token_rows, width), own_global_cot.reshape(own_rows, width)]
    )
    attended = jnp.concatenate(
        [mixed[:, :block_len].reshape(token_rows, width), global_mixed.astype(bf16)]
    )
    residual = tokens + nn(attended, out_weight)
    n_second, inv_second = norm_parts(residual)
    normed_second = (n_second * second_gain + second_shift).astype(bf16)
    inner = nn(normed_second, inner_weight) + inner_bias
    bell = jnp.exp(-0.5 * inner * inner)
    cdf = 0.5 * (1.0 + lax.erf(inner * (0.5 ** 0.5)))
    hidden = (inner * cdf).astype(bf16)
    final = residual + nn(hidden, outer_weight)
    hidden_grad = nt(cotangent, outer_weight)
    slope = cdf + inner * bell * ((0.5 / jnp.pi) ** 0.5)
    inner_grad = (hidden_grad * slope).astype(bf16)
    second_grad = nt(inner_grad, inner_weight)
    through, second_gain_grad, second_shift_grad = norm_back(second_grad, n_second, inv_second, second_gain)
    residual_grad = cotangent.astype(f32) + through
    projection_grad = residual_grad.astype(bf16)
    attended_grad = nt(projection_grad, out_weight).astype(bf16)
    delta = head_sums(attended_grad.astype(f32) * attended.astype(f32))
    outer_grad = wgrad(hidden, cotangent, width)
    inner_wgrad = wgrad(normed_second, inner_grad, width)
    bias_grad = jnp.sum(inner_grad.astype(f32), axis=0)
    out_grad = wgrad(attended, projection_grad, width)

    all_grad, all_lse, all_delta = spread(
        [attended_grad[token_rows:], global_lse, delta[token_rows:]], count, True, 1
    )
    block_grad = jnp.concatenate(
        [attended_grad[:token_rows].reshape(row_count, block_len, width), join_rows(all_grad, row_count)], axis=1
    )
    block_lse = jnp.concatenate([lse[:, :block_len], join_rows(all_lse, row_count)], axis=1)
    block_delta = jnp.concatenate(
        [delta[:token_rows].reshape(row_count, block_len, LANES), join_rows(all_delta, row_count)], axis=1
    )
    layer = final[:token_rows].reshape(row_count, block_len, width)
    layer = jnp.where(valid[:, :, None], layer, 0.0).astype(bf16)
    layer_output = jnp.concatenate([lax.ppermute(layer[:, half:], "seq", forth), layer[:, :half]], axis=1)
    own_out = final[token_rows:].astype(bf16)
    part = width // count
    dqkv = jnp.concatenate(attend_back(qkv, block_grad, block_lse, block_delta, kaug, half, rows), axis=-1)
    (part_dqkv,) = spread([split_rows(dqkv[:, block_len:], count)], count, False, 2)
    global_dqkv = jnp.sum(part_dqkv.astype(f32), axis=0).astype(bf16)
    qkv_grad = jnp.concatenate([dqkv[:, :block_len].reshape(token_rows, 3 * width), global_dqkv])

    first_grad = nt(qkv_grad, qkv_weight)
    n_tokens, inv_tokens = norm_parts(tokens)
    through, first_gain_grad, first_shift_grad = norm_back(first_grad, n_tokens, inv_tokens, first_gain)
    input_grad = (residual_grad + through).astype(bf16)
    normed_tokens = (n_tokens * first_gain + first_shift).astype(bf16)
    qkv_wgrad = wgrad(normed_tokens, qkv_grad, width)

    grad_block = input_grad[:token_rows].reshape(row_count, block_len, width)
    input_out = jnp.concatenate(
        [lax.ppermute(grad_block[:, half:], "seq", forth), grad_block[:, :half]], axis=1
    )
    global_final, global_grad = spread([own_out, input_grad[token_rows:]], count, True, 3)

    def shares(a):
        return a.reshape(count, a.shape[0] // count)

    small = jnp.concatenate(
        [
            shares(first_gain_grad),
            shares(first_shift_grad),
            shares(second_gain_grad),
            shares(second_shift_grad),
            shares(bias_grad),
        ],
        axis=1,
    )
    inner_out = reduce_share(inner_wgrad.transpose(1, 0, 2).reshape(width, -1))
    outer_out = reduce_share(outer_grad.reshape(inner_width, width))
    out_out = reduce_share(out_grad[0])
    qkv_out = reduce_share(qkv_wgrad.transpose(1, 0, 2).reshape(width, -1))
    small = reduce_share(small)[0]
    return (
        layer_output,
        join_rows(global_final, row_count),
        input_out,
        join_rows(global_grad, row_count),
        small[:part],
        small[part:2 * part],
        qkv_out,
        out_out,
        small[2 * part:3 * part],
        small[3 * part:4 * part],
        inner_out,
        small[4 * part:],
        outer_out,
    )


def solution(mesh):
    rows = P("batch", "seq", None)
    globals_at = P("batch", None, None)
    return jax.shard_map(
        body,
        mesh=mesh,
        in_specs=(rows, globals_at, P("batch")) + (P(),) * 9 + (rows, globals_at),
        out_specs=(
            rows,
            globals_at,
            rows,
            globals_at,
            P("seq"),
            P("seq"),
            P("seq", None),
            P("seq", None),
            P("seq"),
            P("seq"),
            P("seq", None),
            P("seq"),
            P("seq", None),
        ),
        check_vma=False,
    )
```

```python
import functools
import math

import jax
import jax.numpy as jnp
from jax import lax
from jax.experimental import pallas as pl
from jax.experimental.pallas import tpu as pltpu
from jax.sharding import PartitionSpec as P

HEADS = 12
NEG = -1e30
LANES = 128
TYPE0 = 3 * HEADS

def nt(a, b):
    return lax.dot_general(a, b, (((1,), (1,)), ((), ())), preferred_element_type=jnp.float32)

def tn(a, b):
    return lax.dot_general(a, b, (((0,), (0,)), ((), ())), preferred_element_type=jnp.float32)

def nn(a, b):
    return jnp.dot(a, b, preferred_element_type=jnp.float32)


def type_marks(rows, half, lane, row):
    kind = jnp.where(row < half, TYPE0, jnp.where(row < 2 * half, TYPE0 + 1, TYPE0 + 2))
    return (lane == kind)


def attend_step(half, scale, tq, *refs):
    attend_kernel(half, scale, tq, pl.program_id(1), *refs)


def attend_kernel(half, scale, tq, pair, q_ref, k_ref, v_ref, kaug_ref, o_ref, lse_ref):
    rows = q_ref.shape[1]
    zero = jnp.zeros((), jnp.bfloat16)
    k, v = k_ref[0], v_ref[0]
    kaug = kaug_ref[0]
    lane_all = lax.broadcasted_iota(jnp.int32, (rows, LANES), 1)
    low_all = lane_all < LANES // 2
    one = jnp.ones((), jnp.bfloat16)
    kx, vx = [], []
    for sel in (low_all, jnp.logical_not(low_all)):
        kx.append(jnp.concatenate([jnp.where(sel, k, zero), kaug], axis=1))
        vx.append(jnp.concatenate([jnp.where(sel, v, zero), jnp.where(sel, one, zero)], axis=1))
    vx = jnp.concatenate(vx, axis=0)
    for start in range(0, rows, tq):
        lane = lax.broadcasted_iota(jnp.int32, (tq, LANES), 1)
        row = lax.broadcasted_iota(jnp.int32, (tq, LANES), 0) + start
        low = lane < LANES // 2
        qaug = jnp.where(type_marks(rows, half, lane, row), one, zero)
        q = (q_ref[0, start:start + tq].astype(jnp.float32) * scale).astype(jnp.bfloat16)
        qx = jnp.concatenate([q, qaug], axis=1)
        probs, peaks = [], []
        for a in (0, 1):
            s = nt(qx, kx[a])
            peak = jnp.max(s, axis=1, keepdims=True)
            probs.append(jnp.exp(s - peak).astype(jnp.bfloat16))
            peaks.append(peak)
        acc = nn(jnp.concatenate(probs, axis=1), vx)
        total = acc[:, LANES:]
        o_ref[0, start:start + tq] = (acc[:, :LANES] / total).astype(jnp.bfloat16)
        lse = jnp.where(low, peaks[0], peaks[1]) + jnp.log(total)
        first, second = lse[:, 0:1], lse[:, LANES // 2:LANES // 2 + 1]
        prev = jnp.where(pair == 0, 0.0, lse_ref[0, start:start + tq])
        head = lax.rem(lane, HEADS)
        inside = lane < 3 * HEADS
        kept = jnp.where(inside & (head == 2 * pair), first, prev)
        lse_ref[0, start:start + tq] = jnp.where(inside & (head == 2 * pair + 1), second, kept)


def attend(qkv, kaug, half, tq=320):
    row_count, rows, cols = qkv.shape
    width = cols // 3
    pairs = width // LANES
    scale = (width // HEADS) ** (-0.5)
    spec = lambda off: pl.BlockSpec((1, rows, LANES), lambda r, p: (r, 0, off + p))
    return pl.pallas_call(
        functools.partial(attend_step, half, scale, tq),
        grid=(row_count, pairs),
        in_specs=[spec(0), spec(pairs), spec(2 * pairs), pl.BlockSpec((1, rows, LANES), lambda r, p: (r, 0, 0))],
        out_specs=[spec(0), pl.BlockSpec((1, rows, LANES), lambda r, p: (r, 0, 0))],
        out_shape=[
            jax.ShapeDtypeStruct((row_count, rows, width), jnp.bfloat16),
            jax.ShapeDtypeStruct((row_count, rows, LANES), jnp.float32),
        ],
        compiler_params=pltpu.CompilerParams(vmem_limit_bytes=48 * 1024 * 1024),
        name="attend",
    )(qkv, qkv, qkv, kaug)


def three_parts(values, lane):
    top = values.astype(jnp.bfloat16)
    rest = values - top.astype(jnp.float32)
    mid = rest.astype(jnp.bfloat16)
    low = (rest - mid.astype(jnp.float32)).astype(jnp.bfloat16)
    zero = jnp.zeros((), jnp.bfloat16)
    return jnp.where(lane < HEADS, top, jnp.where(lane < 2 * HEADS, mid, jnp.where(lane < 3 * HEADS, low, zero)))


def attend_back_step(half, scale, tk, q_ref, k_ref, v_ref, g_ref, lse_ref, delta_ref, *refs):
    attend_back_kernel(
        half, scale, tk, pl.program_id(1), q_ref, k_ref, v_ref, g_ref[0], lse_ref[0], delta_ref[0], *refs
    )


def attend_back_kernel(half, scale, tk, pair, q_ref, k_ref, v_ref, g, lse, delta, kaug_ref, dq_ref, dk_ref, dv_ref):
    rows = q_ref.shape[1]
    zero = jnp.zeros((), jnp.bfloat16)
    one = jnp.ones((), jnp.bfloat16)
    lane = lax.broadcasted_iota(jnp.int32, (rows, LANES), 1)
    row = lax.broadcasted_iota(jnp.int32, (rows, LANES), 0)
    low = lane < LANES // 2
    q = (q_ref[0].astype(jnp.float32) * scale).astype(jnp.bfloat16)
    qaug = jnp.where(type_marks(rows, half, lane, row), one, three_parts(lse, lane))
    gaug = three_parts(delta, lane)
    qx = jnp.concatenate([q, qaug], axis=1)
    gx = jnp.concatenate([g, gaug], axis=1)
    sels = (low, jnp.logical_not(low))
    qh = jnp.concatenate([jnp.where(sel, q, zero) for sel in sels], axis=0)
    gh = jnp.concatenate([jnp.where(sel, g, zero) for sel in sels], axis=0)
    dq = None
    for start in range(0, rows, tk):
        lane_k = lax.broadcasted_iota(jnp.int32, (tk, LANES), 1)
        low_k = lane_k < LANES // 2
        head = lax.rem(lane_k, HEADS)
        inside = lane_k < 3 * HEADS
        k = k_ref[0, start:start + tk]
        v = v_ref[0, start:start + tk]
        kaug = kaug_ref[0, start:start + tk]
        probs, grads, keys = [], [], []
        for a, sel in ((0, low_k), (1, jnp.logical_not(low_k))):
            marks = inside & (head == 2 * pair + a)
            keys.append(jnp.where(sel, k, zero))
            kx = jnp.concatenate([keys[a], jnp.where(marks, -one, kaug)], axis=1)
            vx = jnp.concatenate([jnp.where(sel, v, zero), jnp.where(marks, -one, zero)], axis=1)
            p = jnp.exp(nt(kx, qx))
            grads.append((p * nt(vx, gx)).astype(jnp.bfloat16))
            probs.append(p.astype(jnp.bfloat16))
        dv_ref[0, start:start + tk] = nn(jnp.concatenate(probs, axis=1), gh).astype(jnp.bfloat16)
        dk_ref[0, start:start + tk] = nn(jnp.concatenate(grads, axis=1), qh).astype(jnp.bfloat16)
        part = tn(jnp.concatenate(grads, axis=0), jnp.concatenate(keys, axis=0))
        dq = part if dq is None else dq + part
    dq_ref[0] = (dq * scale).astype(jnp.bfloat16)


def attend_back(qkv, grad, lse, delta, kaug, half, tk=320):
    row_count, rows, cols = qkv.shape
    width = cols // 3
    pairs = width // LANES
    scale = (width // HEADS) ** (-0.5)
    spec = lambda off: pl.BlockSpec((1, rows, LANES), lambda r, p: (r, 0, off + p))
    whole = pl.BlockSpec((1, rows, LANES), lambda r, p: (r, 0, 0))
    out = jax.ShapeDtypeStruct((row_count, rows, width), jnp.bfloat16)
    return pl.pallas_call(
        functools.partial(attend_back_step, half, scale, tk),
        grid=(row_count, pairs),
        in_specs=[spec(0), spec(pairs), spec(2 * pairs), spec(0), whole, whole, whole],
        out_specs=[spec(0)] * 3,
        out_shape=[out] * 3,
        compiler_params=pltpu.CompilerParams(vmem_limit_bytes=48 * 1024 * 1024),
        name="attend_back",
    )(qkv, qkv, qkv, grad, lse, delta, kaug)


EPS = 1e-05
MESH_ID = pl.DeviceIdType.MESH


def spread_kernel(count, sizes, same, *refs):
    ins, outs = refs[:sizes], refs[sizes:2 * sizes]
    send, recv, local = refs[2 * sizes:]
    me = lax.axis_index("seq")
    barrier = pltpu.get_barrier_semaphore()
    for step in range(1, count):
        pl.semaphore_signal(
            barrier, inc=1, device_id={"seq": lax.rem(me + step, count)}, device_id_type=MESH_ID
        )
    pl.semaphore_wait(barrier, count - 1)
    own = []
    for n in range(sizes):
        copy = pltpu.make_async_copy(ins[n] if same else ins[n].at[me], outs[n].at[me], local.at[n])
        copy.start()
        own.append(copy)
    copies = []
    for step in range(1, count):
        peer = lax.rem(me + step, count)
        for n in range(sizes):
            copy = pltpu.make_async_remote_copy(
                src_ref=ins[n] if same else ins[n].at[peer],
                dst_ref=outs[n].at[me],
                send_sem=send.at[n, step],
                recv_sem=recv.at[n, step],
                device_id={"seq": peer},
                device_id_type=MESH_ID,
            )
            copy.start()
            copies.append(copy)
    for copy in own:
        copy.wait()
    for copy in copies:
        copy.wait()


def spread(arrays, count, same, collective_id):
    sizes = len(arrays)
    shapes = [(count,) + a.shape if same else a.shape for a in arrays]
    vmem = pl.BlockSpec(memory_space=pltpu.VMEM)
    return pl.pallas_call(
        functools.partial(spread_kernel, count, sizes, same),
        in_specs=[vmem] * sizes,
        out_specs=[vmem] * sizes,
        out_shape=[jax.ShapeDtypeStruct(s, a.dtype) for s, a in zip(shapes, arrays)],
        scratch_shapes=[
            pltpu.SemaphoreType.DMA((sizes, count)),
            pltpu.SemaphoreType.DMA((sizes, count)),
            pltpu.SemaphoreType.DMA((sizes,)),
        ],
        compiler_params=pltpu.CompilerParams(
            collective_id=collective_id, has_side_effects=True, vmem_limit_bytes=32 * 1024 * 1024
        ),
        name="spread",
    )(*arrays)


SEQ_BITS = (("z1", 4), ("z0", 2), ("x", 1))
BATCH_BITS = (("y", 2), ("c", 1))


class Place:
    def __init__(self):
        self.spot, self.step = {}, {}
        for name, bits in (("seq", SEQ_BITS), ("batch", BATCH_BITS)):
            index = lax.axis_index(name)
            for axis, weight in bits:
                bit = lax.rem(lax.div(index, weight), 2)
                self.spot[axis] = bit
                self.step[axis] = {name: index + weight * (1 - 2 * bit)}

    def __getitem__(self, axis):
        return self.spot[axis]

    def partner(self, axis):
        return self.step[axis]

    def greet(self, others=()):
        barrier = pltpu.get_barrier_semaphore()
        peers = list(self.step.values()) + list(others)
        for to in peers:
            pl.semaphore_signal(barrier, inc=1, device_id=to, device_id_type=MESH_ID)
        pl.semaphore_wait(barrier, len(peers))


def remote(src, dst, send, recv, to):
    return pltpu.make_async_remote_copy(
        src_ref=src, dst_ref=dst, send_sem=send, recv_sem=recv, device_id=to, device_id_type=MESH_ID
    )


class Halve:
    def __init__(self, place, own, lanes, order, bufs, send, recv, first, stages=None):
        self.place, self.own, self.order = place, own, order
        self.lanes = pl.ds(*lanes)
        self.half = own.shape[3] // 2
        stages = range(len(order)) if stages is None else stages
        self.bufs = dict(zip(stages, bufs))
        self.send, self.recv, self.first = send, recv, first

    def copy(self, n):
        at = self.first + n
        return remote(
            self.own.at[self.region(n, False)], self.bufs[n], self.send.at[at], self.recv.at[at],
            self.place.partner(self.order[n]),
        )

    @staticmethod
    def buffers(rows, width, order, stages=None, dtype=jnp.bfloat16):
        shapes = []
        for n in range(len(order)) if stages is None else stages:
            left = [axis for axis, _ in SEQ_BITS if axis not in order[:n + 1]]
            shapes.append((2,) * len(left) + (rows // 2 if "y" in order[:n + 1] else rows, width))
        return [pltpu.VMEM(shape, dtype) for shape in shapes]

    def region(self, n, mine, free=(), piece=None):
        free = list(free)
        at = []
        for axis, _ in SEQ_BITS:
            if axis in self.order[:n]:
                at.append(self.place[axis])
            elif axis == self.order[n]:
                at.append(self.place[axis] if mine else 1 - self.place[axis])
            else:
                at.append(free.pop(0) if free else slice(None))
        first, count = 0, self.own.shape[3]
        if "y" in self.order[:n + 1]:
            y = self.place["y"]
            y = y if mine or self.order[n] != "y" else 1 - y
            first, count = y * self.half, self.half
        if piece is not None:
            first, count = first + piece[0], piece[1]
        rows = pl.ds(pl.multiple_of(first, 16), count)
        return (*at, rows, self.lanes)

    def start(self, n):
        self.copy(n).start()

    def sent(self):
        for n in self.bufs:
            self.copy(n).wait_send()

    def finish(self, n):
        self.copy(n).wait_recv()
        buf = self.bufs[n]
        dims = len(buf.shape) - 2
        count = buf.shape[-2]
        piece = math.gcd(count, 48)
        pieces = count // piece

        def add(i, carry):
            block, row = lax.div(i, pieces), lax.rem(i, pieces) * piece
            free = [lax.rem(lax.div(block, 2 ** (dims - 1 - d)), 2) for d in range(dims)]
            at = self.region(n, True, free, (row, piece))
            self.own[at] = self.own[at] + buf[(*free, pl.ds(pl.multiple_of(row, 16), piece), slice(None))]
            return carry

        lax.fori_loop(0, 2 ** dims * pieces, add, 0)


class Gather:
    order = ("z1", "z0", "x")

    def __init__(self, place, buf, send, recv):
        self.place, self.buf, self.send, self.recv = place, buf, send, recv

    def copy(self, n):
        done = self.order[:n]
        at = (slice(None), *(slice(None) if axis in done else self.place[axis] for axis, _ in SEQ_BITS))
        block = self.buf.at[at]
        return remote(block, block, self.send.at[n], self.recv.at[n], self.place.partner(self.order[n]))

    def stage(self, n):
        if n > 0:
            self.copy(n - 1).wait_recv()
        if n < 3:
            self.copy(n).start()

    def finish(self):
        for n in range(3):
            self.copy(n).wait_send()


PARTS = (
    ((0, 256), ("x", "y", "z0", "z1")),
    ((256, 384), ("y", "x", "z0", "z1")),
    ((640, 128), ("z0", "z1", "x", "y")),
)


class Fold:
    EARLY, LATE = (0, 1), (2, 3)

    def __init__(self, place, pieces, refs, source=None, stages=(0, 1, 2, 3)):
        self.place = place
        c, y = place["c"], place["y"]
        if stages == self.LATE:
            self.own, self.done, send, recv, *bufs = refs
            self.got = local = None
        elif source is None:
            self.own, self.done, *refs = refs
        else:
            self.own, self.done = source.at[:, :, :, c], None
        if stages != self.LATE:
            self.got, send, recv, local, *bufs = refs
        own, got, done = self.own, self.got, self.done
        rows = own.shape[3]
        half = rows // 2
        self.mine = pl.ds(pl.multiple_of(y * half, 16), half)
        self.pieces, self.source, self.done = pieces, source, done
        self.sems = send, recv, local
        first = 1 if source is not None else len(pieces)
        self.first = first + 12
        self.parts = []
        for n, (lanes, order) in enumerate(PARTS):
            own_bufs = bufs[len(stages) * n:len(stages) * (n + 1)]
            self.parts.append(Halve(place, own, lanes, order, own_bufs, send, recv, first + 4 * n, stages))

    def keep(self):
        at, copies = 0, []
        if self.source is None:
            for n, (take, count) in enumerate(self.pieces):
                spot = self.own.at[:, :, :, pl.ds(at, count)]
                copies.append(pltpu.make_async_copy(take(self.place["c"]), spot, self.sems[2].at[n]))
                at += count
        return copies

    def core(self):
        send, recv, _ = self.sems
        to, c = self.place.partner("c"), 1 - self.place["c"]
        if self.source is not None:
            return [remote(self.source.at[:, :, :, c], self.got, send.at[0], recv.at[0], to)]
        at, copies = 0, []
        for n, (take, count) in enumerate(self.pieces):
            copies.append(remote(take(c), self.got.at[:, :, :, pl.ds(at, count)], send.at[n], recv.at[n], to))
            at += count
        return copies

    def across(self):
        send, recv, _ = self.sems
        spot = self.done.at[self.place["c"], self.mine]
        return remote(spot, spot, send.at[self.first], recv.at[self.first], self.place.partner("y"))

    def back(self):
        send, recv, _ = self.sems
        spot = self.done.at[self.place["c"]]
        return remote(spot, spot, send.at[self.first + 1], recv.at[self.first + 1], self.place.partner("c"))

    @staticmethod
    def scratch(rows, width, pieces, sourced=False, stages=(0, 1, 2, 3)):
        vmem = lambda *shape: pltpu.VMEM(shape, jnp.bfloat16)
        refs = [] if sourced else [vmem(2, 2, 2, rows, width), vmem(2, rows, width)]
        if stages != Fold.LATE:
            refs.append(vmem(2, 2, 2, rows, width))
        refs += [
            pltpu.SemaphoreType.DMA((pieces + 14,)),
            pltpu.SemaphoreType.DMA((pieces + 14,)),
        ]
        if stages != Fold.LATE:
            refs.append(pltpu.SemaphoreType.DMA((pieces,)))
        for (_, count), order in PARTS:
            refs += Halve.buffers(rows, count, order, stages)
        return refs

    def stage(self, n):
        if n == 0:
            for copy in self.keep() + self.core():
                copy.start()
        elif n == 1:
            for copy in self.keep():
                copy.wait()
            for copy in self.core():
                copy.wait_recv()

            piece = math.gcd(self.got.shape[3], 48)
            pieces = self.got.shape[3] // piece

            def add(i, carry):
                block = lax.div(i, pieces)
                rows = pl.ds(pl.multiple_of(lax.rem(i, pieces) * piece, 16), piece)
                at = (*(lax.rem(lax.div(block, w), 2) for _, w in SEQ_BITS), rows)
                self.own[at] = self.own[at] + self.got[at]
                return carry

            lax.fori_loop(0, 8 * pieces, add, 0)
            for part in self.parts:
                part.start(0)
        elif n < 5:
            for part in self.parts:
                part.finish(n - 2)
                part.start(n - 1)
        elif n == 5:
            for part in self.parts:
                part.finish(3)
            at = tuple(self.place[axis] for axis, _ in SEQ_BITS)
            self.done[self.place["c"], self.mine] = self.own[(*at, self.mine)]
            self.across().start()
        elif n == 6:
            self.across().wait_recv()
            self.back().start()
        else:
            self.back().wait_recv()

    def held(self):
        z1, z0, x = (self.place[axis] for axis, _ in SEQ_BITS)
        a, b, c = (lanes[1] for lanes, _ in PARTS)
        return (slice(None), slice(None), x, self.mine, pl.ds(0, a + b)), (
            z1, z0, slice(None), slice(None), pl.ds(a + b, c)
        )

    def resume(self):
        for part in self.parts:
            part.start(2)

    def finish(self):
        copies = self.core()
        if self.done is not None:
            copies = copies + [self.across(), self.back()]
        for copy in copies:
            copy.wait_send()
        for part in self.parts:
            part.sent()


class Sum:
    order = ("c", "x", "y", "z0", "z1")

    def __init__(self, place, value, got, send, recv):
        self.place, self.value, self.got, self.send, self.recv = place, value, got, send, recv

    def copy(self, n):
        to = self.place.partner(self.order[n])
        return remote(self.value.at[n], self.got.at[n], self.send.at[n], self.recv.at[n], to)

    def stage(self, n):
        if n > 0:
            self.copy(n - 1).wait_recv()
            self.value[n] = self.value[n - 1] + self.got[n - 1]
        if n < 5:
            self.copy(n).start()

    def finish(self):
        for n in range(5):
            self.copy(n).wait_send()


def share_views(a, count):
    *lead, rows, width = a.shape
    return a.reshape(*lead, 2, 2, 2, rows // count, width)


def half_views(a, count):
    *lead, rows, width = a.shape
    return a.reshape(*lead, 2, 2, 2, 2, rows // (2 * count), width)


def fetch(sources, targets, sems, first=0):
    return [pltpu.make_async_copy(s, t, sems.at[first + n]) for n, (s, t) in enumerate(zip(sources, targets))]


def finish_kernel(
    inner_in, late_in, keys_in, outer_in, small_in, layer, igrad, gout, ggrad,
    inner_o, outer_o, out_o, qkv_o, fg_o, fs_o, sg_o, ss_o, bias_o, layer_o, igrad_o, gout_o, ggrad_o,
    inner, late, keys, outer, small, *scratch,
):
    *held, sems = scratch
    f32 = jnp.float32
    me = lax.axis_index("seq")
    moved = (layer, igrad, gout, ggrad)
    own = fetch((inner_in, late_in, keys_in, outer_in, small_in), (inner, late, keys, outer, small), sems)
    into, away = fetch(moved, held, sems, 6), fetch(held, (layer_o, igrad_o, gout_o, ggrad_o), sems, 10)
    begin(own + into)
    width = outer_o.shape[1]
    part = inner_o.shape[0]
    strips = inner_o.shape[1] // width // 2
    half = outer.shape[1]
    for copy in own:
        copy.wait()
    for c in range(2):
        for j in range(strips):
            inner_o[:, pl.ds((c * strips + j) * width, width)] = inner[c, pl.ds(j * part, part)].astype(f32)
        outer_o[pl.ds(c * half, half)] = outer[c].astype(f32)
        spot = pl.ds(c * part // 2, part // 2)
        first, second = pl.ds(0, part // 2), pl.ds(part // 2, part // 2)
        out_o[spot] = late[c, first].astype(f32)
        for j, (ref, lines) in enumerate(((late, second), (keys, first), (keys, second))):
            qkv_o[spot, pl.ds(j * width, width)] = ref[c, lines].astype(f32)
    for copy, onward in zip(into, away):
        copy.wait()
        onward.start()
    values = small[...]
    turned = pltpu.roll(values, lax.rem(width - part * me, width), 1)
    for n, ref in enumerate((fg_o, fs_o, sg_o, ss_o)):
        ref[...] = turned[n, :part]
    wide = bias_o.shape[0]
    per = width // wide
    row = small[pl.ds(4 + lax.div(me, per), 1)]
    spots = [row[0, n * wide:(n + 1) * wide] for n in range(per)]
    chosen = spots[0]
    for n in range(1, per):
        chosen = jnp.where(lax.rem(me, per) == n, spots[n], chosen)
    bias_o[...] = chosen
    for copy in away:
        copy.wait()


def finish(inner, late, keys, outer, small, layer, igrad, gout, ggrad):
    width = small.shape[1]
    part = keys.shape[1]
    bias = 2 * outer.shape[1]
    vmem, hbm = pl.BlockSpec(memory_space=pltpu.VMEM), pl.BlockSpec(memory_space=pl.ANY)
    shapes = [(part, 4 * width), (bias, width), (part, width), (part, 3 * width)] + [(part,)] * 4 + [(bias,)]
    own, moved = [inner, late, keys, outer, small], [layer, igrad, gout, ggrad]
    return pl.pallas_call(
        finish_kernel,
        in_specs=[hbm] * 9,
        out_specs=[vmem] * 9 + [hbm] * 4,
        out_shape=[jax.ShapeDtypeStruct(s, jnp.float32) for s in shapes]
        + [jax.ShapeDtypeStruct(a.shape, a.dtype) for a in moved],
        scratch_shapes=[pltpu.VMEM(a.shape, a.dtype) for a in own + moved] + [pltpu.SemaphoreType.DMA((14,))],
        compiler_params=pltpu.CompilerParams(vmem_limit_bytes=60 * 1024 * 1024),
        name="finish",
    )(*own, *moved)


def begin(copies):
    for copy in copies:
        copy.start()


def sum_rows(values):
    rows, width = values.shape
    return jnp.sum(values.reshape(rows // 8, 8, width), axis=0)


def ticks(plan, folds, step):
    for t, todo in plan.items():

        @pl.when(step == t)
        def _():
            for f, n in todo:
                folds[f].stage(n)


TILE_AT = ((6, 0, 1), (7, 0, 0), (18, 1, 1), (19, 1, 0))
STRIPS_AT, GLOBALS_AT, LAST = 15, 14, 20
REAR_TICKS = {
    0: ((0, 0),),
    3: ((0, 1),),
    4: ((3, 4),),
    8: ((3, 5),),
    9: ((0, 2),),
    10: ((3, 6),),
    12: ((3, 7),),
    13: ((0, 3),),
    16: ((1, 0),),
    18: ((0, 4), (2, 0), (1, 1)),
    19: ((0, 5),),
}
REAR_END = (
    (7, 0), (2, 1), (5, 0), (1, 2), (7, 1), (5, 1), (2, 2), (0, 6), (1, 3), (7, 2), (5, 2), (6, 0), (2, 3), (0, 7), (1, 4),
    (7, 3), (6, 1), (2, 4), (1, 5), (7, 4), (6, 2), (2, 5), (1, 6), (7, 5), (6, 3), (2, 6), (1, 7), (2, 7),
)


def rear_kernel(
    half, scale, pairs, fold_refs,
    q_ref, k_ref, v_ref, g_ref, lse_ref, delta_ref, kaug_ref,
    x_ref, next_x_ref, res_ref, gg_in, glse_in, gdelta_in, outer_ab, outer_c, gres_in, globals_in, weight_in, gain_in, vectors_in,
    normed_in, inner, out,
    igrad_o, ggrad_o, inner_o, late_o, keys_o, outer_o, small_o,
    gg_ref, glse_ref, gdelta_ref, gres_ref, globals_ref, weight_ref, gain_ref, vectors_ref, normed_ref,
    dqkv, gfirst, sums, qkv_src, grads, ggrad, value, got,
    send, recv, local, *scratch,
):
    step = pl.program_id(0)
    place = Place()
    me = lax.axis_index("seq")
    count = lax.axis_size("seq")
    row_count, rows, cols = dqkv.shape
    block_len = 2 * half
    width = cols // 3
    share = gres_ref.shape[1]
    attn = row_count * pairs
    strips = inner.shape[0] // 2
    part_rows = inner.shape[4]
    half_part = part_rows // 2
    sources = (
        [(lambda c, j=j: inner.at[c * strips + j], part_rows) for j in range(strips)],
        [(lambda c: out.at[:, :, :, c], half_part), (lambda c: qkv_src.at[0, :, :, :, c], half_part)],
        [(lambda c, j=j: qkv_src.at[j, :, :, :, c], half_part) for j in (1, 2)],
    )
    folds, at = [], 0
    for pieces, size in zip(sources, fold_refs[:3]):
        folds.append(Fold(place, pieces, scratch[at:at + size]))
        at += size
    folds.append(Fold(place, (), scratch[at:at + fold_refs[3]], None, Fold.LATE))
    at += fold_refs[3]
    spread = Halve(place, gfirst, (0, width), ("x", "z0", "z1"), scratch[at:], send.at[0], recv.at[0], 0)
    gather = Gather(place, ggrad, send.at[row_count], recv.at[row_count])
    small = Sum(place, value, got, send.at[row_count + 1], recv.at[row_count + 1])
    following = {"seq": lax.rem(me + 1, count)}
    before = {"seq": lax.rem(me + count - 1, count)}
    held = folds[3].held()
    early = lambda: fetch(
        (gg_in, glse_in, gdelta_in, outer_ab, outer_c),
        (gg_ref, glse_ref, gdelta_ref, folds[3].own.at[held[0]], folds[3].own.at[held[1]]), local,
    )
    later = lambda: fetch(
        (gres_in, globals_in, weight_in, gain_in, vectors_in),
        (gres_ref, globals_ref, weight_ref, gain_ref.at[0], vectors_ref), local, 5,
    )
    latest = lambda: fetch((normed_in,), (normed_ref,), local, 11)

    def home(r):
        sems = send.at[row_count + 2, r], recv.at[row_count + 2, r]
        return remote(grads.at[1, r], igrad_o.at[r, pl.ds(0, half)], *sems, following)

    def keep(r):
        return pltpu.make_async_copy(grads.at[0, r], igrad_o.at[r, pl.ds(half, half)], local.at[12 + r])

    @pl.when(step == 0)
    def _():
        begin(early() + later() + latest())
        place.greet([following, before])
        sums[...] = jnp.zeros_like(sums)
        for copy in early():
            copy.wait()
        folds[3].resume()

    ticks(REAR_TICKS, folds, step)

    @pl.when((step < pairs) | ((step >= pairs + 2) & (step < attn + 2)))
    def _():
        r = jnp.where(step < pairs, 0, 1)
        p = step - r * (pairs + 2)
        spots = [pl.ds(pl.multiple_of(j * width + p * LANES, LANES), LANES) for j in range(3)]
        lane = pl.ds(pl.multiple_of(p * LANES, LANES), LANES)
        wide = lambda a, b: jnp.concatenate([a, b.reshape(rows - block_len, LANES)], axis=0)
        attend_back_kernel(
            half, scale, 320, p, q_ref, k_ref, v_ref, wide(g_ref[...], gg_ref[r, :, :, :, :, lane]),
            wide(lse_ref[0], glse_ref[r]), wide(delta_ref[...], gdelta_ref[r]), kaug_ref,
            *(dqkv.at[pl.ds(r, 1), :, spot] for spot in spots),
        )

    def move_spread(n):
        spread.finish(n)
        if n < 2:
            spread.start(n + 1)

    @pl.when(step == TILE_AT[0][0])
    def _():
        for copy in later():
            copy.wait()

    @pl.when(step == STRIPS_AT)
    def _():
        for copy in latest():
            copy.wait()


    strip_at = step - STRIPS_AT

    @pl.when((strip_at >= 0) & (strip_at < 3))
    def _():
        strip = pl.ds(pl.multiple_of(strip_at * width, width), width)
        total = tn(normed_ref[0], dqkv[0, :, strip])
        for r in range(1, row_count):
            total = total + tn(normed_ref[r], dqkv[r, :, strip])
        qkv_src[strip_at] = total.astype(jnp.bfloat16).reshape(qkv_src.shape[1:])

    def stats(x):
        centred = x - jnp.mean(x, axis=-1, keepdims=True)
        inv = lax.rsqrt(jnp.mean(centred * centred, axis=-1, keepdims=True) + EPS)
        return centred * inv, inv

    def add_sums(first, n):
        sums[0] += sum_rows(first * n)
        sums[1] += sum_rows(first)

    def through(first, n, inv):
        eg = first * gain_ref[...]
        return (eg - jnp.mean(eg, axis=-1, keepdims=True) - n * jnp.mean(eg * n, axis=-1, keepdims=True)) * inv

    @pl.when(step == GLOBALS_AT)
    def _():
        own = pl.ds(block_len, rows - block_len)
        partial = jnp.concatenate([dqkv[r, own] for r in range(row_count)], axis=0)
        first = nt(partial, weight_ref[...])
        n, _ = stats(globals_ref[...].astype(jnp.float32).reshape(first.shape))
        add_sums(first, n)
        first = first.astype(jnp.bfloat16).reshape(row_count, 2, 2, 2, share, width)
        for r in range(row_count):
            gfirst[:, :, :, pl.ds(r * share, share)] = first[r]
        spread.start(0)

    @pl.when(functools.reduce(jnp.logical_or, [step == t for t, _, _ in TILE_AT]))
    def _():
        r = jnp.where(step < pairs + 2, 0, 1)
        h = jnp.where((step == TILE_AT[0][0]) | (step == TILE_AT[2][0]), 1, 0)
        first = nt(dqkv[r, pl.ds(pl.multiple_of(h * half, half), half)], weight_ref[...])
        n, inv = stats(jnp.where(h == 0, x_ref[0].astype(jnp.float32), next_x_ref[0].astype(jnp.float32)))
        add_sums(first, n)
        grads[h, r] = (res_ref[...] + through(first, n, inv)).astype(jnp.bfloat16)

    for t, r, h in TILE_AT:

        @pl.when(step == t)
        def _():
            (home if h else keep)(r).start()

    def own_globals():
        own_rows = row_count * share
        at = tuple(place[axis] for axis, _ in SEQ_BITS)
        held = pl.ds(pl.multiple_of(share * me, 16), share)
        n, inv = stats(globals_ref[:, held].astype(jnp.float32).reshape(own_rows, width))
        grad = gres_ref[...].reshape(own_rows, width) + through(gfirst[at].astype(jnp.float32), n, inv)
        ggrad[(slice(None), *at)] = grad.astype(jnp.bfloat16).reshape(row_count, share, width)

    @pl.when(step == LAST)
    def _():
        lines = [jnp.sum(sums[n], axis=0, keepdims=True) for n in range(2)]
        value[0] = jnp.concatenate(lines + [vectors_ref[...]])
        leaves = fetch(
            (folds[0].done, folds[1].done, folds[2].done, folds[3].done, value.at[5], ggrad),
            (inner_o, late_o, keys_o, outer_o, small_o, ggrad_o), local, 12 + row_count,
        )
        ready = {(0, 7): 0, (1, 7): 1, (2, 7): 2, (7, 5): 4, (6, 3): 5}
        leaves[3].start()
        for f, n in REAR_END:
            if f == 5:
                move_spread(n)
                if n == 2:
                    own_globals()
            elif f == 6:
                gather.stage(n)
            elif f == 7:
                small.stage(n)
            else:
                folds[f].stage(n)
            if (f, n) in ready:
                leaves[ready[f, n]].start()
        for fold in folds:
            fold.finish()
        gather.finish()
        small.finish()
        spread.sent()
        for r in range(row_count):
            keep(r).wait()
            home(r).wait()
        for copy in leaves:
            copy.wait()


def rear(
    qkv, grad, lse, delta, kaug, inputs, next_x, res_grad, global_grad, global_lse, global_delta, own_res, normed,
    globals_in, weight, gain, vectors, outer_ab, outer_c, inner, out, half, count,
):
    row_count, rows, cols = qkv.shape
    width = cols // 3
    pairs = width // LANES
    block_len = 2 * half
    global_count = rows - block_len
    share = global_count // count
    part = width // count
    scale = (width // HEADS) ** (-0.5)
    attn = row_count * pairs
    f32, bf16 = jnp.float32, jnp.bfloat16
    turn = lambda t: jnp.where(t < pairs, t, jnp.clip(t - 2, pairs, attn - 1))
    row_of = lambda t: turn(t) // pairs
    pair_of = lambda t: turn(t) % pairs
    spec = lambda off: pl.BlockSpec((1, rows, LANES), lambda t: (row_of(t), 0, off + pair_of(t)))
    whole = pl.BlockSpec((1, rows, LANES), lambda t: (row_of(t), 0, 0))

    def tile_of(t):
        (a, _, _), (b, _, _), (c, _, _), _ = TILE_AT
        return jnp.where(t <= a, 1, jnp.where(t <= b, 0, jnp.where(t <= c, 3, 2))), 0

    tile = pl.BlockSpec((half, width), tile_of)
    hbm = pl.BlockSpec(memory_space=pl.ANY)
    outs = [
        jax.ShapeDtypeStruct((row_count, block_len, width), bf16),
        jax.ShapeDtypeStruct((row_count, 2, 2, 2, share, width), bf16),
        jax.ShapeDtypeStruct((2, 2 * part, width), bf16),
        jax.ShapeDtypeStruct((2, part, width), bf16),
        jax.ShapeDtypeStruct((2, part, width), bf16),
        jax.ShapeDtypeStruct((2, 2 * part, width), bf16),
        jax.ShapeDtypeStruct((8, width), f32),
    ]
    folds, sizes = [], []
    for size, pieces in ((2 * part, 2), (part, 2), (part, 2)):
        refs = Fold.scratch(size, width, pieces)
        folds += refs
        sizes.append(len(refs))
    refs = Fold.scratch(2 * part, width, 0, False, Fold.LATE)
    folds += refs
    sizes.append(len(refs))
    vmem = pltpu.VMEM
    kinds = 4 + row_count
    early = (global_grad, global_lse, global_delta)
    later = (own_res, globals_in, weight, gain, vectors, normed)
    return pl.pallas_call(
        functools.partial(rear_kernel, half, scale, pairs, tuple(sizes)),
        grid=(LAST + 1,),
        in_specs=[spec(0), spec(pairs), spec(2 * pairs)]
        + [pl.BlockSpec((block_len, LANES), lambda t: (row_of(t), pair_of(t)))]
        + [pl.BlockSpec((1, block_len, LANES), lambda t: (row_of(t), 0, 0))]
        + [pl.BlockSpec((block_len, LANES), lambda t: (row_of(t), 0)), whole]
        + [
            pl.BlockSpec((1, half, width), lambda t: (jnp.where(t <= TILE_AT[1][0], 0, 1), 1, 0)),
            pl.BlockSpec((1, half, width), lambda t: (jnp.where(t <= TILE_AT[0][0], 0, 1), 0, 0)),
            tile,
        ]
        + [hbm] * 13,
        out_specs=[hbm] * 7,
        out_shape=outs,
        scratch_shapes=[vmem(a.shape if a.ndim > 1 else (1, *a.shape), a.dtype) for a in early + later]
        + [
            vmem((row_count, rows, cols), bf16),
            vmem((2, 2, 2, row_count * share, width), bf16),
            vmem((2, 8, width), f32),
            vmem((3, 2, 2, 2, 2, part // 2, width), bf16),
            vmem((2, row_count, half, width), bf16),
            vmem((row_count, 2, 2, 2, share, width), bf16),
            vmem((6, 8, width), f32),
            vmem((5, 8, width), f32),
            pltpu.SemaphoreType.DMA((kinds, 5)),
            pltpu.SemaphoreType.DMA((kinds, 5)),
            pltpu.SemaphoreType.DMA((20 + row_count,)),
        ]
        + folds
        + Halve.buffers(row_count * share, width, ("x", "z0", "z1")),
        compiler_params=pltpu.CompilerParams(
            collective_id=9, has_side_effects=True, vmem_limit_bytes=64 * 1024 * 1024
        ),
        name="rear",
    )(
        qkv, qkv, qkv, grad, lse, delta, kaug, inputs, next_x, res_grad, *early, outer_ab, outer_c, *later,
        share_views(inner, count), half_views(out, count),
    )


def cdf_bell(v):
    bell = jnp.exp(-0.5 * v * v)
    t = 1.0 / (1.0 + (0.3275911 * 0.5 ** 0.5) * jnp.abs(v))
    poly = t * (
        0.127414796 + t * (-0.142248368 + t * (0.7107068705 + t * (-0.7265760135 + t * 0.5307027145)))
    )
    tail = poly * bell
    return jnp.where(v < 0, tail, 1.0 - tail), bell


STRIPS_FROM, BACK_FROM = 4, 8
MID_TICKS = {8: 0, 9: 1, 13: 2}
MID_GATHERS = {6: (0, 1), 8: (0, 2), 11: (0, 3), 10: (1, 1), 12: (1, 2), 15: (1, 3)}


def mid_kernel(
    half, fold_refs,
    lengths, x_ref, next_x_ref, mixed_ref, cot_ref, next_cot_ref, gain_in, shift_in, bias_in, out_in, inner_in, outer_in, gx_in, gcot_in,
    mixed_all, lse_all,
    layer_o, res_o, grad_o, delta_o, gres_o, gout_o, ggrad_o, glse_o, gdelta_o, inner_o, outer_ab_o, outer_c_o, out_o,
    vectors_o,
    gain_ref, shift_ref, bias_ref, out_w, inner_w, outer_w, gx_ref, gcot_ref, heads_ref,
    hidden, slope, normed, cot, att, proj, residual, outer_src, sums, bias_sums, layers,
    gout, ggrad, glse, gdelta, part_mixed, part_lse, send, recv, local, *scratch,
):
    f32, bf16 = jnp.float32, jnp.bfloat16
    step = pl.program_id(0)
    place = Place()
    me = lax.axis_index("seq")
    count = lax.axis_size("seq")
    row_count, share = gx_ref.shape[:2]
    block_len = 2 * half
    tokens = row_count * block_len
    own_rows = row_count * share
    width = gx_ref.shape[2]
    strips = inner_w.shape[1] // width
    tiles = 2 * row_count
    fold = Fold(place, None, scratch, outer_src, Fold.EARLY)
    held = pl.ds(pl.multiple_of(share * me, 16), share)
    following = {"seq": lax.rem(me + 1, count)}
    at = tuple(place[axis] for axis, _ in SEQ_BITS)

    def parts(m, to, r, n):
        rows = pl.ds(pl.multiple_of(block_len + share * to, 16), share)
        return (
            (mixed_all.at[r, rows], part_mixed.at[m, r]) if n == 0 else (lse_all.at[r, rows], part_lse.at[m, r])
        )

    def part_copies():
        copies = []
        for r in range(row_count):
            for n in range(2):
                for other in range(1, count):
                    to = lax.rem(me + other, count)
                    src, dst = parts(me, to, r, n)
                    sems = send.at[2 * r + n, other], recv.at[2 * r + n, other]
                    copies.append(remote(src, dst, *sems, {"seq": to}))
        return copies

    def part_own():
        return [
            pltpu.make_async_copy(*parts(me, me, r, n), local.at[2 * r + n]) for r in range(row_count) for n in range(2)
        ]

    base = 2 * row_count
    gathers = [
        Gather(place, buf, send.at[base + n], recv.at[base + n]) for n, buf in enumerate((gout, ggrad, glse, gdelta))
    ]
    leaves = lambda: fetch((gout, ggrad, glse, gdelta), (gout_o, ggrad_o, glse_o, gdelta_o), local, base)
    ends = base + 4

    def home(r):
        return remote(layers.at[1, r], layer_o.at[r, pl.ds(0, half)], send.at[ends, r], recv.at[ends, r], following)

    def keep(r):
        return pltpu.make_async_copy(layers.at[0, r], layer_o.at[r, pl.ds(half, half)], local.at[ends + r])

    loads = lambda: fetch(
        (gain_in, shift_in, bias_in, out_in, inner_in, outer_in, gx_in.at[:, held], gcot_in.at[:, held]),
        (gain_ref.at[0], shift_ref.at[0], bias_ref.at[0], out_w, inner_w, outer_w, gx_ref, gcot_ref), local, ends + row_count,
    )

    @pl.when(step == 0)
    def _():
        begin(loads())
        place.greet([{"seq": lax.rem(me + other, count)} for other in range(1, count)])
        begin(part_own() + part_copies())
        lane = lax.broadcasted_iota(jnp.int32, (width, LANES), 1)
        head = lax.div(lax.broadcasted_iota(jnp.int32, (width, LANES), 0), width // HEADS)
        chosen = jnp.where(lane < 3 * HEADS, lax.rem(lane, HEADS), -1) == head
        heads_ref[...] = jnp.where(chosen, 1.0, 0.0).astype(bf16)
        sums[...] = jnp.zeros_like(sums)
        bias_sums[...] = jnp.zeros_like(bias_sums)
        for copy in loads():
            copy.wait()

    def stats(values):
        centred = values - jnp.mean(values, axis=-1, keepdims=True)
        inv = lax.rsqrt(jnp.mean(centred * centred, axis=-1, keepdims=True) + EPS)
        return centred * inv, inv

    def forward(x, attended, rows, unroll=True):
        att[rows] = attended
        total = x.astype(f32) + nn(attended, out_w[...])
        residual[rows] = total
        n, _ = stats(total)
        second = (n * gain_ref[...] + shift_ref[...]).astype(bf16)
        normed[rows] = second

        def run(j, total):
            strip = pl.ds(pl.multiple_of(j * width, width), width)
            inner = nn(second, inner_w[:, strip]) + bias_ref[:, strip]
            cdf, bell = cdf_bell(inner)
            active = (inner * cdf).astype(bf16)
            hidden[rows, strip] = active
            slope[rows, strip] = (cdf + inner * bell * ((0.5 / math.pi) ** 0.5)).astype(bf16)
            return total + nn(active, outer_w[strip, :])

        return lax.fori_loop(0, strips, run, total, unroll=unroll)

    def backward(cotangent, rows, unroll=True):
        def run(j, total):
            strip = pl.ds(pl.multiple_of(j * width, width), width)
            grad = (nt(cotangent, outer_w[strip, :]) * slope[rows, strip].astype(f32)).astype(bf16)
            slope[rows, strip] = grad
            bias_sums[j] += sum_rows(grad.astype(f32))
            return total + nt(grad, inner_w[:, strip])

        second_grad = lax.fori_loop(0, strips, run, jnp.zeros(cotangent.shape, f32), unroll=unroll)
        n, inv = stats(residual[rows])
        eg = second_grad * gain_ref[...]
        through = (eg - jnp.mean(eg, axis=-1, keepdims=True) - n * jnp.mean(eg * n, axis=-1, keepdims=True)) * inv
        sums[0] += sum_rows(second_grad * n)
        sums[1] += sum_rows(second_grad)
        res = cotangent.astype(f32) + through
        projected = res.astype(bf16)
        proj[rows] = projected
        grad = nt(projected, out_w[...]).astype(bf16)
        product = grad.astype(f32) * att[rows].astype(f32)
        top = product.astype(bf16)
        rest = (product - top.astype(f32)).astype(bf16)
        return res, grad, nn(top, heads_ref[...]) + nn(rest, heads_ref[...])

    def turn(n):
        return lax.div(n, 2), jnp.where(n == 0, 1, 0)

    def is_valid(r, h):
        owner = lax.rem(me + h, count)
        spot = owner * block_len + (1 - h) * half + lax.broadcasted_iota(jnp.int32, (half, width), 0)
        return spot < lengths[r]

    @pl.when(step < tiles - 1)
    def _():
        r, h = turn(step)
        rows = pl.ds(pl.multiple_of((2 * r + h) * half, half), half)
        valid = is_valid(r, h)
        pick = lambda a, b: jnp.where(h == 0, a[0].astype(f32), b[0].astype(f32))
        cot[rows] = jnp.where(valid, pick(cot_ref, next_cot_ref), 0.0).astype(bf16)
        final = forward(pick(x_ref, next_x_ref), mixed_ref[0], rows)
        layers[h, r] = jnp.where(valid, final, 0.0).astype(bf16)

    back = step - (BACK_FROM + 1)

    @pl.when((back >= 0) & (back < tiles - 1))
    def _():
        r, h = turn(back)
        rows = pl.ds(pl.multiple_of((2 * r + h) * half, half), half)
        res, grad, delta = backward(cot[rows], rows)
        res_o[...] = res
        grad_o[...] = grad
        delta_o[...] = delta

    last_row = row_count - 1
    joint = pl.ds(tokens - half, half + own_rows)

    @pl.when(step == tiles - 1)
    def _():
        for copy in part_own():
            copy.wait()
        for copy in part_copies():
            copy.wait_recv()
        peak = jnp.max(part_lse[...], axis=0)
        shares = jnp.exp(part_lse[...] - peak)
        total = jnp.sum(shares, axis=0)
        lse = peak + jnp.log(total)
        glse[(slice(None), *at)] = lse
        shares = (shares / total).reshape(count * own_rows, LANES)
        lane = lax.broadcasted_iota(jnp.int32, shares.shape, 1)
        shares = jnp.where(lane < HEADS, shares, 0.0)
        top = shares.astype(bf16)
        rest = (shares - top.astype(f32)).astype(bf16)
        wide = nt(top, heads_ref[...]) + nt(rest, heads_ref[...])
        mixed = wide * part_mixed[...].reshape(count * own_rows, width).astype(f32)
        mixed = jnp.sum(mixed.reshape(count, own_rows, width), axis=0).astype(bf16)
        valid = is_valid(last_row, 1)
        local_cot = jnp.where(valid, next_cot_ref[0].astype(f32), 0.0).astype(bf16)
        cot[joint] = jnp.concatenate([local_cot, gcot_ref[...].reshape(own_rows, width)], axis=0)
        x = jnp.concatenate([next_x_ref[0], gx_ref[...].reshape(own_rows, width)], axis=0)
        final = forward(x, jnp.concatenate([mixed_ref[0], mixed], axis=0), joint, False)
        layers[1, last_row] = jnp.where(valid, final[:half], 0.0).astype(bf16)
        gout[(slice(None), *at)] = final[half:].astype(bf16).reshape(row_count, share, width)
        gathers[0].stage(0)

    @pl.when(step == 0)
    def _():
        home(0).start()

    for t, h, r in ((1, 0, 0), (2, 0, 1), (3, 1, 1)):

        @pl.when(step == t)
        def _():
            (home if h else keep)(r).start()

    strip_at = step - STRIPS_FROM

    @pl.when((strip_at >= 0) & (strip_at < strips))
    def _():
        strip = pl.ds(pl.multiple_of(strip_at * width, width), width)
        grad = tn(hidden[:, strip], cot[...]).astype(bf16)
        outer_src[lax.div(strip_at, 2), lax.rem(strip_at, 2)] = grad.reshape(outer_src.shape[2:])

    for t, (kind, n) in MID_GATHERS.items():

        @pl.when(step == t)
        def _():
            chosen = range(1, 4) if kind else range(1)
            for g in chosen:
                gathers[g].stage(n)
                if n == 3:
                    leaves()[g].start()

    for t, n in MID_TICKS.items():

        @pl.when(step == t)
        def _():
            fold.stage(n)

    after = BACK_FROM + tiles

    @pl.when(step == BACK_FROM)
    def _():
        res, grad, delta = backward(cot[joint], joint, False)
        res_o[...], gres_o[...] = res[:half], res[half:].reshape(row_count, share, width)
        grad_o[...], delta_o[...] = grad[:half], delta[:half]
        ggrad[(slice(None), *at)] = grad[half:].reshape(row_count, share, width)
        gdelta[(slice(None), *at)] = delta[half:].reshape(row_count, share, LANES)
        for gather in gathers[1:]:
            gather.stage(0)

    inner_at = step - after

    @pl.when((inner_at >= 0) & (inner_at < strips))
    def _():
        strip = pl.ds(pl.multiple_of(inner_at * width, width), width)
        inner_o[0] = tn(normed[...], slope[:, strip]).astype(bf16)

    @pl.when(step == after + strips)
    def _():
        out_o[...] = tn(att[...], proj[...]).astype(bf16)
        lines = [jnp.sum(sums[n], axis=0, keepdims=True) for n in range(2)]
        lines += [jnp.sum(bias_sums[n], axis=0, keepdims=True) for n in range(strips)]
        vectors_o[...] = jnp.concatenate(lines)
        for part in fold.parts:
            part.finish(1)
        first, second = fold.held()
        outer_ab_o[...] = fold.own[first]
        outer_c_o[...] = fold.own[second]
        fold.finish()
        for gather in gathers:
            gather.finish()
        for copy in part_copies():
            copy.wait_send()
        for r in range(row_count):
            keep(r).wait()
            home(r).wait()
        for copy in leaves():
            copy.wait()


def mid(
    lengths, inputs, next_x, mixed, lse, cotangent, next_cot, globals_in, global_cot, out_weight, inner_weight, outer_weight, bias, gain, shift,
    half, count,
):
    f32, bf16 = jnp.float32, jnp.bfloat16
    row_count, rows, width = mixed.shape
    block_len = 2 * half
    share = (rows - block_len) // count
    own_rows = row_count * share
    inner_width = inner_weight.shape[1]
    strips = inner_width // width
    part = width // count
    tiles = 2 * row_count
    total = row_count * block_len + own_rows

    def flat(cols):
        def index(t):
            n = t - BACK_FROM
            return jnp.where(n <= 0, 3, jnp.where(n == 1, 1, jnp.where(n == 2, 0, 2))), 0

        return pl.BlockSpec((half, cols), index)

    own_spec = pl.BlockSpec((1, half, width), lambda t: (jnp.where(t <= 1, 0, 1), 1, 0))
    next_spec = pl.BlockSpec((1, half, width), lambda t: (jnp.where(t <= 0, 0, 1), 0, 0))
    whole = lambda *shape: pl.BlockSpec(shape, lambda t: (0,) * len(shape))
    hbm = pl.BlockSpec(memory_space=pl.ANY)
    fixeds = (gain, shift, bias, out_weight, inner_weight, outer_weight, globals_in, global_cot)
    shared = (row_count, 2, 2, 2, share)
    after = BACK_FROM + tiles
    of = jax.ShapeDtypeStruct
    outs = [
        of((row_count, block_len, width), bf16),
        of((row_count * block_len, width), f32),
        of((row_count * block_len, width), bf16),
        of((row_count * block_len, LANES), f32),
        of((row_count, share, width), f32),
        of((*shared, width), bf16),
        of((*shared, width), bf16),
        of((*shared, LANES), f32),
        of((*shared, LANES), f32),
        of((strips, width, width), bf16),
        of((2, 2, strips * part // 4, 640), bf16),
        of((2, strips * part // 2, 128), bf16),
        of((width, width), bf16),
        of((2 + strips, width), f32),
    ]
    vmem = pltpu.VMEM
    fold = Fold.scratch(strips * part // 2, width, 1, True, Fold.EARLY)
    kinds = 2 * row_count + 5
    return pl.pallas_call(
        functools.partial(mid_kernel, half, len(fold)),
        grid=(after + strips + 1,),
        in_specs=[
            pl.BlockSpec(memory_space=pltpu.SMEM),
            own_spec,
            next_spec,
            pl.BlockSpec((1, half, width), lambda t: (jnp.where(t <= 1, 0, 1), jnp.where((t == 0) | (t >= 3), 1, 0), 0)),
            own_spec,
            next_spec,
        ]
        + [hbm] * (len(fixeds) + 2),
        out_specs=[
            hbm,
            flat(width),
            flat(width),
            flat(LANES),
            whole(row_count, share, width),
            hbm,
            hbm,
            hbm,
            hbm,
            pl.BlockSpec((1, width, width), lambda t: (jnp.clip(t - after, 0, strips - 1), 0, 0)),
            whole(*outs[10].shape),
            whole(*outs[11].shape),
            whole(width, width),
            whole(2 + strips, width),
        ],
        out_shape=outs,
        scratch_shapes=[vmem((1, a.shape[0]), f32) for a in fixeds[:3]]
        + [vmem(a.shape, bf16) for a in fixeds[3:6]]
        + [vmem((row_count, share, width), bf16)] * 2
        + [
            vmem((width, LANES), bf16),
            vmem((total, inner_width), bf16),
            vmem((total, inner_width), bf16),
            vmem((total, width), bf16),
            vmem((total, width), bf16),
            vmem((total, width), bf16),
            vmem((total, width), bf16),
            vmem((total, width), f32),
            vmem((2, 2, 2, 2, strips * part // 2, width), bf16),
            vmem((2, 8, width), f32),
            vmem((strips, 8, width), f32),
            vmem((2, row_count, half, width), bf16),
            vmem((*shared, width), bf16),
            vmem((*shared, width), bf16),
            vmem((*shared, LANES), f32),
            vmem((*shared, LANES), f32),
            vmem((count, row_count, share, width), bf16),
            vmem((count, row_count, share, LANES), f32),
            pltpu.SemaphoreType.DMA((kinds, count)),
            pltpu.SemaphoreType.DMA((kinds, count)),
            pltpu.SemaphoreType.DMA((kinds + row_count + len(fixeds),)),
        ]
        + fold,
        compiler_params=pltpu.CompilerParams(
            collective_id=10, has_side_effects=True, vmem_limit_bytes=64 * 1024 * 1024
        ),
        name="mid",
    )(lengths, inputs, next_x, mixed, cotangent, next_cot, *fixeds, mixed, lse)


def key_marks(me, count, length, half, rows):
    lane = lax.broadcasted_iota(jnp.int32, (rows, LANES), 1)
    row = lax.broadcasted_iota(jnp.int32, (rows, LANES), 0)
    kind = lane - TYPE0
    side = jnp.where(row < half, 0, 1)
    owner = lax.rem(me + side, count)
    position = owner * (2 * half) + jnp.where(row < half, row + half, row - half)
    apart = (me == count - 1) & (kind < 2) & (kind != side)
    of_token = jnp.where((position >= length) | apart, NEG, 0.0)
    of_global = jnp.where((kind == 2) & (me != 0), NEG, 0.0)
    marks = jnp.where(row < 2 * half, of_token, of_global)
    return jnp.where((kind >= 0) & (kind < 3), marks, 0.0).astype(jnp.bfloat16)


def head_kernel(
    half, scale, pairs, tq,
    lengths, inputs, cotangent, globals_in, gain_in, shift_in, weight_in,
    next_x, next_cot, qkv_o, mixed_o, lse_o, normed_o, kaug_o,
    gain, shift, weight, xs, qkv, mixed, lse, normed, kaug, send, recv, local,
):
    bf16, f32 = jnp.bfloat16, jnp.float32
    step = pl.program_id(0)
    me, count = lax.axis_index("seq"), lax.axis_size("seq")
    row_count, rows, width = xs.shape
    block_len = 2 * half
    previous = {"seq": lax.rem(me + count - 1, count)}
    following = {"seq": lax.rem(me + 1, count)}
    lower, upper, tail = pl.ds(0, half), pl.ds(half, half), pl.ds(block_len, rows - block_len)
    turns = [row_count + 1 + r * (pairs + 1) for r in range(row_count)]

    def arrive(r):
        return remote(inputs.at[r, lower], xs.at[r, upper], send.at[0, r], recv.at[0, r], previous)

    def arrive_cot(r):
        return remote(cotangent.at[r, lower], next_cot.at[r], send.at[1, r], recv.at[1, r], previous)

    def loads():
        own = [(inputs.at[r, upper], xs.at[r, lower]) for r in range(row_count)]
        own += [(globals_in.at[r], xs.at[r, tail]) for r in range(row_count)]
        own += [(gain_in, gain.at[0]), (shift_in, shift.at[0]), (weight_in, weight)]
        return fetch(*zip(*own), local)

    def leaves(r):
        pairs_of = ((qkv, qkv_o), (mixed, mixed_o), (lse, lse_o), (normed, normed_o), (kaug, kaug_o))
        moved = [(a.at[r], b.at[r]) for a, b in pairs_of] + [(xs.at[r, upper], next_x.at[r])]
        return fetch(*zip(*moved), local, 16 + 8 * r)

    def project(x):
        x = x.astype(f32)
        centred = x - jnp.mean(x, axis=-1, keepdims=True)
        inv = lax.rsqrt(jnp.mean(centred * centred, axis=-1, keepdims=True) + EPS)
        n = (centred * inv * gain[...] + shift[...]).astype(bf16)
        return n, nn(n, weight[...]).astype(bf16)

    @pl.when(step == 0)
    def _():
        begin(loads())
        barrier = pltpu.get_barrier_semaphore()
        for to in (previous, following):
            pl.semaphore_signal(barrier, inc=1, device_id=to, device_id_type=MESH_ID)
        pl.semaphore_wait(barrier, 2)
        arrive(0).start()
        for r in range(row_count):
            kaug[r] = key_marks(me, count, lengths[r], half, rows)
        for copy in loads():
            copy.wait()

    for r in range(row_count):

        @pl.when(step == turns[r])
        def _():
            arrive(r).wait_recv()
            if r + 1 < row_count:
                arrive(r + 1).start()

    first = turns[0]
    is_turn = functools.reduce(jnp.logical_or, [step == t for t in turns])

    @pl.when((step < row_count) | is_turn)
    def _():
        h = jnp.where(step < row_count, 0, 1)
        r = jnp.where(step < row_count, step, lax.div(step - first, pairs + 1))
        spot = pl.ds(pl.multiple_of(h * half, half), half)
        normed[r, spot], qkv[r, spot] = project(xs[r, spot])

    @pl.when(step == row_count)
    def _():
        n, p = project(jnp.concatenate([xs[r, tail] for r in range(row_count)], axis=0))
        many = rows - block_len
        for r in range(row_count):
            normed[r, tail] = n[r * many:(r + 1) * many]
            qkv[r, tail] = p[r * many:(r + 1) * many]

    @pl.when(step == first + 4)
    def _():
        begin([arrive_cot(r) for r in range(row_count)])

    @pl.when((step > first) & jnp.logical_not(is_turn))
    def _():
        r, p = lax.div(step - first, pairs + 1), lax.rem(step - first, pairs + 1) - 1
        lane = lambda j: pl.ds(pl.multiple_of(j * width + p * LANES, LANES), LANES)
        row = pl.ds(r, 1)
        attend_kernel(
            half, scale, tq, p, qkv.at[row, :, lane(0)], qkv.at[row, :, lane(1)], qkv.at[row, :, lane(2)], kaug.at[row],
            mixed.at[row, :, lane(0)], lse.at[row],
        )

    for r in range(row_count):

        @pl.when(step == turns[r] + pairs)
        def _():
            begin(leaves(r))

    @pl.when(step == turns[-1] + pairs)
    def _():
        for r in range(row_count):
            for copy in leaves(r):
                copy.wait()
            arrive(r).wait_send()
            arrive_cot(r).wait()


def head(lengths, inputs, cotangent, globals_in, gain, shift, weight, tq):
    bf16, f32 = jnp.bfloat16, jnp.float32
    row_count, block_len, width = inputs.shape
    half = block_len // 2
    rows = block_len + globals_in.shape[1]
    pairs = width // LANES
    scale = (width // HEADS) ** (-0.5)
    hbm = pl.BlockSpec(memory_space=pl.ANY)
    of, vmem = jax.ShapeDtypeStruct, pltpu.VMEM
    results = [
        ((row_count, rows, 3 * width), bf16),
        ((row_count, rows, width), bf16),
        ((row_count, rows, LANES), f32),
        ((row_count, rows, width), bf16),
        ((row_count, rows, LANES), bf16),
    ]
    return pl.pallas_call(
        functools.partial(head_kernel, half, scale, pairs, tq),
        grid=(row_count + 1 + row_count * (pairs + 1),),
        in_specs=[pl.BlockSpec(memory_space=pltpu.SMEM)] + [hbm] * 6,
        out_specs=[hbm] * 7,
        out_shape=[of((row_count, half, width), bf16)] * 2 + [of(*r) for r in results],
        scratch_shapes=[
            vmem((1, width), f32),
            vmem((1, width), f32),
            vmem(weight.shape, bf16),
            vmem((row_count, rows, width), bf16),
        ]
        + [vmem(*r) for r in results]
        + [
            pltpu.SemaphoreType.DMA((2, row_count)),
            pltpu.SemaphoreType.DMA((2, row_count)),
            pltpu.SemaphoreType.DMA((16 + 8 * row_count,)),
        ],
        compiler_params=pltpu.CompilerParams(
            collective_id=11, has_side_effects=True, vmem_limit_bytes=60 * 1024 * 1024
        ),
        name="head",
    )(lengths, inputs, cotangent, globals_in, gain, shift, weight)


def wgrad_kernel(a_ref, b_ref, o_ref):
    o_ref[...] = tn(a_ref[...], b_ref[...]).astype(o_ref.dtype).reshape(o_ref.shape)


def wgrad(a, b, strip):
    rows, a_cols = a.shape
    b_cols = b.shape[1]
    split_a = a_cols > b_cols
    strips = max(a_cols, b_cols) // strip
    fixed = lambda n: (0, 0)
    moving = lambda n: (0, n)
    return pl.pallas_call(
        wgrad_kernel,
        grid=(strips,),
        in_specs=[
            pl.BlockSpec((rows, strip), moving if split_a else fixed),
            pl.BlockSpec((rows, strip), fixed if split_a else moving),
        ],
        out_specs=pl.BlockSpec((1, strip, strip), lambda n: (n, 0, 0)),
        out_shape=jax.ShapeDtypeStruct((strips, strip, strip), jnp.bfloat16),
        compiler_params=pltpu.CompilerParams(vmem_limit_bytes=40 * 1024 * 1024),
        name="wgrad",
    )(a, b)


def norm_parts(values):
    average = jnp.mean(values, axis=-1, keepdims=True)
    centred = values - average
    variance = jnp.mean(centred * centred, axis=-1, keepdims=True)
    inv = lax.rsqrt(variance + EPS)
    return centred * inv, inv


def norm_back(grad, n, inv, gain):
    eg = grad * gain
    through = (
        eg - jnp.mean(eg, axis=-1, keepdims=True) - n * jnp.mean(eg * n, axis=-1, keepdims=True)
    ) * inv
    return through, jnp.sum(grad * n, axis=0), jnp.sum(grad, axis=0)


def split_rows(a, count):
    row_count, rows, width = a.shape
    part = rows // count
    moved = a.reshape(row_count, count, part, width).transpose(1, 0, 2, 3)
    return moved.reshape(count, row_count * part, width)


def join_rows(a, row_count):
    count, rows, width = a.shape
    part = rows // row_count
    moved = a.reshape(count, row_count, part, width).transpose(1, 0, 2, 3)
    return moved.reshape(row_count, count * part, width)


def per_head(values, width):
    lanes = values[..., :HEADS]
    return jnp.repeat(lanes, width // HEADS, axis=-1)


def head_sums(values):
    rows, width = values.shape
    lane = jnp.arange(LANES)
    head = jnp.arange(width) // (width // HEADS)
    place = ((lane[None, :] % HEADS == head[:, None]) & (lane[None, :] < 3 * HEADS)).astype(jnp.bfloat16)
    top = values.astype(jnp.bfloat16)
    rest = (values - top.astype(jnp.float32)).astype(jnp.bfloat16)
    return nn(top, place) + nn(rest, place)


def reduce_share(a):
    a = lax.psum_scatter(a, "seq", scatter_dimension=0, tiled=True)
    return lax.psum(a.astype(jnp.bfloat16), "batch").astype(jnp.float32)


def body(
    inputs,
    global_inputs,
    lengths,
    first_gain,
    first_shift,
    qkv_weight,
    out_weight,
    second_gain,
    second_shift,
    inner_weight,
    inner_bias,
    outer_weight,
    output_cotangent,
    global_cotangent,
):
    f32, bf16 = jnp.float32, jnp.bfloat16
    row_count, block_len, width = inputs.shape
    half = block_len // 2
    global_count = global_inputs.shape[1]
    rows = block_len + global_count
    inner_width = inner_weight.shape[1]
    count = lax.axis_size("seq")
    me = lax.axis_index("seq")
    after = lax.rem(me + 1, count)
    back = [(i, (i - 1) % count) for i in range(count)]
    forth = [(i, (i + 1) % count) for i in range(count)]
    token_rows = row_count * block_len
    share = global_count // count
    own_rows = row_count * share

    if count == 8 and lax.axis_size("batch") == 4:
        next_x, next_cot, qkv, mixed, lse, normed, kaug = head(
            lengths, inputs, output_cotangent, global_inputs, first_gain, first_shift, qkv_weight, 320
        )
        (
            layer_output, residual_grad, block_grad, block_delta, own_res, global_out, global_grad, global_lse, global_delta,
            inner_wgrad, outer_ab, outer_c, out_grad, vectors,
        ) = mid(
            lengths, inputs, next_x, mixed, lse, output_cotangent, next_cot, global_inputs, global_cotangent, out_weight, inner_weight,
            outer_weight, inner_bias, second_gain, second_shift, half, count,
        )
        input_out, global_grad, *reduced = rear(
            qkv, block_grad, lse, block_delta, kaug, inputs, next_x, residual_grad, global_grad, global_lse, global_delta,
            own_res, normed, global_inputs, qkv_weight, first_gain, vectors, outer_ab, outer_c, inner_wgrad,
            out_grad, half, count,
        )
        joined = lambda a: a.reshape(row_count, global_count, width)
        inner_out, outer_out, out_out, qkv_out, *lines, layer_output, input_out, global_out, global_grad = finish(
            *reduced, layer_output, input_out, joined(global_out), joined(global_grad)
        )
        fg, fs, sg, ss, bias = lines
        return (
            layer_output, global_out, input_out, global_grad, fg, fs, qkv_out, out_out, sg, ss, inner_out, bias, outer_out,
        )

    own_globals = lax.dynamic_slice_in_dim(global_inputs, me * share, share, axis=1)
    own_global_cot = lax.dynamic_slice_in_dim(global_cotangent, me * share, share, axis=1)
    next_inputs = lax.ppermute(inputs[:, :half], "seq", back)
    next_cotangent = lax.ppermute(output_cotangent[:, :half], "seq", back)
    block = jnp.concatenate([inputs[:, half:], next_inputs], axis=1)
    spots = jnp.arange(half, dtype=jnp.int32)
    positions = jnp.concatenate([me * block_len + half + spots, after * block_len + spots])
    valid = positions[None, :] < lengths[:, None]

    kind = jnp.arange(LANES)[None, None, :] - TYPE0
    key_half = (jnp.arange(block_len) // half)[None, :, None]
    last = me == count - 1
    hidden_key = jnp.logical_not(valid)[:, :, None] | (last & (kind < 2) & (kind != key_half))
    token_marks = jnp.where(hidden_key & (kind >= 0) & (kind < 3), NEG, 0.0)
    global_marks = jnp.where((kind == 2) & (me != 0), NEG, 0.0)
    global_marks = jnp.broadcast_to(global_marks, (row_count, global_count, LANES))
    kaug = jnp.concatenate([token_marks, global_marks], axis=1).astype(bf16)

    states = jnp.concatenate([block, global_inputs], axis=1)
    n_first, inv_first = norm_parts(states.astype(f32))
    normed = (n_first * first_gain + first_shift).astype(bf16)
    qkv = nn(normed.reshape(row_count * rows, width), qkv_weight).astype(bf16)
    qkv = qkv.reshape(row_count, rows, 3 * width)

    mixed, lse = attend(qkv, kaug, half)
    tokens_in = block.reshape(token_rows, width)
    cot_block = jnp.concatenate([output_cotangent[:, half:], next_cotangent], axis=1)
    part_mixed, part_lse = spread(
        [split_rows(mixed[:, block_len:], count), split_rows(lse[:, block_len:], count)], count, False, 0
    )
    highest = jnp.max(part_lse, axis=0)
    part_weight = jnp.exp(part_lse - highest)
    total = jnp.sum(part_weight, axis=0)
    global_lse = highest + jnp.log(total)
    global_mixed = jnp.sum(per_head(part_weight / total, width) * part_mixed.astype(f32), axis=0)

    tokens = jnp.concatenate([tokens_in, own_globals.reshape(own_rows, width)]).astype(f32)
    cot_block = jnp.where(valid[:, :, None], cot_block, 0)
    cotangent = jnp.concatenate(
        [cot_block.reshape(token_rows, width), own_global_cot.reshape(own_rows, width)]
    )
    attended = jnp.concatenate(
        [mixed[:, :block_len].reshape(token_rows, width), global_mixed.astype(bf16)]
    )
    residual = tokens + nn(attended, out_weight)
    n_second, inv_second = norm_parts(residual)
    normed_second = (n_second * second_gain + second_shift).astype(bf16)
    inner = nn(normed_second, inner_weight) + inner_bias
    bell = jnp.exp(-0.5 * inner * inner)
    cdf = 0.5 * (1.0 + lax.erf(inner * (0.5 ** 0.5)))
    hidden = (inner * cdf).astype(bf16)
    final = residual + nn(hidden, outer_weight)
    hidden_grad = nt(cotangent, outer_weight)
    slope = cdf + inner * bell * ((0.5 / jnp.pi) ** 0.5)
    inner_grad = (hidden_grad * slope).astype(bf16)
    second_grad = nt(inner_grad, inner_weight)
    through, second_gain_grad, second_shift_grad = norm_back(second_grad, n_second, inv_second, second_gain)
    residual_grad = cotangent.astype(f32) + through
    projection_grad = residual_grad.astype(bf16)
    attended_grad = nt(projection_grad, out_weight).astype(bf16)
    delta = head_sums(attended_grad.astype(f32) * attended.astype(f32))
    outer_grad = wgrad(hidden, cotangent, width)
    inner_wgrad = wgrad(normed_second, inner_grad, width)
    bias_grad = jnp.sum(inner_grad.astype(f32), axis=0)
    out_grad = wgrad(attended, projection_grad, width)

    all_grad, all_lse, all_delta = spread(
        [attended_grad[token_rows:], global_lse, delta[token_rows:]], count, True, 1
    )
    block_grad = jnp.concatenate(
        [attended_grad[:token_rows].reshape(row_count, block_len, width), join_rows(all_grad, row_count)], axis=1
    )
    block_lse = jnp.concatenate([lse[:, :block_len], join_rows(all_lse, row_count)], axis=1)
    block_delta = jnp.concatenate(
        [delta[:token_rows].reshape(row_count, block_len, LANES), join_rows(all_delta, row_count)], axis=1
    )
    layer = final[:token_rows].reshape(row_count, block_len, width)
    layer = jnp.where(valid[:, :, None], layer, 0.0).astype(bf16)
    layer_output = jnp.concatenate([lax.ppermute(layer[:, half:], "seq", forth), layer[:, :half]], axis=1)
    own_out = final[token_rows:].astype(bf16)
    part = width // count
    dqkv = jnp.concatenate(attend_back(qkv, block_grad, block_lse, block_delta, kaug, half, rows), axis=-1)
    (part_dqkv,) = spread([split_rows(dqkv[:, block_len:], count)], count, False, 2)
    global_dqkv = jnp.sum(part_dqkv.astype(f32), axis=0).astype(bf16)
    qkv_grad = jnp.concatenate([dqkv[:, :block_len].reshape(token_rows, 3 * width), global_dqkv])

    first_grad = nt(qkv_grad, qkv_weight)
    n_tokens, inv_tokens = norm_parts(tokens)
    through, first_gain_grad, first_shift_grad = norm_back(first_grad, n_tokens, inv_tokens, first_gain)
    input_grad = (residual_grad + through).astype(bf16)
    normed_tokens = (n_tokens * first_gain + first_shift).astype(bf16)
    qkv_wgrad = wgrad(normed_tokens, qkv_grad, width)

    grad_block = input_grad[:token_rows].reshape(row_count, block_len, width)
    input_out = jnp.concatenate(
        [lax.ppermute(grad_block[:, half:], "seq", forth), grad_block[:, :half]], axis=1
    )
    global_final, global_grad = spread([own_out, input_grad[token_rows:]], count, True, 3)

    def shares(a):
        return a.reshape(count, a.shape[0] // count)

    small = jnp.concatenate(
        [
            shares(first_gain_grad),
            shares(first_shift_grad),
            shares(second_gain_grad),
            shares(second_shift_grad),
            shares(bias_grad),
        ],
        axis=1,
    )
    inner_out = reduce_share(inner_wgrad.transpose(1, 0, 2).reshape(width, -1))
    outer_out = reduce_share(outer_grad.reshape(inner_width, width))
    out_out = reduce_share(out_grad[0])
    qkv_out = reduce_share(qkv_wgrad.transpose(1, 0, 2).reshape(width, -1))
    small = reduce_share(small)[0]
    return (
        layer_output,
        join_rows(global_final, row_count),
        input_out,
        join_rows(global_grad, row_count),
        small[:part],
        small[part:2 * part],
        qkv_out,
        out_out,
        small[2 * part:3 * part],
        small[3 * part:4 * part],
        inner_out,
        small[4 * part:],
        outer_out,
    )


def solution(mesh):
    rows = P("batch", "seq", None)
    globals_at = P("batch", None, None)
    return jax.shard_map(
        body,
        mesh=mesh,
        in_specs=(rows, globals_at, P("batch")) + (P(),) * 9 + (rows, globals_at),
        out_specs=(
            rows,
            globals_at,
            rows,
            globals_at,
            P("seq"),
            P("seq"),
            P("seq", None),
            P("seq", None),
            P("seq"),
            P("seq"),
            P("seq", None),
            P("seq"),
            P("seq", None),
        ),
        check_vma=False,
    )
```
